32 devices in a mesh: groups: 2 (over y), dom: 8 (over z, x), edge: 2 (over core).
Axes of the slice: x: 2, y: 2, z: 4, core: 2. Of those that a mesh axis runs over, the one named last changes fastest.
Arguments:
- entities: float32 [400, 4096], P(None, ('groups', 'dom')), parts along dimension 1, may hold values from -2.5 to 2.5
- entity_state: float32 [4096], P(('groups', 'dom')), parts along dimension 0, may hold values from 0.1 to 1
- relations: float32 [400, 4096], P(None, 'groups'), parts along dimension 1, may hold values from -4 to 4
- relation_state: float32 [4096], P('groups'), parts along dimension 0, may hold values from 0.1 to 1
- src_rows: int32 [6, 128, 128], P(None, ('groups', 'dom', 'edge')), parts along dimension 1, may hold values from 0 to 255
- rel_ids: int32 [6, 128, 128], P(None, ('groups', 'dom', 'edge')), parts along dimension 1, may hold values from 0 to 2047
- dst_rows: int32 [6, 128, 128], P(None, ('groups', 'dom', 'edge')), parts along dimension 1, may hold values from 0 to 255
- counts: int32 [6, 128], P(None, ('groups', 'dom', 'edge')), parts along dimension 1, may hold values from 1 to 128
- neg_blocks: int32 [6, 128], P(None, ('groups', 'dom', 'edge')), parts along dimension 1, may hold values from 0 to 3
Outputs:
- new_entities: float32 [400, 4096], P(None, ('groups', 'dom')), parts along dimension 1
- new_entity_state: float32 [4096], P(('groups', 'dom')), parts along dimension 0
- new_relations: float32 [400, 4096], P(None, 'groups'), parts along dimension 1
- new_relation_state: float32 [4096], P('groups'), parts along dimension 0
The draws below stay inside these ranges and needn't reach their ends.
There are 2 independent parts, one for each index of `groups`. The reference program is written for one: setup_inputs(seed, part) draws one part's arguments, and reference() takes and returns one part's arrays. A program takes and returns all parts, laid end to end along the dimension named above; each array names one. Nothing has to cross between parts.
All inputs are finite; a program needn't handle non-finite values.
Results may differ from the reference program's by a relative error of at most 0.0024.
Values may be sent and summed in bfloat16 or wider, within the bound.
No kernel may reach another device: no remote copies, remote signals or barrier semaphores. Data moves between devices by JAX's collectives and lax.ppermute only.
A program may use at most 128 MiB of HBM per device.

```python
import math
import jax
import jax.numpy as jnp
import numpy as np
from jax import lax

DIM = 400
RELS = 2048
ROWS_DEV = 256
BLK_E = 4
EDGE_BLOCK = 128
ROUNDS = 6
ENTITIES = 2048
BLOCKS = 64
N_DOM = 8
N_EDGE = 2


def touch_ends(result, key, low, high):
    longest = result.shape.index(max(result.shape))
    spots = []
    for shift in (0, 1):
        where = [jax.random.randint(jax.random.fold_in(key, axis), (), 0, length) for axis, length in enumerate(result.shape)]
        where[longest] = (where[longest] + shift) % result.shape[longest]
        spots.append(tuple(where))
    return result.at[spots[0]].set(low).at[spots[1]].set(high)


def block_levels(stream_key, extent, shards, low, top_value):
    def one(axis_at, blocks):
        steps = jax.random.uniform(jax.random.fold_in(jax.random.fold_in(stream_key, 6), axis_at), (blocks,), jnp.float32, low / len(shards), top_value / len(shards))
        return jnp.repeat(jnp.exp(steps), extent[axis_at] // blocks).reshape((-1,) + (1,) * (len(extent) - axis_at - 1))

    gain = one(*shards[0])
    for cut in shards[1:]:
        gain = gain * one(*cut)
    return gain


def rank_table(amount, slope):
    weights = [(1 << 20) // math.isqrt(grade ** slope) + 1 for grade in range(1, amount + 1)]
    scale = 1 + sum(weights) // (1 << 30)
    return np.cumsum(np.array([max(1, weight // scale) for weight in weights]))


def ranked(own_key, dims, number_of, slope):
    table = rank_table(number_of, slope)
    pick = jax.random.randint(jax.random.fold_in(own_key, 1), dims, 0, int(table[number_of - 1]))
    grade = jnp.searchsorted(jnp.asarray(table, jnp.int32), pick, side="right")
    return jax.random.permutation(jax.random.fold_in(own_key, 2), number_of)[grade].astype(jnp.int32)


def scatter_about(key, extent, scale, bound, cuts=(), held_as=jnp.bfloat16):
    level = block_levels(key, extent, cuts, -0.22, 0.18) if cuts else 1.0
    drawn = jax.random.normal(key, extent, jnp.float32) * scale * level
    return jnp.minimum(jnp.maximum(drawn, -bound), bound).astype(held_as)


def setup_inputs(seed: int = 0, part: int = 0) -> dict:
    key_of = jax.random.split(jax.random.key(seed), 10)
    part_keys = jax.random.split(jax.random.fold_in(key_of[9], part), 10)
    entities = scatter_about(part_keys[0], (DIM, ENTITIES), 0.3, 2.5, ((1, 8),), jnp.float32)
    entity_state = jnp.clip(jnp.exp(math.log(1.0) - 2.3025851 * jax.random.uniform(part_keys[1], (ENTITIES,), jnp.float32) ** block_levels(part_keys[1], (ENTITIES,), ((0, 8),), -0.2, 0.2)), 0.1, 1.0)
    relations = scatter_about(part_keys[2], (DIM, RELS), 1.0, 4.0, (), jnp.float32)
    relation_state = jnp.clip(jnp.exp(jax.random.uniform(part_keys[3], (RELS,), jnp.float32, math.log(0.1), math.log(1.0))), 0.1, 1.0)
    src_rows = touch_ends(jax.random.randint(part_keys[4], (ROUNDS, BLOCKS, EDGE_BLOCK), 0, ROWS_DEV), jax.random.fold_in(part_keys[4], 1), 0, ROWS_DEV - 1).astype(jnp.int32)
    rel_ids = touch_ends(ranked(part_keys[5], (ROUNDS, BLOCKS, EDGE_BLOCK), RELS, 2), jax.random.fold_in(part_keys[5], 3), 0, RELS - 1).astype(jnp.int32)
    dst_rows = touch_ends(jax.random.randint(part_keys[6], (ROUNDS, BLOCKS, EDGE_BLOCK), 0, ROWS_DEV), jax.random.fold_in(part_keys[6], 1), 0, ROWS_DEV - 1).astype(jnp.int32)
    counts = touch_ends(jax.random.randint(part_keys[7], (ROUNDS, BLOCKS), 1, EDGE_BLOCK + 1), jax.random.fold_in(part_keys[7], 1), 1, EDGE_BLOCK).astype(jnp.int32)
    neg_blocks = touch_ends(jax.random.randint(part_keys[8], (ROUNDS, BLOCKS), 0, BLK_E), jax.random.fold_in(part_keys[8], 1), 0, BLK_E - 1).astype(jnp.int32)
    return dict(entities=entities, entity_state=entity_state, relations=relations, relation_state=relation_state, src_rows=src_rows, rel_ids=rel_ids, dst_rows=dst_rows, counts=counts, neg_blocks=neg_blocks)


learn_rate = 0.1

def block_terms(src_table, dst_table, rel_table, src_idx, rel_idx, dst_idx, valid_count, negative, rel_total):
    half_dim = src_table.shape[0] // 2
    source = src_table[:, src_idx].astype(jnp.float32)
    target = dst_table[:, dst_idx].astype(jnp.float32)
    relvec = rel_table[:, rel_idx].astype(jnp.float32)
    query_re = source[:half_dim] * relvec[:half_dim] - source[half_dim:] * relvec[half_dim:]
    query_im = source[:half_dim] * relvec[half_dim:] + source[half_dim:] * relvec[:half_dim]
    query_lo = jnp.concatenate([query_re, query_im], axis=0).astype(jnp.bfloat16)
    query_f = query_lo.astype(jnp.float32)
    slots = jnp.arange(src_idx.shape[1], dtype=jnp.int32)
    valid = (slots[None, :] < valid_count[:, None]).astype(jnp.float32)
    neg_valid = valid[negative]
    neg_target = target[:, negative, :]
    positive = lax.optimization_barrier(jnp.sum(query_f * target, axis=0))
    scores = jnp.einsum('dbi,dbj->bij', query_f, neg_target, precision=lax.Precision.HIGHEST)
    grad_pos = -jax.nn.sigmoid(-positive) * valid
    weight = (jax.nn.sigmoid(scores) * valid[:, :, None] * neg_valid[:, None, :] / src_idx.shape[1]).astype(jnp.bfloat16)
    weight_f = weight.astype(jnp.float32)
    dquery = grad_pos[None] * target + jnp.einsum('bij,dbj->dbi', weight_f, neg_target, precision=lax.Precision.HIGHEST)
    dpos = grad_pos[None] * query_f
    dneg = jnp.einsum('bij,dbi->dbj', weight_f, query_f, precision=lax.Precision.HIGHEST)
    dq_re, dq_im = (dquery[:half_dim], dquery[half_dim:])
    dsource = jnp.concatenate([dq_re * relvec[:half_dim] + dq_im * relvec[half_dim:], dq_im * relvec[:half_dim] - dq_re * relvec[half_dim:]], axis=0)
    drelation = jnp.concatenate([dq_re * source[:half_dim] + dq_im * source[half_dim:], dq_im * source[:half_dim] - dq_re * source[half_dim:]], axis=0)
    width = src_table.shape[0]
    rows = src_table.shape[1]
    grad_src = jnp.zeros((width, rows), jnp.float32).at[:, src_idx.reshape(-1)].add(dsource.reshape(width, -1))
    grad_dst = jnp.zeros((width, rows), jnp.float32).at[:, dst_idx.reshape(-1)].add(dpos.reshape(width, -1))
    grad_dst = grad_dst.at[:, dst_idx[negative].reshape(-1)].add(dneg.reshape(width, -1))
    rel_total = rel_total.at[:, rel_idx.reshape(-1)].add(drelation.reshape(width, -1))
    return (grad_src, grad_dst, rel_total)

def reference(entities, entity_state, relations, relation_state, src_rows, rel_ids, dst_rows, counts, neg_blocks):
    parts = N_DOM
    per_part = BLK_E * N_EDGE
    rel16 = relations.astype(jnp.bfloat16)
    offset = jnp.arange(per_part, dtype=jnp.int32) // BLK_E * BLK_E
    rel_grad = jnp.zeros((DIM, RELS), jnp.float32)
    embedding = entities
    state = entity_state
    for round_index in range(ROUNDS):
        tables = embedding.astype(jnp.bfloat16).reshape(DIM, parts, ROWS_DEV).transpose(1, 0, 2)
        dest_tables = jnp.roll(tables, -round_index, axis=0)
        items = (tables, dest_tables, src_rows[round_index].reshape(parts, per_part, EDGE_BLOCK), rel_ids[round_index].reshape(parts, per_part, EDGE_BLOCK), dst_rows[round_index].reshape(parts, per_part, EDGE_BLOCK), counts[round_index].reshape(parts, per_part), neg_blocks[round_index].reshape(parts, per_part) + offset[None, :])

        def visit(carry, item):
            grad_src, grad_dst, carry = block_terms(item[0], item[1], rel16, item[2], item[3], item[4], item[5], item[6], carry)
            return (carry, (grad_src, grad_dst))
        rel_grad, (src_grads, dst_grads) = lax.scan(visit, rel_grad, items)
        total = src_grads + jnp.roll(dst_grads, round_index, axis=0)
        grad = total.transpose(1, 0, 2).reshape(DIM, parts * ROWS_DEV)
        state = state + lax.optimization_barrier(jnp.mean(grad * grad, axis=0))
        embedding = embedding - learn_rate * grad / jnp.sqrt(state)[None, :]
    rel_state = relation_state + lax.optimization_barrier(jnp.mean(rel_grad * rel_grad, axis=0))
    rel_new = relations - learn_rate * rel_grad / jnp.sqrt(rel_state)[None, :]
    return (embedding, state, rel_new, rel_state)
```

```python
import functools

import jax
import jax.numpy as jnp
from jax import lax
from jax.experimental import pallas as pl
from jax.experimental.pallas import tpu as pltpu
from jax.sharding import PartitionSpec as P

learn_rate = 0.1
BF = jnp.bfloat16
F32 = jnp.float32
VMEM_LIMIT = 40 * 1024 * 1024
NN = (((1,), (0,)), ((), ()))
NT = (((1,), (1,)), ((), ()))
TN = (((0,), (0,)), ((), ()))


def mm(a, b, dims=NN):
    return lax.dot_general(a, b, dims, preferred_element_type=F32)


def vmem():
    return pl.BlockSpec(memory_space=pltpu.VMEM)


def smem():
    return pl.BlockSpec(memory_space=pltpu.SMEM)


def cost(flops, size):
    return pl.CostEstimate(flops=flops, bytes_accessed=size, transcendentals=0)


def params():
    return pltpu.CompilerParams(vmem_limit_bytes=VMEM_LIMIT)


def shifted(x, by):
    n = lax.axis_size("dom")
    return lax.ppermute(x, "dom", [(i, (i + by) % n) for i in range(n)])


def across(x):
    return lax.ppermute(x, "edge", [(0, 1), (1, 0)])


def shifted_across(x, by):
    n = lax.axis_size("dom")
    pairs = [(2 * i + c, 2 * ((i + by) % n) + 1 - c) for i in range(n) for c in range(2)]
    return lax.ppermute(x, ("dom", "edge"), pairs)


def one_hot(rows_ref, t, count, base):
    blocks, width = rows_ref.shape[1:]
    at = lax.broadcasted_iota(jnp.int32, (count, width), 0)
    idx = rows_ref[t]
    return jnp.concatenate(
        [
            jnp.where(at == base(idx[b : b + 1, :]), 1.0, 0.0).astype(BF)
            for b in range(blocks)
        ],
        axis=1,
    )


def relvec_kernel(t, ids_ref, rel_ref, out_ref, acc):
    step = pl.program_id(0)
    tile = rel_ref.shape[1]
    hot = one_hot(ids_ref, t, tile, lambda i: i - step * tile)
    part = mm(rel_ref[...].astype(BF), hot)

    @pl.when(step == 0)
    def _():
        acc[...] = part

    @pl.when(step > 0)
    def _():
        acc[...] += part

    @pl.when(step == pl.num_programs(0) - 1)
    def _():
        out_ref[...] = acc[...].astype(BF)


def relvec(t, rel_ids, relations):
    width, rels = relations.shape
    slots = rel_ids.shape[1] * rel_ids.shape[2]
    tile = min(rels, 512)
    return pl.pallas_call(
        functools.partial(relvec_kernel, t),
        grid=(rels // tile,),
        in_specs=[
            pl.BlockSpec(rel_ids.shape, lambda i: (0, 0, 0)),
            pl.BlockSpec((width, tile), lambda i: (0, i)),
        ],
        out_specs=pl.BlockSpec((width, slots), lambda i: (0, 0)),
        out_shape=jax.ShapeDtypeStruct((width, slots), BF),
        scratch_shapes=[pltpu.VMEM((width, slots), F32)],
        compiler_params=params(),
        cost_estimate=cost(2 * width * rels * slots, 4 * width * rels),
        name="relvec",
    )(rel_ids, relations)


def relsum_kernel(t, first, ids_ref, drel_ref, *refs):
    step = pl.program_id(0)
    out_ref = refs[-1]
    tile = out_ref.shape[1]
    hot = one_hot(ids_ref, t, tile, lambda i: i - step * tile)
    part = mm(drel_ref[...], hot, NT)
    out_ref[...] = part if first else refs[0][...] + part


def relsum(t, rel_ids, drel, acc, rels):
    width, slots = drel.shape
    tile = min(rels, 512)
    wide = pl.BlockSpec((width, tile), lambda i: (0, i))
    ins = [rel_ids, drel] + ([] if acc is None else [acc])
    return pl.pallas_call(
        functools.partial(relsum_kernel, t, acc is None),
        grid=(rels // tile,),
        in_specs=[
            pl.BlockSpec(rel_ids.shape, lambda i: (0, 0, 0)),
            pl.BlockSpec((width, slots), lambda i: (0, 0)),
        ]
        + ([] if acc is None else [wide]),
        out_specs=wide,
        out_shape=jax.ShapeDtypeStruct((width, rels), F32),
        input_output_aliases={} if acc is None else {2: 0},
        compiler_params=params(),
        cost_estimate=cost(2 * width * rels * slots, 8 * width * rels),
        name="relsum",
    )(*ins)


def edge_kernel(t, me_ref, src_ref, dst_ref, cnt_ref, neg_ref, rel_ref, *refs):
    first = t == 0
    blocks, width = src_ref.shape[1:]
    if first:
        (ent_ref, g_mine, g_other, drel_ref, o_scr, d_scr) = refs
        half = ent_ref.shape[1] // 2
    else:
        (own0, own1, far0, far1, gs_mine, gs_other, gd_mine, gd_other, drel_ref, o_scr, d_scr) = refs
        half = own0.shape[1]
    rows = 2 * half
    edge = me_ref[1]
    dim = o_scr.shape[0]
    hd = dim // 2

    if first:
        table = jnp.concatenate(
            [
                ent_ref[:, pl.ds(pl.multiple_of(h * half, half), half)].astype(BF)
                for h in (edge, 1 - edge)
            ],
            axis=1,
        )
        far = table
    else:
        table = jnp.concatenate([own0[...], own1[...]], axis=1)
        far = jnp.concatenate([far0[...], far1[...]], axis=1)

    def local(idx):
        moved = idx + edge * half
        return jnp.where(moved >= rows, moved - rows, moved)

    s_hot = one_hot(src_ref, t, rows, local)
    d_hot = one_hot(dst_ref, t, rows, local)
    source = mm(table, s_hot)
    target = mm(far, d_hot)
    o_scr[...] = target.astype(BF)
    rel = rel_ref[...].astype(F32)
    s_re, s_im, w_re, w_im = source[:hd], source[hd:], rel[:hd], rel[hd:]
    query = jnp.concatenate([s_re * w_re - s_im * w_im, s_re * w_im + s_im * w_re], axis=0).astype(BF)
    query_f = query.astype(F32)
    pos = jnp.sum(query_f * target, axis=0, keepdims=True)
    lane = lax.broadcasted_iota(jnp.int32, (1, width), 1)
    valid = jnp.concatenate(
        [jnp.where(lane < cnt_ref[t, b], 1.0, 0.0) for b in range(blocks)], axis=1
    )
    gpos = -jax.nn.sigmoid(-pos) * valid
    d_scr[...] = gpos * query_f
    row_j = lax.broadcasted_iota(jnp.int32, (width, width), 0)
    col_i = lax.broadcasted_iota(jnp.int32, (width, width), 1)
    dq = []
    for b in range(blocks):
        lo = b * width
        nb = neg_ref[t, b]
        at = pl.ds(pl.multiple_of(nb * width, width), width)
        neg = o_scr[:, at]
        qb = query[:, lo : lo + width]
        scores = mm(neg, qb, TN)
        keep = jnp.logical_and(row_j < cnt_ref[t, nb], col_i < cnt_ref[t, b])
        weight = jnp.where(keep, jax.nn.sigmoid(scores) / width, 0.0).astype(BF)
        dq.append(gpos[:, lo : lo + width] * target[:, lo : lo + width] + mm(neg, weight))
        d_scr[:, at] += mm(qb, weight, NT)
    dq = jnp.concatenate(dq, axis=1)
    dq_re, dq_im = dq[:hd], dq[hd:]
    drel_ref[...] = jnp.concatenate(
        [dq_re * s_re + dq_im * s_im, dq_im * s_re - dq_re * s_im], axis=0
    ).astype(BF)
    dsource = jnp.concatenate(
        [dq_re * w_re + dq_im * w_im, dq_im * w_re - dq_re * w_im], axis=0
    ).astype(BF)
    gs = mm(dsource, s_hot, NT)
    gd = mm(d_scr[...].astype(BF), d_hot, NT)
    if first:
        total = gs + gd
        g_mine[...] = total[:, :half]
        g_other[...] = total[:, half:].astype(BF)
    else:
        gs_mine[...] = gs[:, :half]
        gs_other[...] = gs[:, half:].astype(BF)
        gd_mine[...] = gd[:, :half].astype(BF)
        gd_other[...] = gd[:, half:].astype(BF)


def edge_round(t, me, src, dst, cnt, neg, rel, tables):
    dim, slots = rel.shape
    rows = sum(x.shape[1] for x in tables[:2])
    half = rows // 2
    lo = jax.ShapeDtypeStruct((dim, half), BF)
    hi = jax.ShapeDtypeStruct((dim, half), F32)
    outs = ([hi, lo] if t == 0 else [hi, lo, lo, lo]) + [jax.ShapeDtypeStruct((dim, slots), BF)]
    return pl.pallas_call(
        functools.partial(edge_kernel, t),
        in_specs=[smem(), vmem(), vmem(), smem(), smem(), vmem()] + [vmem()] * len(tables),
        out_specs=[vmem()] * len(outs),
        out_shape=outs,
        scratch_shapes=[pltpu.VMEM((dim, slots), BF), pltpu.VMEM((dim, slots), F32)],
        compiler_params=params(),
        cost_estimate=cost(8 * dim * rows * slots, 12 * dim * slots),
        name="edges",
    )(me, src, dst, cnt, neg, rel, *tables)


def update_kernel(t, me_ref, ent_ref, state_ref, *refs):
    grads, (ent_out, state_out, low_out) = refs[:-3], refs[-3:]
    half = ent_out.shape[1]
    if t == 0:
        at = pl.ds(pl.multiple_of(me_ref[1] * half, half), half)
        ent, state = ent_ref[:, at], state_ref[:, at]
    else:
        ent, state = ent_ref[...], state_ref[...]
    grad = grads[0][...].astype(F32)
    for g in grads[1:]:
        grad = grad + g[...].astype(F32)
    state = state + jnp.sum(grad * grad, axis=0, keepdims=True) / grad.shape[0]
    new = ent - learn_rate * grad / jnp.sqrt(state)
    ent_out[...] = new
    state_out[...] = state
    low_out[...] = new.astype(BF)


def update(t, me, ent, state, grads):
    dim, half = grads[0].shape
    return pl.pallas_call(
        functools.partial(update_kernel, t),
        in_specs=[smem()] + [vmem()] * (2 + len(grads)),
        out_specs=[vmem()] * 3,
        out_shape=[
            jax.ShapeDtypeStruct((dim, half), F32),
            jax.ShapeDtypeStruct((1, half), F32),
            jax.ShapeDtypeStruct((dim, half), BF),
        ],
        compiler_params=params(),
        cost_estimate=cost(10 * dim * half, 16 * dim * half),
        name="update",
    )(me, ent, state, *grads)


def pieces_kernel(t, n, me_ref, ids_ref, drel_ref, acc_ref, *refs):
    outs, total = refs[:-1], refs[-1]
    slots = drel_ref.shape[1]
    rels = total.shape[1]
    tile = min(rels, 512)
    drel = drel_ref[...]
    for lo in range(0, rels, tile):
        hot = one_hot(ids_ref, t, tile, lambda i, lo=lo: i - lo)
        total[:, lo : lo + tile] = acc_ref[:, lo : lo + tile] + mm(drel, hot, NT)
    w = outs[0].shape[1]
    for k in range(n):
        owner = lax.rem(me_ref[0] + k, n)
        for c in range(2):
            core = me_ref[1] if c == 0 else 1 - me_ref[1]
            at = pl.ds(pl.multiple_of((2 * owner + core) * w, w), w)
            outs[c * n + k][...] = total[:, at].astype(BF)


def pieces(t, n, me, rel_ids, drel, acc):
    dim, rels = acc.shape
    w = rels // (2 * n)
    return pl.pallas_call(
        functools.partial(pieces_kernel, t, n),
        in_specs=[smem()] + [vmem()] * 3,
        out_specs=[vmem()] * (2 * n),
        out_shape=[jax.ShapeDtypeStruct((dim, w), BF)] * (2 * n),
        scratch_shapes=[pltpu.VMEM((dim, rels), F32)],
        compiler_params=params(),
        cost_estimate=cost(2 * dim * rels * drel.shape[1], 8 * dim * rels),
        name="pieces",
    )(me, rel_ids, drel, acc)


def add_kernel(n, *refs):
    for k in range(n):
        refs[2 * n + k][...] = (refs[k][...].astype(F32) + refs[n + k][...].astype(F32)).astype(BF)


def add_pairs(mine, theirs):
    n = len(mine)
    return pl.pallas_call(
        functools.partial(add_kernel, n),
        in_specs=[vmem()] * (2 * n),
        out_specs=[vmem()] * n,
        out_shape=[jax.ShapeDtypeStruct(x.shape, BF) for x in mine],
        compiler_params=params(),
        name="add_pairs",
    )(*mine, *theirs)


def sum_kernel(*refs):
    total = refs[0][...].astype(F32)
    for r in refs[1:-1]:
        total = total + r[...].astype(F32)
    refs[-1][...] = total.astype(BF)


def sum_all(parts):
    return pl.pallas_call(
        sum_kernel,
        in_specs=[vmem()] * len(parts),
        out_specs=vmem(),
        out_shape=jax.ShapeDtypeStruct(parts[0].shape, BF),
        compiler_params=params(),
        name="sum_all",
    )(*parts)


def relnew_kernel(n, me_ref, rel_ref, state_ref, *refs):
    got, (rel_out, state_out) = refs[:-2], refs[-2:]
    w = got[0].shape[1]
    for k in range(n):
        owner = lax.rem(me_ref[0] + n - k, n)
        for c in range(2):
            core = me_ref[1] if c == 0 else 1 - me_ref[1]
            at = pl.ds(pl.multiple_of((2 * owner + core) * w, w), w)
            grad = got[c * n + k][...].astype(F32)
            state = state_ref[:, at] + jnp.sum(grad * grad, axis=0, keepdims=True) / grad.shape[0]
            state_out[:, at] = state
            rel_out[:, at] = rel_ref[:, at] - learn_rate * grad / jnp.sqrt(state)


def relnew(n, me, relations, state, got):
    dim, rels = relations.shape
    return pl.pallas_call(
        functools.partial(relnew_kernel, n),
        in_specs=[smem()] + [vmem()] * (2 + len(got)),
        out_specs=[vmem()] * 2,
        out_shape=[jax.ShapeDtypeStruct((dim, rels), F32), jax.ShapeDtypeStruct((1, rels), F32)],
        compiler_params=params(),
        name="relnew",
    )(me, relations, state, *got)


def relation_update(t, me, rel_ids, drel, acc, relations, state):
    n = lax.axis_size("dom")
    dim, rels = relations.shape
    if rels % (256 * n):
        total = relsum(t, rel_ids, drel, acc, rels)
        total = lax.psum(total, ("dom", "edge"))
        state = state + jnp.mean(total * total, axis=0)
        return relations - learn_rate * total / jnp.sqrt(state)[None, :], state
    parts = pieces(t, n, me, rel_ids, drel, acc)
    mine, other = parts[:n], parts[n:]
    theirs = [across(x) for x in other]
    mine = add_pairs(mine, theirs)
    summed = sum_all([mine[0]] + [shifted(mine[k], k) for k in range(1, n)])
    got = [summed] + [shifted(summed, k) for k in range(1, n)]
    got = got + [across(x) for x in got]
    rel_new, state_new = relnew(n, me, relations, state.reshape(1, rels), got)
    return rel_new, state_new.reshape(rels)


def on_device(
    entities,
    entity_state,
    relations,
    relation_state,
    src_rows,
    rel_ids,
    dst_rows,
    counts,
    neg_blocks,
):
    rounds = src_rows.shape[0]
    rels = relations.shape[1]
    me = jnp.stack([lax.axis_index("dom"), lax.axis_index("edge")]).astype(jnp.int32)
    ent, state = entities, entity_state.reshape(1, -1)
    tables = (entities,) * 1
    acc = None
    for t in range(rounds):
        rel = relvec(t, rel_ids, relations)
        if t == 0:
            g_mine, g_other, drel = edge_round(t, me, src_rows, dst_rows, counts, neg_blocks, rel, tables)
            grads = [g_mine, across(g_other)]
        else:
            gs_mine, gs_other, gd_mine, gd_other, drel = edge_round(
                t, me, src_rows, dst_rows, counts, neg_blocks, rel, tables
            )
            grads = [gs_mine, across(gs_other), shifted(gd_mine, t), shifted_across(gd_other, t)]
        if t < rounds - 1:
            acc = relsum(t, rel_ids, drel, acc, rels)
        ent, state, low = update(t, me, ent, state, grads)
        if t < rounds - 1:
            tables = (low, across(low), shifted(low, -t - 1), shifted_across(low, -t - 1))
    rel_new, rel_state = relation_update(
        rounds - 1, me, rel_ids, drel, acc, relations, relation_state
    )
    first = lax.axis_index("edge") == 0
    ent_there, state_there = across(ent), across(state)
    ent = jnp.where(
        first,
        jnp.concatenate([ent, ent_there], axis=1),
        jnp.concatenate([ent_there, ent], axis=1),
    )
    state = jnp.where(
        first,
        jnp.concatenate([state, state_there], axis=1),
        jnp.concatenate([state_there, state], axis=1),
    )
    return (ent, state.reshape(-1), rel_new, rel_state)


def solution(mesh):
    return jax.shard_map(
        on_device,
        mesh=mesh,
        in_specs=(
            P(None, ("groups", "dom")),
            P(("groups", "dom")),
            P(None, "groups"),
            P("groups"),
            P(None, ("groups", "dom", "edge"), None),
            P(None, ("groups", "dom", "edge"), None),
            P(None, ("groups", "dom", "edge"), None),
            P(None, ("groups", "dom", "edge")),
            P(None, ("groups", "dom", "edge")),
        ),
        out_specs=(
            P(None, ("groups", "dom")),
            P(("groups", "dom")),
            P(None, "groups"),
            P("groups"),
        ),
        check_vma=False,
    )
```

```python
import functools

import jax
import jax.numpy as jnp
from jax import lax
from jax.experimental import pallas as pl
from jax.experimental.pallas import tpu as pltpu
from jax.sharding import PartitionSpec as P

learn_rate = 0.1
BF = jnp.bfloat16
F32 = jnp.float32
VMEM_LIMIT = 40 * 1024 * 1024
NN = (((1,), (0,)), ((), ()))
NT = (((1,), (1,)), ((), ()))
TN = (((0,), (0,)), ((), ()))


def mm(a, b, dims=NN):
    return lax.dot_general(a, b, dims, preferred_element_type=F32)


def vmem():
    return pl.BlockSpec(memory_space=pltpu.VMEM)


def smem():
    return pl.BlockSpec(memory_space=pltpu.SMEM)


def cost(flops, size):
    return pl.CostEstimate(flops=flops, bytes_accessed=size, transcendentals=0)


def params():
    return pltpu.CompilerParams(vmem_limit_bytes=VMEM_LIMIT)


def shifted(x, by):
    n = lax.axis_size("dom")
    return lax.ppermute(x, "dom", [(i, (i + by) % n) for i in range(n)])


def across(x):
    return lax.ppermute(x, "edge", [(0, 1), (1, 0)])


def shifted_across(x, by):
    n = lax.axis_size("dom")
    pairs = [(2 * i + c, 2 * ((i + by) % n) + 1 - c) for i in range(n) for c in range(2)]
    return lax.ppermute(x, ("dom", "edge"), pairs)


def one_hot(rows_ref, t, count, base):
    blocks, width = rows_ref.shape[1:]
    at = lax.broadcasted_iota(jnp.int32, (count, width), 0)
    idx = rows_ref[t]
    return jnp.concatenate(
        [
            jnp.where(at == base(idx[b : b + 1, :]), 1.0, 0.0).astype(BF)
            for b in range(blocks)
        ],
        axis=1,
    )


def relvec_kernel(t, ids_ref, rel_ref, out_ref):
    rels = rel_ref.shape[1]
    tile = min(rels, 512)
    out = None
    for lo in range(0, rels, tile):
        hot = one_hot(ids_ref, t, tile, lambda i, lo=lo: i - lo)
        part = mm(rel_ref[:, lo : lo + tile], hot)
        out = part if out is None else out + part
    out_ref[...] = out.astype(BF)


def relvec(t, rel_ids, rel16):
    width, rels = rel16.shape
    slots = rel_ids.shape[1] * rel_ids.shape[2]
    return pl.pallas_call(
        functools.partial(relvec_kernel, t),
        in_specs=[vmem()] * 2,
        out_specs=vmem(),
        out_shape=jax.ShapeDtypeStruct((width, slots), BF),
        compiler_params=params(),
        cost_estimate=cost(2 * width * rels * slots, 4 * width * rels),
        name="relvec",
    )(rel_ids, rel16)


def relsum_kernel(t, first, ids_ref, drel_ref, *refs):
    step = pl.program_id(0)
    out_ref = refs[-1]
    tile = out_ref.shape[1]
    hot = one_hot(ids_ref, t, tile, lambda i: i - step * tile)
    part = mm(drel_ref[...], hot, NT)
    out_ref[...] = part if first else refs[0][...] + part


def relsum(t, rel_ids, drel, acc, rels):
    width, slots = drel.shape
    tile = min(rels, 512)
    wide = pl.BlockSpec((width, tile), lambda i: (0, i))
    ins = [rel_ids, drel] + ([] if acc is None else [acc])
    return pl.pallas_call(
        functools.partial(relsum_kernel, t, acc is None),
        grid=(rels // tile,),
        in_specs=[
            pl.BlockSpec(rel_ids.shape, lambda i: (0, 0, 0)),
            pl.BlockSpec((width, slots), lambda i: (0, 0)),
        ]
        + ([] if acc is None else [wide]),
        out_specs=wide,
        out_shape=jax.ShapeDtypeStruct((width, rels), F32),
        input_output_aliases={} if acc is None else {2: 0},
        compiler_params=params(),
        cost_estimate=cost(2 * width * rels * slots, 8 * width * rels),
        name="relsum",
    )(*ins)


def localize(edge, half):
    def local(idx):
        moved = idx + edge * half
        return jnp.where(moved >= 2 * half, moved - 2 * half, moved)

    return local


def halves(x):
    hd = x.shape[0] // 2
    return x[:hd], x[hd:]


def make_query(source, rel):
    (s_re, s_im), (w_re, w_im) = halves(source), halves(rel)
    return jnp.concatenate(
        [s_re * w_re - s_im * w_im, s_re * w_im + s_im * w_re], axis=0
    ).astype(BF)


def conj_times(dq, v):
    (dq_re, dq_im), (v_re, v_im) = halves(dq), halves(v)
    return jnp.concatenate(
        [dq_re * v_re + dq_im * v_im, dq_im * v_re - dq_re * v_im], axis=0
    ).astype(BF)


def target_side(t, shape, meta, query, target, o_ref, d_ref, w_ref):
    rounds, blocks, width = shape
    lanes = lambda b: pl.ds(pl.multiple_of(b * width, width), width)
    count = lambda b: meta[t * blocks + b]
    o_ref[...] = target.astype(BF)
    query_f = query.astype(F32)
    pos = jnp.sum(query_f * target, axis=0, keepdims=True)
    lane = lax.broadcasted_iota(jnp.int32, (1, width), 1)
    valid = jnp.concatenate(
        [jnp.where(lane < count(b), 1.0, 0.0) for b in range(blocks)], axis=1
    )
    gpos = -jax.nn.sigmoid(-pos) * valid
    d_ref[...] = gpos * query_f
    row_j = lax.broadcasted_iota(jnp.int32, (width, width), 0)
    col_i = lax.broadcasted_iota(jnp.int32, (width, width), 1)
    for b in range(blocks):
        nb = meta[(rounds + t) * blocks + b]
        qb = query[:, b * width : (b + 1) * width]
        scores = mm(o_ref[:, lanes(nb)], qb, TN)
        keep = jnp.logical_and(row_j < count(nb), col_i < count(b))
        weight = jnp.where(keep, jax.nn.sigmoid(scores) / width, 0.0).astype(BF)
        w_ref[:, b * width : (b + 1) * width] = weight
        d_ref[:, lanes(nb)] += mm(qb, weight, NT)
    return gpos


def make_dquery(t, shape, meta, gpos, o_ref, w_ref):
    rounds, blocks, width = shape
    lanes = lambda b: pl.ds(pl.multiple_of(b * width, width), width)
    out = []
    for b in range(blocks):
        nb = meta[(rounds + t) * blocks + b]
        at = slice(b * width, (b + 1) * width)
        own = gpos[:, at] * o_ref[:, at].astype(F32)
        out.append(own + mm(o_ref[:, lanes(nb)], w_ref[:, at]))
    return jnp.concatenate(out, axis=1)


def first_kernel(
    shape, meta, src_ref, dst_ref, ids_ref, ent_ref, rel_ref,
    g_mine, g_other, drel_ref, rel16_ref, rel_buf, o_scr, d_scr, w_scr, sems,
):
    rels = rel_buf.shape[1]
    tile = min(rels, 512)
    spans = range(0, rels, tile)
    loads = [
        pltpu.make_async_copy(
            rel_ref.at[:, lo : lo + tile], rel_buf.at[:, lo : lo + tile], sems.at[i]
        )
        for i, lo in enumerate(spans)
    ]
    for load in loads:
        load.start()
    half = ent_ref.shape[1] // 2
    edge = meta[meta.shape[0] - 1]
    table = jnp.concatenate(
        [ent_ref[:, pl.ds(pl.multiple_of(h * half, half), half)].astype(BF) for h in (edge, 1 - edge)],
        axis=1,
    )
    local = localize(edge, half)
    s_hot = one_hot(src_ref, 0, 2 * half, local)
    d_hot = one_hot(dst_ref, 0, 2 * half, local)
    source = mm(table, s_hot)
    target = mm(table, d_hot)
    rel = None
    for load, lo in zip(loads, spans):
        load.wait()
        low = rel_buf[:, lo : lo + tile].astype(BF)
        rel16_ref[:, lo : lo + tile] = low
        part = mm(low, one_hot(ids_ref, 0, tile, lambda i, lo=lo: i - lo))
        rel = part if rel is None else rel + part
    query = make_query(source, rel)
    gpos = target_side(0, shape, meta, query, target, o_scr, d_scr, w_scr)
    dq = make_dquery(0, shape, meta, gpos, o_scr, w_scr)
    drel_ref[...] = conj_times(dq, source)
    total = mm(conj_times(dq, rel), s_hot, NT) + mm(d_scr[...].astype(BF), d_hot, NT)
    g_mine[...] = total[:, :half]
    g_other[...] = total[:, half:].astype(BF)


def first_round(meta, src, dst, rel_ids, entities, relations):
    dim, rows = entities.shape
    rels = relations.shape[1]
    _, blocks, width = src.shape
    slots = blocks * width
    sds = jax.ShapeDtypeStruct
    return pl.pallas_call(
        functools.partial(first_kernel, src.shape),
        in_specs=[smem()] + [vmem()] * 4 + [pl.BlockSpec(memory_space=pltpu.HBM)],
        out_specs=[vmem()] * 4,
        out_shape=[
            sds((dim, rows // 2), F32),
            sds((dim, rows // 2), BF),
            sds((dim, slots), BF),
            sds((dim, rels), BF),
        ],
        scratch_shapes=[
            pltpu.VMEM((dim, rels), F32),
            pltpu.VMEM((dim, slots), BF),
            pltpu.VMEM((dim, slots), F32),
            pltpu.VMEM((width, slots), BF),
            pltpu.SemaphoreType.DMA((-(-rels // min(rels, 512)),)),
        ],
        compiler_params=params(),
        cost_estimate=cost(2 * dim * slots * (rels + 4 * rows), 8 * dim * rels),
        name="first_round",
    )(meta, src, dst, rel_ids, entities, relations)


def source_kernel(t, meta, src_ref, dst_ref, own0, own1, rel_ref, query_ref, source_ref, s_hot_ref, d_hot_ref):
    half = own0.shape[1]
    local = localize(meta[meta.shape[0] - 1], half)
    s_hot = one_hot(src_ref, t, 2 * half, local)
    s_hot_ref[...] = s_hot
    d_hot_ref[...] = one_hot(dst_ref, t, 2 * half, local)
    source = mm(jnp.concatenate([own0[...], own1[...]], axis=1), s_hot)
    source_ref[...] = source.astype(BF)
    query_ref[...] = make_query(source, rel_ref[...].astype(F32))


def source_side(t, meta, src, dst, own, rel):
    dim, slots = rel.shape
    rows = 2 * own[0].shape[1]
    sds = jax.ShapeDtypeStruct
    return pl.pallas_call(
        functools.partial(source_kernel, t),
        in_specs=[smem()] + [vmem()] * 5,
        out_specs=[vmem()] * 4,
        out_shape=[sds((dim, slots), BF)] * 2 + [sds((rows, slots), BF)] * 2,
        compiler_params=params(),
        cost_estimate=cost(2 * dim * slots * rows, 12 * dim * slots),
        name="source_side",
    )(meta, src, dst, *own, rel)


def target_kernel(t, shape, meta, far0, far1, query_ref, d_hot_ref, gd_mine, gd_other, o_ref, w_ref, gpos_ref, d_scr):
    half = far0.shape[1]
    far = jnp.concatenate([far0[...], far1[...]], axis=1)
    target = mm(far, d_hot_ref[...])
    gpos_ref[...] = target_side(t, shape, meta, query_ref[...], target, o_ref, d_scr, w_ref)
    gd = mm(d_scr[...].astype(BF), d_hot_ref[...], NT)
    gd_mine[...] = gd[:, :half]
    gd_other[...] = gd[:, half:].astype(BF)


def target_grad(t, shape, meta, far, query, d_hot):
    dim, slots = query.shape
    half = far[0].shape[1]
    width = shape[2]
    sds = jax.ShapeDtypeStruct
    return pl.pallas_call(
        functools.partial(target_kernel, t, shape),
        in_specs=[smem()] + [vmem()] * 4,
        out_specs=[vmem()] * 5,
        out_shape=[
            sds((dim, half), F32),
            sds((dim, half), BF),
            sds((dim, slots), BF),
            sds((width, slots), BF),
            sds((1, slots), F32),
        ],
        scratch_shapes=[pltpu.VMEM((dim, slots), F32)],
        compiler_params=params(),
        cost_estimate=cost(4 * dim * slots * (2 * half + width), 12 * dim * slots),
        name="target_grad",
    )(meta, *far, query, d_hot)


def source_grad_kernel(t, shape, meta, o_ref, w_ref, gpos_ref, source_ref, rel_ref, s_hot_ref, gs_mine, gs_other, drel_ref):
    half = gs_mine.shape[1]
    dq = make_dquery(t, shape, meta, gpos_ref[...], o_ref, w_ref)
    drel_ref[...] = conj_times(dq, source_ref[...].astype(F32))
    gs = mm(conj_times(dq, rel_ref[...].astype(F32)), s_hot_ref[...], NT)
    gs_mine[...] = gs[:, :half]
    gs_other[...] = gs[:, half:].astype(BF)


def source_grad(t, shape, meta, target, weight, gpos, source, rel, s_hot):
    dim, slots = rel.shape
    half = s_hot.shape[0] // 2
    sds = jax.ShapeDtypeStruct
    return pl.pallas_call(
        functools.partial(source_grad_kernel, t, shape),
        in_specs=[smem()] + [vmem()] * 6,
        out_specs=[vmem()] * 3,
        out_shape=[sds((dim, half), F32), sds((dim, half), BF), sds((dim, slots), BF)],
        compiler_params=params(),
        cost_estimate=cost(4 * dim * slots * half, 12 * dim * slots),
        name="source_grad",
    )(meta, target, weight, gpos, source, rel, s_hot)


def last_kernel(
    t, shape, meta, far0, far1, query_ref, d_hot_ref, source_ref, rel_ref,
    drel_ref, dsource_ref, dterm_ref, o_scr, d_scr, w_scr,
):
    far = jnp.concatenate([far0[...], far1[...]], axis=1)
    target = mm(far, d_hot_ref[...])
    gpos = target_side(t, shape, meta, query_ref[...], target, o_scr, d_scr, w_scr)
    dterm_ref[...] = d_scr[...].astype(BF)
    dq = make_dquery(t, shape, meta, gpos, o_scr, w_scr)
    drel_ref[...] = conj_times(dq, source_ref[...].astype(F32))
    dsource_ref[...] = conj_times(dq, rel_ref[...].astype(F32))


def last_terms(t, shape, meta, far, query, d_hot, source, rel):
    dim, slots = query.shape
    return pl.pallas_call(
        functools.partial(last_kernel, t, shape),
        in_specs=[smem()] + [vmem()] * 6,
        out_specs=[vmem()] * 3,
        out_shape=[jax.ShapeDtypeStruct((dim, slots), BF)] * 3,
        scratch_shapes=[
            pltpu.VMEM((dim, slots), BF),
            pltpu.VMEM((dim, slots), F32),
            pltpu.VMEM((shape[2], slots), BF),
        ],
        compiler_params=params(),
        cost_estimate=cost(6 * dim * slots * shape[2], 12 * dim * slots),
        name="last_terms",
    )(meta, *far, query, d_hot, source, rel)


def both_kernel(dsource_ref, s_hot_ref, dterm_ref, d_hot_ref, gs_mine, gs_other, gd_mine, gd_other):
    half = gs_mine.shape[1]
    for terms, hot, mine, other in (
        (dterm_ref, d_hot_ref, gd_mine, gd_other),
        (dsource_ref, s_hot_ref, gs_mine, gs_other),
    ):
        grad = mm(terms[...], hot[...], NT)
        mine[...] = grad[:, :half]
        other[...] = grad[:, half:].astype(BF)


def both_grads(dsource, s_hot, dterm, d_hot):
    dim, slots = dterm.shape
    half = s_hot.shape[0] // 2
    sds = jax.ShapeDtypeStruct
    return pl.pallas_call(
        both_kernel,
        in_specs=[vmem()] * 4,
        out_specs=[vmem()] * 4,
        out_shape=[sds((dim, half), F32), sds((dim, half), BF)] * 2,
        compiler_params=params(),
        cost_estimate=cost(8 * dim * slots * half, 12 * dim * slots),
        name="both_grads",
    )(dsource, s_hot, dterm, d_hot)


def update_kernel(t, meta, ent_ref, state_ref, *refs):
    grads, (ent_out, state_out, low_out) = refs[:-3], refs[-3:]
    half = ent_out.shape[1]
    if t == 0:
        at = pl.ds(pl.multiple_of(meta[meta.shape[0] - 1] * half, half), half)
        ent, state = ent_ref[:, at], state_ref[:, at]
    else:
        ent, state = ent_ref[...], state_ref[...]
    grad = grads[0][...].astype(F32)
    for g in grads[1:]:
        grad = grad + g[...].astype(F32)
    state = state + jnp.sum(grad * grad, axis=0, keepdims=True) / grad.shape[0]
    new = ent - learn_rate * grad / jnp.sqrt(state)
    ent_out[...] = new
    state_out[...] = state
    low_out[...] = new.astype(BF)


def update(t, meta, ent, state, grads):
    dim, half = grads[0].shape
    return pl.pallas_call(
        functools.partial(update_kernel, t),
        in_specs=[smem()] + [vmem()] * (2 + len(grads)),
        out_specs=[vmem()] * 3,
        out_shape=[
            jax.ShapeDtypeStruct((dim, half), F32),
            jax.ShapeDtypeStruct((1, half), F32),
            jax.ShapeDtypeStruct((dim, half), BF),
        ],
        compiler_params=params(),
        cost_estimate=cost(10 * dim * half, 16 * dim * half),
        name="update",
    )(meta, ent, state, *grads)


def whole_kernel(meta, ent0, ent1, state0, state1, ent_out, state_out):
    half = ent0.shape[1]
    edge = meta[meta.shape[0] - 1]
    for core, ent, state in ((edge, ent0, state0), (1 - edge, ent1, state1)):
        at = pl.ds(pl.multiple_of(core * half, half), half)
        ent_out[:, at] = ent[...]
        state_out[:, at] = state[...]


def whole_partition(meta, ent, ent_there, state, state_there):
    dim, half = ent.shape
    return pl.pallas_call(
        whole_kernel,
        in_specs=[smem()] + [vmem()] * 4,
        out_specs=[vmem()] * 2,
        out_shape=[
            jax.ShapeDtypeStruct((dim, 2 * half), F32),
            jax.ShapeDtypeStruct((1, 2 * half), F32),
        ],
        compiler_params=params(),
        name="whole_partition",
    )(meta, ent, ent_there, state, state_there)


def pieces_kernel(t, n, meta, ids_ref, drel_ref, acc_ref, *refs):
    outs, total = refs[:-1], refs[-1]
    slots = drel_ref.shape[1]
    rels = total.shape[1]
    tile = min(rels, 512)
    drel = drel_ref[...]
    for lo in range(0, rels, tile):
        hot = one_hot(ids_ref, t, tile, lambda i, lo=lo: i - lo)
        total[:, lo : lo + tile] = acc_ref[:, lo : lo + tile] + mm(drel, hot, NT)
    w = outs[0].shape[1]
    for k in range(n):
        owner = lax.rem(meta[meta.shape[0] - 2] + k, n)
        for c in range(2):
            core = meta[meta.shape[0] - 1] if c == 0 else 1 - meta[meta.shape[0] - 1]
            at = pl.ds(pl.multiple_of((2 * owner + core) * w, w), w)
            outs[c * n + k][...] = total[:, at].astype(BF)


def pieces(t, n, meta, rel_ids, drel, acc):
    dim, rels = acc.shape
    w = rels // (2 * n)
    return pl.pallas_call(
        functools.partial(pieces_kernel, t, n),
        in_specs=[smem()] + [vmem()] * 3,
        out_specs=[vmem()] * (2 * n),
        out_shape=[jax.ShapeDtypeStruct((dim, w), BF)] * (2 * n),
        scratch_shapes=[pltpu.VMEM((dim, rels), F32)],
        compiler_params=params(),
        cost_estimate=cost(2 * dim * rels * drel.shape[1], 8 * dim * rels),
        name="pieces",
    )(meta, rel_ids, drel, acc)


def add_kernel(n, *refs):
    for k in range(n):
        refs[2 * n + k][...] = (refs[k][...].astype(F32) + refs[n + k][...].astype(F32)).astype(BF)


def add_pairs(mine, theirs):
    n = len(mine)
    return pl.pallas_call(
        functools.partial(add_kernel, n),
        in_specs=[vmem()] * (2 * n),
        out_specs=[vmem()] * n,
        out_shape=[jax.ShapeDtypeStruct(x.shape, BF) for x in mine],
        compiler_params=params(),
        name="add_pairs",
    )(*mine, *theirs)


def sum_kernel(*refs):
    total = refs[0][...].astype(F32)
    for r in refs[1:-1]:
        total = total + r[...].astype(F32)
    refs[-1][...] = total.astype(BF)


def sum_all(parts):
    return pl.pallas_call(
        sum_kernel,
        in_specs=[vmem()] * len(parts),
        out_specs=vmem(),
        out_shape=jax.ShapeDtypeStruct(parts[0].shape, BF),
        compiler_params=params(),
        name="sum_all",
    )(*parts)


def relnew_kernel(n, meta, rel_ref, state_ref, *refs):
    got, (rel_out, state_out) = refs[:-2], refs[-2:]
    w = got[0].shape[1]
    for k in range(n):
        owner = lax.rem(meta[meta.shape[0] - 2] + n - k, n)
        for c in range(2):
            core = meta[meta.shape[0] - 1] if c == 0 else 1 - meta[meta.shape[0] - 1]
            at = pl.ds(pl.multiple_of((2 * owner + core) * w, w), w)
            grad = got[c * n + k][...].astype(F32)
            state = state_ref[:, at] + jnp.sum(grad * grad, axis=0, keepdims=True) / grad.shape[0]
            state_out[:, at] = state
            rel_out[:, at] = rel_ref[:, at] - learn_rate * grad / jnp.sqrt(state)


def relnew(n, meta, relations, state, got):
    dim, rels = relations.shape
    return pl.pallas_call(
        functools.partial(relnew_kernel, n),
        in_specs=[smem()] + [vmem()] * (2 + len(got)),
        out_specs=[vmem()] * 2,
        out_shape=[jax.ShapeDtypeStruct((dim, rels), F32), jax.ShapeDtypeStruct((1, rels), F32)],
        compiler_params=params(),
        name="relnew",
    )(meta, relations, state, *got)


def relation_update(t, meta, rel_ids, drel, acc, relations, state):
    n = lax.axis_size("dom")
    dim, rels = relations.shape
    if rels % (256 * n):
        total = relsum(t, rel_ids, drel, acc, rels)
        total = lax.psum(total, ("dom", "edge"))
        state = state + jnp.mean(total * total, axis=0)
        return relations - learn_rate * total / jnp.sqrt(state)[None, :], state
    parts = pieces(t, n, meta, rel_ids, drel, acc)
    mine, other = parts[:n], parts[n:]
    theirs = [across(x) for x in other]
    mine = add_pairs(mine, theirs)
    summed = sum_all([mine[0]] + [shifted(mine[k], k) for k in range(1, n)])
    got = [summed] + [shifted(summed, k) for k in range(1, n)]
    got = got + [across(x) for x in got]
    rel_new, state_new = relnew(n, meta, relations, state.reshape(1, rels), got)
    return rel_new, state_new.reshape(rels)


def on_device(
    entities,
    entity_state,
    relations,
    relation_state,
    src_rows,
    rel_ids,
    dst_rows,
    counts,
    neg_blocks,
):
    rounds = src_rows.shape[0]
    rels = relations.shape[1]
    shape = src_rows.shape
    meta = jnp.concatenate(
        [
            counts.reshape(-1),
            neg_blocks.reshape(-1),
            lax.axis_index("dom").reshape(1).astype(jnp.int32),
            lax.axis_index("edge").reshape(1).astype(jnp.int32),
        ]
    )
    g_mine, g_other, drel, rel16 = first_round(meta, src_rows, dst_rows, rel_ids, entities, relations)
    acc = relsum(0, rel_ids, drel, None, rels)
    ent, state, low = update(
        0, meta, entities, entity_state.reshape(1, -1), [g_mine, across(g_other)]
    )
    for t in range(1, rounds):
        far = shifted(low, -t)
        own = (low, across(low))
        rel = relvec(t, rel_ids, rel16)
        query, source, s_hot, d_hot = source_side(t, meta, src_rows, dst_rows, own, rel)
        far = (far, across(far))
        if t < rounds - 1:
            gd_mine, gd_other, target, weight, gpos = target_grad(t, shape, meta, far, query, d_hot)
            gs_mine, gs_other, drel = source_grad(
                t, shape, meta, target, weight, gpos, source, rel, s_hot
            )
            acc = relsum(t, rel_ids, drel, acc, rels)
        else:
            drel, dsource, dterm = last_terms(t, shape, meta, far, query, d_hot, source, rel)
            gs_mine, gs_other, gd_mine, gd_other = both_grads(dsource, s_hot, dterm, d_hot)
        gd = sum_all([gd_mine, across(gd_other)])
        grads = [gs_mine, across(gs_other), shifted(gd, t)]
        ent, state, low = update(t, meta, ent, state, grads)
    rel_new, rel_state = relation_update(
        rounds - 1, meta, rel_ids, drel, acc, relations, relation_state
    )
    ent, state = whole_partition(meta, ent, across(ent), state, across(state))
    return (ent, state.reshape(-1), rel_new, rel_state)


def solution(mesh):
    return jax.shard_map(
        on_device,
        mesh=mesh,
        in_specs=(
            P(None, ("groups", "dom")),
            P(("groups", "dom")),
            P(None, "groups"),
            P("groups"),
            P(None, ("groups", "dom", "edge"), None),
            P(None, ("groups", "dom", "edge"), None),
            P(None, ("groups", "dom", "edge"), None),
            P(None, ("groups", "dom", "edge")),
            P(None, ("groups", "dom", "edge")),
        ),
        out_specs=(
            P(None, ("groups", "dom")),
            P(("groups", "dom")),
            P(None, "groups"),
            P("groups"),
        ),
        check_vma=False,
    )
```

```python
import functools

import jax
import jax.numpy as jnp
from jax import lax
from jax.experimental import pallas as pl
from jax.experimental.pallas import tpu as pltpu
from jax.sharding import PartitionSpec as P

learn_rate = 0.1
BF = jnp.bfloat16
F32 = jnp.float32
VMEM_LIMIT = 40 * 1024 * 1024
NN = (((1,), (0,)), ((), ()))
NT = (((1,), (1,)), ((), ()))
TN = (((0,), (0,)), ((), ()))


def mm(a, b, dims=NN):
    return lax.dot_general(a, b, dims, preferred_element_type=F32)


def vmem():
    return pl.BlockSpec(memory_space=pltpu.VMEM)


def smem():
    return pl.BlockSpec(memory_space=pltpu.SMEM)


def anywhere():
    return pl.BlockSpec(memory_space=pl.ANY)


def in_hbm(x):
    return pltpu.with_memory_space_constraint(x, pltpu.HBM)


def cost(flops, size):
    return pl.CostEstimate(flops=flops, bytes_accessed=size, transcendentals=0)


def params():
    return pltpu.CompilerParams(vmem_limit_bytes=VMEM_LIMIT)


def shifted(x, by):
    n = lax.axis_size("dom")
    return lax.ppermute(x, "dom", [(i, (i + by) % n) for i in range(n)])


def beside(x):
    n = lax.axis_size("dom")
    return lax.ppermute(x, "dom", [(i, i ^ 1) for i in range(n)])


def across(x):
    return lax.ppermute(x, "edge", [(0, 1), (1, 0)])


def one_hot(rows_ref, t, count, base):
    blocks, width = rows_ref.shape[1:]
    at = lax.broadcasted_iota(jnp.int32, (count, width), 0)
    idx = rows_ref[t]
    return jnp.concatenate(
        [
            jnp.where(at == base(idx[b : b + 1, :]), 1.0, 0.0).astype(BF)
            for b in range(blocks)
        ],
        axis=1,
    )


def relvec_kernel(t, ids_ref, rel_ref, out_ref):
    rels = rel_ref.shape[1]
    tile = min(rels, 512)
    out = None
    for lo in range(0, rels, tile):
        hot = one_hot(ids_ref, t, tile, lambda i, lo=lo: i - lo)
        part = mm(rel_ref[:, lo : lo + tile], hot)
        out = part if out is None else out + part
    out_ref[...] = out.astype(BF)


def relvec(t, rel_ids, rel16):
    width, rels = rel16.shape
    slots = rel_ids.shape[1] * rel_ids.shape[2]
    return pl.pallas_call(
        functools.partial(relvec_kernel, t),
        in_specs=[vmem()] * 2,
        out_specs=vmem(),
        out_shape=jax.ShapeDtypeStruct((width, slots), BF),
        compiler_params=params(),
        cost_estimate=cost(2 * width * rels * slots, 4 * width * rels),
        name="relvec",
    )(rel_ids, rel16)


def relsum_kernel(t, first, ids_ref, drel_ref, *refs):
    step = pl.program_id(0)
    out_ref = refs[-1]
    tile = out_ref.shape[1]
    hot = one_hot(ids_ref, t, tile, lambda i: i - step * tile)
    part = mm(drel_ref[...], hot, NT)
    out_ref[...] = part if first else refs[0][...] + part


def relsum(t, rel_ids, drel, acc, rels):
    width, slots = drel.shape
    tile = min(rels, 512)
    wide = pl.BlockSpec((width, tile), lambda i: (0, i))
    ins = [rel_ids, drel] + ([] if acc is None else [acc])
    return pl.pallas_call(
        functools.partial(relsum_kernel, t, acc is None),
        grid=(rels // tile,),
        in_specs=[
            pl.BlockSpec(rel_ids.shape, lambda i: (0, 0, 0)),
            pl.BlockSpec((width, slots), lambda i: (0, 0)),
        ]
        + ([] if acc is None else [wide]),
        out_specs=wide,
        out_shape=jax.ShapeDtypeStruct((width, rels), F32),
        input_output_aliases={} if acc is None else {2: 0},
        compiler_params=params(),
        cost_estimate=cost(2 * width * rels * slots, 8 * width * rels),
        name="relsum",
    )(*ins)


class Limits:
    scratch = lambda shape: [
        pltpu.SMEM((shape[1], shape[0]), jnp.int32),
        pltpu.SMEM((shape[1], shape[0]), jnp.int32),
        pltpu.SemaphoreType.DMA((2,)),
    ]

    def __init__(self, t, from_cnt, from_neg, cnt, neg, sems):
        self.t, self.cnt, self.neg = t, cnt, neg
        self.copies = [
            pltpu.make_async_copy(from_cnt, cnt, sems.at[0]),
            pltpu.make_async_copy(from_neg, neg, sems.at[1]),
        ]
        for copy in self.copies:
            copy.start()

    def wait(self):
        for copy in self.copies:
            copy.wait()

    def count(self, b):
        return self.cnt[b, self.t]

    def negative(self, b):
        return self.neg[b, self.t]


def localize(edge, half):
    def local(idx):
        moved = idx + edge * half
        return jnp.where(moved >= 2 * half, moved - 2 * half, moved)

    return local


def halves(x):
    hd = x.shape[0] // 2
    return x[:hd], x[hd:]


def make_query(source, rel):
    (s_re, s_im), (w_re, w_im) = halves(source), halves(rel)
    return jnp.concatenate(
        [s_re * w_re - s_im * w_im, s_re * w_im + s_im * w_re], axis=0
    ).astype(BF)


def conj_times(dq, v):
    (dq_re, dq_im), (v_re, v_im) = halves(dq), halves(v)
    return jnp.concatenate(
        [dq_re * v_re + dq_im * v_im, dq_im * v_re - dq_re * v_im], axis=0
    ).astype(BF)


def target_side(shape, limits, query, target, o_ref, d_ref, w_ref):
    _, blocks, width = shape
    lanes = lambda b: pl.ds(pl.multiple_of(b * width, width), width)
    count = limits.count
    o_ref[...] = target.astype(BF)
    query_f = query.astype(F32)
    pos = jnp.sum(query_f * target, axis=0, keepdims=True)
    lane = lax.broadcasted_iota(jnp.int32, (1, width), 1)
    limits.wait()
    valid = jnp.concatenate(
        [jnp.where(lane < count(b), 1.0, 0.0) for b in range(blocks)], axis=1
    )
    gpos = -jax.nn.sigmoid(-pos) * valid
    d_ref[...] = gpos * query_f
    row_j = lax.broadcasted_iota(jnp.int32, (width, width), 0)
    col_i = lax.broadcasted_iota(jnp.int32, (width, width), 1)
    for b in range(blocks):
        nb = limits.negative(b)
        qb = query[:, b * width : (b + 1) * width]
        scores = mm(o_ref[:, lanes(nb)], qb, TN)
        keep = jnp.logical_and(row_j < count(nb), col_i < count(b))
        weight = jnp.where(keep, jax.nn.sigmoid(scores) / width, 0.0).astype(BF)
        w_ref[:, b * width : (b + 1) * width] = weight
        d_ref[:, lanes(nb)] += mm(qb, weight, NT)
    return gpos


def make_dquery(shape, limits, gpos, o_ref, w_ref):
    _, blocks, width = shape
    lanes = lambda b: pl.ds(pl.multiple_of(b * width, width), width)
    out = []
    for b in range(blocks):
        nb = limits.negative(b)
        at = slice(b * width, (b + 1) * width)
        own = gpos[:, at] * o_ref[:, at].astype(F32)
        out.append(own + mm(o_ref[:, lanes(nb)], w_ref[:, at]))
    return jnp.concatenate(out, axis=1)


def first_kernel(
    shape, me, cnt_ref, neg_ref, src_ref, dst_ref, ids_ref, ent_ref, rel_ref,
    g_mine, g_other, drel_ref, rel16_ref,
    cnt, neg, lim_sems, src, dst, ids, ent, rel_buf, o_scr, d_scr, w_scr, in_sems, sems,
):
    rels = rel_buf.shape[1]
    tile = min(rels, 512)
    spans = range(0, rels, tile)
    inputs = [
        pltpu.make_async_copy(there, here, in_sems.at[i])
        for i, (there, here) in enumerate(
            [(src_ref.at[:1], src), (dst_ref.at[:1], dst), (ids_ref.at[:1], ids), (ent_ref, ent)]
        )
    ]
    loads = [
        pltpu.make_async_copy(
            rel_ref.at[:, lo : lo + tile], rel_buf.at[:, lo : lo + tile], sems.at[i]
        )
        for i, lo in enumerate(spans)
    ]
    for load in inputs:
        load.start()
    limits = Limits(0, cnt_ref, neg_ref, cnt, neg, lim_sems)
    for load in loads:
        load.start()
    half = ent.shape[1] // 2
    edge = me[1]
    local = localize(edge, half)
    inputs[0].wait()
    s_hot = one_hot(src, 0, 2 * half, local)
    inputs[1].wait()
    d_hot = one_hot(dst, 0, 2 * half, local)
    inputs[2].wait()
    inputs[3].wait()
    table = jnp.concatenate(
        [ent[:, pl.ds(pl.multiple_of(h * half, half), half)].astype(BF) for h in (edge, 1 - edge)],
        axis=1,
    )
    source = mm(table, s_hot)
    target = mm(table, d_hot)
    rel = None
    for load, lo in zip(loads, spans):
        load.wait()
        low = rel_buf[:, lo : lo + tile].astype(BF)
        rel16_ref[:, lo : lo + tile] = low
        part = mm(low, one_hot(ids, 0, tile, lambda i, lo=lo: i - lo))
        rel = part if rel is None else rel + part
    query = make_query(source, rel)
    gpos = target_side(shape, limits, query, target, o_scr, d_scr, w_scr)
    dq = make_dquery(shape, limits, gpos, o_scr, w_scr)
    drel_ref[...] = conj_times(dq, source)
    total = mm(conj_times(dq, rel), s_hot, NT) + mm(d_scr[...].astype(BF), d_hot, NT)
    g_mine[...] = total[:, :half]
    g_other[...] = total[:, half:].astype(BF)


def first_round(me, cnt, neg, src, dst, rel_ids, entities, relations):
    dim, rows = entities.shape
    rels = relations.shape[1]
    _, blocks, width = src.shape
    slots = blocks * width
    sds = jax.ShapeDtypeStruct
    return pl.pallas_call(
        functools.partial(first_kernel, src.shape),
        in_specs=[smem()] + [anywhere()] * 7,
        out_specs=[vmem()] * 4,
        out_shape=[
            sds((dim, rows // 2), F32),
            sds((dim, rows // 2), BF),
            sds((dim, slots), BF),
            sds((dim, rels), BF),
        ],
        scratch_shapes=Limits.scratch(src.shape)
        + [
            pltpu.VMEM((1, blocks, width), jnp.int32),
            pltpu.VMEM((1, blocks, width), jnp.int32),
            pltpu.VMEM((1, blocks, width), jnp.int32),
            pltpu.VMEM((dim, rows), F32),
            pltpu.VMEM((dim, rels), F32),
            pltpu.VMEM((dim, slots), BF),
            pltpu.VMEM((dim, slots), F32),
            pltpu.VMEM((width, slots), BF),
            pltpu.SemaphoreType.DMA((4,)),
            pltpu.SemaphoreType.DMA((-(-rels // min(rels, 512)),)),
        ],
        compiler_params=params(),
        cost_estimate=cost(2 * dim * slots * (rels + 4 * rows), 8 * dim * rels),
        name="first_round",
    )(me, *(in_hbm(x) for x in (cnt, neg, src, dst, rel_ids, entities, relations)))


def source_kernel(t, me, src_ref, dst_ref, own0, own1, rel_ref, query_ref, source_ref, s_hot_ref, d_hot_ref):
    half = own0.shape[1]
    local = localize(me[1], half)
    s_hot = one_hot(src_ref, t, 2 * half, local)
    s_hot_ref[...] = s_hot
    d_hot_ref[...] = one_hot(dst_ref, t, 2 * half, local)
    source = mm(jnp.concatenate([own0[...], own1[...]], axis=1), s_hot)
    source_ref[...] = source.astype(BF)
    query_ref[...] = make_query(source, rel_ref[...].astype(F32))


def source_side(t, me, src, dst, own, rel):
    dim, slots = rel.shape
    rows = 2 * own[0].shape[1]
    sds = jax.ShapeDtypeStruct
    return pl.pallas_call(
        functools.partial(source_kernel, t),
        in_specs=[smem()] + [vmem()] * 5,
        out_specs=[vmem()] * 4,
        out_shape=[sds((dim, slots), BF)] * 2 + [sds((rows, slots), BF)] * 2,
        compiler_params=params(),
        cost_estimate=cost(2 * dim * slots * rows, 12 * dim * slots),
        name="source_side",
    )(me, src, dst, *own, rel)


def target_kernel(
    t, shape, cnt_ref, neg_ref, far0, far1, query_ref, d_hot_ref,
    gd_mine, gd_other, o_ref, w_ref, gpos_ref, cnt, neg, sems, d_scr,
):
    limits = Limits(t, cnt_ref, neg_ref, cnt, neg, sems)
    half = far0.shape[1]
    far = jnp.concatenate([far0[...], far1[...]], axis=1)
    target = mm(far, d_hot_ref[...])
    gpos_ref[...] = target_side(shape, limits, query_ref[...], target, o_ref, d_scr, w_ref)
    gd = mm(d_scr[...].astype(BF), d_hot_ref[...], NT)
    gd_mine[...] = gd[:, :half]
    gd_other[...] = gd[:, half:].astype(BF)


def target_grad(t, shape, cnt, neg, far, query, d_hot):
    dim, slots = query.shape
    half = far[0].shape[1]
    width = shape[2]
    sds = jax.ShapeDtypeStruct
    return pl.pallas_call(
        functools.partial(target_kernel, t, shape),
        in_specs=[anywhere()] * 2 + [vmem()] * 4,
        out_specs=[vmem()] * 5,
        out_shape=[
            sds((dim, half), F32),
            sds((dim, half), BF),
            sds((dim, slots), BF),
            sds((width, slots), BF),
            sds((1, slots), F32),
        ],
        scratch_shapes=Limits.scratch(shape) + [pltpu.VMEM((dim, slots), F32)],
        compiler_params=params(),
        cost_estimate=cost(4 * dim * slots * (2 * half + width), 12 * dim * slots),
        name="target_grad",
    )(cnt, neg, *far, query, d_hot)


def source_grad_kernel(
    t, shape, cnt_ref, neg_ref, o_ref, w_ref, gpos_ref, source_ref, rel_ref, s_hot_ref,
    gs_mine, gs_other, drel_ref, cnt, neg, sems,
):
    limits = Limits(t, cnt_ref, neg_ref, cnt, neg, sems)
    limits.wait()
    half = gs_mine.shape[1]
    dq = make_dquery(shape, limits, gpos_ref[...], o_ref, w_ref)
    drel_ref[...] = conj_times(dq, source_ref[...].astype(F32))
    gs = mm(conj_times(dq, rel_ref[...].astype(F32)), s_hot_ref[...], NT)
    gs_mine[...] = gs[:, :half]
    gs_other[...] = gs[:, half:].astype(BF)


def source_grad(t, shape, cnt, neg, target, weight, gpos, source, rel, s_hot):
    dim, slots = rel.shape
    half = s_hot.shape[0] // 2
    sds = jax.ShapeDtypeStruct
    return pl.pallas_call(
        functools.partial(source_grad_kernel, t, shape),
        in_specs=[anywhere()] * 2 + [vmem()] * 6,
        out_specs=[vmem()] * 3,
        out_shape=[sds((dim, half), F32), sds((dim, half), BF), sds((dim, slots), BF)],
        scratch_shapes=Limits.scratch(shape),
        compiler_params=params(),
        cost_estimate=cost(4 * dim * slots * half, 12 * dim * slots),
        name="source_grad",
    )(cnt, neg, target, weight, gpos, source, rel, s_hot)


def last_kernel(
    t, shape, cnt_ref, neg_ref, far0, far1, query_ref, d_hot_ref, source_ref, rel_ref,
    drel_ref, dsource_ref, dterm_ref, cnt, neg, sems, o_scr, d_scr, w_scr,
):
    limits = Limits(t, cnt_ref, neg_ref, cnt, neg, sems)
    far = jnp.concatenate([far0[...], far1[...]], axis=1)
    target = mm(far, d_hot_ref[...])
    gpos = target_side(shape, limits, query_ref[...], target, o_scr, d_scr, w_scr)
    dterm_ref[...] = d_scr[...].astype(BF)
    dq = make_dquery(shape, limits, gpos, o_scr, w_scr)
    drel_ref[...] = conj_times(dq, source_ref[...].astype(F32))
    dsource_ref[...] = conj_times(dq, rel_ref[...].astype(F32))


def last_terms(t, shape, cnt, neg, far, query, d_hot, source, rel):
    dim, slots = query.shape
    return pl.pallas_call(
        functools.partial(last_kernel, t, shape),
        in_specs=[anywhere()] * 2 + [vmem()] * 6,
        out_specs=[vmem()] * 3,
        out_shape=[jax.ShapeDtypeStruct((dim, slots), BF)] * 3,
        scratch_shapes=Limits.scratch(shape)
        + [
            pltpu.VMEM((dim, slots), BF),
            pltpu.VMEM((dim, slots), F32),
            pltpu.VMEM((shape[2], slots), BF),
        ],
        compiler_params=params(),
        cost_estimate=cost(6 * dim * slots * shape[2], 12 * dim * slots),
        name="last_terms",
    )(cnt, neg, *far, query, d_hot, source, rel)


def both_kernel(dsource_ref, s_hot_ref, dterm_ref, d_hot_ref, gs_mine, gs_other, gd_mine, gd_other):
    half = gs_mine.shape[1]
    for terms, hot, mine, other in (
        (dterm_ref, d_hot_ref, gd_mine, gd_other),
        (dsource_ref, s_hot_ref, gs_mine, gs_other),
    ):
        grad = mm(terms[...], hot[...], NT)
        mine[...] = grad[:, :half]
        other[...] = grad[:, half:].astype(BF)


def both_grads(dsource, s_hot, dterm, d_hot):
    dim, slots = dterm.shape
    half = s_hot.shape[0] // 2
    sds = jax.ShapeDtypeStruct
    return pl.pallas_call(
        both_kernel,
        in_specs=[vmem()] * 4,
        out_specs=[vmem()] * 4,
        out_shape=[sds((dim, half), F32), sds((dim, half), BF)] * 2,
        compiler_params=params(),
        cost_estimate=cost(8 * dim * slots * half, 12 * dim * slots),
        name="both_grads",
    )(dsource, s_hot, dterm, d_hot)


def update_kernel(n_grads, first, *refs):
    if first:
        me, refs = refs[0], refs[1:]
    ent_ref, state_ref, grads = refs[0], refs[1], refs[2 : 2 + n_grads]
    ent_out, state_out, low_out = refs[-3:]
    half = ent_out.shape[1]
    if first:
        at = pl.ds(pl.multiple_of(me[1] * half, half), half)
        ent, state = ent_ref[:, at], state_ref[:, at]
    else:
        ent, state = ent_ref[...], state_ref[...]
    grad = grads[0][...].astype(F32)
    for g in grads[1:]:
        grad = grad + g[...].astype(F32)
    state = state + jnp.sum(grad * grad, axis=0, keepdims=True) / grad.shape[0]
    new = ent - grad * (learn_rate / jnp.sqrt(state))
    ent_out[...] = new
    state_out[...] = state
    low_out[...] = new.astype(BF)


def update(me, ent, state, grads, after):
    dim, half = grads[0].shape
    ins = ([] if me is None else [me]) + [ent, state, *grads]
    specs = ([] if me is None else [smem()]) + [vmem()] * (2 + len(grads))
    return pl.pallas_call(
        functools.partial(update_kernel, len(grads), me is not None),
        in_specs=specs + [anywhere()] * len(after),
        out_specs=[vmem()] * 3,
        out_shape=[
            jax.ShapeDtypeStruct((dim, half), F32),
            jax.ShapeDtypeStruct((1, half), F32),
            jax.ShapeDtypeStruct((dim, half), BF),
        ],
        compiler_params=params(),
        cost_estimate=cost(10 * dim * half, 16 * dim * half),
        name="update",
    )(*ins, *after)


def pair_kernel(a_ref, b_ref, out_ref):
    out_ref[...] = (a_ref[...] + b_ref[...].astype(F32)).astype(BF)


def sum_pair(a, b):
    return pl.pallas_call(
        pair_kernel,
        in_specs=[vmem()] * 2,
        out_specs=vmem(),
        out_shape=jax.ShapeDtypeStruct(a.shape, BF),
        compiler_params=params(),
        name="sum_pair",
    )(a, b)


def held_kernel(x_ref, *refs):
    pass


def held(x, after):
    return pl.pallas_call(
        held_kernel,
        in_specs=[anywhere()] * (1 + len(after)),
        out_specs=anywhere(),
        out_shape=jax.ShapeDtypeStruct(x.shape, x.dtype),
        input_output_aliases={0: 0},
        compiler_params=params(),
        name="held",
    )(x, *after)


def whole_kernel(me, ent0, ent1, state0, state1, ent_out, state_out):
    half = ent0.shape[1]
    edge = me[1]
    for core, ent, state in ((edge, ent0, state0), (1 - edge, ent1, state1)):
        at = pl.ds(pl.multiple_of(core * half, half), half)
        ent_out[:, at] = ent[...]
        state_out[:, at] = state[...]


def whole_partition(me, ent, ent_there, state, state_there):
    dim, half = ent.shape
    return pl.pallas_call(
        whole_kernel,
        in_specs=[smem()] + [vmem()] * 4,
        out_specs=[vmem()] * 2,
        out_shape=[
            jax.ShapeDtypeStruct((dim, 2 * half), F32),
            jax.ShapeDtypeStruct((1, 2 * half), F32),
        ],
        compiler_params=params(),
        name="whole_partition",
    )(me, ent, ent_there, state, state_there)


def first_column(owner, core, w):
    return pl.multiple_of((2 * owner + core) * w, w)


def pieces_kernel(t, nz, same, me, ids_ref, drel_ref, acc_ref, *refs):
    mine, other = refs[-nz - 1 : -1], refs[-1]
    w = other.shape[2]
    z, x, edge = me[0] // 2, lax.rem(me[0], 2), me[1]
    drel = drel_ref[...]
    for k in range(nz):
        owner = 2 * lax.rem(z + k, nz) + (x if same else 1 - x)
        at = [first_column(owner, core, w) for core in (edge, 1 - edge)]
        hot = jnp.concatenate([one_hot(ids_ref, t, w, lambda i, lo=lo: i - lo) for lo in at], axis=0)
        part = mm(drel, hot, NT)
        mine[k][...] = acc_ref[:, pl.ds(at[0], w)] + part[:, :w]
        other[k] = (acc_ref[:, pl.ds(at[1], w)] + part[:, w:]).astype(BF)


def pieces(t, n, same, me, rel_ids, drel, acc, after):
    dim, rels = acc.shape
    w = rels // (2 * n)
    sds = jax.ShapeDtypeStruct
    out = pl.pallas_call(
        functools.partial(pieces_kernel, t, n // 2, same),
        in_specs=[smem()] + [vmem()] * 3 + [anywhere()] * len(after),
        out_specs=[vmem()] * (n // 2 + 1),
        out_shape=[sds((dim, w), F32)] * (n // 2) + [sds((n // 2, dim, w), BF)],
        compiler_params=params(),
        cost_estimate=cost(dim * rels * drel.shape[1], 4 * dim * rels),
        name="pieces",
    )(me, rel_ids, drel, acc, *after)
    return out[:-1], out[-1]


def add_kernel(n, *refs):
    for k in range(n):
        refs[n + 1 + k][...] = (refs[k][...] + refs[n][k].astype(F32)).astype(BF)


def add_each(mine, theirs):
    n = len(mine)
    return pl.pallas_call(
        functools.partial(add_kernel, n),
        in_specs=[vmem()] * (n + 1),
        out_specs=[vmem()] * n,
        out_shape=[jax.ShapeDtypeStruct(x.shape, BF) for x in mine],
        compiler_params=params(),
        name="add_each",
    )(*mine, theirs)


def sum_kernel(k, mine, theirs, *refs):
    total = mine[...] + theirs[k].astype(F32)
    for r in refs[:-1]:
        total = total + r[...].astype(F32)
    refs[-1][...] = total.astype(BF)


def sum_piece(k, mine, theirs, parts):
    return pl.pallas_call(
        functools.partial(sum_kernel, k),
        in_specs=[vmem()] * (2 + len(parts)),
        out_specs=vmem(),
        out_shape=jax.ShapeDtypeStruct(mine.shape, BF),
        compiler_params=params(),
        name="sum_piece",
    )(mine, theirs, *parts)


def relnew_kernel(nz, same, me, rel_ref, state_ref, *refs):
    got = refs[: 2 * nz]
    rel_out, state_out, buf, sems = refs[-4:]
    w = got[0].shape[1]
    state_out[...] = refs[2 * nz if same else 2 * nz + 1][...]
    z, x, edge = me[0] // 2, lax.rem(me[0], 2), me[1]
    copies = []
    for k in range(nz):
        owner = 2 * lax.rem(z + nz - k, nz) + (x if same else 1 - x)
        for c in range(2):
            i = c * nz + k
            at = pl.ds(first_column(owner, edge if c == 0 else 1 - edge, w), w)
            grad = got[i][...].astype(F32)
            state = state_ref[:, at] + jnp.sum(grad * grad, axis=0, keepdims=True) / grad.shape[0]
            state_out[:, at] = state
            buf[i] = rel_ref[:, at] - grad * (learn_rate / jnp.sqrt(state))
            copy = pltpu.make_async_copy(buf.at[i], rel_out.at[:, at], sems.at[i])
            copy.start()
            copies.append(copy)
    for copy in copies:
        copy.wait()


def relnew(n, same, me, relations, state, got, before):
    dim, rels = relations.shape
    w = got[0].shape[1]
    start = [state] if same else list(before)
    return pl.pallas_call(
        functools.partial(relnew_kernel, n // 2, same),
        in_specs=[smem()] + [vmem()] * (2 + len(got)) + ([vmem()] if same else [anywhere(), vmem()]),
        out_specs=[anywhere(), vmem()],
        out_shape=[jax.ShapeDtypeStruct((dim, rels), F32), jax.ShapeDtypeStruct((1, rels), F32)],
        input_output_aliases={} if same else {3 + len(got): 0},
        scratch_shapes=[pltpu.VMEM((n, dim, w), F32), pltpu.SemaphoreType.DMA((n,))],
        compiler_params=params(),
        cost_estimate=cost(4 * dim * rels, 4 * dim * rels),
        name="relnew",
    )(me, relations, state, *got, *start)


def relation_update(t, me, rel_ids, drel, acc, relations, state, after_x, after_s):
    n = lax.axis_size("dom")
    dim, rels = relations.shape
    if n % 2 or rels % (256 * n):
        total = lax.psum(relsum(t, rel_ids, drel, acc, rels), ("dom", "edge"))
        state = state + jnp.mean(total * total, axis=0)
        return relations - learn_rate * total / jnp.sqrt(state)[None, :], state, total
    nz = n // 2
    mine_x, other_x = pieces(t, n, False, me, rel_ids, drel, acc, after_x)
    mine_s, other_s = pieces(t, n, True, me, rel_ids, drel, acc, after_s)
    to_x = add_each(mine_x, across(other_x))
    theirs = across(other_s)
    from_x = [beside(piece) for piece in to_x]
    from_z = [
        shifted(sum_piece(k, mine_s[k], theirs, [from_x[k]]), 2 * k) for k in range(1, nz)
    ]
    summed = sum_piece(0, mine_s[0], theirs, [from_x[0]] + from_z)
    got = [summed] + [shifted(summed, 2 * k) for k in range(1, nz)]
    got_x = [beside(piece) for piece in got]
    state = state.reshape(1, rels)
    part = relnew(n, True, me, relations, state, got + [across(x) for x in got], None)
    rel_new, state_new = relnew(
        n, False, me, relations, state, got_x + [across(x) for x in got_x], part
    )
    return rel_new, state_new.reshape(rels), summed


def on_device(
    entities,
    entity_state,
    relations,
    relation_state,
    src_rows,
    rel_ids,
    dst_rows,
    counts,
    neg_blocks,
):
    rounds = src_rows.shape[0]
    rels = relations.shape[1]
    shape = src_rows.shape
    me = jnp.stack([lax.axis_index("dom"), lax.axis_index("edge")]).astype(jnp.int32)
    cnt, neg = counts.T, neg_blocks.T
    g_mine, g_other, drel, rel16 = first_round(
        me, cnt, neg, src_rows, dst_rows, rel_ids, entities, relations
    )
    acc = relsum(0, rel_ids, drel, None, rels)
    ent, state, low = update(
        me, entities, entity_state.reshape(1, -1), [g_mine, across(g_other)], []
    )
    rel = relvec(1, rel_ids, rel16)
    for t in range(1, rounds - 1):
        far = shifted(low, -t)
        own = (low, across(low))
        query, source, s_hot, d_hot = source_side(t, me, src_rows, dst_rows, own, rel)
        far = held(far, [query, acc])
        far = (far, across(far))
        gd_mine, gd_other, target, weight, gpos = target_grad(t, shape, cnt, neg, far, query, d_hot)
        gs_mine, gs_other, drel = source_grad(
            t, shape, cnt, neg, target, weight, gpos, source, rel, s_hot
        )
        acc = relsum(t, rel_ids, drel, acc, rels)
        rel = relvec(t + 1, rel_ids, rel16)
        gd = sum_pair(gd_mine, across(gd_other))
        grads = [gs_mine, across(gs_other), shifted(gd, t)]
        ent, state, low = update(None, ent, state, grads, [rel])
    t = rounds - 1
    far = shifted(low, -t)
    own = (low, across(low))
    query, source, s_hot, d_hot = source_side(t, me, src_rows, dst_rows, own, rel)
    far = held(far, [query, acc])
    far = (far, across(far))
    drel, dsource, dterm = last_terms(t, shape, cnt, neg, far, query, d_hot, source, rel)
    gs_mine, gs_other, gd_mine, gd_other = both_grads(dsource, s_hot, dterm, d_hot)
    gd = sum_pair(gd_mine, across(gd_other))
    rel_new, rel_state, summed = relation_update(
        t, me, rel_ids, drel, acc, relations, relation_state, [gd_other], [gd]
    )
    grads = [gs_mine, across(gs_other), shifted(gd, t)]
    ent, state, low = update(None, ent, state, grads, [summed])
    ent, state = whole_partition(me, ent, across(ent), state, across(state))
    return (ent, state.reshape(-1), rel_new, rel_state)


def solution(mesh):
    return jax.shard_map(
        on_device,
        mesh=mesh,
        in_specs=(
            P(None, ("groups", "dom")),
            P(("groups", "dom")),
            P(None, "groups"),
            P("groups"),
            P(None, ("groups", "dom", "edge"), None),
            P(None, ("groups", "dom", "edge"), None),
            P(None, ("groups", "dom", "edge"), None),
            P(None, ("groups", "dom", "edge")),
            P(None, ("groups", "dom", "edge")),
        ),
        out_specs=(
            P(None, ("groups", "dom")),
            P(("groups", "dom")),
            P(None, "groups"),
            P("groups"),
        ),
        check_vma=False,
    )
```

```python
import functools

import jax
import jax.numpy as jnp
from jax import lax
from jax.experimental import pallas as pl
from jax.experimental.pallas import tpu as pltpu
from jax.sharding import PartitionSpec as P

learn_rate = 0.1
BF = jnp.bfloat16
F32 = jnp.float32
VMEM_LIMIT = 40 * 1024 * 1024
NN = (((1,), (0,)), ((), ()))
NT = (((1,), (1,)), ((), ()))
TN = (((0,), (0,)), ((), ()))


def mm(a, b, dims=NN):
    return lax.dot_general(a, b, dims, preferred_element_type=F32)


def vmem():
    return pl.BlockSpec(memory_space=pltpu.VMEM)


def smem():
    return pl.BlockSpec(memory_space=pltpu.SMEM)


def anywhere():
    return pl.BlockSpec(memory_space=pl.ANY)


def in_hbm(x):
    return pltpu.with_memory_space_constraint(x, pltpu.HBM)


def cost(flops, size):
    return pl.CostEstimate(flops=flops, bytes_accessed=size, transcendentals=0)


def params():
    return pltpu.CompilerParams(vmem_limit_bytes=VMEM_LIMIT)


def shifted(x, by):
    n = lax.axis_size("dom")
    return lax.ppermute(x, "dom", [(i, (i + by) % n) for i in range(n)])


def beside(x):
    n = lax.axis_size("dom")
    return lax.ppermute(x, "dom", [(i, i ^ 1) for i in range(n)])


def across(x):
    return lax.ppermute(x, "edge", [(0, 1), (1, 0)])


def one_hot(rows_ref, t, count, base):
    blocks, width = rows_ref.shape[1:]
    at = lax.broadcasted_iota(jnp.int32, (count, width), 0)
    idx = rows_ref[t]
    return jnp.concatenate(
        [
            jnp.where(at == base(idx[b : b + 1, :]), 1.0, 0.0).astype(BF)
            for b in range(blocks)
        ],
        axis=1,
    )


def relvec_kernel(t, ids_ref, rel_ref, out_ref):
    rels = rel_ref.shape[1]
    tile = min(rels, 512)
    out = None
    for lo in range(0, rels, tile):
        hot = one_hot(ids_ref, t, tile, lambda i, lo=lo: i - lo)
        part = mm(rel_ref[:, lo : lo + tile], hot)
        out = part if out is None else out + part
    out_ref[...] = out.astype(BF)


def relvec(t, rel_ids, rel16):
    width, rels = rel16.shape
    slots = rel_ids.shape[1] * rel_ids.shape[2]
    return pl.pallas_call(
        functools.partial(relvec_kernel, t),
        in_specs=[vmem()] * 2,
        out_specs=vmem(),
        out_shape=jax.ShapeDtypeStruct((width, slots), BF),
        compiler_params=params(),
        cost_estimate=cost(2 * width * rels * slots, 4 * width * rels),
        name="relvec",
    )(rel_ids, rel16)


def relsum_kernel(t, first, ids_ref, drel_ref, *refs):
    step = pl.program_id(0)
    out_ref = refs[-1]
    tile = out_ref.shape[1]
    hot = one_hot(ids_ref, t, tile, lambda i: i - step * tile)
    part = mm(drel_ref[...], hot, NT)
    out_ref[...] = part if first else refs[0][...] + part


def relsum(t, rel_ids, drel, acc, rels):
    width, slots = drel.shape
    tile = min(rels, 512)
    wide = pl.BlockSpec((width, tile), lambda i: (0, i))
    ins = [rel_ids, drel] + ([] if acc is None else [acc])
    return pl.pallas_call(
        functools.partial(relsum_kernel, t, acc is None),
        grid=(rels // tile,),
        in_specs=[
            pl.BlockSpec(rel_ids.shape, lambda i: (0, 0, 0)),
            pl.BlockSpec((width, slots), lambda i: (0, 0)),
        ]
        + ([] if acc is None else [wide]),
        out_specs=wide,
        out_shape=jax.ShapeDtypeStruct((width, rels), F32),
        input_output_aliases={} if acc is None else {2: 0},
        compiler_params=params(),
        cost_estimate=cost(2 * width * rels * slots, 8 * width * rels),
        name="relsum",
    )(*ins)


class Limits:
    scratch = lambda shape: [
        pltpu.SMEM((shape[1], shape[0]), jnp.int32),
        pltpu.SMEM((shape[1], shape[0]), jnp.int32),
        pltpu.SemaphoreType.DMA((2,)),
    ]

    def __init__(self, t, from_cnt, from_neg, cnt, neg, sems):
        self.t, self.cnt, self.neg = t, cnt, neg
        self.copies = [
            pltpu.make_async_copy(from_cnt, cnt, sems.at[0]),
            pltpu.make_async_copy(from_neg, neg, sems.at[1]),
        ]
        for copy in self.copies:
            copy.start()

    def wait(self):
        for copy in self.copies:
            copy.wait()

    def count(self, b):
        return self.cnt[b, self.t]

    def negative(self, b):
        return self.neg[b, self.t]


def place():
    dom = lax.axis_index("dom")
    return dom // 2, lax.rem(dom, 2), lax.axis_index("edge")


def localize(edge, half):
    def local(idx):
        moved = idx + edge * half
        return jnp.where(moved >= 2 * half, moved - 2 * half, moved)

    return local


def halves(x):
    hd = x.shape[0] // 2
    return x[:hd], x[hd:]


def make_query(source, rel):
    (s_re, s_im), (w_re, w_im) = halves(source), halves(rel)
    return jnp.concatenate(
        [s_re * w_re - s_im * w_im, s_re * w_im + s_im * w_re], axis=0
    ).astype(BF)


def conj_times(dq, v):
    (dq_re, dq_im), (v_re, v_im) = halves(dq), halves(v)
    return jnp.concatenate(
        [dq_re * v_re + dq_im * v_im, dq_im * v_re - dq_re * v_im], axis=0
    ).astype(BF)


def target_side(shape, limits, query, query_t, target, o_ref, d_ref, w_ref):
    _, blocks, width = shape
    lanes = lambda b: pl.ds(pl.multiple_of(b * width, width), width)
    count = limits.count
    o_ref[...] = target.astype(BF)
    query_f = query.astype(F32)
    pos = jnp.sum(query_f * target, axis=0, keepdims=True)
    lane = lax.broadcasted_iota(jnp.int32, (1, width), 1)
    limits.wait()
    row_i = lax.broadcasted_iota(jnp.int32, (width, width), 0)
    col_j = lax.broadcasted_iota(jnp.int32, (width, width), 1)
    weights = []
    for b in range(blocks):
        nb = limits.negative(b)
        neg = o_ref[:, lanes(nb)]
        at = slice(b * width, (b + 1) * width)
        scores = mm(query[:, at], neg, TN) if query_t is None else mm(query_t[at], neg)
        keep = jnp.logical_and(row_i < count(b), col_j < count(nb))
        weight = jnp.where(keep, jax.nn.sigmoid(scores) / width, 0.0).astype(BF)
        w_ref[:, at] = weight
        weights.append(weight)
    valid = jnp.concatenate(
        [jnp.where(lane < count(b), 1.0, 0.0) for b in range(blocks)], axis=1
    )
    gpos = -jax.nn.sigmoid(-pos) * valid
    d_ref[...] = gpos * query_f
    for b in range(blocks):
        d_ref[:, lanes(limits.negative(b))] += mm(query[:, b * width : (b + 1) * width], weights[b])
    return gpos


def make_dquery(shape, limits, gpos, o_ref, w_ref):
    _, blocks, width = shape
    lanes = lambda b: pl.ds(pl.multiple_of(b * width, width), width)
    out = []
    for b in range(blocks):
        nb = limits.negative(b)
        at = slice(b * width, (b + 1) * width)
        own = gpos[:, at] * o_ref[:, at].astype(F32)
        out.append(own + mm(o_ref[:, lanes(nb)], w_ref[:, at], NT))
    return jnp.concatenate(out, axis=1)


def first_kernel(
    shape, cnt_ref, neg_ref, src_ref, dst_ref, ids_ref, ent_ref, state_ref, rel_ref,
    g_mine, g_other, drel_ref, rel16_ref, ent_mine, state_mine,
    cnt, neg, lim_sems, src, dst, ids, ent, state, rel_buf, o_scr, d_scr, w_scr, in_sems, sems,
):
    rels = rel_buf.shape[1]
    tile = min(rels, 512)
    spans = range(0, rels, tile)
    inputs = [
        pltpu.make_async_copy(there, here, in_sems.at[i])
        for i, (there, here) in enumerate(
            [(src_ref.at[:1], src), (dst_ref.at[:1], dst), (ids_ref.at[:1], ids), (ent_ref, ent), (state_ref, state)]
        )
    ]
    loads = [
        pltpu.make_async_copy(
            rel_ref.at[:, lo : lo + tile], rel_buf.at[:, lo : lo + tile], sems.at[i]
        )
        for i, lo in enumerate(spans)
    ]
    for load in inputs:
        load.start()
    limits = Limits(0, cnt_ref, neg_ref, cnt, neg, lim_sems)
    for load in loads:
        load.start()
    half = ent.shape[1] // 2
    _, _, edge = place()
    local = localize(edge, half)
    inputs[0].wait()
    s_hot = one_hot(src, 0, 2 * half, local)
    inputs[1].wait()
    d_hot = one_hot(dst, 0, 2 * half, local)
    inputs[2].wait()
    ids_hot = [one_hot(ids, 0, tile, lambda i, lo=lo: i - lo) for lo in spans]
    inputs[3].wait()
    inputs[4].wait()
    mine = pl.ds(pl.multiple_of(edge * half, half), half)
    ent_mine[...] = ent[:, mine]
    state_mine[...] = state[:, mine]
    table = jnp.concatenate(
        [ent[:, pl.ds(pl.multiple_of(h * half, half), half)].astype(BF) for h in (edge, 1 - edge)],
        axis=1,
    )
    source = mm(table, s_hot)
    target = mm(table, d_hot)
    rel = None
    for load, lo, hot in zip(loads, spans, ids_hot):
        load.wait()
        low = rel_buf[:, lo : lo + tile].astype(BF)
        rel16_ref[:, lo : lo + tile] = low
        part = mm(low, hot)
        rel = part if rel is None else rel + part
    query = make_query(source, rel)
    gpos = target_side(shape, limits, query, None, target, o_scr, d_scr, w_scr)
    dq = make_dquery(shape, limits, gpos, o_scr, w_scr)
    drel_ref[...] = conj_times(dq, source)
    total = mm(conj_times(dq, rel), s_hot, NT) + mm(d_scr[...].astype(BF), d_hot, NT)
    g_mine[...] = total[:, :half]
    g_other[...] = total[:, half:].astype(BF)


def first_round(cnt, neg, src, dst, rel_ids, entities, state, relations):
    dim, rows = entities.shape
    rels = relations.shape[1]
    _, blocks, width = src.shape
    slots = blocks * width
    sds = jax.ShapeDtypeStruct
    return pl.pallas_call(
        functools.partial(first_kernel, src.shape),
        in_specs=[anywhere()] * 8,
        out_specs=[vmem()] * 6,
        out_shape=[
            sds((dim, rows // 2), F32),
            sds((dim, rows // 2), BF),
            sds((dim, slots), BF),
            sds((dim, rels), BF),
            sds((dim, rows // 2), F32),
            sds((1, rows // 2), F32),
        ],
        scratch_shapes=Limits.scratch(src.shape)
        + [
            pltpu.VMEM((1, blocks, width), jnp.int32),
            pltpu.VMEM((1, blocks, width), jnp.int32),
            pltpu.VMEM((1, blocks, width), jnp.int32),
            pltpu.VMEM((dim, rows), F32),
            pltpu.VMEM((1, rows), F32),
            pltpu.VMEM((dim, rels), F32),
            pltpu.VMEM((dim, slots), BF),
            pltpu.VMEM((dim, slots), F32),
            pltpu.VMEM((width, slots), BF),
            pltpu.SemaphoreType.DMA((5,)),
            pltpu.SemaphoreType.DMA((-(-rels // min(rels, 512)),)),
        ],
        compiler_params=params(),
        cost_estimate=cost(2 * dim * slots * (rels + 4 * rows), 8 * dim * rels),
        name="first_round",
    )(*(in_hbm(x) for x in (cnt, neg, src, dst, rel_ids, entities, state, relations)))


def source_kernel(
    t, src_ref, dst_ref, own0, own1, rel_ref,
    query_ref, query_t_ref, source_ref, s_hot_ref, d_hot_ref, d_hot_t_ref,
):
    half = own0.shape[1]
    local = localize(place()[2], half)
    s_hot = one_hot(src_ref, t, 2 * half, local)
    d_hot = one_hot(dst_ref, t, 2 * half, local)
    s_hot_ref[...] = s_hot
    d_hot_ref[...] = d_hot
    d_hot_t_ref[...] = d_hot.T
    source = mm(jnp.concatenate([own0[...], own1[...]], axis=1), s_hot)
    source_ref[...] = source.astype(BF)
    query = make_query(source, rel_ref[...].astype(F32))
    query_ref[...] = query
    query_t_ref[...] = query.T


def source_side(t, src, dst, own, rel):
    dim, slots = rel.shape
    rows = 2 * own[0].shape[1]
    sds = lambda *shape: jax.ShapeDtypeStruct(shape, BF)
    return pl.pallas_call(
        functools.partial(source_kernel, t),
        in_specs=[vmem()] * 5,
        out_specs=[vmem()] * 6,
        out_shape=[
            sds(dim, slots), sds(slots, dim), sds(dim, slots),
            sds(rows, slots), sds(rows, slots), sds(slots, rows),
        ],
        compiler_params=params(),
        cost_estimate=cost(2 * dim * slots * rows, 12 * dim * slots),
        name="source_side",
    )(src, dst, *own, rel)


def target_kernel(
    t, shape, cnt_ref, neg_ref, far0, far1, query_ref, query_t_ref, d_hot_ref, d_hot_t_ref,
    gd_mine, gd_other, o_ref, w_ref, gpos_ref, cnt, neg, sems, d_scr,
):
    limits = Limits(t, cnt_ref, neg_ref, cnt, neg, sems)
    half = far0.shape[1]
    far = jnp.concatenate([far0[...], far1[...]], axis=1)
    target = mm(far, d_hot_ref[...])
    gpos_ref[...] = target_side(
        shape, limits, query_ref[...], query_t_ref, target, o_ref, d_scr, w_ref
    )
    gd = mm(d_scr[...].astype(BF), d_hot_t_ref[...])
    gd_mine[...] = gd[:, :half]
    gd_other[...] = gd[:, half:].astype(BF)


def target_grad(t, shape, cnt, neg, far, query, query_t, d_hot, d_hot_t):
    dim, slots = query.shape
    half = far[0].shape[1]
    width = shape[2]
    sds = jax.ShapeDtypeStruct
    return pl.pallas_call(
        functools.partial(target_kernel, t, shape),
        in_specs=[anywhere()] * 2 + [vmem()] * 6,
        out_specs=[vmem()] * 5,
        out_shape=[
            sds((dim, half), F32),
            sds((dim, half), BF),
            sds((dim, slots), BF),
            sds((width, slots), BF),
            sds((1, slots), F32),
        ],
        scratch_shapes=Limits.scratch(shape) + [pltpu.VMEM((dim, slots), F32)],
        compiler_params=params(),
        cost_estimate=cost(4 * dim * slots * (2 * half + width), 12 * dim * slots),
        name="target_grad",
    )(cnt, neg, *far, query, query_t, d_hot, d_hot_t)


def source_grad_kernel(
    t, shape, cnt_ref, neg_ref, _, o_ref, w_ref, gpos_ref, source_ref, rel_ref, s_hot_ref,
    gs_mine, gs_other, drel_ref, cnt, neg, sems,
):
    limits = Limits(t, cnt_ref, neg_ref, cnt, neg, sems)
    limits.wait()
    half = gs_mine.shape[1]
    dq = make_dquery(shape, limits, gpos_ref[...], o_ref, w_ref)
    drel_ref[...] = conj_times(dq, source_ref[...].astype(F32))
    gs = mm(conj_times(dq, rel_ref[...].astype(F32)), s_hot_ref[...], NT)
    gs_mine[...] = gs[:, :half]
    gs_other[...] = gs[:, half:].astype(BF)


def source_grad(t, shape, cnt, neg, after, target, weight, gpos, source, rel, s_hot):
    dim, slots = rel.shape
    half = s_hot.shape[0] // 2
    sds = jax.ShapeDtypeStruct
    return pl.pallas_call(
        functools.partial(source_grad_kernel, t, shape),
        in_specs=[anywhere()] * 3 + [vmem()] * 6,
        out_specs=[vmem()] * 3,
        out_shape=[sds((dim, half), F32), sds((dim, half), BF), sds((dim, slots), BF)],
        scratch_shapes=Limits.scratch(shape),
        compiler_params=params(),
        cost_estimate=cost(4 * dim * slots * half, 12 * dim * slots),
        name="source_grad",
    )(cnt, neg, after, target, weight, gpos, source, rel, s_hot)


def last_kernel(
    t, shape, cnt_ref, neg_ref, far0, far1, query_ref, query_t_ref, d_hot_ref, source_ref, rel_ref,
    drel_ref, dsource_ref, dterm_ref, cnt, neg, sems, o_scr, d_scr, w_scr,
):
    limits = Limits(t, cnt_ref, neg_ref, cnt, neg, sems)
    far = jnp.concatenate([far0[...], far1[...]], axis=1)
    target = mm(far, d_hot_ref[...])
    gpos = target_side(
        shape, limits, query_ref[...], query_t_ref, target, o_scr, d_scr, w_scr
    )
    dterm_ref[...] = d_scr[...].astype(BF)
    dq = make_dquery(shape, limits, gpos, o_scr, w_scr)
    drel_ref[...] = conj_times(dq, source_ref[...].astype(F32))
    dsource_ref[...] = conj_times(dq, rel_ref[...].astype(F32))


def last_terms(t, shape, cnt, neg, far, query, query_t, d_hot, source, rel):
    dim, slots = query.shape
    return pl.pallas_call(
        functools.partial(last_kernel, t, shape),
        in_specs=[anywhere()] * 2 + [vmem()] * 7,
        out_specs=[vmem()] * 3,
        out_shape=[jax.ShapeDtypeStruct((dim, slots), BF)] * 3,
        scratch_shapes=Limits.scratch(shape)
        + [
            pltpu.VMEM((dim, slots), BF),
            pltpu.VMEM((dim, slots), F32),
            pltpu.VMEM((shape[2], slots), BF),
        ],
        compiler_params=params(),
        cost_estimate=cost(6 * dim * slots * shape[2], 12 * dim * slots),
        name="last_terms",
    )(cnt, neg, *far, query, query_t, d_hot, source, rel)


def both_kernel(dsource_ref, s_hot_ref, dterm_ref, d_hot_t_ref, gs_mine, gs_other, gd_mine, gd_other):
    half = gs_mine.shape[1]
    for terms, hot, dims, mine, other in (
        (dterm_ref, d_hot_t_ref, NN, gd_mine, gd_other),
        (dsource_ref, s_hot_ref, NT, gs_mine, gs_other),
    ):
        grad = mm(terms[...], hot[...], dims)
        mine[...] = grad[:, :half]
        other[...] = grad[:, half:].astype(BF)


def both_grads(dsource, s_hot, dterm, d_hot_t):
    dim, slots = dterm.shape
    half = s_hot.shape[0] // 2
    sds = jax.ShapeDtypeStruct
    return pl.pallas_call(
        both_kernel,
        in_specs=[vmem()] * 4,
        out_specs=[vmem()] * 4,
        out_shape=[sds((dim, half), F32), sds((dim, half), BF)] * 2,
        compiler_params=params(),
        cost_estimate=cost(8 * dim * slots * half, 12 * dim * slots),
        name="both_grads",
    )(dsource, s_hot, dterm, d_hot_t)


def update_kernel(n_grads, last, *refs):
    ent_ref, state_ref, grads = refs[0], refs[1], refs[2 : 2 + n_grads]
    grad = grads[0][...].astype(F32)
    for g in grads[1:]:
        grad = grad + g[...].astype(F32)
    dim = grad.shape[0]
    state = state_ref[...] + jnp.sum(grad * grad, axis=0, keepdims=True) / dim
    new = ent_ref[...] - grad * (learn_rate / jnp.sqrt(state))
    if last:
        refs[-1][:dim] = new
        refs[-1][dim:] = jnp.broadcast_to(state, (refs[-1].shape[0] - dim, state.shape[1]))
    else:
        refs[-3][...] = new
        refs[-2][...] = state
        refs[-1][...] = new.astype(BF)


def update(ent, state, grads, after, last=False):
    dim, half = ent.shape
    sds = jax.ShapeDtypeStruct
    outs = [sds((dim, half), F32), sds((1, half), F32), sds((dim, half), BF)]
    if last:
        outs = [sds((dim + 8, half), F32)]
    return pl.pallas_call(
        functools.partial(update_kernel, len(grads), last),
        in_specs=[vmem()] * (2 + len(grads)) + [anywhere()] * len(after),
        out_specs=[vmem()] * len(outs),
        out_shape=outs,
        compiler_params=params(),
        cost_estimate=cost(10 * dim * half, 16 * dim * half),
        name="update",
    )(ent, state, *grads, *after)


def pair_kernel(a_ref, b_ref, out_ref):
    out_ref[...] = (a_ref[...] + b_ref[...].astype(F32)).astype(BF)


def sum_pair(a, b):
    return pl.pallas_call(
        pair_kernel,
        in_specs=[vmem()] * 2,
        out_specs=vmem(),
        out_shape=jax.ShapeDtypeStruct(a.shape, BF),
        compiler_params=params(),
        name="sum_pair",
    )(a, b)


def held_kernel(x_ref, *refs):
    pass


def held(x, after):
    return pl.pallas_call(
        held_kernel,
        in_specs=[anywhere()] * (1 + len(after)),
        out_specs=anywhere(),
        out_shape=jax.ShapeDtypeStruct(x.shape, x.dtype),
        input_output_aliases={0: 0},
        compiler_params=params(),
        name="held",
    )(x, *after)


def whole_kernel(mine, theirs, ent_out, state_out):
    dim, rows = ent_out.shape
    half = rows // 2
    edge = place()[2]
    for core, part in ((edge, mine), (1 - edge, theirs)):
        at = pl.ds(pl.multiple_of(core * half, half), half)
        ent_out[:, at] = part[:dim]
        state_out[:, at] = part[dim : dim + 1]


def whole_partition(mine, theirs):
    dim, half = mine.shape[0] - 8, mine.shape[1]
    return pl.pallas_call(
        whole_kernel,
        in_specs=[vmem()] * 2,
        out_specs=[vmem()] * 2,
        out_shape=[
            jax.ShapeDtypeStruct((dim, 2 * half), F32),
            jax.ShapeDtypeStruct((1, 2 * half), F32),
        ],
        compiler_params=params(),
        name="whole_partition",
    )(mine, theirs)


def first_column(owner, core, w):
    return pl.multiple_of((2 * owner + core) * w, w)


def pieces_kernel(t, nz, same, ids_ref, drel_ref, acc_ref, *refs):
    mine, other = refs[-nz - 1 : -1], refs[-1]
    w = other.shape[2]
    z, x, edge = place()
    drel = drel_ref[...]
    for k in range(nz):
        owner = 2 * lax.rem(z + k, nz) + (x if same else 1 - x)
        at = [first_column(owner, core, w) for core in (edge, 1 - edge)]
        hot = jnp.concatenate([one_hot(ids_ref, t, w, lambda i, lo=lo: i - lo) for lo in at], axis=0)
        part = mm(drel, hot, NT)
        mine[k][...] = acc_ref[:, pl.ds(at[0], w)] + part[:, :w]
        other[k] = (acc_ref[:, pl.ds(at[1], w)] + part[:, w:]).astype(BF)


def pieces(t, n, same, rel_ids, drel, acc, after):
    dim, rels = acc.shape
    w = rels // (2 * n)
    sds = jax.ShapeDtypeStruct
    out = pl.pallas_call(
        functools.partial(pieces_kernel, t, n // 2, same),
        in_specs=[vmem()] * 3 + [anywhere()] * len(after),
        out_specs=[vmem()] * (n // 2 + 1),
        out_shape=[sds((dim, w), F32)] * (n // 2) + [sds((n // 2, dim, w), BF)],
        compiler_params=params(),
        cost_estimate=cost(dim * rels * drel.shape[1], 4 * dim * rels),
        name="pieces",
    )(rel_ids, drel, acc, *after)
    return out[:-1], out[-1]


def add_kernel(n, *refs):
    for k in range(n):
        refs[n + 1 + k][...] = (refs[k][...] + refs[n][k].astype(F32)).astype(BF)


def add_each(mine, theirs):
    n = len(mine)
    return pl.pallas_call(
        functools.partial(add_kernel, n),
        in_specs=[vmem()] * (n + 1),
        out_specs=[vmem()] * n,
        out_shape=[jax.ShapeDtypeStruct(x.shape, BF) for x in mine],
        compiler_params=params(),
        name="add_each",
    )(*mine, theirs)


def sum_kernel(k, count, mine, theirs, *refs):
    total = mine[...] + theirs[k].astype(F32)
    for r in refs[:count]:
        total = total + r[...].astype(F32)
    refs[-1][...] = total.astype(BF)


def sum_piece(k, mine, theirs, parts, after):
    return pl.pallas_call(
        functools.partial(sum_kernel, k, len(parts)),
        in_specs=[vmem()] * (2 + len(parts)) + [anywhere()] * len(after),
        out_specs=vmem(),
        out_shape=jax.ShapeDtypeStruct(mine.shape, BF),
        compiler_params=params(),
        name="sum_piece",
    )(mine, theirs, *parts, *after)


def relnew_kernel(nz, same, ks, rel_ref, state_ref, *refs):
    got = refs[: 2 * len(ks)]
    rel_out, state_out, buf, sems = refs[-4:]
    w = got[0].shape[1]
    state_out[...] = refs[-5][...]
    z, x, edge = place()
    copies = []
    for i, grad_ref in enumerate(got):
        owner = 2 * lax.rem(z + nz - ks[i // 2], nz) + (x if same else 1 - x)
        at = pl.ds(first_column(owner, edge if i % 2 == 0 else 1 - edge, w), w)
        grad = grad_ref[...].astype(F32)
        state = state_ref[:, at] + jnp.sum(grad * grad, axis=0, keepdims=True) / grad.shape[0]
        state_out[:, at] = state
        buf[i] = rel_ref[:, at] - grad * (learn_rate / jnp.sqrt(state))
        copy = pltpu.make_async_copy(buf.at[i], rel_out.at[:, at], sems.at[i])
        copy.start()
        copies.append(copy)
    for copy in copies:
        copy.wait()


def relnew(nz, same, ks, relations, state, got, before):
    dim, rels = relations.shape
    w = got[0].shape[1]
    start = [state] if before is None else list(before)
    return pl.pallas_call(
        functools.partial(relnew_kernel, nz, same, ks),
        in_specs=[vmem()] * (2 + len(got)) + ([anywhere()] if before else []) + [vmem()],
        out_specs=[anywhere(), vmem()],
        out_shape=[jax.ShapeDtypeStruct((dim, rels), F32), jax.ShapeDtypeStruct((1, rels), F32)],
        input_output_aliases={2 + len(got): 0} if before else {},
        scratch_shapes=[pltpu.VMEM((len(got), dim, w), F32), pltpu.SemaphoreType.DMA((len(got),))],
        compiler_params=params(),
        cost_estimate=cost(4 * dim * w * len(got), 4 * dim * w * len(got)),
        name="relnew",
    )(relations, state, *got, *start)


def relation_update(t, rel_ids, drel, acc, relations, state, gd_other, gd, finish):
    n = lax.axis_size("dom")
    dim, rels = relations.shape
    if n % 2 or rels % (256 * n):
        total = lax.psum(relsum(t, rel_ids, drel, acc, rels), ("dom", "edge"))
        state = state + jnp.mean(total * total, axis=0)
        return relations - learn_rate * total / jnp.sqrt(state)[None, :], state, finish()
    nz = n // 2
    near = sorted(range(nz), key=lambda k: min(k, nz - k))
    mine_x, other_x = pieces(t, n, False, rel_ids, drel, acc, [gd_other])
    mine_s, other_s = pieces(t, n, True, rel_ids, drel, acc, [gd])
    to_x = add_each(mine_x, across(other_x))
    theirs = across(other_s)
    from_x = [beside(piece) for piece in to_x]
    done = finish()
    from_z = []
    for k in reversed(near[1:]):
        after = [done[0]] if k == near[1] else []
        piece = sum_piece(k, mine_s[k], theirs, [from_x[k]], after)
        from_z.append(shifted(piece, 2 * k))
    summed = sum_piece(0, mine_s[0], theirs, [from_x[0]] + from_z, [done[1]])
    got = [summed if k == 0 else shifted(summed, 2 * k) for k in range(nz)]
    got_x = [beside(piece) for piece in got]
    state = state.reshape(1, rels)
    pairs = lambda ks, parts: [y for k in ks for y in (parts[k], across(parts[k]))]
    new = relnew(nz, True, near, relations, state, pairs(near, got), None)
    early, late = near[: nz // 2], near[nz // 2 :]
    new = relnew(nz, False, early, relations, state, pairs(early, got_x), new)
    got_x[near[-1]] = held(got_x[near[-1]], [new[0]])
    rel_new, state_new = relnew(nz, False, late, relations, state, pairs(late, got_x), new)
    return rel_new, state_new.reshape(rels), done


def on_device(
    entities,
    entity_state,
    relations,
    relation_state,
    src_rows,
    rel_ids,
    dst_rows,
    counts,
    neg_blocks,
):
    rounds = src_rows.shape[0]
    rels = relations.shape[1]
    shape = src_rows.shape
    cnt, neg = counts.T, neg_blocks.T
    g_mine, g_other, drel, rel16, ent, state = first_round(
        cnt, neg, src_rows, dst_rows, rel_ids, entities, entity_state.reshape(1, -1), relations
    )
    acc = relsum(0, rel_ids, drel, None, rels)
    ent, state, low = update(ent, state, [g_mine, across(g_other)], [])
    rel = relvec(1, rel_ids, rel16)
    for t in range(1, rounds):
        far = shifted(low, -t)
        own = (low, across(low))
        query, query_t, source, s_hot, d_hot, d_hot_t = source_side(t, src_rows, dst_rows, own, rel)
        far = held(far, [query, acc])
        far = (far, across(far))
        if t == rounds - 1:
            break
        gd_mine, gd_other, target, weight, gpos = target_grad(
            t, shape, cnt, neg, far, query, query_t, d_hot, d_hot_t
        )
        gd = sum_pair(gd_mine, across(gd_other))
        gs_mine, gs_other, drel = source_grad(
            t, shape, cnt, neg, gd, target, weight, gpos, source, rel, s_hot
        )
        acc = relsum(t, rel_ids, drel, acc, rels)
        rel = relvec(t + 1, rel_ids, rel16)
        grads = [gs_mine, across(gs_other), shifted(gd, t)]
        ent, state, low = update(ent, state, grads, [rel])
    drel, dsource, dterm = last_terms(t, shape, cnt, neg, far, query, query_t, d_hot, source, rel)
    gs_mine, gs_other, gd_mine, gd_other = both_grads(dsource, s_hot, dterm, d_hot_t)
    gd = sum_pair(gd_mine, across(gd_other))

    def finish():
        (mine,) = update(ent, state, [gs_mine, across(gs_other), shifted(gd, t)], [], last=True)
        ent_out, state_out = whole_partition(mine, across(mine))
        return mine, ent_out, state_out

    rel_new, rel_state, done = relation_update(
        t, rel_ids, drel, acc, relations, relation_state, gd_other, gd, finish
    )
    return (done[1], done[2].reshape(-1), rel_new, rel_state)


def solution(mesh):
    return jax.shard_map(
        on_device,
        mesh=mesh,
        in_specs=(
            P(None, ("groups", "dom")),
            P(("groups", "dom")),
            P(None, "groups"),
            P("groups"),
            P(None, ("groups", "dom", "edge"), None),
            P(None, ("groups", "dom", "edge"), None),
            P(None, ("groups", "dom", "edge"), None),
            P(None, ("groups", "dom", "edge")),
            P(None, ("groups", "dom", "edge")),
        ),
        out_specs=(
            P(None, ("groups", "dom")),
            P(("groups", "dom")),
            P(None, "groups"),
            P("groups"),
        ),
        check_vma=False,
    )
```

```python
import functools

import jax
import jax.numpy as jnp
from jax import lax
from jax.experimental import pallas as pl
from jax.experimental.pallas import tpu as pltpu
from jax.sharding import PartitionSpec as P

learn_rate = 0.1
BF = jnp.bfloat16
F32 = jnp.float32
VMEM_LIMIT = 40 * 1024 * 1024
NN = (((1,), (0,)), ((), ()))
NT = (((1,), (1,)), ((), ()))
TN = (((0,), (0,)), ((), ()))


def mm(a, b, dims=NN):
    return lax.dot_general(a, b, dims, preferred_element_type=F32)


def vmem():
    return pl.BlockSpec(memory_space=pltpu.VMEM)


def smem():
    return pl.BlockSpec(memory_space=pltpu.SMEM)


def anywhere():
    return pl.BlockSpec(memory_space=pl.ANY)


def in_hbm(x):
    return pltpu.with_memory_space_constraint(x, pltpu.HBM)


def cost(flops, size):
    return pl.CostEstimate(flops=flops, bytes_accessed=size, transcendentals=0)


def params():
    return pltpu.CompilerParams(vmem_limit_bytes=VMEM_LIMIT)


def shifted(x, by):
    n = lax.axis_size("dom")
    return lax.ppermute(x, "dom", [(i, (i + by) % n) for i in range(n)])


def beside(x):
    n = lax.axis_size("dom")
    return lax.ppermute(x, "dom", [(i, i ^ 1) for i in range(n)])


def across(x):
    return lax.ppermute(x, "edge", [(0, 1), (1, 0)])


def one_hot(rows_ref, t, count, base):
    blocks, width = rows_ref.shape[1:]
    at = lax.broadcasted_iota(jnp.int32, (count, width), 0)
    idx = rows_ref[t]
    return jnp.concatenate(
        [
            jnp.where(at == base(idx[b : b + 1, :]), 1.0, 0.0).astype(BF)
            for b in range(blocks)
        ],
        axis=1,
    )


def relvec_kernel(t, ids_ref, rel_ref, out_ref):
    rels = rel_ref.shape[1]
    tile = min(rels, 512)
    out = None
    for lo in range(0, rels, tile):
        hot = one_hot(ids_ref, t, tile, lambda i, lo=lo: i - lo)
        part = mm(rel_ref[:, lo : lo + tile], hot)
        out = part if out is None else out + part
    out_ref[...] = out.astype(BF)


def relvec(t, rel_ids, rel16):
    width, rels = rel16.shape
    slots = rel_ids.shape[1] * rel_ids.shape[2]
    return pl.pallas_call(
        functools.partial(relvec_kernel, t),
        in_specs=[vmem()] * 2,
        out_specs=vmem(),
        out_shape=jax.ShapeDtypeStruct((width, slots), BF),
        compiler_params=params(),
        cost_estimate=cost(width * slots, width * slots),
        name="relvec",
    )(rel_ids, rel16)


def relsum_kernel(t, first, ids_ref, drel_ref, *refs):
    step = pl.program_id(0)
    out_ref = refs[-1]
    tile = out_ref.shape[1]
    hot = one_hot(ids_ref, t, tile, lambda i: i - step * tile)
    part = mm(drel_ref[...], hot, NT)
    out_ref[...] = part if first else refs[0][...] + part


def relsum(t, rel_ids, drel, acc, rels):
    width, slots = drel.shape
    tile = min(rels, 512)
    wide = pl.BlockSpec((width, tile), lambda i: (0, i))
    ins = [rel_ids, drel] + ([] if acc is None else [acc])
    return pl.pallas_call(
        functools.partial(relsum_kernel, t, acc is None),
        grid=(rels // tile,),
        in_specs=[
            pl.BlockSpec(rel_ids.shape, lambda i: (0, 0, 0)),
            pl.BlockSpec((width, slots), lambda i: (0, 0)),
        ]
        + ([] if acc is None else [wide]),
        out_specs=wide,
        out_shape=jax.ShapeDtypeStruct((width, rels), F32),
        input_output_aliases={} if acc is None else {2: 0},
        compiler_params=params(),
        cost_estimate=cost(width * slots, width * slots),
        name="relsum",
    )(*ins)


class Limits:
    scratch = lambda shape: [
        pltpu.SMEM((shape[1], shape[0]), jnp.int32),
        pltpu.SMEM((shape[1], shape[0]), jnp.int32),
        pltpu.SemaphoreType.DMA((2,)),
    ]

    def __init__(self, t, from_cnt, from_neg, cnt, neg, sems):
        self.t, self.cnt, self.neg = t, cnt, neg
        self.copies = [
            pltpu.make_async_copy(from_cnt, cnt, sems.at[0]),
            pltpu.make_async_copy(from_neg, neg, sems.at[1]),
        ]
        for copy in self.copies:
            copy.start()

    def wait(self):
        for copy in self.copies:
            copy.wait()

    def count(self, b):
        return self.cnt[b, self.t]

    def negative(self, b):
        return self.neg[b, self.t]


def place():
    dom = lax.axis_index("dom")
    return dom // 2, lax.rem(dom, 2), lax.axis_index("edge")


def localize(edge, half):
    def local(idx):
        moved = idx + edge * half
        return jnp.where(moved >= 2 * half, moved - 2 * half, moved)

    return local


def halves(x):
    hd = x.shape[0] // 2
    return x[:hd], x[hd:]


def make_query(source, rel):
    (s_re, s_im), (w_re, w_im) = halves(source), halves(rel)
    return jnp.concatenate(
        [s_re * w_re - s_im * w_im, s_re * w_im + s_im * w_re], axis=0
    ).astype(BF)


def conj_times(dq, v):
    (dq_re, dq_im), (v_re, v_im) = halves(dq), halves(v)
    return jnp.concatenate(
        [dq_re * v_re + dq_im * v_im, dq_im * v_re - dq_re * v_im], axis=0
    ).astype(BF)


def target_side(shape, limits, query, query_t, target, o_ref, d_ref, w_ref):
    _, blocks, width = shape
    lanes = lambda b: pl.ds(pl.multiple_of(b * width, width), width)
    count = limits.count
    o_ref[...] = target.astype(BF)
    query_f = query.astype(F32)
    pos = jnp.sum(query_f * target, axis=0, keepdims=True)
    lane = lax.broadcasted_iota(jnp.int32, (1, width), 1)
    limits.wait()
    row_i = lax.broadcasted_iota(jnp.int32, (width, width), 0)
    col_j = lax.broadcasted_iota(jnp.int32, (width, width), 1)
    weights = []
    for b in range(blocks):
        nb = limits.negative(b)
        neg = o_ref[:, lanes(nb)]
        at = slice(b * width, (b + 1) * width)
        scores = mm(query[:, at], neg, TN) if query_t is None else mm(query_t[at], neg)
        keep = jnp.logical_and(row_i < count(b), col_j < count(nb))
        weight = jnp.where(keep, jax.nn.sigmoid(scores) / width, 0.0).astype(BF)
        w_ref[:, at] = weight
        weights.append(weight)
    valid = jnp.concatenate(
        [jnp.where(lane < count(b), 1.0, 0.0) for b in range(blocks)], axis=1
    )
    gpos = -jax.nn.sigmoid(-pos) * valid
    d_ref[...] = gpos * query_f
    for b in range(blocks):
        d_ref[:, lanes(limits.negative(b))] += mm(query[:, b * width : (b + 1) * width], weights[b])
    return gpos


def make_dquery(shape, limits, gpos, o_ref, w_ref):
    _, blocks, width = shape
    lanes = lambda b: pl.ds(pl.multiple_of(b * width, width), width)
    out = []
    for b in range(blocks):
        nb = limits.negative(b)
        at = slice(b * width, (b + 1) * width)
        own = gpos[:, at] * o_ref[:, at].astype(F32)
        out.append(own + mm(o_ref[:, lanes(nb)], w_ref[:, at], NT))
    return jnp.concatenate(out, axis=1)


def first_kernel(
    shape, cnt_ref, neg_ref, src_ref, dst_ref, ids_ref, ent_ref, state_ref, rel_ref,
    g_mine, g_other, drel_ref, rel16_ref, ent_mine, state_mine,
    cnt, neg, lim_sems, src, dst, ids, ent, state, rel_buf, o_scr, d_scr, w_scr, in_sems, sems,
):
    rels = rel_buf.shape[1]
    tile = min(rels, 512)
    spans = range(0, rels, tile)
    inputs = [
        pltpu.make_async_copy(there, here, in_sems.at[i])
        for i, (there, here) in enumerate(
            [(src_ref.at[:1], src), (dst_ref.at[:1], dst), (ids_ref.at[:1], ids), (ent_ref, ent), (state_ref, state)]
        )
    ]
    loads = [
        pltpu.make_async_copy(
            rel_ref.at[:, lo : lo + tile], rel_buf.at[:, lo : lo + tile], sems.at[i]
        )
        for i, lo in enumerate(spans)
    ]
    for load in inputs:
        load.start()
    limits = Limits(0, cnt_ref, neg_ref, cnt, neg, lim_sems)
    for load in loads:
        load.start()
    half = ent.shape[1] // 2
    _, _, edge = place()
    local = localize(edge, half)
    inputs[0].wait()
    s_hot = one_hot(src, 0, 2 * half, local)
    inputs[1].wait()
    d_hot = one_hot(dst, 0, 2 * half, local)
    inputs[2].wait()
    ids_hot = [one_hot(ids, 0, tile, lambda i, lo=lo: i - lo) for lo in spans]
    inputs[3].wait()
    inputs[4].wait()
    mine = pl.ds(pl.multiple_of(edge * half, half), half)
    ent_mine[...] = ent[:, mine]
    state_mine[...] = state[:, mine]
    table = jnp.concatenate(
        [ent[:, pl.ds(pl.multiple_of(h * half, half), half)].astype(BF) for h in (edge, 1 - edge)],
        axis=1,
    )
    source = mm(table, s_hot)
    target = mm(table, d_hot)
    rel = None
    for load, lo, hot in zip(loads, spans, ids_hot):
        load.wait()
        low = rel_buf[:, lo : lo + tile].astype(BF)
        rel16_ref[:, lo : lo + tile] = low
        part = mm(low, hot)
        rel = part if rel is None else rel + part
    query = make_query(source, rel)
    gpos = target_side(shape, limits, query, None, target, o_scr, d_scr, w_scr)
    dq = make_dquery(shape, limits, gpos, o_scr, w_scr)
    drel_ref[...] = conj_times(dq, source)
    total = mm(conj_times(dq, rel), s_hot, NT) + mm(d_scr[...].astype(BF), d_hot, NT)
    g_mine[...] = total[:, :half]
    g_other[...] = total[:, half:].astype(BF)


def first_round(cnt, neg, src, dst, rel_ids, entities, state, relations):
    dim, rows = entities.shape
    rels = relations.shape[1]
    _, blocks, width = src.shape
    slots = blocks * width
    sds = jax.ShapeDtypeStruct
    return pl.pallas_call(
        functools.partial(first_kernel, src.shape),
        in_specs=[anywhere()] * 8,
        out_specs=[vmem()] * 6,
        out_shape=[
            sds((dim, rows // 2), F32),
            sds((dim, rows // 2), BF),
            sds((dim, slots), BF),
            sds((dim, rels), BF),
            sds((dim, rows // 2), F32),
            sds((1, rows // 2), F32),
        ],
        scratch_shapes=Limits.scratch(src.shape)
        + [
            pltpu.VMEM((1, blocks, width), jnp.int32),
            pltpu.VMEM((1, blocks, width), jnp.int32),
            pltpu.VMEM((1, blocks, width), jnp.int32),
            pltpu.VMEM((dim, rows), F32),
            pltpu.VMEM((1, rows), F32),
            pltpu.VMEM((dim, rels), F32),
            pltpu.VMEM((dim, slots), BF),
            pltpu.VMEM((dim, slots), F32),
            pltpu.VMEM((width, slots), BF),
            pltpu.SemaphoreType.DMA((5,)),
            pltpu.SemaphoreType.DMA((-(-rels // min(rels, 512)),)),
        ],
        compiler_params=params(),
        cost_estimate=cost(2 * dim * slots * (rels + 4 * rows), 8 * dim * rels),
        name="first_round",
    )(*(in_hbm(x) for x in (cnt, neg, src, dst, rel_ids, entities, state, relations)))


def source_kernel(
    t, src_ref, dst_ref, own0, own1, rel_ref,
    query_ref, query_t_ref, source_ref, s_hot_ref, d_hot_ref, d_hot_t_ref,
):
    half = own0.shape[1]
    local = localize(place()[2], half)
    s_hot = one_hot(src_ref, t, 2 * half, local)
    d_hot = one_hot(dst_ref, t, 2 * half, local)
    s_hot_ref[...] = s_hot
    d_hot_ref[...] = d_hot
    d_hot_t_ref[...] = d_hot.T
    source = mm(jnp.concatenate([own0[...], own1[...]], axis=1), s_hot)
    source_ref[...] = source.astype(BF)
    query = make_query(source, rel_ref[...].astype(F32))
    query_ref[...] = query
    query_t_ref[...] = query.T


def source_side(t, src, dst, own, rel):
    dim, slots = rel.shape
    rows = 2 * own[0].shape[1]
    sds = lambda *shape: jax.ShapeDtypeStruct(shape, BF)
    return pl.pallas_call(
        functools.partial(source_kernel, t),
        in_specs=[vmem()] * 5,
        out_specs=[vmem()] * 6,
        out_shape=[
            sds(dim, slots), sds(slots, dim), sds(dim, slots),
            sds(rows, slots), sds(rows, slots), sds(slots, rows),
        ],
        compiler_params=params(),
        cost_estimate=cost(dim * slots, dim * slots),
        name="source_side",
    )(src, dst, *own, rel)


def target_kernel(
    t, shape, cnt_ref, neg_ref, far0, far1, query_ref, query_t_ref, d_hot_ref, d_hot_t_ref,
    gd_mine, gd_other, o_ref, w_ref, gpos_ref, cnt, neg, sems, d_scr,
):
    limits = Limits(t, cnt_ref, neg_ref, cnt, neg, sems)
    half = far0.shape[1]
    far = jnp.concatenate([far0[...], far1[...]], axis=1)
    target = mm(far, d_hot_ref[...])
    gpos_ref[...] = target_side(
        shape, limits, query_ref[...], query_t_ref, target, o_ref, d_scr, w_ref
    )
    gd = mm(d_scr[...].astype(BF), d_hot_t_ref[...])
    gd_mine[...] = gd[:, :half]
    gd_other[...] = gd[:, half:].astype(BF)


def target_grad(t, shape, cnt, neg, far, query, query_t, d_hot, d_hot_t):
    dim, slots = query.shape
    half = far[0].shape[1]
    width = shape[2]
    sds = jax.ShapeDtypeStruct
    return pl.pallas_call(
        functools.partial(target_kernel, t, shape),
        in_specs=[anywhere()] * 2 + [vmem()] * 6,
        out_specs=[vmem()] * 5,
        out_shape=[
            sds((dim, half), F32),
            sds((dim, half), BF),
            sds((dim, slots), BF),
            sds((width, slots), BF),
            sds((1, slots), F32),
        ],
        scratch_shapes=Limits.scratch(shape) + [pltpu.VMEM((dim, slots), F32)],
        compiler_params=params(),
        cost_estimate=cost(4 * dim * slots * (2 * half + width), 12 * dim * slots),
        name="target_grad",
    )(cnt, neg, *far, query, query_t, d_hot, d_hot_t)


def source_grad_kernel(
    t, shape, cnt_ref, neg_ref, _, o_ref, w_ref, gpos_ref, source_ref, rel_ref, s_hot_ref,
    gs_mine, gs_other, drel_ref, cnt, neg, sems,
):
    limits = Limits(t, cnt_ref, neg_ref, cnt, neg, sems)
    limits.wait()
    half = gs_mine.shape[1]
    dq = make_dquery(shape, limits, gpos_ref[...], o_ref, w_ref)
    drel_ref[...] = conj_times(dq, source_ref[...].astype(F32))
    gs = mm(conj_times(dq, rel_ref[...].astype(F32)), s_hot_ref[...], NT)
    gs_mine[...] = gs[:, :half]
    gs_other[...] = gs[:, half:].astype(BF)


def source_grad(t, shape, cnt, neg, after, target, weight, gpos, source, rel, s_hot):
    dim, slots = rel.shape
    half = s_hot.shape[0] // 2
    sds = jax.ShapeDtypeStruct
    return pl.pallas_call(
        functools.partial(source_grad_kernel, t, shape),
        in_specs=[anywhere()] * 3 + [vmem()] * 6,
        out_specs=[vmem()] * 3,
        out_shape=[sds((dim, half), F32), sds((dim, half), BF), sds((dim, slots), BF)],
        scratch_shapes=Limits.scratch(shape),
        compiler_params=params(),
        cost_estimate=cost(dim * slots, dim * slots),
        name="source_grad",
    )(cnt, neg, after, target, weight, gpos, source, rel, s_hot)


def last_kernel(
    t, shape, cnt_ref, neg_ref, far0, far1, query_ref, query_t_ref, d_hot_ref, source_ref, rel_ref,
    drel_ref, dsource_ref, dterm_ref, cnt, neg, sems, o_scr, d_scr, w_scr,
):
    limits = Limits(t, cnt_ref, neg_ref, cnt, neg, sems)
    far = jnp.concatenate([far0[...], far1[...]], axis=1)
    target = mm(far, d_hot_ref[...])
    gpos = target_side(
        shape, limits, query_ref[...], query_t_ref, target, o_scr, d_scr, w_scr
    )
    dterm_ref[...] = d_scr[...].astype(BF)
    dq = make_dquery(shape, limits, gpos, o_scr, w_scr)
    drel_ref[...] = conj_times(dq, source_ref[...].astype(F32))
    dsource_ref[...] = conj_times(dq, rel_ref[...].astype(F32))


def last_terms(t, shape, cnt, neg, far, query, query_t, d_hot, source, rel):
    dim, slots = query.shape
    return pl.pallas_call(
        functools.partial(last_kernel, t, shape),
        in_specs=[anywhere()] * 2 + [vmem()] * 7,
        out_specs=[vmem()] * 3,
        out_shape=[jax.ShapeDtypeStruct((dim, slots), BF)] * 3,
        scratch_shapes=Limits.scratch(shape)
        + [
            pltpu.VMEM((dim, slots), BF),
            pltpu.VMEM((dim, slots), F32),
            pltpu.VMEM((shape[2], slots), BF),
        ],
        compiler_params=params(),
        cost_estimate=cost(6 * dim * slots * shape[2], 12 * dim * slots),
        name="last_terms",
    )(cnt, neg, *far, query, query_t, d_hot, source, rel)


def both_kernel(dsource_ref, s_hot_ref, dterm_ref, d_hot_t_ref, gs_mine, gs_other, gd_mine, gd_other):
    half = gs_mine.shape[1]
    for terms, hot, dims, mine, other in (
        (dterm_ref, d_hot_t_ref, NN, gd_mine, gd_other),
        (dsource_ref, s_hot_ref, NT, gs_mine, gs_other),
    ):
        grad = mm(terms[...], hot[...], dims)
        mine[...] = grad[:, :half]
        other[...] = grad[:, half:].astype(BF)


def both_grads(dsource, s_hot, dterm, d_hot_t):
    dim, slots = dterm.shape
    half = s_hot.shape[0] // 2
    sds = jax.ShapeDtypeStruct
    return pl.pallas_call(
        both_kernel,
        in_specs=[vmem()] * 4,
        out_specs=[vmem()] * 4,
        out_shape=[sds((dim, half), F32), sds((dim, half), BF)] * 2,
        compiler_params=params(),
        cost_estimate=cost(8 * dim * slots * half, 12 * dim * slots),
        name="both_grads",
    )(dsource, s_hot, dterm, d_hot_t)


def update_kernel(n_grads, last, *refs):
    ent_ref, state_ref, grads = refs[0], refs[1], refs[2 : 2 + n_grads]
    grad = grads[0][...].astype(F32)
    for g in grads[1:]:
        grad = grad + g[...].astype(F32)
    dim = grad.shape[0]
    state = state_ref[...] + jnp.sum(grad * grad, axis=0, keepdims=True) / dim
    new = ent_ref[...] - grad * (learn_rate / jnp.sqrt(state))
    if last:
        refs[-1][:dim] = new
        refs[-1][dim:] = jnp.broadcast_to(state, (refs[-1].shape[0] - dim, state.shape[1]))
    else:
        refs[-3][...] = new
        refs[-2][...] = state
        refs[-1][...] = new.astype(BF)


def update(ent, state, grads, after, last=False):
    dim, half = ent.shape
    sds = jax.ShapeDtypeStruct
    outs = [sds((dim, half), F32), sds((1, half), F32), sds((dim, half), BF)]
    if last:
        outs = [sds((dim + 8, half), F32)]
    return pl.pallas_call(
        functools.partial(update_kernel, len(grads), last),
        in_specs=[vmem()] * (2 + len(grads)) + [anywhere()] * len(after),
        out_specs=[vmem()] * len(outs),
        out_shape=outs,
        compiler_params=params(),
        cost_estimate=cost(10 * dim * half, 16 * dim * half),
        name="update",
    )(ent, state, *grads, *after)


def pair_kernel(a_ref, b_ref, out_ref):
    out_ref[...] = (a_ref[...] + b_ref[...].astype(F32)).astype(out_ref.dtype)


def sum_pair(a, b, dtype=BF):
    return pl.pallas_call(
        pair_kernel,
        in_specs=[vmem()] * 2,
        out_specs=vmem(),
        out_shape=jax.ShapeDtypeStruct(a.shape, dtype),
        compiler_params=params(),
        name="sum_pair",
    )(a, b)


def held_kernel(x_ref, *refs):
    pass


def held(x, after):
    return pl.pallas_call(
        held_kernel,
        in_specs=[anywhere()] * (1 + len(after)),
        out_specs=anywhere(),
        out_shape=jax.ShapeDtypeStruct(x.shape, x.dtype),
        input_output_aliases={0: 0},
        compiler_params=params(),
        name="held",
    )(x, *after)


def whole_kernel(mine, theirs, ent_out, state_out, token):
    token[...] = jnp.zeros_like(token)
    dim, rows = ent_out.shape
    half = rows // 2
    edge = place()[2]
    for core, part in ((edge, mine), (1 - edge, theirs)):
        at = pl.ds(pl.multiple_of(core * half, half), half)
        ent_out[:, at] = part[:dim]
        state_out[:, at] = part[dim : dim + 1]


def whole_partition(mine, theirs):
    dim, half = mine.shape[0] - 8, mine.shape[1]
    return pl.pallas_call(
        whole_kernel,
        in_specs=[vmem()] * 2,
        out_specs=[vmem()] * 3,
        out_shape=[
            jax.ShapeDtypeStruct((dim, 2 * half), F32),
            jax.ShapeDtypeStruct((1, 2 * half), F32),
            jax.ShapeDtypeStruct((8, 128), F32),
        ],
        compiler_params=params(),
        name="whole_partition",
    )(mine, theirs)


def first_column(owner, core, w):
    return pl.multiple_of((2 * owner + core) * w, w)


def pieces_kernel(t, nz, same, ids_ref, drel_ref, acc_ref, *refs):
    mine, other = refs[-nz - 1 : -1], refs[-1]
    w = other.shape[2]
    z, x, edge = place()
    drel = drel_ref[...]
    for k in range(nz):
        owner = 2 * lax.rem(z + k, nz) + (x if same else 1 - x)
        at = [first_column(owner, core, w) for core in (edge, 1 - edge)]
        hot = jnp.concatenate([one_hot(ids_ref, t, w, lambda i, lo=lo: i - lo) for lo in at], axis=0)
        part = mm(drel, hot, NT)
        mine[k][...] = acc_ref[:, pl.ds(at[0], w)] + part[:, :w]
        other[k] = (acc_ref[:, pl.ds(at[1], w)] + part[:, w:]).astype(BF)


def pieces(t, n, same, rel_ids, drel, acc, after):
    dim, rels = acc.shape
    w = rels // (2 * n)
    sds = jax.ShapeDtypeStruct
    out = pl.pallas_call(
        functools.partial(pieces_kernel, t, n // 2, same),
        in_specs=[vmem()] * 3 + [anywhere()] * len(after),
        out_specs=[vmem()] * (n // 2 + 1),
        out_shape=[sds((dim, w), F32)] * (n // 2) + [sds((n // 2, dim, w), BF)],
        compiler_params=params(),
        cost_estimate=cost(dim * rels * drel.shape[1], 4 * dim * rels),
        name="pieces",
    )(rel_ids, drel, acc, *after)
    return out[:-1], out[-1]


def add_kernel(n, *refs):
    for k in range(n):
        refs[n + 1 + k][...] = (refs[k][...] + refs[n][k].astype(F32)).astype(BF)


def add_each(mine, theirs):
    n = len(mine)
    return pl.pallas_call(
        functools.partial(add_kernel, n),
        in_specs=[vmem()] * (n + 1),
        out_specs=[vmem()] * n,
        out_shape=[jax.ShapeDtypeStruct(x.shape, BF) for x in mine],
        compiler_params=params(),
        name="add_each",
    )(*mine, theirs)


def sum_kernel(k, count, mine, theirs, *refs):
    total = mine[...] + theirs[k].astype(F32)
    for r in refs[:count]:
        total = total + r[...].astype(F32)
    refs[-1][...] = total.astype(BF)


def sum_piece(k, mine, theirs, parts, after):
    return pl.pallas_call(
        functools.partial(sum_kernel, k, len(parts)),
        in_specs=[vmem()] * (2 + len(parts)) + [anywhere()] * len(after),
        out_specs=vmem(),
        out_shape=jax.ShapeDtypeStruct(mine.shape, BF),
        compiler_params=params(),
        name="sum_piece",
    )(mine, theirs, *parts, *after)


def relnew_kernel(nz, same, ks, rel_ref, state_ref, *refs):
    got = refs[: 2 * len(ks)]
    rel_out, state_out, buf, sems = refs[-4:]
    w = got[0].shape[1]
    state_out[...] = refs[len(got) + (0 if same else 1)][...]
    z, x, edge = place()
    copies = []
    for i, grad_ref in enumerate(got):
        owner = 2 * lax.rem(z + nz - ks[i // 2], nz) + (x if same else 1 - x)
        at = pl.ds(first_column(owner, edge if i % 2 == 0 else 1 - edge, w), w)
        grad = grad_ref[...].astype(F32)
        state = state_ref[:, at] + jnp.sum(grad * grad, axis=0, keepdims=True) / grad.shape[0]
        state_out[:, at] = state
        buf[i] = rel_ref[:, at] - grad * (learn_rate / jnp.sqrt(state))
        copy = pltpu.make_async_copy(buf.at[i], rel_out.at[:, at], sems.at[i])
        copy.start()
        copies.append(copy)
    for copy in copies:
        copy.wait()


def relnew(nz, same, ks, relations, state, got, before, after):
    dim, rels = relations.shape
    w = got[0].shape[1]
    start = [state] if before is None else list(before)
    return pl.pallas_call(
        functools.partial(relnew_kernel, nz, same, ks),
        in_specs=[vmem()] * (2 + len(got)) + ([anywhere()] if before else [])
        + [vmem()]
        + [anywhere()] * len(after),
        out_specs=[anywhere(), vmem()],
        out_shape=[jax.ShapeDtypeStruct((dim, rels), F32), jax.ShapeDtypeStruct((1, rels), F32)],
        input_output_aliases={2 + len(got): 0} if before else {},
        scratch_shapes=[pltpu.VMEM((len(got), dim, w), F32), pltpu.SemaphoreType.DMA((len(got),))],
        compiler_params=params(),
        cost_estimate=cost(4 * dim * w * len(got), 4 * dim * w * len(got)),
        name="relnew",
    )(relations, state, *got, *start, *after)


def relation_update(t, rel_ids, drel, acc, relations, state, gd_other, gd, grads, finish):
    n = lax.axis_size("dom")
    dim, rels = relations.shape
    if n % 2 or rels % (256 * n):
        total = lax.psum(relsum(t, rel_ids, drel, acc, rels), ("dom", "edge"))
        state = state + jnp.mean(total * total, axis=0)
        return relations - learn_rate * total / jnp.sqrt(state)[None, :], state, finish([])
    nz = n // 2
    near = sorted(range(nz), key=lambda k: min(k, nz - k))
    mine_x, other_x = pieces(t, n, False, rel_ids, drel, acc, [gd_other])
    mine_s, other_s = pieces(t, n, True, rel_ids, drel, acc, [gd])
    to_x = add_each(mine_x, across(other_x))
    theirs = across(other_s)
    from_x = {k: beside(to_x[k]) for k in reversed(near)}
    from_z = []
    for i, k in enumerate(reversed(near[1:])):
        after = [grads[i]] if i < len(grads) else []
        piece = sum_piece(k, mine_s[k], theirs, [from_x[k]], after)
        from_z.append(shifted(piece, 2 * k))
    done = finish([piece])
    summed = sum_piece(0, mine_s[0], theirs, [from_x[0]] + from_z, [])
    got = [summed if k == 0 else shifted(summed, 2 * k) for k in range(nz)]
    got_x = [beside(piece) for piece in got]
    state = state.reshape(1, rels)
    pairs = lambda ks, parts: [y for k in ks for y in (parts[k], across(parts[k]))]
    early, late = near[:-1], near[-1:]
    new = relnew(nz, True, near, relations, state, pairs(near, got), None, [done[2]])
    new = relnew(nz, False, early, relations, state, pairs(early, got_x), new, [])
    rel_new, state_new = relnew(nz, False, late, relations, state, pairs(late, got_x), new, [])
    return rel_new, state_new.reshape(rels), done


def on_device(
    entities,
    entity_state,
    relations,
    relation_state,
    src_rows,
    rel_ids,
    dst_rows,
    counts,
    neg_blocks,
):
    rounds = src_rows.shape[0]
    rels = relations.shape[1]
    shape = src_rows.shape
    cnt, neg = counts.T, neg_blocks.T
    g_mine, g_other, drel, rel16, ent, state = first_round(
        cnt, neg, src_rows, dst_rows, rel_ids, entities, entity_state.reshape(1, -1), relations
    )
    acc = relsum(0, rel_ids, drel, None, rels)
    ent, state, low = update(ent, state, [g_mine, across(g_other)], [])
    rel = relvec(1, rel_ids, rel16)
    for t in range(1, rounds):
        far = shifted(low, -t)
        own = (low, across(low))
        query, query_t, source, s_hot, d_hot, d_hot_t = source_side(t, src_rows, dst_rows, own, rel)
        far = held(far, [query, acc])
        far = (far, across(far))
        if t == rounds - 1:
            break
        gd_mine, gd_other, target, weight, gpos = target_grad(
            t, shape, cnt, neg, far, query, query_t, d_hot, d_hot_t
        )
        gd = sum_pair(gd_mine, across(gd_other))
        gs_mine, gs_other, drel = source_grad(
            t, shape, cnt, neg, gd, target, weight, gpos, source, rel, s_hot
        )
        acc = relsum(t, rel_ids, drel, acc, rels)
        rel = relvec(t + 1, rel_ids, rel16)
        grads = [sum_pair(gs_mine, shifted(gd, t), F32), across(gs_other)]
        ent, state, low = update(ent, state, grads, [rel])
    drel, dsource, dterm = last_terms(t, shape, cnt, neg, far, query, query_t, d_hot, source, rel)
    gs_mine, gs_other, gd_mine, gd_other = both_grads(dsource, s_hot, dterm, d_hot_t)
    gd = sum_pair(gd_mine, across(gd_other))

    grads = [across(gs_other), shifted(gd, t)]

    def finish(after):
        (mine,) = update(ent, state, [gs_mine, *grads], after, last=True)
        return whole_partition(mine, across(mine))

    rel_new, rel_state, done = relation_update(
        t, rel_ids, drel, acc, relations, relation_state, gd_other, gd, grads, finish
    )
    return (done[0], done[1].reshape(-1), rel_new, rel_state)


def solution(mesh):
    return jax.shard_map(
        on_device,
        mesh=mesh,
        in_specs=(
            P(None, ("groups", "dom")),
            P(("groups", "dom")),
            P(None, "groups"),
            P("groups"),
            P(None, ("groups", "dom", "edge"), None),
            P(None, ("groups", "dom", "edge"), None),
            P(None, ("groups", "dom", "edge"), None),
            P(None, ("groups", "dom", "edge")),
            P(None, ("groups", "dom", "edge")),
        ),
        out_specs=(
            P(None, ("groups", "dom")),
            P(("groups", "dom")),
            P(None, "groups"),
            P("groups"),
        ),
        check_vma=False,
    )
```

```python
import functools

import jax
import jax.numpy as jnp
from jax import lax
from jax.experimental import pallas as pl
from jax.experimental.pallas import tpu as pltpu
from jax.sharding import PartitionSpec as P

learn_rate = 0.1
BF = jnp.bfloat16
F32 = jnp.float32
VMEM_LIMIT = 40 * 1024 * 1024
NN = (((1,), (0,)), ((), ()))
NT = (((1,), (1,)), ((), ()))
TN = (((0,), (0,)), ((), ()))


def mm(a, b, dims=NN):
    return lax.dot_general(a, b, dims, preferred_element_type=F32)


def vmem():
    return pl.BlockSpec(memory_space=pltpu.VMEM)


def smem():
    return pl.BlockSpec(memory_space=pltpu.SMEM)


def anywhere():
    return pl.BlockSpec(memory_space=pl.ANY)


def in_hbm(x):
    return pltpu.with_memory_space_constraint(x, pltpu.HBM)


def cost(flops, size):
    return pl.CostEstimate(flops=flops, bytes_accessed=size, transcendentals=0)


def params():
    return pltpu.CompilerParams(vmem_limit_bytes=VMEM_LIMIT)


def shifted(x, by):
    n = lax.axis_size("dom")
    return lax.ppermute(x, "dom", [(i, (i + by) % n) for i in range(n)])


def beside(x):
    n = lax.axis_size("dom")
    return lax.ppermute(x, "dom", [(i, i ^ 1) for i in range(n)])


def across(x):
    return lax.ppermute(x, "edge", [(0, 1), (1, 0)])


def one_hot(rows_ref, t, count, base):
    blocks, width = rows_ref.shape[1:]
    at = lax.broadcasted_iota(jnp.int32, (count, width), 0)
    idx = rows_ref[t]
    return jnp.concatenate(
        [
            jnp.where(at == base(idx[b : b + 1, :]), 1.0, 0.0).astype(BF)
            for b in range(blocks)
        ],
        axis=1,
    )


def relvec_kernel(t, ids_ref, rel_ref, out_ref):
    rels = rel_ref.shape[1]
    tile = min(rels, 512)
    out = None
    for lo in range(0, rels, tile):
        hot = one_hot(ids_ref, t, tile, lambda i, lo=lo: i - lo)
        part = mm(rel_ref[:, lo : lo + tile], hot)
        out = part if out is None else out + part
    out_ref[...] = out.astype(BF)


def relvec(t, rel_ids, rel16):
    width, rels = rel16.shape
    slots = rel_ids.shape[1] * rel_ids.shape[2]
    return pl.pallas_call(
        functools.partial(relvec_kernel, t),
        in_specs=[vmem()] * 2,
        out_specs=vmem(),
        out_shape=jax.ShapeDtypeStruct((width, slots), BF),
        compiler_params=params(),
        cost_estimate=cost(width * slots, width * slots),
        name="relvec",
    )(rel_ids, rel16)


def relsum_kernel(t, first, ids_ref, drel_ref, *refs):
    step = pl.program_id(0)
    out_ref = refs[-1]
    tile = out_ref.shape[1]
    hot = one_hot(ids_ref, t, tile, lambda i: i - step * tile)
    part = mm(drel_ref[...], hot, NT)
    out_ref[...] = part if first else refs[0][...] + part


def relsum(t, rel_ids, drel, acc, rels):
    width, slots = drel.shape
    tile = min(rels, 512)
    wide = pl.BlockSpec((width, tile), lambda i: (0, i))
    ins = [rel_ids, drel] + ([] if acc is None else [acc])
    return pl.pallas_call(
        functools.partial(relsum_kernel, t, acc is None),
        grid=(rels // tile,),
        in_specs=[
            pl.BlockSpec(rel_ids.shape, lambda i: (0, 0, 0)),
            pl.BlockSpec((width, slots), lambda i: (0, 0)),
        ]
        + ([] if acc is None else [wide]),
        out_specs=wide,
        out_shape=jax.ShapeDtypeStruct((width, rels), F32),
        input_output_aliases={} if acc is None else {2: 0},
        compiler_params=params(),
        cost_estimate=cost(width * slots, width * slots),
        name="relsum",
    )(*ins)


class Limits:
    scratch = lambda shape: [
        pltpu.SMEM((shape[1], shape[0]), jnp.int32),
        pltpu.SMEM((shape[1], shape[0]), jnp.int32),
        pltpu.SemaphoreType.DMA((2,)),
    ]

    def __init__(self, t, from_cnt, from_neg, cnt, neg, sems):
        self.t, self.cnt, self.neg = t, cnt, neg
        self.copies = [
            pltpu.make_async_copy(from_cnt, cnt, sems.at[0]),
            pltpu.make_async_copy(from_neg, neg, sems.at[1]),
        ]
        for copy in self.copies:
            copy.start()

    def wait(self):
        for copy in self.copies:
            copy.wait()

    def count(self, b):
        return self.cnt[b, self.t]

    def negative(self, b):
        return self.neg[b, self.t]


def place():
    dom = lax.axis_index("dom")
    return dom // 2, lax.rem(dom, 2), lax.axis_index("edge")


def localize(edge, half):
    def local(idx):
        moved = idx + edge * half
        return jnp.where(moved >= 2 * half, moved - 2 * half, moved)

    return local


def halves(x):
    hd = x.shape[0] // 2
    return x[:hd], x[hd:]


def make_query(source, rel):
    (s_re, s_im), (w_re, w_im) = halves(source), halves(rel)
    return jnp.concatenate(
        [s_re * w_re - s_im * w_im, s_re * w_im + s_im * w_re], axis=0
    ).astype(BF)


def conj_times(dq, v):
    (dq_re, dq_im), (v_re, v_im) = halves(dq), halves(v)
    return jnp.concatenate(
        [dq_re * v_re + dq_im * v_im, dq_im * v_re - dq_re * v_im], axis=0
    ).astype(BF)


def target_side(shape, limits, query, query_t, target, o_ref, d_ref, w_ref):
    _, blocks, width = shape
    lanes = lambda b: pl.ds(pl.multiple_of(b * width, width), width)
    count = limits.count
    o_ref[...] = target.astype(BF)
    query_f = query.astype(F32)
    pos = jnp.sum(query_f * target, axis=0, keepdims=True)
    lane = lax.broadcasted_iota(jnp.int32, (1, width), 1)
    limits.wait()
    row_i = lax.broadcasted_iota(jnp.int32, (width, width), 0)
    col_j = lax.broadcasted_iota(jnp.int32, (width, width), 1)
    weights = []
    for b in range(blocks):
        nb = limits.negative(b)
        neg = o_ref[:, lanes(nb)]
        at = slice(b * width, (b + 1) * width)
        scores = mm(query[:, at], neg, TN) if query_t is None else mm(query_t[at], neg)
        keep = jnp.logical_and(row_i < count(b), col_j < count(nb))
        weight = jnp.where(keep, jax.nn.sigmoid(scores) / width, 0.0).astype(BF)
        w_ref[:, at] = weight
        weights.append(weight)
    valid = jnp.concatenate(
        [jnp.where(lane < count(b), 1.0, 0.0) for b in range(blocks)], axis=1
    )
    gpos = -jax.nn.sigmoid(-pos) * valid
    d_ref[...] = gpos * query_f
    for b in range(blocks):
        d_ref[:, lanes(limits.negative(b))] += mm(query[:, b * width : (b + 1) * width], weights[b])
    return gpos


def make_dquery(shape, limits, gpos, o_ref, w_ref):
    _, blocks, width = shape
    lanes = lambda b: pl.ds(pl.multiple_of(b * width, width), width)
    out = []
    for b in range(blocks):
        nb = limits.negative(b)
        at = slice(b * width, (b + 1) * width)
        own = gpos[:, at] * o_ref[:, at].astype(F32)
        out.append(own + mm(o_ref[:, lanes(nb)], w_ref[:, at], NT))
    return jnp.concatenate(out, axis=1)


def first_kernel(
    shape, cnt_ref, neg_ref, src_ref, dst_ref, ids_ref, ent_ref, state_ref, rel_ref,
    g_mine, g_other, drel_ref, rel16_ref, ent_mine, state_mine,
    cnt, neg, lim_sems, src, dst, ids, ent, state, rel_buf, o_scr, d_scr, w_scr, in_sems, sems,
):
    rels = rel_buf.shape[1]
    tile = min(rels, 512)
    spans = range(0, rels, tile)
    inputs = [
        pltpu.make_async_copy(there, here, in_sems.at[i])
        for i, (there, here) in enumerate(
            [(src_ref.at[:1], src), (dst_ref.at[:1], dst), (ids_ref.at[:1], ids), (ent_ref, ent), (state_ref, state)]
        )
    ]
    loads = [
        pltpu.make_async_copy(
            rel_ref.at[:, lo : lo + tile], rel_buf.at[:, lo : lo + tile], sems.at[i]
        )
        for i, lo in enumerate(spans)
    ]
    for load in inputs:
        load.start()
    limits = Limits(0, cnt_ref, neg_ref, cnt, neg, lim_sems)
    for load in loads:
        load.start()
    half = ent.shape[1] // 2
    _, _, edge = place()
    local = localize(edge, half)
    inputs[0].wait()
    s_hot = one_hot(src, 0, 2 * half, local)
    inputs[1].wait()
    d_hot = one_hot(dst, 0, 2 * half, local)
    inputs[2].wait()
    ids_hot = [one_hot(ids, 0, tile, lambda i, lo=lo: i - lo) for lo in spans]
    inputs[3].wait()
    inputs[4].wait()
    mine = pl.ds(pl.multiple_of(edge * half, half), half)
    ent_mine[...] = ent[:, mine]
    state_mine[...] = state[:, mine]
    table = jnp.concatenate(
        [ent[:, pl.ds(pl.multiple_of(h * half, half), half)].astype(BF) for h in (edge, 1 - edge)],
        axis=1,
    )
    source = mm(table, s_hot)
    target = mm(table, d_hot)
    rel = None
    for load, lo, hot in zip(loads, spans, ids_hot):
        load.wait()
        low = rel_buf[:, lo : lo + tile].astype(BF)
        rel16_ref[:, lo : lo + tile] = low
        part = mm(low, hot)
        rel = part if rel is None else rel + part
    query = make_query(source, rel)
    gpos = target_side(shape, limits, query, None, target, o_scr, d_scr, w_scr)
    dq = make_dquery(shape, limits, gpos, o_scr, w_scr)
    drel_ref[...] = conj_times(dq, source)
    total = mm(conj_times(dq, rel), s_hot, NT) + mm(d_scr[...].astype(BF), d_hot, NT)
    g_mine[...] = total[:, :half]
    g_other[...] = total[:, half:].astype(BF)


def first_round(cnt, neg, src, dst, rel_ids, entities, state, relations):
    dim, rows = entities.shape
    rels = relations.shape[1]
    _, blocks, width = src.shape
    slots = blocks * width
    sds = jax.ShapeDtypeStruct
    return pl.pallas_call(
        functools.partial(first_kernel, src.shape),
        in_specs=[anywhere()] * 8,
        out_specs=[vmem()] * 6,
        out_shape=[
            sds((dim, rows // 2), F32),
            sds((dim, rows // 2), BF),
            sds((dim, slots), BF),
            sds((dim, rels), BF),
            sds((dim, rows // 2), F32),
            sds((1, rows // 2), F32),
        ],
        scratch_shapes=Limits.scratch(src.shape)
        + [
            pltpu.VMEM((1, blocks, width), jnp.int32),
            pltpu.VMEM((1, blocks, width), jnp.int32),
            pltpu.VMEM((1, blocks, width), jnp.int32),
            pltpu.VMEM((dim, rows), F32),
            pltpu.VMEM((1, rows), F32),
            pltpu.VMEM((dim, rels), F32),
            pltpu.VMEM((dim, slots), BF),
            pltpu.VMEM((dim, slots), F32),
            pltpu.VMEM((width, slots), BF),
            pltpu.SemaphoreType.DMA((5,)),
            pltpu.SemaphoreType.DMA((-(-rels // min(rels, 512)),)),
        ],
        compiler_params=params(),
        cost_estimate=cost(2 * dim * slots * (rels + 4 * rows), 8 * dim * rels),
        name="first_round",
    )(*(in_hbm(x) for x in (cnt, neg, src, dst, rel_ids, entities, state, relations)))


def source_kernel(
    t, src_ref, dst_ref, own0, own1, rel_ref,
    query_ref, query_t_ref, source_ref, s_hot_ref, d_hot_ref, d_hot_t_ref,
):
    half = own0.shape[1]
    local = localize(place()[2], half)
    s_hot = one_hot(src_ref, t, 2 * half, local)
    d_hot = one_hot(dst_ref, t, 2 * half, local)
    s_hot_ref[...] = s_hot
    d_hot_ref[...] = d_hot
    d_hot_t_ref[...] = d_hot.T
    source = mm(jnp.concatenate([own0[...], own1[...]], axis=1), s_hot)
    source_ref[...] = source.astype(BF)
    query = make_query(source, rel_ref[...].astype(F32))
    query_ref[...] = query
    query_t_ref[...] = query.T


def source_side(t, src, dst, own, rel):
    dim, slots = rel.shape
    rows = 2 * own[0].shape[1]
    sds = lambda *shape: jax.ShapeDtypeStruct(shape, BF)
    return pl.pallas_call(
        functools.partial(source_kernel, t),
        in_specs=[vmem()] * 5,
        out_specs=[vmem()] * 6,
        out_shape=[
            sds(dim, slots), sds(slots, dim), sds(dim, slots),
            sds(rows, slots), sds(rows, slots), sds(slots, rows),
        ],
        compiler_params=params(),
        cost_estimate=cost(dim * slots, dim * slots),
        name="source_side",
    )(src, dst, *own, rel)


def target_kernel(
    t, shape, cnt_ref, neg_ref, far0, far1, query_ref, query_t_ref, d_hot_ref, d_hot_t_ref,
    gd_mine, gd_other, o_ref, w_ref, gpos_ref, cnt, neg, sems, d_scr,
):
    limits = Limits(t, cnt_ref, neg_ref, cnt, neg, sems)
    half = far0.shape[1]
    far = jnp.concatenate([far0[...], far1[...]], axis=1)
    target = mm(far, d_hot_ref[...])
    gpos_ref[...] = target_side(
        shape, limits, query_ref[...], query_t_ref, target, o_ref, d_scr, w_ref
    )
    gd = mm(d_scr[...].astype(BF), d_hot_t_ref[...])
    gd_mine[...] = gd[:, :half]
    gd_other[...] = gd[:, half:].astype(BF)


def target_grad(t, shape, cnt, neg, far, query, query_t, d_hot, d_hot_t):
    dim, slots = query.shape
    half = far[0].shape[1]
    width = shape[2]
    sds = jax.ShapeDtypeStruct
    return pl.pallas_call(
        functools.partial(target_kernel, t, shape),
        in_specs=[anywhere()] * 2 + [vmem()] * 6,
        out_specs=[vmem()] * 5,
        out_shape=[
            sds((dim, half), F32),
            sds((dim, half), BF),
            sds((dim, slots), BF),
            sds((width, slots), BF),
            sds((1, slots), F32),
        ],
        scratch_shapes=Limits.scratch(shape) + [pltpu.VMEM((dim, slots), F32)],
        compiler_params=params(),
        cost_estimate=cost(4 * dim * slots * (2 * half + width), 12 * dim * slots),
        name="target_grad",
    )(cnt, neg, *far, query, query_t, d_hot, d_hot_t)


def source_grad_kernel(
    t, shape, cnt_ref, neg_ref, _, o_ref, w_ref, gpos_ref, source_ref, rel_ref, s_hot_ref,
    gs_mine, gs_other, drel_ref, cnt, neg, sems,
):
    limits = Limits(t, cnt_ref, neg_ref, cnt, neg, sems)
    limits.wait()
    half = gs_mine.shape[1]
    dq = make_dquery(shape, limits, gpos_ref[...], o_ref, w_ref)
    drel_ref[...] = conj_times(dq, source_ref[...].astype(F32))
    gs = mm(conj_times(dq, rel_ref[...].astype(F32)), s_hot_ref[...], NT)
    gs_mine[...] = gs[:, :half]
    gs_other[...] = gs[:, half:].astype(BF)


def source_grad(t, shape, cnt, neg, after, target, weight, gpos, source, rel, s_hot):
    dim, slots = rel.shape
    half = s_hot.shape[0] // 2
    sds = jax.ShapeDtypeStruct
    return pl.pallas_call(
        functools.partial(source_grad_kernel, t, shape),
        in_specs=[anywhere()] * 3 + [vmem()] * 6,
        out_specs=[vmem()] * 3,
        out_shape=[sds((dim, half), F32), sds((dim, half), BF), sds((dim, slots), BF)],
        scratch_shapes=Limits.scratch(shape),
        compiler_params=params(),
        cost_estimate=cost(dim * slots, dim * slots),
        name="source_grad",
    )(cnt, neg, after, target, weight, gpos, source, rel, s_hot)


def last_kernel(
    t, shape, cnt_ref, neg_ref, far0, far1, query_ref, query_t_ref, d_hot_ref, source_ref, rel_ref,
    drel_ref, dsource_ref, dterm_ref, cnt, neg, sems, o_scr, d_scr, w_scr,
):
    limits = Limits(t, cnt_ref, neg_ref, cnt, neg, sems)
    far = jnp.concatenate([far0[...], far1[...]], axis=1)
    target = mm(far, d_hot_ref[...])
    gpos = target_side(
        shape, limits, query_ref[...], query_t_ref, target, o_scr, d_scr, w_scr
    )
    dterm_ref[...] = d_scr[...].astype(BF)
    dq = make_dquery(shape, limits, gpos, o_scr, w_scr)
    drel_ref[...] = conj_times(dq, source_ref[...].astype(F32))
    dsource_ref[...] = conj_times(dq, rel_ref[...].astype(F32))


def last_terms(t, shape, cnt, neg, far, query, query_t, d_hot, source, rel):
    dim, slots = query.shape
    return pl.pallas_call(
        functools.partial(last_kernel, t, shape),
        in_specs=[anywhere()] * 2 + [vmem()] * 7,
        out_specs=[vmem()] * 3,
        out_shape=[jax.ShapeDtypeStruct((dim, slots), BF)] * 3,
        scratch_shapes=Limits.scratch(shape)
        + [
            pltpu.VMEM((dim, slots), BF),
            pltpu.VMEM((dim, slots), F32),
            pltpu.VMEM((shape[2], slots), BF),
        ],
        compiler_params=params(),
        cost_estimate=cost(6 * dim * slots * shape[2], 12 * dim * slots),
        name="last_terms",
    )(cnt, neg, *far, query, query_t, d_hot, source, rel)


def both_kernel(dsource_ref, s_hot_ref, dterm_ref, d_hot_t_ref, gs_mine, gs_other, gd_mine, gd_other):
    half = gs_mine.shape[1]
    for terms, hot, dims, mine, other in (
        (dterm_ref, d_hot_t_ref, NN, gd_mine, gd_other),
        (dsource_ref, s_hot_ref, NT, gs_mine, gs_other),
    ):
        grad = mm(terms[...], hot[...], dims)
        mine[...] = grad[:, :half]
        other[...] = grad[:, half:].astype(BF)


def both_grads(dsource, s_hot, dterm, d_hot_t):
    dim, slots = dterm.shape
    half = s_hot.shape[0] // 2
    sds = jax.ShapeDtypeStruct
    return pl.pallas_call(
        both_kernel,
        in_specs=[vmem()] * 4,
        out_specs=[vmem()] * 4,
        out_shape=[sds((dim, half), F32), sds((dim, half), BF)] * 2,
        compiler_params=params(),
        cost_estimate=cost(8 * dim * slots * half, 12 * dim * slots),
        name="both_grads",
    )(dsource, s_hot, dterm, d_hot_t)


def update_kernel(n_grads, last, *refs):
    ent_ref, state_ref, grads = refs[0], refs[1], refs[2 : 2 + n_grads]
    grad = grads[0][...].astype(F32)
    for g in grads[1:]:
        grad = grad + g[...].astype(F32)
    dim = grad.shape[0]
    state = state_ref[...] + jnp.sum(grad * grad, axis=0, keepdims=True) / dim
    new = ent_ref[...] - grad * (learn_rate / jnp.sqrt(state))
    if last:
        refs[-1][:dim] = new
        refs[-1][dim:] = jnp.broadcast_to(state, (refs[-1].shape[0] - dim, state.shape[1]))
    else:
        refs[-3][...] = new
        refs[-2][...] = state
        refs[-1][...] = new.astype(BF)


def update(ent, state, grads, after, last=False):
    dim, half = ent.shape
    sds = jax.ShapeDtypeStruct
    outs = [sds((dim, half), F32), sds((1, half), F32), sds((dim, half), BF)]
    if last:
        outs = [sds((dim + 8, half), F32)]
    return pl.pallas_call(
        functools.partial(update_kernel, len(grads), last),
        in_specs=[vmem()] * (2 + len(grads)) + [anywhere()] * len(after),
        out_specs=[vmem()] * len(outs),
        out_shape=outs,
        compiler_params=params(),
        cost_estimate=cost(10 * dim * half, 16 * dim * half),
        name="update",
    )(ent, state, *grads, *after)


def pair_kernel(a_ref, b_ref, out_ref):
    out_ref[...] = (a_ref[...] + b_ref[...].astype(F32)).astype(out_ref.dtype)


def sum_pair(a, b, dtype=BF):
    return pl.pallas_call(
        pair_kernel,
        in_specs=[vmem()] * 2,
        out_specs=vmem(),
        out_shape=jax.ShapeDtypeStruct(a.shape, dtype),
        compiler_params=params(),
        name="sum_pair",
    )(a, b)


def held_kernel(x_ref, *refs):
    pass


def held(x, after):
    return pl.pallas_call(
        held_kernel,
        in_specs=[anywhere()] * (1 + len(after)),
        out_specs=anywhere(),
        out_shape=jax.ShapeDtypeStruct(x.shape, x.dtype),
        input_output_aliases={0: 0},
        compiler_params=params(),
        name="held",
    )(x, *after)


def whole_kernel(mine, theirs, ent_out, state_out, token):
    token[...] = jnp.zeros_like(token)
    dim, rows = ent_out.shape
    half = rows // 2
    edge = place()[2]
    for core, part in ((edge, mine), (1 - edge, theirs)):
        at = pl.ds(pl.multiple_of(core * half, half), half)
        ent_out[:, at] = part[:dim]
        state_out[:, at] = part[dim : dim + 1]


def whole_partition(mine, theirs):
    dim, half = mine.shape[0] - 8, mine.shape[1]
    return pl.pallas_call(
        whole_kernel,
        in_specs=[vmem()] * 2,
        out_specs=[vmem()] * 3,
        out_shape=[
            jax.ShapeDtypeStruct((dim, 2 * half), F32),
            jax.ShapeDtypeStruct((1, 2 * half), F32),
            jax.ShapeDtypeStruct((8, 128), F32),
        ],
        compiler_params=params(),
        name="whole_partition",
    )(mine, theirs)


def first_column(owner, core, w):
    return pl.multiple_of((2 * owner + core) * w, w)


def pieces_kernel(t, nz, same, ids_ref, drel_ref, acc_ref, *refs):
    mine, other = refs[-nz - 1 : -1], refs[-1]
    w = other.shape[2]
    z, x, edge = place()
    drel = drel_ref[...]
    for k in range(nz):
        owner = 2 * lax.rem(z + k, nz) + (x if same else 1 - x)
        at = [first_column(owner, core, w) for core in (edge, 1 - edge)]
        hot = jnp.concatenate([one_hot(ids_ref, t, w, lambda i, lo=lo: i - lo) for lo in at], axis=0)
        part = mm(drel, hot, NT)
        mine[k][...] = acc_ref[:, pl.ds(at[0], w)] + part[:, :w]
        other[k] = (acc_ref[:, pl.ds(at[1], w)] + part[:, w:]).astype(BF)


def pieces(t, n, same, rel_ids, drel, acc, after):
    dim, rels = acc.shape
    w = rels // (2 * n)
    sds = jax.ShapeDtypeStruct
    out = pl.pallas_call(
        functools.partial(pieces_kernel, t, n // 2, same),
        in_specs=[vmem()] * 3 + [anywhere()] * len(after),
        out_specs=[vmem()] * (n // 2 + 1),
        out_shape=[sds((dim, w), F32)] * (n // 2) + [sds((n // 2, dim, w), BF)],
        compiler_params=params(),
        cost_estimate=cost(dim * rels * drel.shape[1], 4 * dim * rels),
        name="pieces",
    )(rel_ids, drel, acc, *after)
    return out[:-1], out[-1]


def add_kernel(n, *refs):
    for k in range(n):
        refs[n + 1 + k][...] = (refs[k][...] + refs[n][k].astype(F32)).astype(BF)


def add_each(mine, theirs):
    n = len(mine)
    return pl.pallas_call(
        functools.partial(add_kernel, n),
        in_specs=[vmem()] * (n + 1),
        out_specs=[vmem()] * n,
        out_shape=[jax.ShapeDtypeStruct(x.shape, BF) for x in mine],
        compiler_params=params(),
        name="add_each",
    )(*mine, theirs)


def sum_kernel(k, count, mine, theirs, *refs):
    total = mine[...] + theirs[k].astype(F32)
    for r in refs[:count]:
        total = total + r[...].astype(F32)
    refs[-1][...] = total.astype(BF)


def sum_piece(k, mine, theirs, parts, after):
    return pl.pallas_call(
        functools.partial(sum_kernel, k, len(parts)),
        in_specs=[vmem()] * (2 + len(parts)) + [anywhere()] * len(after),
        out_specs=vmem(),
        out_shape=jax.ShapeDtypeStruct(mine.shape, BF),
        compiler_params=params(),
        name="sum_piece",
    )(mine, theirs, *parts, *after)


def stacked_kernel(*refs):
    for i in range(refs[-1].shape[0]):
        refs[-1][i] = refs[i][...]


def stacked(parts, after):
    return pl.pallas_call(
        stacked_kernel,
        in_specs=[vmem()] * len(parts) + [anywhere()] * len(after),
        out_specs=vmem(),
        out_shape=jax.ShapeDtypeStruct((len(parts), *parts[0].shape), parts[0].dtype),
        compiler_params=params(),
        name="stacked",
    )(*parts, *after)


def relnew_kernel(nz, same, ks, rel_ref, state_ref, *refs):
    mine, theirs = refs[: len(ks)], refs[len(ks)]
    rel_out, state_out, buf, sems = refs[-4:]
    w = mine[0].shape[1]
    state_out[...] = refs[len(ks) + (1 if same else 2)][...]
    z, x, edge = place()
    copies = []
    for i in range(2 * len(ks)):
        owner = 2 * lax.rem(z + nz - ks[i // 2], nz) + (x if same else 1 - x)
        at = pl.ds(first_column(owner, edge if i % 2 == 0 else 1 - edge, w), w)
        grad = (mine[i // 2][...] if i % 2 == 0 else theirs[i // 2]).astype(F32)
        state = state_ref[:, at] + jnp.sum(grad * grad, axis=0, keepdims=True) / grad.shape[0]
        state_out[:, at] = state
        buf[i] = rel_ref[:, at] - grad * (learn_rate / jnp.sqrt(state))
        copy = pltpu.make_async_copy(buf.at[i], rel_out.at[:, at], sems.at[i])
        copy.start()
        copies.append(copy)
    for copy in copies:
        copy.wait()


def relnew(nz, same, ks, relations, state, mine, theirs, before, after):
    dim, rels = relations.shape
    w = mine[0].shape[1]
    count = 2 * len(ks)
    start = [state] if before is None else list(before)
    return pl.pallas_call(
        functools.partial(relnew_kernel, nz, same, ks),
        in_specs=[vmem()] * (3 + len(ks))
        + ([anywhere()] if before else [])
        + [vmem()]
        + [anywhere()] * len(after),
        out_specs=[anywhere(), vmem()],
        out_shape=[jax.ShapeDtypeStruct((dim, rels), F32), jax.ShapeDtypeStruct((1, rels), F32)],
        input_output_aliases={3 + len(ks): 0} if before else {},
        scratch_shapes=[pltpu.VMEM((count, dim, w), F32), pltpu.SemaphoreType.DMA((count,))],
        compiler_params=params(),
        cost_estimate=cost(4 * dim * w * count, 4 * dim * w * count),
        name="relnew",
    )(relations, state, *mine, theirs, *start, *after)


def relation_update(t, rel_ids, drel, acc, relations, state, gd_other, gd, grads, finish):
    n = lax.axis_size("dom")
    dim, rels = relations.shape
    if n % 2 or rels % (256 * n):
        total = lax.psum(relsum(t, rel_ids, drel, acc, rels), ("dom", "edge"))
        state = state + jnp.mean(total * total, axis=0)
        return relations - learn_rate * total / jnp.sqrt(state)[None, :], state, finish([])
    nz = n // 2
    near = sorted(range(nz), key=lambda k: min(k, nz - k))
    mine_x, other_x = pieces(t, n, False, rel_ids, drel, acc, [gd_other])
    mine_s, other_s = pieces(t, n, True, rel_ids, drel, acc, [gd])
    to_x = add_each(mine_x, across(other_x))
    theirs = across(other_s)
    from_x = {k: beside(to_x[k]) for k in reversed(near)}
    from_z = []
    for i, k in enumerate(reversed(near[1:])):
        after = [grads[i]] if i < len(grads) else []
        piece = sum_piece(k, mine_s[k], theirs, [from_x[k]], after)
        from_z.append(shifted(piece, 2 * k))
    done = finish([piece])
    summed = sum_piece(0, mine_s[0], theirs, [from_x[0]] + from_z, [])
    got = [summed if k == 0 else shifted(summed, 2 * k) for k in range(nz)]
    got_x = [beside(piece) for piece in got]
    state = state.reshape(1, rels)
    ks = near[:1] + near[:0:-1]
    mine = [got[k] for k in ks]
    new = relnew(nz, True, ks, relations, state, mine, across(stacked(mine, [done[2]])), None, [])
    mine = [got_x[k] for k in ks]
    theirs = across(stacked(mine, []))
    rel_new, state_new = relnew(nz, False, ks, relations, state, mine, theirs, new, [])
    return rel_new, state_new.reshape(rels), done


def on_device(
    entities,
    entity_state,
    relations,
    relation_state,
    src_rows,
    rel_ids,
    dst_rows,
    counts,
    neg_blocks,
):
    rounds = src_rows.shape[0]
    rels = relations.shape[1]
    shape = src_rows.shape
    cnt, neg = counts.T, neg_blocks.T
    g_mine, g_other, drel, rel16, ent, state = first_round(
        cnt, neg, src_rows, dst_rows, rel_ids, entities, entity_state.reshape(1, -1), relations
    )
    acc = relsum(0, rel_ids, drel, None, rels)
    ent, state, low = update(ent, state, [g_mine, across(g_other)], [])
    rel = relvec(1, rel_ids, rel16)
    for t in range(1, rounds):
        far = shifted(low, -t)
        own = (low, across(low))
        query, query_t, source, s_hot, d_hot, d_hot_t = source_side(t, src_rows, dst_rows, own, rel)
        far = held(far, [query, acc])
        far = (far, across(far))
        if t == rounds - 1:
            break
        gd_mine, gd_other, target, weight, gpos = target_grad(
            t, shape, cnt, neg, far, query, query_t, d_hot, d_hot_t
        )
        gd = sum_pair(gd_mine, across(gd_other))
        gs_mine, gs_other, drel = source_grad(
            t, shape, cnt, neg, gd, target, weight, gpos, source, rel, s_hot
        )
        acc = relsum(t, rel_ids, drel, acc, rels)
        rel = relvec(t + 1, rel_ids, rel16)
        grads = [sum_pair(gs_mine, shifted(gd, t), F32), across(gs_other)]
        ent, state, low = update(ent, state, grads, [rel])
    drel, dsource, dterm = last_terms(t, shape, cnt, neg, far, query, query_t, d_hot, source, rel)
    gs_mine, gs_other, gd_mine, gd_other = both_grads(dsource, s_hot, dterm, d_hot_t)
    gd = sum_pair(gd_mine, across(gd_other))

    grads = [across(gs_other), shifted(gd, t)]

    def finish(after):
        (mine,) = update(ent, state, [gs_mine, *grads], after, last=True)
        return whole_partition(mine, across(mine))

    rel_new, rel_state, done = relation_update(
        t, rel_ids, drel, acc, relations, relation_state, gd_other, gd, grads, finish
    )
    return (done[0], done[1].reshape(-1), rel_new, rel_state)


def solution(mesh):
    return jax.shard_map(
        on_device,
        mesh=mesh,
        in_specs=(
            P(None, ("groups", "dom")),
            P(("groups", "dom")),
            P(None, "groups"),
            P("groups"),
            P(None, ("groups", "dom", "edge"), None),
            P(None, ("groups", "dom", "edge"), None),
            P(None, ("groups", "dom", "edge"), None),
            P(None, ("groups", "dom", "edge")),
            P(None, ("groups", "dom", "edge")),
        ),
        out_specs=(
            P(None, ("groups", "dom")),
            P(("groups", "dom")),
            P(None, "groups"),
            P("groups"),
        ),
        check_vma=False,
    )
```

```python
import functools

import jax
import jax.numpy as jnp
from jax import lax
from jax.experimental import pallas as pl
from jax.experimental.pallas import tpu as pltpu
from jax.sharding import PartitionSpec as P

learn_rate = 0.1
BF = jnp.bfloat16
F32 = jnp.float32
VMEM_LIMIT = 40 * 1024 * 1024
NN = (((1,), (0,)), ((), ()))
NT = (((1,), (1,)), ((), ()))
TN = (((0,), (0,)), ((), ()))


def mm(a, b, dims=NN):
    return lax.dot_general(a, b, dims, preferred_element_type=F32)


def vmem():
    return pl.BlockSpec(memory_space=pltpu.VMEM)


def smem():
    return pl.BlockSpec(memory_space=pltpu.SMEM)


def anywhere():
    return pl.BlockSpec(memory_space=pl.ANY)


def in_hbm(x):
    return pltpu.with_memory_space_constraint(x, pltpu.HBM)


def cost(flops, size):
    return pl.CostEstimate(flops=flops, bytes_accessed=size, transcendentals=0)


def params():
    return pltpu.CompilerParams(vmem_limit_bytes=VMEM_LIMIT)


def shifted(x, by):
    n = lax.axis_size("dom")
    return lax.ppermute(x, "dom", [(i, (i + by) % n) for i in range(n)])


def beside(x):
    n = lax.axis_size("dom")
    return lax.ppermute(x, "dom", [(i, i ^ 1) for i in range(n)])


def across(x):
    return lax.ppermute(x, "edge", [(0, 1), (1, 0)])


def one_hot(rows_ref, t, count, base):
    blocks, width = rows_ref.shape[1:]
    at = lax.broadcasted_iota(jnp.int32, (count, width), 0)
    idx = rows_ref[t]
    return jnp.concatenate(
        [
            jnp.where(at == base(idx[b : b + 1, :]), 1.0, 0.0).astype(BF)
            for b in range(blocks)
        ],
        axis=1,
    )


def relvec_kernel(t, ids_ref, rel_ref, out_ref):
    rels = rel_ref.shape[1]
    tile = min(rels, 512)
    out = None
    for lo in range(0, rels, tile):
        hot = one_hot(ids_ref, t, tile, lambda i, lo=lo: i - lo)
        part = mm(rel_ref[:, lo : lo + tile], hot)
        out = part if out is None else out + part
    out_ref[...] = out.astype(BF)


def relvec(t, rel_ids, rel16):
    width, rels = rel16.shape
    slots = rel_ids.shape[1] * rel_ids.shape[2]
    return pl.pallas_call(
        functools.partial(relvec_kernel, t),
        in_specs=[vmem()] * 2,
        out_specs=vmem(),
        out_shape=jax.ShapeDtypeStruct((width, slots), BF),
        compiler_params=params(),
        cost_estimate=cost(width * slots, width * slots),
        name="relvec",
    )(rel_ids, rel16)


def relsum_kernel(t, first, ids_ref, drel_ref, *refs):
    step = pl.program_id(0)
    out_ref = refs[-1]
    tile = out_ref.shape[1]
    hot = one_hot(ids_ref, t, tile, lambda i: i - step * tile)
    part = mm(drel_ref[...], hot, NT)
    out_ref[...] = part if first else refs[0][...] + part


def relsum(t, rel_ids, drel, acc, rels):
    width, slots = drel.shape
    tile = min(rels, 512)
    wide = pl.BlockSpec((width, tile), lambda i: (0, i))
    ins = [rel_ids, drel] + ([] if acc is None else [acc])
    return pl.pallas_call(
        functools.partial(relsum_kernel, t, acc is None),
        grid=(rels // tile,),
        in_specs=[
            pl.BlockSpec(rel_ids.shape, lambda i: (0, 0, 0)),
            pl.BlockSpec((width, slots), lambda i: (0, 0)),
        ]
        + ([] if acc is None else [wide]),
        out_specs=wide,
        out_shape=jax.ShapeDtypeStruct((width, rels), F32),
        input_output_aliases={} if acc is None else {2: 0},
        compiler_params=params(),
        cost_estimate=cost(width * slots, width * slots),
        name="relsum",
    )(*ins)


class Limits:
    scratch = lambda shape: [
        pltpu.SMEM((shape[1], shape[0]), jnp.int32),
        pltpu.SMEM((shape[1], shape[0]), jnp.int32),
        pltpu.SemaphoreType.DMA((2,)),
    ]

    def __init__(self, t, from_cnt, from_neg, cnt, neg, sems):
        self.t, self.cnt, self.neg = t, cnt, neg
        self.copies = [
            pltpu.make_async_copy(from_cnt, cnt, sems.at[0]),
            pltpu.make_async_copy(from_neg, neg, sems.at[1]),
        ]
        for copy in self.copies:
            copy.start()

    def wait(self):
        for copy in self.copies:
            copy.wait()

    def count(self, b):
        return self.cnt[b, self.t]

    def negative(self, b):
        return self.neg[b, self.t]


def place():
    dom = lax.axis_index("dom")
    return dom // 2, lax.rem(dom, 2), lax.axis_index("edge")


def localize(edge, half):
    def local(idx):
        moved = idx + edge * half
        return jnp.where(moved >= 2 * half, moved - 2 * half, moved)

    return local


def halves(x):
    hd = x.shape[0] // 2
    return x[:hd], x[hd:]


def make_query(source, rel):
    (s_re, s_im), (w_re, w_im) = halves(source), halves(rel)
    return jnp.concatenate(
        [s_re * w_re - s_im * w_im, s_re * w_im + s_im * w_re], axis=0
    ).astype(BF)


def conj_times(dq, v):
    (dq_re, dq_im), (v_re, v_im) = halves(dq), halves(v)
    return jnp.concatenate(
        [dq_re * v_re + dq_im * v_im, dq_im * v_re - dq_re * v_im], axis=0
    ).astype(BF)


def target_side(shape, limits, query, query_t, target, o_ref, w_ref):
    _, blocks, width = shape
    lanes = lambda b: pl.ds(pl.multiple_of(b * width, width), width)
    count = limits.count
    o_ref[...] = target.astype(BF)
    pos = jnp.sum(query.astype(F32) * target, axis=0, keepdims=True)
    lane = lax.broadcasted_iota(jnp.int32, (1, width), 1)
    limits.wait()
    row_i = lax.broadcasted_iota(jnp.int32, (width, width), 0)
    col_j = lax.broadcasted_iota(jnp.int32, (width, width), 1)
    for b in range(blocks):
        nb = limits.negative(b)
        neg = o_ref[:, lanes(nb)]
        at = slice(b * width, (b + 1) * width)
        scores = mm(query[:, at], neg, TN) if query_t is None else mm(query_t[at], neg)
        keep = jnp.logical_and(row_i < count(b), col_j < count(nb))
        w_ref[:, at] = jnp.where(keep, jax.nn.sigmoid(scores) / width, 0.0).astype(BF)
    valid = jnp.concatenate(
        [jnp.where(lane < count(b), 1.0, 0.0) for b in range(blocks)], axis=1
    )
    return -jax.nn.sigmoid(-pos) * valid


def target_sum(shape, limits, query, gpos, w_ref, m_ref, hot, dims):
    _, blocks, width = shape
    m_ref[...] = jnp.zeros_like(m_ref)
    eye = lax.broadcasted_iota(jnp.int32, (width, width), 0) == lax.broadcasted_iota(
        jnp.int32, (width, width), 1
    )
    for b in range(blocks):
        at = slice(b * width, (b + 1) * width)
        m_ref[at, at] = jnp.where(eye, gpos[:, at], 0.0).astype(BF)
    for b in range(blocks):
        at = slice(b * width, (b + 1) * width)
        to = pl.ds(pl.multiple_of(limits.negative(b) * width, width), width)
        m_ref[at, to] = (m_ref[at, to].astype(F32) + w_ref[:, at].astype(F32)).astype(BF)
    return mm(query, mm(m_ref[...], hot, dims).astype(BF))


def make_dquery(shape, limits, gpos, o_ref, w_ref):
    _, blocks, width = shape
    lanes = lambda b: pl.ds(pl.multiple_of(b * width, width), width)
    out = []
    for b in range(blocks):
        nb = limits.negative(b)
        at = slice(b * width, (b + 1) * width)
        own = gpos[:, at] * o_ref[:, at].astype(F32)
        out.append(own + mm(o_ref[:, lanes(nb)], w_ref[:, at], NT))
    return jnp.concatenate(out, axis=1)


def first_kernel(
    shape, cnt_ref, neg_ref, src_ref, dst_ref, ids_ref, ent_ref, state_ref, rel_ref,
    g_mine, g_other, drel_ref, rel16_ref, ent_mine, state_mine,
    cnt, neg, lim_sems, src, dst, ids, ent, state, rel_buf, o_scr, m_scr, w_scr, in_sems, sems,
):
    rels = rel_buf.shape[1]
    tile = min(rels, 512)
    spans = range(0, rels, tile)
    inputs = [
        pltpu.make_async_copy(there, here, in_sems.at[i])
        for i, (there, here) in enumerate(
            [(src_ref.at[:1], src), (dst_ref.at[:1], dst), (ids_ref.at[:1], ids), (ent_ref, ent), (state_ref, state)]
        )
    ]
    loads = [
        pltpu.make_async_copy(
            rel_ref.at[:, lo : lo + tile], rel_buf.at[:, lo : lo + tile], sems.at[i]
        )
        for i, lo in enumerate(spans)
    ]
    for load in inputs:
        load.start()
    limits = Limits(0, cnt_ref, neg_ref, cnt, neg, lim_sems)
    for load in loads:
        load.start()
    half = ent.shape[1] // 2
    _, _, edge = place()
    local = localize(edge, half)
    inputs[0].wait()
    s_hot = one_hot(src, 0, 2 * half, local)
    inputs[1].wait()
    d_hot = one_hot(dst, 0, 2 * half, local)
    inputs[2].wait()
    ids_hot = [one_hot(ids, 0, tile, lambda i, lo=lo: i - lo) for lo in spans]
    inputs[3].wait()
    inputs[4].wait()
    mine = pl.ds(pl.multiple_of(edge * half, half), half)
    ent_mine[...] = ent[:, mine]
    state_mine[...] = state[:, mine]
    table = jnp.concatenate(
        [ent[:, pl.ds(pl.multiple_of(h * half, half), half)].astype(BF) for h in (edge, 1 - edge)],
        axis=1,
    )
    source = mm(table, s_hot)
    target = mm(table, d_hot)
    rel = None
    for load, lo, hot in zip(loads, spans, ids_hot):
        load.wait()
        low = rel_buf[:, lo : lo + tile].astype(BF)
        rel16_ref[:, lo : lo + tile] = low
        part = mm(low, hot)
        rel = part if rel is None else rel + part
    query = make_query(source, rel)
    gpos = target_side(shape, limits, query, None, target, o_scr, w_scr)
    dq = make_dquery(shape, limits, gpos, o_scr, w_scr)
    drel_ref[...] = conj_times(dq, source)
    total = mm(conj_times(dq, rel), s_hot, NT) + target_sum(
        shape, limits, query, gpos, w_scr, m_scr, d_hot, NT
    )
    g_mine[...] = total[:, :half]
    g_other[...] = total[:, half:].astype(BF)


def first_round(cnt, neg, src, dst, rel_ids, entities, state, relations):
    dim, rows = entities.shape
    rels = relations.shape[1]
    _, blocks, width = src.shape
    slots = blocks * width
    sds = jax.ShapeDtypeStruct
    return pl.pallas_call(
        functools.partial(first_kernel, src.shape),
        in_specs=[anywhere()] * 8,
        out_specs=[vmem()] * 6,
        out_shape=[
            sds((dim, rows // 2), F32),
            sds((dim, rows // 2), BF),
            sds((dim, slots), BF),
            sds((dim, rels), BF),
            sds((dim, rows // 2), F32),
            sds((1, rows // 2), F32),
        ],
        scratch_shapes=Limits.scratch(src.shape)
        + [
            pltpu.VMEM((1, blocks, width), jnp.int32),
            pltpu.VMEM((1, blocks, width), jnp.int32),
            pltpu.VMEM((1, blocks, width), jnp.int32),
            pltpu.VMEM((dim, rows), F32),
            pltpu.VMEM((1, rows), F32),
            pltpu.VMEM((dim, rels), F32),
            pltpu.VMEM((dim, slots), BF),
            pltpu.VMEM((slots, slots), BF),
            pltpu.VMEM((width, slots), BF),
            pltpu.SemaphoreType.DMA((5,)),
            pltpu.SemaphoreType.DMA((-(-rels // min(rels, 512)),)),
        ],
        compiler_params=params(),
        cost_estimate=cost(2 * dim * slots * (rels + 4 * rows), 8 * dim * rels),
        name="first_round",
    )(*(in_hbm(x) for x in (cnt, neg, src, dst, rel_ids, entities, state, relations)))


def source_kernel(
    t, src_ref, dst_ref, own0, own1, rel_ref,
    query_ref, query_t_ref, source_ref, s_hot_ref, d_hot_ref, d_hot_t_ref,
):
    half = own0.shape[1]
    local = localize(place()[2], half)
    s_hot = one_hot(src_ref, t, 2 * half, local)
    d_hot = one_hot(dst_ref, t, 2 * half, local)
    s_hot_ref[...] = s_hot
    d_hot_ref[...] = d_hot
    d_hot_t_ref[...] = d_hot.T
    source = mm(jnp.concatenate([own0[...], own1[...]], axis=1), s_hot)
    source_ref[...] = source.astype(BF)
    query = make_query(source, rel_ref[...].astype(F32))
    query_ref[...] = query
    query_t_ref[...] = query.T


def source_side(t, src, dst, own, rel):
    dim, slots = rel.shape
    rows = 2 * own[0].shape[1]
    sds = lambda *shape: jax.ShapeDtypeStruct(shape, BF)
    return pl.pallas_call(
        functools.partial(source_kernel, t),
        in_specs=[vmem()] * 5,
        out_specs=[vmem()] * 6,
        out_shape=[
            sds(dim, slots), sds(slots, dim), sds(dim, slots),
            sds(rows, slots), sds(rows, slots), sds(slots, rows),
        ],
        compiler_params=params(),
        cost_estimate=cost(dim * slots, dim * slots),
        name="source_side",
    )(src, dst, *own, rel)


def target_kernel(
    t, shape, cnt_ref, neg_ref, far0, far1, query_ref, query_t_ref, d_hot_ref, d_hot_t_ref,
    gd_mine, gd_other, o_ref, w_ref, gpos_ref, cnt, neg, sems, m_scr,
):
    limits = Limits(t, cnt_ref, neg_ref, cnt, neg, sems)
    half = far0.shape[1]
    far = jnp.concatenate([far0[...], far1[...]], axis=1)
    target = mm(far, d_hot_ref[...])
    query = query_ref[...]
    gpos = target_side(shape, limits, query, query_t_ref, target, o_ref, w_ref)
    gpos_ref[...] = gpos
    gd = target_sum(shape, limits, query, gpos, w_ref, m_scr, d_hot_t_ref[...], NN)
    gd_mine[...] = gd[:, :half]
    gd_other[...] = gd[:, half:].astype(BF)


def target_grad(t, shape, cnt, neg, far, query, query_t, d_hot, d_hot_t):
    dim, slots = query.shape
    half = far[0].shape[1]
    width = shape[2]
    sds = jax.ShapeDtypeStruct
    return pl.pallas_call(
        functools.partial(target_kernel, t, shape),
        in_specs=[anywhere()] * 2 + [vmem()] * 6,
        out_specs=[vmem()] * 5,
        out_shape=[
            sds((dim, half), F32),
            sds((dim, half), BF),
            sds((dim, slots), BF),
            sds((width, slots), BF),
            sds((1, slots), F32),
        ],
        scratch_shapes=Limits.scratch(shape) + [pltpu.VMEM((slots, slots), BF)],
        compiler_params=params(),
        cost_estimate=cost(4 * dim * slots * (2 * half + width), 12 * dim * slots),
        name="target_grad",
    )(cnt, neg, *far, query, query_t, d_hot, d_hot_t)


def source_grad_kernel(
    t, shape, cnt_ref, neg_ref, _, o_ref, w_ref, gpos_ref, source_ref, rel_ref, s_hot_ref,
    gs_mine, gs_other, drel_ref, cnt, neg, sems,
):
    limits = Limits(t, cnt_ref, neg_ref, cnt, neg, sems)
    limits.wait()
    half = gs_mine.shape[1]
    dq = make_dquery(shape, limits, gpos_ref[...], o_ref, w_ref)
    drel_ref[...] = conj_times(dq, source_ref[...].astype(F32))
    gs = mm(conj_times(dq, rel_ref[...].astype(F32)), s_hot_ref[...], NT)
    gs_mine[...] = gs[:, :half]
    gs_other[...] = gs[:, half:].astype(BF)


def source_grad(t, shape, cnt, neg, after, target, weight, gpos, source, rel, s_hot):
    dim, slots = rel.shape
    half = s_hot.shape[0] // 2
    sds = jax.ShapeDtypeStruct
    return pl.pallas_call(
        functools.partial(source_grad_kernel, t, shape),
        in_specs=[anywhere()] * 3 + [vmem()] * 6,
        out_specs=[vmem()] * 3,
        out_shape=[sds((dim, half), F32), sds((dim, half), BF), sds((dim, slots), BF)],
        scratch_shapes=Limits.scratch(shape),
        compiler_params=params(),
        cost_estimate=cost(dim * slots, dim * slots),
        name="source_grad",
    )(cnt, neg, after, target, weight, gpos, source, rel, s_hot)


def last_kernel(
    t, shape, cnt_ref, neg_ref, far0, far1, query_ref, query_t_ref, d_hot_ref, source_ref, rel_ref,
    drel_ref, dsource_ref, w_ref, gpos_ref, cnt, neg, sems, o_scr,
):
    limits = Limits(t, cnt_ref, neg_ref, cnt, neg, sems)
    far = jnp.concatenate([far0[...], far1[...]], axis=1)
    target = mm(far, d_hot_ref[...])
    gpos = target_side(shape, limits, query_ref[...], query_t_ref, target, o_scr, w_ref)
    gpos_ref[...] = gpos
    dq = make_dquery(shape, limits, gpos, o_scr, w_ref)
    drel_ref[...] = conj_times(dq, source_ref[...].astype(F32))
    dsource_ref[...] = conj_times(dq, rel_ref[...].astype(F32))


def last_terms(t, shape, cnt, neg, far, query, query_t, d_hot, source, rel):
    dim, slots = query.shape
    sds = jax.ShapeDtypeStruct
    return pl.pallas_call(
        functools.partial(last_kernel, t, shape),
        in_specs=[anywhere()] * 2 + [vmem()] * 7,
        out_specs=[vmem()] * 4,
        out_shape=[
            sds((dim, slots), BF),
            sds((dim, slots), BF),
            sds((shape[2], slots), BF),
            sds((1, slots), F32),
        ],
        scratch_shapes=Limits.scratch(shape) + [pltpu.VMEM((dim, slots), BF)],
        compiler_params=params(),
        cost_estimate=cost(6 * dim * slots * shape[2], 12 * dim * slots),
        name="last_terms",
    )(cnt, neg, *far, query, query_t, d_hot, source, rel)


def both_kernel(
    t, shape, cnt_ref, neg_ref, _, dsource_ref, s_hot_ref, query_ref, gpos_ref, w_ref, d_hot_t_ref,
    gs_mine, gs_other, gd_mine, gd_other, cnt, neg, sems, m_scr,
):
    limits = Limits(t, cnt_ref, neg_ref, cnt, neg, sems)
    limits.wait()
    half = gs_mine.shape[1]
    gd = target_sum(
        shape, limits, query_ref[...], gpos_ref[...], w_ref, m_scr, d_hot_t_ref[...], NN
    )
    gs = mm(dsource_ref[...], s_hot_ref[...], NT)
    for grad, mine, other in ((gd, gd_mine, gd_other), (gs, gs_mine, gs_other)):
        mine[...] = grad[:, :half]
        other[...] = grad[:, half:].astype(BF)


def both_grads(t, shape, cnt, neg, after, dsource, s_hot, query, gpos, weight, d_hot_t):
    dim, slots = dsource.shape
    half = s_hot.shape[0] // 2
    sds = jax.ShapeDtypeStruct
    return pl.pallas_call(
        functools.partial(both_kernel, t, shape),
        in_specs=[anywhere()] * 3 + [vmem()] * 6,
        out_specs=[vmem()] * 4,
        out_shape=[sds((dim, half), F32), sds((dim, half), BF)] * 2,
        scratch_shapes=Limits.scratch(shape) + [pltpu.VMEM((slots, slots), BF)],
        compiler_params=params(),
        cost_estimate=cost(8 * dim * slots * half, 12 * dim * slots),
        name="both_grads",
    )(cnt, neg, after, dsource, s_hot, query, gpos, weight, d_hot_t)


def update_kernel(n_grads, last, *refs):
    ent_ref, state_ref, grads = refs[0], refs[1], refs[2 : 2 + n_grads]
    grad = grads[0][...].astype(F32)
    for g in grads[1:]:
        grad = grad + g[...].astype(F32)
    dim = grad.shape[0]
    state = state_ref[...] + jnp.sum(grad * grad, axis=0, keepdims=True) / dim
    new = ent_ref[...] - grad * (learn_rate / jnp.sqrt(state))
    if last:
        refs[-1][:dim] = new
        refs[-1][dim:] = jnp.broadcast_to(state, (refs[-1].shape[0] - dim, state.shape[1]))
    else:
        refs[-3][...] = new
        refs[-2][...] = state
        refs[-1][...] = new.astype(BF)


def update(ent, state, grads, after, last=False):
    dim, half = ent.shape
    sds = jax.ShapeDtypeStruct
    outs = [sds((dim, half), F32), sds((1, half), F32), sds((dim, half), BF)]
    if last:
        outs = [sds((dim + 8, half), F32)]
    return pl.pallas_call(
        functools.partial(update_kernel, len(grads), last),
        in_specs=[vmem()] * (2 + len(grads)) + [anywhere()] * len(after),
        out_specs=[vmem()] * len(outs),
        out_shape=outs,
        compiler_params=params(),
        cost_estimate=cost(10 * dim * half, 16 * dim * half),
        name="update",
    )(ent, state, *grads, *after)


def pair_kernel(a_ref, b_ref, out_ref):
    out_ref[...] = (a_ref[...] + b_ref[...].astype(F32)).astype(out_ref.dtype)


def sum_pair(a, b, dtype=BF):
    return pl.pallas_call(
        pair_kernel,
        in_specs=[vmem()] * 2,
        out_specs=vmem(),
        out_shape=jax.ShapeDtypeStruct(a.shape, dtype),
        compiler_params=params(),
        name="sum_pair",
    )(a, b)


def held_kernel(x_ref, *refs):
    pass


def held(x, after):
    return pl.pallas_call(
        held_kernel,
        in_specs=[anywhere()] * (1 + len(after)),
        out_specs=anywhere(),
        out_shape=jax.ShapeDtypeStruct(x.shape, x.dtype),
        input_output_aliases={0: 0},
        compiler_params=params(),
        name="held",
    )(x, *after)


def whole_kernel(mine, theirs, ent_out, state_out, token):
    token[...] = jnp.zeros_like(token)
    dim, rows = ent_out.shape
    half = rows // 2
    edge = place()[2]
    for core, part in ((edge, mine), (1 - edge, theirs)):
        at = pl.ds(pl.multiple_of(core * half, half), half)
        ent_out[:, at] = part[:dim]
        state_out[:, at] = part[dim : dim + 1]


def whole_partition(mine, theirs):
    dim, half = mine.shape[0] - 8, mine.shape[1]
    return pl.pallas_call(
        whole_kernel,
        in_specs=[vmem()] * 2,
        out_specs=[vmem()] * 3,
        out_shape=[
            jax.ShapeDtypeStruct((dim, 2 * half), F32),
            jax.ShapeDtypeStruct((1, 2 * half), F32),
            jax.ShapeDtypeStruct((8, 128), F32),
        ],
        compiler_params=params(),
        name="whole_partition",
    )(mine, theirs)


def first_column(owner, core, w):
    return pl.multiple_of((2 * owner + core) * w, w)


def pieces_kernel(t, nz, same, ids_ref, drel_ref, acc_ref, *refs):
    mine, other = refs[-nz - 1 : -1], refs[-1]
    w = other.shape[2]
    z, x, edge = place()
    drel = drel_ref[...]
    for k in range(nz):
        owner = 2 * lax.rem(z + k, nz) + (x if same else 1 - x)
        at = [first_column(owner, core, w) for core in (edge, 1 - edge)]
        hot = jnp.concatenate([one_hot(ids_ref, t, w, lambda i, lo=lo: i - lo) for lo in at], axis=0)
        part = mm(drel, hot, NT)
        mine[k][...] = acc_ref[:, pl.ds(at[0], w)] + part[:, :w]
        other[k] = (acc_ref[:, pl.ds(at[1], w)] + part[:, w:]).astype(BF)


def pieces(t, n, same, rel_ids, drel, acc, after):
    dim, rels = acc.shape
    w = rels // (2 * n)
    sds = jax.ShapeDtypeStruct
    out = pl.pallas_call(
        functools.partial(pieces_kernel, t, n // 2, same),
        in_specs=[vmem()] * 3 + [anywhere()] * len(after),
        out_specs=[vmem()] * (n // 2 + 1),
        out_shape=[sds((dim, w), F32)] * (n // 2) + [sds((n // 2, dim, w), BF)],
        compiler_params=params(),
        cost_estimate=cost(dim * rels * drel.shape[1], 4 * dim * rels),
        name="pieces",
    )(rel_ids, drel, acc, *after)
    return out[:-1], out[-1]


def add_kernel(n, *refs):
    for k in range(n):
        refs[n + 1 + k][...] = (refs[k][...] + refs[n][k].astype(F32)).astype(BF)


def add_each(mine, theirs):
    n = len(mine)
    return pl.pallas_call(
        functools.partial(add_kernel, n),
        in_specs=[vmem()] * (n + 1),
        out_specs=[vmem()] * n,
        out_shape=[jax.ShapeDtypeStruct(x.shape, BF) for x in mine],
        compiler_params=params(),
        name="add_each",
    )(*mine, theirs)


def sum_kernel(k, count, mine, theirs, *refs):
    total = mine[...] + theirs[k].astype(F32)
    for r in refs[:count]:
        total = total + r[...].astype(F32)
    refs[-1][...] = total.astype(BF)


def sum_piece(k, mine, theirs, parts, after):
    return pl.pallas_call(
        functools.partial(sum_kernel, k, len(parts)),
        in_specs=[vmem()] * (2 + len(parts)) + [anywhere()] * len(after),
        out_specs=vmem(),
        out_shape=jax.ShapeDtypeStruct(mine.shape, BF),
        compiler_params=params(),
        name="sum_piece",
    )(mine, theirs, *parts, *after)


def stacked_kernel(*refs):
    for i in range(refs[-1].shape[0]):
        refs[-1][i] = refs[i][...]


def stacked(parts, after):
    return pl.pallas_call(
        stacked_kernel,
        in_specs=[vmem()] * len(parts) + [anywhere()] * len(after),
        out_specs=vmem(),
        out_shape=jax.ShapeDtypeStruct((len(parts), *parts[0].shape), parts[0].dtype),
        compiler_params=params(),
        name="stacked",
    )(*parts, *after)


def relnew_kernel(nz, same, ks, rel_ref, state_ref, *refs):
    mine, theirs = refs[: len(ks)], refs[len(ks)]
    rel_out, state_out, buf, sems = refs[-4:]
    w = mine[0].shape[1]
    state_out[...] = refs[len(ks) + (1 if same else 2)][...]
    z, x, edge = place()
    copies = []
    for i in range(2 * len(ks)):
        owner = 2 * lax.rem(z + nz - ks[i // 2], nz) + (x if same else 1 - x)
        at = pl.ds(first_column(owner, edge if i % 2 == 0 else 1 - edge, w), w)
        grad = (mine[i // 2][...] if i % 2 == 0 else theirs[i // 2]).astype(F32)
        state = state_ref[:, at] + jnp.sum(grad * grad, axis=0, keepdims=True) / grad.shape[0]
        state_out[:, at] = state
        buf[i] = rel_ref[:, at] - grad * (learn_rate / jnp.sqrt(state))
        copy = pltpu.make_async_copy(buf.at[i], rel_out.at[:, at], sems.at[i])
        copy.start()
        copies.append(copy)
    for copy in copies:
        copy.wait()


def relnew(nz, same, ks, relations, state, mine, theirs, before, after):
    dim, rels = relations.shape
    w = mine[0].shape[1]
    count = 2 * len(ks)
    start = [state] if before is None else list(before)
    return pl.pallas_call(
        functools.partial(relnew_kernel, nz, same, ks),
        in_specs=[vmem()] * (3 + len(ks))
        + ([anywhere()] if before else [])
        + [vmem()]
        + [anywhere()] * len(after),
        out_specs=[anywhere(), vmem()],
        out_shape=[jax.ShapeDtypeStruct((dim, rels), F32), jax.ShapeDtypeStruct((1, rels), F32)],
        input_output_aliases={3 + len(ks): 0} if before else {},
        scratch_shapes=[pltpu.VMEM((count, dim, w), F32), pltpu.SemaphoreType.DMA((count,))],
        compiler_params=params(),
        cost_estimate=cost(4 * dim * w * count, 4 * dim * w * count),
        name="relnew",
    )(relations, state, *mine, theirs, *start, *after)


def relation_update(t, rel_ids, drel, acc, relations, state, send, finish):
    n = lax.axis_size("dom")
    dim, rels = relations.shape
    if n % 2 or rels % (256 * n):
        total = lax.psum(relsum(t, rel_ids, drel, acc, rels), ("dom", "edge"))
        state = state + jnp.mean(total * total, axis=0)
        return relations - learn_rate * total / jnp.sqrt(state)[None, :], state, finish(send(drel), [])
    nz = n // 2
    near = sorted(range(nz), key=lambda k: min(k, nz - k))
    mine_x, other_x = pieces(t, n, False, rel_ids, drel, acc, [])
    mine_s, other_s = pieces(t, n, True, rel_ids, drel, acc, [other_x])
    to_x = add_each(mine_x, across(other_x))
    theirs = across(other_s)
    from_x = {k: beside(to_x[k]) for k in reversed(near)}
    grads = send(other_x)
    turned = {
        k: sum_piece(k, mine_s[k], theirs, [from_x[k]], grads[1:2] if k == near[-1] else [])
        for k in near[1:]
    }
    from_z = [shifted(turned[k], 2 * k) for k in near[1:]]
    done = finish(grads, [turned[near[-1]]])
    summed = sum_piece(0, mine_s[0], theirs, [from_x[0]] + from_z, [])
    got = [summed if k == 0 else shifted(summed, 2 * k) for k in range(nz)]
    got_x = [beside(piece) for piece in got]
    state = state.reshape(1, rels)
    ks = near[:1] + near[:0:-1]
    mine = [got[k] for k in ks]
    new = relnew(nz, True, ks, relations, state, mine, across(stacked(mine, [done[2]])), None, [])
    mine = [got_x[k] for k in ks]
    theirs = across(stacked(mine, []))
    rel_new, state_new = relnew(nz, False, ks, relations, state, mine, theirs, new, [])
    return rel_new, state_new.reshape(rels), done


def on_device(
    entities,
    entity_state,
    relations,
    relation_state,
    src_rows,
    rel_ids,
    dst_rows,
    counts,
    neg_blocks,
):
    rounds = src_rows.shape[0]
    rels = relations.shape[1]
    shape = src_rows.shape
    cnt, neg = counts.T, neg_blocks.T
    g_mine, g_other, drel, rel16, ent, state = first_round(
        cnt, neg, src_rows, dst_rows, rel_ids, entities, entity_state.reshape(1, -1), relations
    )
    acc = relsum(0, rel_ids, drel, None, rels)
    ent, state, low = update(ent, state, [g_mine, across(g_other)], [])
    rel = relvec(1, rel_ids, rel16)
    for t in range(1, rounds):
        far = shifted(low, -t)
        own = (low, across(low))
        query, query_t, source, s_hot, d_hot, d_hot_t = source_side(t, src_rows, dst_rows, own, rel)
        far = held(far, [query, acc])
        far = (far, across(far))
        if t == rounds - 1:
            break
        gd_mine, gd_other, target, weight, gpos = target_grad(
            t, shape, cnt, neg, far, query, query_t, d_hot, d_hot_t
        )
        gd = sum_pair(gd_mine, across(gd_other))
        gs_mine, gs_other, drel = source_grad(
            t, shape, cnt, neg, gd, target, weight, gpos, source, rel, s_hot
        )
        acc = relsum(t, rel_ids, drel, acc, rels)
        rel = relvec(t + 1, rel_ids, rel16)
        grads = [sum_pair(gs_mine, shifted(gd, t), F32), across(gs_other)]
        ent, state, low = update(ent, state, grads, [rel])
    drel, dsource, weight, gpos = last_terms(
        t, shape, cnt, neg, far, query, query_t, d_hot, source, rel
    )

    def send(after):
        gs_mine, gs_other, gd_mine, gd_other = both_grads(
            t, shape, cnt, neg, after, dsource, s_hot, query, gpos, weight, d_hot_t
        )
        gd = sum_pair(gd_mine, across(gd_other))
        return gs_mine, across(gs_other), shifted(gd, t)

    def finish(grads, after):
        (mine,) = update(ent, state, grads, after, last=True)
        return whole_partition(mine, across(mine))

    rel_new, rel_state, done = relation_update(
        t, rel_ids, drel, acc, relations, relation_state, send, finish
    )
    return (done[0], done[1].reshape(-1), rel_new, rel_state)


def solution(mesh):
    return jax.shard_map(
        on_device,
        mesh=mesh,
        in_specs=(
            P(None, ("groups", "dom")),
            P(("groups", "dom")),
            P(None, "groups"),
            P("groups"),
            P(None, ("groups", "dom", "edge"), None),
            P(None, ("groups", "dom", "edge"), None),
            P(None, ("groups", "dom", "edge"), None),
            P(None, ("groups", "dom", "edge")),
            P(None, ("groups", "dom", "edge")),
        ),
        out_specs=(
            P(None, ("groups", "dom")),
            P(("groups", "dom")),
            P(None, "groups"),
            P("groups"),
        ),
        check_vma=False,
    )
```

```python
import functools

import jax
import jax.numpy as jnp
from jax import lax
from jax.experimental import pallas as pl
from jax.experimental.pallas import tpu as pltpu
from jax.sharding import PartitionSpec as P

learn_rate = 0.1
BF = jnp.bfloat16
F32 = jnp.float32
VMEM_LIMIT = 40 * 1024 * 1024
NN = (((1,), (0,)), ((), ()))
NT = (((1,), (1,)), ((), ()))
TN = (((0,), (0,)), ((), ()))


def mm(a, b, dims=NN):
    return lax.dot_general(a, b, dims, preferred_element_type=F32)


def vmem():
    return pl.BlockSpec(memory_space=pltpu.VMEM)


def smem():
    return pl.BlockSpec(memory_space=pltpu.SMEM)


def anywhere():
    return pl.BlockSpec(memory_space=pl.ANY)


def in_hbm(x):
    return pltpu.with_memory_space_constraint(x, pltpu.HBM)


def cost(flops, size):
    return pl.CostEstimate(flops=flops, bytes_accessed=size, transcendentals=0)


def params():
    return pltpu.CompilerParams(vmem_limit_bytes=VMEM_LIMIT)


def shifted(x, by):
    n = lax.axis_size("dom")
    return lax.ppermute(x, "dom", [(i, (i + by) % n) for i in range(n)])


def swapped(x, bits):
    n = lax.axis_size("dom")
    return lax.ppermute(x, "dom", [(i, i ^ bits) for i in range(n)])


def across(x):
    return lax.ppermute(x, "edge", [(0, 1), (1, 0)])


def one_hot(rows_ref, t, count, base):
    blocks, width = rows_ref.shape[1:]
    at = lax.broadcasted_iota(jnp.int32, (count, width), 0)
    idx = rows_ref[t]
    return jnp.concatenate(
        [
            jnp.where(at == base(idx[b : b + 1, :]), 1.0, 0.0).astype(BF)
            for b in range(blocks)
        ],
        axis=1,
    )


def relvec_kernel(t, ids_ref, rel_ref, out_ref):
    rels = rel_ref.shape[1]
    tile = min(rels, 512)
    out = None
    for lo in range(0, rels, tile):
        hot = one_hot(ids_ref, t, tile, lambda i, lo=lo: i - lo)
        part = mm(rel_ref[:, lo : lo + tile], hot)
        out = part if out is None else out + part
    out_ref[...] = out.astype(BF)


def relvec(t, rel_ids, rel16):
    width, rels = rel16.shape
    slots = rel_ids.shape[1] * rel_ids.shape[2]
    return pl.pallas_call(
        functools.partial(relvec_kernel, t),
        in_specs=[vmem()] * 2,
        out_specs=vmem(),
        out_shape=jax.ShapeDtypeStruct((width, slots), BF),
        compiler_params=params(),
        cost_estimate=cost(width * slots, width * slots),
        name="relvec",
    )(rel_ids, rel16)


def relsum_kernel(t, first, ids_ref, drel_ref, *refs):
    step = pl.program_id(0)
    out_ref = refs[-1]
    tile = out_ref.shape[1]
    hot = one_hot(ids_ref, t, tile, lambda i: i - step * tile)
    part = mm(drel_ref[...], hot, NT)
    out_ref[...] = part if first else refs[0][...] + part


def relsum(t, rel_ids, drel, acc, rels):
    width, slots = drel.shape
    tile = min(rels, 512)
    wide = pl.BlockSpec((width, tile), lambda i: (0, i))
    ins = [rel_ids, drel] + ([] if acc is None else [acc])
    return pl.pallas_call(
        functools.partial(relsum_kernel, t, acc is None),
        grid=(rels // tile,),
        in_specs=[
            pl.BlockSpec(rel_ids.shape, lambda i: (0, 0, 0)),
            pl.BlockSpec((width, slots), lambda i: (0, 0)),
        ]
        + ([] if acc is None else [wide]),
        out_specs=wide,
        out_shape=jax.ShapeDtypeStruct((width, rels), F32),
        input_output_aliases={} if acc is None else {2: 0},
        compiler_params=params(),
        cost_estimate=cost(width * slots, width * slots),
        name="relsum",
    )(*ins)


class Limits:
    scratch = lambda shape: [
        pltpu.SMEM((shape[1], shape[0]), jnp.int32),
        pltpu.SMEM((shape[1], shape[0]), jnp.int32),
        pltpu.SemaphoreType.DMA((2,)),
    ]

    def __init__(self, t, from_cnt, from_neg, cnt, neg, sems):
        self.t, self.cnt, self.neg = t, cnt, neg
        self.copies = [
            pltpu.make_async_copy(from_cnt, cnt, sems.at[0]),
            pltpu.make_async_copy(from_neg, neg, sems.at[1]),
        ]
        for copy in self.copies:
            copy.start()

    def wait(self):
        for copy in self.copies:
            copy.wait()

    def count(self, b):
        return self.cnt[b, self.t]

    def negative(self, b):
        return self.neg[b, self.t]


def place():
    dom = lax.axis_index("dom")
    return dom // 2, lax.rem(dom, 2), lax.axis_index("edge")


def localize(edge, half):
    def local(idx):
        moved = idx + edge * half
        return jnp.where(moved >= 2 * half, moved - 2 * half, moved)

    return local


def halves(x):
    hd = x.shape[0] // 2
    return x[:hd], x[hd:]


def make_query(source, rel):
    (s_re, s_im), (w_re, w_im) = halves(source), halves(rel)
    return jnp.concatenate(
        [s_re * w_re - s_im * w_im, s_re * w_im + s_im * w_re], axis=0
    ).astype(BF)


def conj_times(dq, v):
    (dq_re, dq_im), (v_re, v_im) = halves(dq), halves(v)
    return jnp.concatenate(
        [dq_re * v_re + dq_im * v_im, dq_im * v_re - dq_re * v_im], axis=0
    ).astype(BF)


def target_side(shape, limits, query, query_t, target, o_ref, w_ref):
    _, blocks, width = shape
    lanes = lambda b: pl.ds(pl.multiple_of(b * width, width), width)
    count = limits.count
    o_ref[...] = target.astype(BF)
    pos = jnp.sum(query.astype(F32) * target, axis=0, keepdims=True)
    lane = lax.broadcasted_iota(jnp.int32, (1, width), 1)
    limits.wait()
    row_i = lax.broadcasted_iota(jnp.int32, (width, width), 0)
    col_j = lax.broadcasted_iota(jnp.int32, (width, width), 1)
    for b in range(blocks):
        nb = limits.negative(b)
        neg = o_ref[:, lanes(nb)]
        at = slice(b * width, (b + 1) * width)
        scores = mm(query[:, at], neg, TN) if query_t is None else mm(query_t[at], neg)
        keep = jnp.logical_and(row_i < count(b), col_j < count(nb))
        w_ref[:, at] = jnp.where(keep, jax.nn.sigmoid(scores) / width, 0.0).astype(BF)
    valid = jnp.concatenate(
        [jnp.where(lane < count(b), 1.0, 0.0) for b in range(blocks)], axis=1
    )
    return -jax.nn.sigmoid(-pos) * valid


def target_sum(shape, limits, query, gpos, w_ref, d_ref, hot, dims):
    _, blocks, width = shape
    d_ref[...] = gpos * query.astype(F32)
    for b in range(blocks):
        at = slice(b * width, (b + 1) * width)
        to = pl.ds(pl.multiple_of(limits.negative(b) * width, width), width)
        d_ref[:, to] += mm(query[:, at], w_ref[:, at])
    return mm(d_ref[...].astype(BF), hot, dims)


def make_dquery(shape, limits, gpos, o_ref, w_ref):
    _, blocks, width = shape
    lanes = lambda b: pl.ds(pl.multiple_of(b * width, width), width)
    out = []
    for b in range(blocks):
        nb = limits.negative(b)
        at = slice(b * width, (b + 1) * width)
        own = gpos[:, at] * o_ref[:, at].astype(F32)
        out.append(own + mm(o_ref[:, lanes(nb)], w_ref[:, at], NT))
    return jnp.concatenate(out, axis=1)


def first_kernel(
    shape, cnt_ref, neg_ref, src_ref, dst_ref, ids_ref, ent_ref, state_ref, rel_ref,
    g_mine, g_other, drel_ref, rel16_ref, ent_mine, state_mine,
    cnt, neg, lim_sems, src, dst, ids, ent, state, rel_buf, o_scr, d_scr, w_scr, in_sems, sems,
):
    rels = rel_buf.shape[1]
    tile = min(rels, 512)
    spans = range(0, rels, tile)
    inputs = [
        pltpu.make_async_copy(there, here, in_sems.at[i])
        for i, (there, here) in enumerate(
            [(src_ref.at[:1], src), (dst_ref.at[:1], dst), (ids_ref.at[:1], ids), (ent_ref, ent), (state_ref, state)]
        )
    ]
    loads = [
        pltpu.make_async_copy(
            rel_ref.at[:, lo : lo + tile], rel_buf.at[:, lo : lo + tile], sems.at[i]
        )
        for i, lo in enumerate(spans)
    ]
    for load in inputs:
        load.start()
    limits = Limits(0, cnt_ref, neg_ref, cnt, neg, lim_sems)
    for load in loads:
        load.start()
    half = ent.shape[1] // 2
    _, _, edge = place()
    local = localize(edge, half)
    inputs[0].wait()
    s_hot = one_hot(src, 0, 2 * half, local)
    inputs[1].wait()
    d_hot = one_hot(dst, 0, 2 * half, local)
    inputs[2].wait()
    ids_hot = [one_hot(ids, 0, tile, lambda i, lo=lo: i - lo) for lo in spans]
    inputs[3].wait()
    inputs[4].wait()
    mine = pl.ds(pl.multiple_of(edge * half, half), half)
    ent_mine[...] = ent[:, mine]
    state_mine[...] = state[:, mine]
    table = jnp.concatenate(
        [ent[:, pl.ds(pl.multiple_of(h * half, half), half)].astype(BF) for h in (edge, 1 - edge)],
        axis=1,
    )
    source = mm(table, s_hot)
    target = mm(table, d_hot)
    rel = None
    for load, lo, hot in zip(loads, spans, ids_hot):
        load.wait()
        low = rel_buf[:, lo : lo + tile].astype(BF)
        rel16_ref[:, lo : lo + tile] = low
        part = mm(low, hot)
        rel = part if rel is None else rel + part
    query = make_query(source, rel)
    gpos = target_side(shape, limits, query, None, target, o_scr, w_scr)
    dq = make_dquery(shape, limits, gpos, o_scr, w_scr)
    drel_ref[...] = conj_times(dq, source)
    total = mm(conj_times(dq, rel), s_hot, NT) + target_sum(
        shape, limits, query, gpos, w_scr, d_scr, d_hot, NT
    )
    g_mine[...] = total[:, :half]
    g_other[...] = total[:, half:].astype(BF)


def first_round(cnt, neg, src, dst, rel_ids, entities, state, relations):
    dim, rows = entities.shape
    rels = relations.shape[1]
    _, blocks, width = src.shape
    slots = blocks * width
    sds = jax.ShapeDtypeStruct
    return pl.pallas_call(
        functools.partial(first_kernel, src.shape),
        in_specs=[anywhere()] * 8,
        out_specs=[vmem()] * 6,
        out_shape=[
            sds((dim, rows // 2), F32),
            sds((dim, rows // 2), BF),
            sds((dim, slots), BF),
            sds((dim, rels), BF),
            sds((dim, rows // 2), F32),
            sds((1, rows // 2), F32),
        ],
        scratch_shapes=Limits.scratch(src.shape)
        + [
            pltpu.VMEM((1, blocks, width), jnp.int32),
            pltpu.VMEM((1, blocks, width), jnp.int32),
            pltpu.VMEM((1, blocks, width), jnp.int32),
            pltpu.VMEM((dim, rows), F32),
            pltpu.VMEM((1, rows), F32),
            pltpu.VMEM((dim, rels), F32),
            pltpu.VMEM((dim, slots), BF),
            pltpu.VMEM((dim, slots), F32),
            pltpu.VMEM((width, slots), BF),
            pltpu.SemaphoreType.DMA((5,)),
            pltpu.SemaphoreType.DMA((-(-rels // min(rels, 512)),)),
        ],
        compiler_params=params(),
        cost_estimate=cost(2 * dim * slots * (rels + 4 * rows), 8 * dim * rels),
        name="first_round",
    )(*(in_hbm(x) for x in (cnt, neg, src, dst, rel_ids, entities, state, relations)))


def source_kernel(
    t, src_ref, dst_ref, own0, own1, rel_ref,
    query_ref, query_t_ref, source_ref, s_hot_ref, d_hot_ref, d_hot_t_ref,
):
    half = own0.shape[1]
    local = localize(place()[2], half)
    s_hot = one_hot(src_ref, t, 2 * half, local)
    d_hot = one_hot(dst_ref, t, 2 * half, local)
    s_hot_ref[...] = s_hot
    d_hot_ref[...] = d_hot
    d_hot_t_ref[...] = d_hot.T
    source = mm(jnp.concatenate([own0[...], own1[...]], axis=1), s_hot)
    source_ref[...] = source.astype(BF)
    query = make_query(source, rel_ref[...].astype(F32))
    query_ref[...] = query
    query_t_ref[...] = query.T


def source_side(t, src, dst, own, rel):
    dim, slots = rel.shape
    rows = 2 * own[0].shape[1]
    sds = lambda *shape: jax.ShapeDtypeStruct(shape, BF)
    return pl.pallas_call(
        functools.partial(source_kernel, t),
        in_specs=[vmem()] * 5,
        out_specs=[vmem()] * 6,
        out_shape=[
            sds(dim, slots), sds(slots, dim), sds(dim, slots),
            sds(rows, slots), sds(rows, slots), sds(slots, rows),
        ],
        compiler_params=params(),
        cost_estimate=cost(dim * slots, dim * slots),
        name="source_side",
    )(src, dst, *own, rel)


def target_kernel(
    t, shape, cnt_ref, neg_ref, far0, far1, query_ref, query_t_ref, d_hot_ref, d_hot_t_ref,
    gd_mine, gd_other, o_ref, w_ref, gpos_ref, cnt, neg, sems, d_scr,
):
    limits = Limits(t, cnt_ref, neg_ref, cnt, neg, sems)
    half = far0.shape[1]
    far = jnp.concatenate([far0[...], far1[...]], axis=1)
    target = mm(far, d_hot_ref[...])
    query = query_ref[...]
    gpos = target_side(shape, limits, query, query_t_ref, target, o_ref, w_ref)
    gpos_ref[...] = gpos
    gd = target_sum(shape, limits, query, gpos, w_ref, d_scr, d_hot_t_ref[...], NN)
    gd_mine[...] = gd[:, :half]
    gd_other[...] = gd[:, half:].astype(BF)


def target_grad(t, shape, cnt, neg, far, query, query_t, d_hot, d_hot_t):
    dim, slots = query.shape
    half = far[0].shape[1]
    width = shape[2]
    sds = jax.ShapeDtypeStruct
    return pl.pallas_call(
        functools.partial(target_kernel, t, shape),
        in_specs=[anywhere()] * 2 + [vmem()] * 6,
        out_specs=[vmem()] * 5,
        out_shape=[
            sds((dim, half), F32),
            sds((dim, half), BF),
            sds((dim, slots), BF),
            sds((width, slots), BF),
            sds((1, slots), F32),
        ],
        scratch_shapes=Limits.scratch(shape) + [pltpu.VMEM((dim, slots), F32)],
        compiler_params=params(),
        cost_estimate=cost(4 * dim * slots * (2 * half + width), 12 * dim * slots),
        name="target_grad",
    )(cnt, neg, *far, query, query_t, d_hot, d_hot_t)


def source_grad_kernel(
    t, shape, cnt_ref, neg_ref, _, o_ref, w_ref, gpos_ref, source_ref, rel_ref, s_hot_ref,
    gs_mine, gs_other, drel_ref, cnt, neg, sems,
):
    limits = Limits(t, cnt_ref, neg_ref, cnt, neg, sems)
    limits.wait()
    half = gs_mine.shape[1]
    dq = make_dquery(shape, limits, gpos_ref[...], o_ref, w_ref)
    drel_ref[...] = conj_times(dq, source_ref[...].astype(F32))
    gs = mm(conj_times(dq, rel_ref[...].astype(F32)), s_hot_ref[...], NT)
    gs_mine[...] = gs[:, :half]
    gs_other[...] = gs[:, half:].astype(BF)


def source_grad(t, shape, cnt, neg, after, target, weight, gpos, source, rel, s_hot):
    dim, slots = rel.shape
    half = s_hot.shape[0] // 2
    sds = jax.ShapeDtypeStruct
    return pl.pallas_call(
        functools.partial(source_grad_kernel, t, shape),
        in_specs=[anywhere()] * 3 + [vmem()] * 6,
        out_specs=[vmem()] * 3,
        out_shape=[sds((dim, half), F32), sds((dim, half), BF), sds((dim, slots), BF)],
        scratch_shapes=Limits.scratch(shape),
        compiler_params=params(),
        cost_estimate=cost(dim * slots, dim * slots),
        name="source_grad",
    )(cnt, neg, after, target, weight, gpos, source, rel, s_hot)


def last_kernel(
    t, shape, cnt_ref, neg_ref, far0, far1, query_ref, query_t_ref, d_hot_ref, source_ref, rel_ref,
    drel_ref, dsource_ref, w_ref, gpos_ref, cnt, neg, sems, o_scr,
):
    limits = Limits(t, cnt_ref, neg_ref, cnt, neg, sems)
    far = jnp.concatenate([far0[...], far1[...]], axis=1)
    target = mm(far, d_hot_ref[...])
    gpos = target_side(shape, limits, query_ref[...], query_t_ref, target, o_scr, w_ref)
    gpos_ref[...] = gpos
    dq = make_dquery(shape, limits, gpos, o_scr, w_ref)
    drel_ref[...] = conj_times(dq, source_ref[...].astype(F32))
    dsource_ref[...] = conj_times(dq, rel_ref[...].astype(F32))


def last_terms(t, shape, cnt, neg, far, query, query_t, d_hot, source, rel):
    dim, slots = query.shape
    sds = jax.ShapeDtypeStruct
    return pl.pallas_call(
        functools.partial(last_kernel, t, shape),
        in_specs=[anywhere()] * 2 + [vmem()] * 7,
        out_specs=[vmem()] * 4,
        out_shape=[
            sds((dim, slots), BF),
            sds((dim, slots), BF),
            sds((shape[2], slots), BF),
            sds((1, slots), F32),
        ],
        scratch_shapes=Limits.scratch(shape) + [pltpu.VMEM((dim, slots), BF)],
        compiler_params=params(),
        cost_estimate=cost(6 * dim * slots * shape[2], 12 * dim * slots),
        name="last_terms",
    )(cnt, neg, *far, query, query_t, d_hot, source, rel)


def both_kernel(
    t, shape, cnt_ref, neg_ref, _, dsource_ref, s_hot_ref, query_ref, gpos_ref, w_ref, d_hot_t_ref,
    gs_mine, gs_other, gd_mine, gd_other, cnt, neg, sems, d_scr,
):
    limits = Limits(t, cnt_ref, neg_ref, cnt, neg, sems)
    limits.wait()
    half = gs_mine.shape[1]
    gd = target_sum(
        shape, limits, query_ref[...], gpos_ref[...], w_ref, d_scr, d_hot_t_ref[...], NN
    )
    gs = mm(dsource_ref[...], s_hot_ref[...], NT)
    for grad, mine, other in ((gd, gd_mine, gd_other), (gs, gs_mine, gs_other)):
        mine[...] = grad[:, :half]
        other[...] = grad[:, half:].astype(BF)


def both_grads(t, shape, cnt, neg, after, dsource, s_hot, query, gpos, weight, d_hot_t):
    dim, slots = dsource.shape
    half = s_hot.shape[0] // 2
    sds = jax.ShapeDtypeStruct
    return pl.pallas_call(
        functools.partial(both_kernel, t, shape),
        in_specs=[anywhere()] * 3 + [vmem()] * 6,
        out_specs=[vmem()] * 4,
        out_shape=[sds((dim, half), F32), sds((dim, half), BF)] * 2,
        scratch_shapes=Limits.scratch(shape) + [pltpu.VMEM((dim, slots), F32)],
        compiler_params=params(),
        cost_estimate=cost(8 * dim * slots * half, 12 * dim * slots),
        name="both_grads",
    )(cnt, neg, after, dsource, s_hot, query, gpos, weight, d_hot_t)


def update_kernel(n_grads, last, *refs):
    ent_ref, state_ref, grads = refs[0], refs[1], refs[2 : 2 + n_grads]
    grad = grads[0][...].astype(F32)
    for g in grads[1:]:
        grad = grad + g[...].astype(F32)
    dim = grad.shape[0]
    state = state_ref[...] + jnp.sum(grad * grad, axis=0, keepdims=True) / dim
    new = ent_ref[...] - grad * (learn_rate / jnp.sqrt(state))
    if last:
        refs[-1][:dim] = new
        refs[-1][dim:] = jnp.broadcast_to(state, (refs[-1].shape[0] - dim, state.shape[1]))
    else:
        refs[-3][...] = new
        refs[-2][...] = state
        refs[-1][...] = new.astype(BF)


def update(ent, state, grads, after, last=False):
    dim, half = ent.shape
    sds = jax.ShapeDtypeStruct
    outs = [sds((dim, half), F32), sds((1, half), F32), sds((dim, half), BF)]
    if last:
        outs = [sds((dim + 8, half), F32)]
    return pl.pallas_call(
        functools.partial(update_kernel, len(grads), last),
        in_specs=[vmem()] * (2 + len(grads)) + [anywhere()] * len(after),
        out_specs=[vmem()] * len(outs),
        out_shape=outs,
        compiler_params=params(),
        cost_estimate=cost(10 * dim * half, 16 * dim * half),
        name="update",
    )(ent, state, *grads, *after)


def pair_kernel(a_ref, b_ref, out_ref):
    out_ref[...] = (a_ref[...] + b_ref[...].astype(F32)).astype(out_ref.dtype)


def sum_pair(a, b, dtype=BF):
    return pl.pallas_call(
        pair_kernel,
        in_specs=[vmem()] * 2,
        out_specs=vmem(),
        out_shape=jax.ShapeDtypeStruct(a.shape, dtype),
        compiler_params=params(),
        name="sum_pair",
    )(a, b)


def held_kernel(x_ref, *refs):
    pass


def held(x, after):
    return pl.pallas_call(
        held_kernel,
        in_specs=[anywhere()] * (1 + len(after)),
        out_specs=anywhere(),
        out_shape=jax.ShapeDtypeStruct(x.shape, x.dtype),
        input_output_aliases={0: 0},
        compiler_params=params(),
        name="held",
    )(x, *after)


def whole_kernel(mine, theirs, ent_out, state_out, token):
    token[...] = jnp.zeros_like(token)
    dim, rows = ent_out.shape
    half = rows // 2
    edge = place()[2]
    for core, part in ((edge, mine), (1 - edge, theirs)):
        at = pl.ds(pl.multiple_of(core * half, half), half)
        ent_out[:, at] = part[:dim]
        state_out[:, at] = part[dim : dim + 1]


def whole_partition(mine, theirs):
    dim, half = mine.shape[0] - 8, mine.shape[1]
    return pl.pallas_call(
        whole_kernel,
        in_specs=[vmem()] * 2,
        out_specs=[vmem()] * 3,
        out_shape=[
            jax.ShapeDtypeStruct((dim, 2 * half), F32),
            jax.ShapeDtypeStruct((1, 2 * half), F32),
            jax.ShapeDtypeStruct((8, 128), F32),
        ],
        compiler_params=params(),
        name="whole_partition",
    )(mine, theirs)


def first_column(owner, core, w):
    return pl.multiple_of((2 * owner + core) * w, w)


def pieces_kernel(t, nz, same, ids_ref, drel_ref, acc_ref, *refs):
    mine, other = refs[-nz - 1 : -1], refs[-1]
    w = other.shape[2]
    z, x, edge = place()
    drel = drel_ref[...]
    for k in range(nz):
        owner = 2 * lax.bitwise_xor(z, k) + (x if same else 1 - x)
        at = [first_column(owner, core, w) for core in (edge, 1 - edge)]
        hot = jnp.concatenate([one_hot(ids_ref, t, w, lambda i, lo=lo: i - lo) for lo in at], axis=0)
        part = mm(drel, hot, NT)
        mine[k][...] = acc_ref[:, pl.ds(at[0], w)] + part[:, :w]
        other[k] = (acc_ref[:, pl.ds(at[1], w)] + part[:, w:]).astype(BF)


def pieces(t, n, same, rel_ids, drel, acc, after):
    dim, rels = acc.shape
    w = rels // (2 * n)
    sds = jax.ShapeDtypeStruct
    out = pl.pallas_call(
        functools.partial(pieces_kernel, t, n // 2, same),
        in_specs=[vmem()] * 3 + [anywhere()] * len(after),
        out_specs=[vmem()] * (n // 2 + 1),
        out_shape=[sds((dim, w), F32)] * (n // 2) + [sds((n // 2, dim, w), BF)],
        compiler_params=params(),
        cost_estimate=cost(dim * rels * drel.shape[1], 4 * dim * rels),
        name="pieces",
    )(rel_ids, drel, acc, *after)
    return out[:-1], out[-1]


def add_kernel(n, *refs):
    for k in range(n):
        refs[n + 1 + k][...] = (refs[k][...] + refs[n][k].astype(F32)).astype(BF)


def add_each(mine, theirs):
    n = len(mine)
    return pl.pallas_call(
        functools.partial(add_kernel, n),
        in_specs=[vmem()] * (n + 1),
        out_specs=[vmem()] * n,
        out_shape=[jax.ShapeDtypeStruct(x.shape, BF) for x in mine],
        compiler_params=params(),
        name="add_each",
    )(*mine, theirs)


def sum_kernel(k, count, mine, theirs, *refs):
    total = mine[...] + theirs[k].astype(F32)
    for r in refs[:count]:
        total = total + r[...].astype(F32)
    refs[-1][...] = total.astype(BF)


def sum_piece(k, mine, theirs, parts, after):
    return pl.pallas_call(
        functools.partial(sum_kernel, k, len(parts)),
        in_specs=[vmem()] * (2 + len(parts)) + [anywhere()] * len(after),
        out_specs=vmem(),
        out_shape=jax.ShapeDtypeStruct(mine.shape, BF),
        compiler_params=params(),
        name="sum_piece",
    )(mine, theirs, *parts, *after)


def stacked_kernel(*refs):
    for i in range(refs[-1].shape[0]):
        refs[-1][i] = refs[i][...]


def stacked(parts, after):
    return pl.pallas_call(
        stacked_kernel,
        in_specs=[vmem()] * len(parts) + [anywhere()] * len(after),
        out_specs=vmem(),
        out_shape=jax.ShapeDtypeStruct((len(parts), *parts[0].shape), parts[0].dtype),
        compiler_params=params(),
        name="stacked",
    )(*parts, *after)


def relnew_kernel(nz, same, ks, rel_ref, state_ref, *refs):
    mine, theirs = refs[: len(ks)], refs[len(ks)]
    rel_out, state_out, buf, sems = refs[-4:]
    w = mine[0].shape[1]
    state_out[...] = refs[len(ks) + (1 if same else 2)][...]
    z, x, edge = place()
    copies = []
    for i in range(2 * len(ks)):
        owner = 2 * lax.bitwise_xor(z, ks[i // 2]) + (x if same else 1 - x)
        at = pl.ds(first_column(owner, edge if i % 2 == 0 else 1 - edge, w), w)
        grad = (mine[i // 2][...] if i % 2 == 0 else theirs[i // 2]).astype(F32)
        state = state_ref[:, at] + jnp.sum(grad * grad, axis=0, keepdims=True) / grad.shape[0]
        state_out[:, at] = state
        buf[i] = rel_ref[:, at] - grad * (learn_rate / jnp.sqrt(state))
        copy = pltpu.make_async_copy(buf.at[i], rel_out.at[:, at], sems.at[i])
        copy.start()
        copies.append(copy)
    for copy in copies:
        copy.wait()


def relnew(nz, same, ks, relations, state, mine, theirs, before, after):
    dim, rels = relations.shape
    w = mine[0].shape[1]
    count = 2 * len(ks)
    start = [state] if before is None else list(before)
    return pl.pallas_call(
        functools.partial(relnew_kernel, nz, same, ks),
        in_specs=[vmem()] * (3 + len(ks))
        + ([anywhere()] if before else [])
        + [vmem()]
        + [anywhere()] * len(after),
        out_specs=[anywhere(), vmem()],
        out_shape=[jax.ShapeDtypeStruct((dim, rels), F32), jax.ShapeDtypeStruct((1, rels), F32)],
        input_output_aliases={3 + len(ks): 0} if before else {},
        scratch_shapes=[pltpu.VMEM((count, dim, w), F32), pltpu.SemaphoreType.DMA((count,))],
        compiler_params=params(),
        cost_estimate=cost(4 * dim * w * count, 4 * dim * w * count),
        name="relnew",
    )(relations, state, *mine, theirs, *start, *after)


def relation_update(t, rel_ids, drel, acc, relations, state, send, finish):
    n = lax.axis_size("dom")
    dim, rels = relations.shape
    if n < 4 or n & (n - 1) or rels % (256 * n):
        total = lax.psum(relsum(t, rel_ids, drel, acc, rels), ("dom", "edge"))
        state = state + jnp.mean(total * total, axis=0)
        return relations - learn_rate * total / jnp.sqrt(state)[None, :], state, finish(send(drel), [])
    nz = n // 2
    mine_x, other_x = pieces(t, n, False, rel_ids, drel, acc, [])
    mine_s, other_s = pieces(t, n, True, rel_ids, drel, acc, [other_x])
    to_x = add_each(mine_x, across(other_x))
    theirs = across(other_s)
    down = range(nz - 1, -1, -1)
    from_x = {k: swapped(to_x[k], 1) for k in down}
    grads = send(other_x)
    turned = {
        k: sum_piece(k, mine_s[k], theirs, [from_x[k]], grads[1:2] if k == nz - 1 else [])
        for k in down[:-1]
    }
    from_z = [swapped(turned[k], 2 * k) for k in down[:-1]]
    done = finish(grads, [turned[nz - 1]])
    summed = sum_piece(0, mine_s[0], theirs, [from_x[0]] + from_z, [])
    got = [summed if k == 0 else swapped(summed, 2 * k) for k in range(nz)]
    got_x = [swapped(piece, 1) for piece in got]
    state = state.reshape(1, rels)
    ks = [0, *down[:-1]]
    mine = [got[k] for k in ks]
    new = relnew(nz, True, ks, relations, state, mine, across(stacked(mine, [done[2]])), None, [])
    mine = [got_x[k] for k in ks]
    theirs = across(stacked(mine, []))
    rel_new, state_new = relnew(nz, False, ks, relations, state, mine, theirs, new, [])
    return rel_new, state_new.reshape(rels), done


def on_device(
    entities,
    entity_state,
    relations,
    relation_state,
    src_rows,
    rel_ids,
    dst_rows,
    counts,
    neg_blocks,
):
    rounds = src_rows.shape[0]
    rels = relations.shape[1]
    shape = src_rows.shape
    cnt, neg = counts.T, neg_blocks.T
    g_mine, g_other, drel, rel16, ent, state = first_round(
        cnt, neg, src_rows, dst_rows, rel_ids, entities, entity_state.reshape(1, -1), relations
    )
    acc = relsum(0, rel_ids, drel, None, rels)
    ent, state, low = update(ent, state, [g_mine, across(g_other)], [])
    rel = relvec(1, rel_ids, rel16)
    for t in range(1, rounds):
        far = shifted(low, -t)
        own = (low, across(low))
        query, query_t, source, s_hot, d_hot, d_hot_t = source_side(t, src_rows, dst_rows, own, rel)
        far = held(far, [query, acc])
        far = (far, across(far))
        if t == rounds - 1:
            break
        gd_mine, gd_other, target, weight, gpos = target_grad(
            t, shape, cnt, neg, far, query, query_t, d_hot, d_hot_t
        )
        gd = sum_pair(gd_mine, across(gd_other))
        gs_mine, gs_other, drel = source_grad(
            t, shape, cnt, neg, gd, target, weight, gpos, source, rel, s_hot
        )
        acc = relsum(t, rel_ids, drel, acc, rels)
        rel = relvec(t + 1, rel_ids, rel16)
        grads = [sum_pair(gs_mine, shifted(gd, t), F32), across(gs_other)]
        ent, state, low = update(ent, state, grads, [rel])
    drel, dsource, weight, gpos = last_terms(
        t, shape, cnt, neg, far, query, query_t, d_hot, source, rel
    )

    def send(after):
        gs_mine, gs_other, gd_mine, gd_other = both_grads(
            t, shape, cnt, neg, after, dsource, s_hot, query, gpos, weight, d_hot_t
        )
        gd = sum_pair(gd_mine, across(gd_other))
        return gs_mine, across(gs_other), shifted(gd, t)

    def finish(grads, after):
        (mine,) = update(ent, state, grads, after, last=True)
        return whole_partition(mine, across(mine))

    rel_new, rel_state, done = relation_update(
        t, rel_ids, drel, acc, relations, relation_state, send, finish
    )
    return (done[0], done[1].reshape(-1), rel_new, rel_state)


def solution(mesh):
    return jax.shard_map(
        on_device,
        mesh=mesh,
        in_specs=(
            P(None, ("groups", "dom")),
            P(("groups", "dom")),
            P(None, "groups"),
            P("groups"),
            P(None, ("groups", "dom", "edge"), None),
            P(None, ("groups", "dom", "edge"), None),
            P(None, ("groups", "dom", "edge"), None),
            P(None, ("groups", "dom", "edge")),
            P(None, ("groups", "dom", "edge")),
        ),
        out_specs=(
            P(None, ("groups", "dom")),
            P(("groups", "dom")),
            P(None, "groups"),
            P("groups"),
        ),
        check_vma=False,
    )
```

```python
import functools

import jax
import jax.numpy as jnp
from jax import lax
from jax.experimental import pallas as pl
from jax.experimental.pallas import tpu as pltpu
from jax.sharding import PartitionSpec as P

learn_rate = 0.1
BF = jnp.bfloat16
F32 = jnp.float32
VMEM_LIMIT = 40 * 1024 * 1024
NN = (((1,), (0,)), ((), ()))
NT = (((1,), (1,)), ((), ()))
TN = (((0,), (0,)), ((), ()))


def mm(a, b, dims=NN):
    return lax.dot_general(a, b, dims, preferred_element_type=F32)


def vmem():
    return pl.BlockSpec(memory_space=pltpu.VMEM)


def smem():
    return pl.BlockSpec(memory_space=pltpu.SMEM)


def anywhere():
    return pl.BlockSpec(memory_space=pl.ANY)


def in_hbm(x):
    return pltpu.with_memory_space_constraint(x, pltpu.HBM)


def cost(flops, size):
    return pl.CostEstimate(flops=flops, bytes_accessed=size, transcendentals=0)


def params():
    return pltpu.CompilerParams(vmem_limit_bytes=VMEM_LIMIT)


def shifted(x, by):
    n = lax.axis_size("dom")
    return lax.ppermute(x, "dom", [(i, (i + by) % n) for i in range(n)])


def swapped(x, bits):
    n = lax.axis_size("dom")
    return lax.ppermute(x, "dom", [(i, i ^ bits) for i in range(n)])


def across(x):
    return lax.ppermute(x, "edge", [(0, 1), (1, 0)])


def one_hot(rows_ref, t, count, base):
    blocks, width = rows_ref.shape[1:]
    at = lax.broadcasted_iota(jnp.int32, (count, width), 0)
    idx = rows_ref[t]
    return jnp.concatenate(
        [
            jnp.where(at == base(idx[b : b + 1, :]), 1.0, 0.0).astype(BF)
            for b in range(blocks)
        ],
        axis=1,
    )


def relvec_kernel(t, ids_ref, rel_ref, out_ref):
    rels = rel_ref.shape[1]
    tile = min(rels, 512)
    out = None
    for lo in range(0, rels, tile):
        hot = one_hot(ids_ref, t, tile, lambda i, lo=lo: i - lo)
        part = mm(rel_ref[:, lo : lo + tile], hot)
        out = part if out is None else out + part
    out_ref[...] = out.astype(BF)


def relvec(t, rel_ids, rel16):
    width, rels = rel16.shape
    slots = rel_ids.shape[1] * rel_ids.shape[2]
    return pl.pallas_call(
        functools.partial(relvec_kernel, t),
        in_specs=[vmem()] * 2,
        out_specs=vmem(),
        out_shape=jax.ShapeDtypeStruct((width, slots), BF),
        compiler_params=params(),
        cost_estimate=cost(width * slots, width * slots),
        name="relvec",
    )(rel_ids, rel16)


def relsum_kernel(t, first, ids_ref, drel_ref, *refs):
    step = pl.program_id(0)
    out_ref = refs[-1]
    tile = out_ref.shape[1]
    hot = one_hot(ids_ref, t, tile, lambda i: i - step * tile)
    part = mm(drel_ref[...], hot, NT)
    out_ref[...] = part if first else refs[0][...] + part


def relsum(t, rel_ids, drel, acc, rels):
    width, slots = drel.shape
    tile = min(rels, 512)
    wide = pl.BlockSpec((width, tile), lambda i: (0, i))
    ins = [rel_ids, drel] + ([] if acc is None else [acc])
    return pl.pallas_call(
        functools.partial(relsum_kernel, t, acc is None),
        grid=(rels // tile,),
        in_specs=[
            pl.BlockSpec(rel_ids.shape, lambda i: (0, 0, 0)),
            pl.BlockSpec((width, slots), lambda i: (0, 0)),
        ]
        + ([] if acc is None else [wide]),
        out_specs=wide,
        out_shape=jax.ShapeDtypeStruct((width, rels), F32),
        input_output_aliases={} if acc is None else {2: 0},
        compiler_params=params(),
        cost_estimate=cost(width * slots, width * slots),
        name="relsum",
    )(*ins)


class Limits:
    scratch = lambda shape: [
        pltpu.SMEM((shape[1], shape[0]), jnp.int32),
        pltpu.SMEM((shape[1], shape[0]), jnp.int32),
        pltpu.SemaphoreType.DMA((2,)),
    ]

    def __init__(self, t, from_cnt, from_neg, cnt, neg, sems):
        self.t, self.cnt, self.neg = t, cnt, neg
        self.copies = [
            pltpu.make_async_copy(from_cnt, cnt, sems.at[0]),
            pltpu.make_async_copy(from_neg, neg, sems.at[1]),
        ]
        for copy in self.copies:
            copy.start()

    def wait(self):
        for copy in self.copies:
            copy.wait()

    def count(self, b):
        return self.cnt[b, self.t]

    def negative(self, b):
        return self.neg[b, self.t]


def place():
    dom = lax.axis_index("dom")
    return dom // 2, lax.rem(dom, 2), lax.axis_index("edge")


def localize(edge, half):
    def local(idx):
        moved = idx + edge * half
        return jnp.where(moved >= 2 * half, moved - 2 * half, moved)

    return local


def halves(x):
    hd = x.shape[0] // 2
    return x[:hd], x[hd:]


def make_query(source, rel):
    (s_re, s_im), (w_re, w_im) = halves(source), halves(rel)
    return jnp.concatenate(
        [s_re * w_re - s_im * w_im, s_re * w_im + s_im * w_re], axis=0
    ).astype(BF)


def conj_times(dq, v):
    (dq_re, dq_im), (v_re, v_im) = halves(dq), halves(v)
    return jnp.concatenate(
        [dq_re * v_re + dq_im * v_im, dq_im * v_re - dq_re * v_im], axis=0
    ).astype(BF)


def target_side(shape, limits, query, query_t, target, o_ref, w_ref):
    _, blocks, width = shape
    lanes = lambda b: pl.ds(pl.multiple_of(b * width, width), width)
    count = limits.count
    o_ref[...] = target.astype(BF)
    pos = jnp.sum(query.astype(F32) * target, axis=0, keepdims=True)
    lane = lax.broadcasted_iota(jnp.int32, (1, width), 1)
    limits.wait()
    row_i = lax.broadcasted_iota(jnp.int32, (width, width), 0)
    col_j = lax.broadcasted_iota(jnp.int32, (width, width), 1)
    for b in range(blocks):
        nb = limits.negative(b)
        neg = o_ref[:, lanes(nb)]
        at = slice(b * width, (b + 1) * width)
        scores = mm(query[:, at], neg, TN) if query_t is None else mm(query_t[at], neg)
        keep = jnp.logical_and(row_i < count(b), col_j < count(nb))
        w_ref[:, at] = jnp.where(keep, jax.nn.sigmoid(scores) / width, 0.0).astype(BF)
    valid = jnp.concatenate(
        [jnp.where(lane < count(b), 1.0, 0.0) for b in range(blocks)], axis=1
    )
    return -jax.nn.sigmoid(-pos) * valid


def target_terms(shape, limits, query, gpos, w_ref, d_ref):
    _, blocks, width = shape
    d_ref[...] = gpos * query.astype(F32)
    for b in range(blocks):
        at = slice(b * width, (b + 1) * width)
        to = pl.ds(pl.multiple_of(limits.negative(b) * width, width), width)
        d_ref[:, to] += mm(query[:, at], w_ref[:, at])
    return d_ref[...].astype(BF)


def make_dquery(shape, limits, gpos, o_ref, w_ref):
    _, blocks, width = shape
    lanes = lambda b: pl.ds(pl.multiple_of(b * width, width), width)
    out = []
    for b in range(blocks):
        nb = limits.negative(b)
        at = slice(b * width, (b + 1) * width)
        own = gpos[:, at] * o_ref[:, at].astype(F32)
        out.append(own + mm(o_ref[:, lanes(nb)], w_ref[:, at], NT))
    return jnp.concatenate(out, axis=1)


def first_kernel(
    shape, cnt_ref, neg_ref, src_ref, dst_ref, ids_ref, ent_ref, state_ref, rel_ref,
    g_mine, g_other, drel_ref, rel16_ref, ent_mine, state_mine,
    cnt, neg, lim_sems, src, dst, ids, ent, state, rel_buf, o_scr, d_scr, w_scr, in_sems, sems,
):
    rels = rel_buf.shape[1]
    tile = min(rels, 512)
    spans = range(0, rels, tile)
    inputs = [
        pltpu.make_async_copy(there, here, in_sems.at[i])
        for i, (there, here) in enumerate(
            [(src_ref.at[:1], src), (dst_ref.at[:1], dst), (ids_ref.at[:1], ids), (ent_ref, ent), (state_ref, state)]
        )
    ]
    loads = [
        pltpu.make_async_copy(
            rel_ref.at[:, lo : lo + tile], rel_buf.at[:, lo : lo + tile], sems.at[i]
        )
        for i, lo in enumerate(spans)
    ]
    for load in inputs:
        load.start()
    limits = Limits(0, cnt_ref, neg_ref, cnt, neg, lim_sems)
    for load in loads:
        load.start()
    half = ent.shape[1] // 2
    _, _, edge = place()
    local = localize(edge, half)
    inputs[0].wait()
    s_hot = one_hot(src, 0, 2 * half, local)
    inputs[1].wait()
    d_hot = one_hot(dst, 0, 2 * half, local)
    inputs[2].wait()
    ids_hot = [one_hot(ids, 0, tile, lambda i, lo=lo: i - lo) for lo in spans]
    inputs[3].wait()
    inputs[4].wait()
    mine = pl.ds(pl.multiple_of(edge * half, half), half)
    ent_mine[...] = ent[:, mine]
    state_mine[...] = state[:, mine]
    table = jnp.concatenate(
        [ent[:, pl.ds(pl.multiple_of(h * half, half), half)].astype(BF) for h in (edge, 1 - edge)],
        axis=1,
    )
    source = mm(table, s_hot)
    target = mm(table, d_hot)
    rel = None
    for load, lo, hot in zip(loads, spans, ids_hot):
        load.wait()
        low = rel_buf[:, lo : lo + tile].astype(BF)
        rel16_ref[:, lo : lo + tile] = low
        part = mm(low, hot)
        rel = part if rel is None else rel + part
    query = make_query(source, rel)
    gpos = target_side(shape, limits, query, None, target, o_scr, w_scr)
    dq = make_dquery(shape, limits, gpos, o_scr, w_scr)
    drel_ref[...] = conj_times(dq, source)
    total = mm(conj_times(dq, rel), s_hot, NT) + mm(
        target_terms(shape, limits, query, gpos, w_scr, d_scr), d_hot, NT
    )
    g_mine[...] = total[:, :half]
    g_other[...] = total[:, half:].astype(BF)


def first_round(cnt, neg, src, dst, rel_ids, entities, state, relations):
    dim, rows = entities.shape
    rels = relations.shape[1]
    _, blocks, width = src.shape
    slots = blocks * width
    sds = jax.ShapeDtypeStruct
    return pl.pallas_call(
        functools.partial(first_kernel, src.shape),
        in_specs=[anywhere()] * 8,
        out_specs=[vmem()] * 6,
        out_shape=[
            sds((dim, rows // 2), F32),
            sds((dim, rows // 2), BF),
            sds((dim, slots), BF),
            sds((dim, rels), BF),
            sds((dim, rows // 2), F32),
            sds((1, rows // 2), F32),
        ],
        scratch_shapes=Limits.scratch(src.shape)
        + [
            pltpu.VMEM((1, blocks, width), jnp.int32),
            pltpu.VMEM((1, blocks, width), jnp.int32),
            pltpu.VMEM((1, blocks, width), jnp.int32),
            pltpu.VMEM((dim, rows), F32),
            pltpu.VMEM((1, rows), F32),
            pltpu.VMEM((dim, rels), F32),
            pltpu.VMEM((dim, slots), BF),
            pltpu.VMEM((dim, slots), F32),
            pltpu.VMEM((width, slots), BF),
            pltpu.SemaphoreType.DMA((5,)),
            pltpu.SemaphoreType.DMA((-(-rels // min(rels, 512)),)),
        ],
        compiler_params=params(),
        cost_estimate=cost(2 * dim * slots * (rels + 4 * rows), 8 * dim * rels),
        name="first_round",
    )(*(in_hbm(x) for x in (cnt, neg, src, dst, rel_ids, entities, state, relations)))


def source_kernel(
    t, src_ref, dst_ref, own0, own1, rel_ref,
    query_ref, query_t_ref, source_ref, s_hot_ref, d_hot_ref, d_hot_t_ref,
):
    half = own0.shape[1]
    local = localize(place()[2], half)
    s_hot = one_hot(src_ref, t, 2 * half, local)
    d_hot = one_hot(dst_ref, t, 2 * half, local)
    s_hot_ref[...] = s_hot
    d_hot_ref[...] = d_hot
    d_hot_t_ref[...] = d_hot.T
    source = mm(jnp.concatenate([own0[...], own1[...]], axis=1), s_hot)
    source_ref[...] = source.astype(BF)
    query = make_query(source, rel_ref[...].astype(F32))
    query_ref[...] = query
    query_t_ref[...] = query.T


def source_side(t, src, dst, own, rel):
    dim, slots = rel.shape
    rows = 2 * own[0].shape[1]
    sds = lambda *shape: jax.ShapeDtypeStruct(shape, BF)
    return pl.pallas_call(
        functools.partial(source_kernel, t),
        in_specs=[vmem()] * 5,
        out_specs=[vmem()] * 6,
        out_shape=[
            sds(dim, slots), sds(slots, dim), sds(dim, slots),
            sds(rows, slots), sds(rows, slots), sds(slots, rows),
        ],
        compiler_params=params(),
        cost_estimate=cost(dim * slots, dim * slots),
        name="source_side",
    )(src, dst, *own, rel)


def target_kernel(
    t, shape, cnt_ref, neg_ref, far0, far1, query_ref, query_t_ref, d_hot_ref, d_hot_t_ref,
    gd_mine, gd_other, o_ref, w_ref, gpos_ref, cnt, neg, sems, d_scr,
):
    limits = Limits(t, cnt_ref, neg_ref, cnt, neg, sems)
    half = far0.shape[1]
    far = jnp.concatenate([far0[...], far1[...]], axis=1)
    target = mm(far, d_hot_ref[...])
    query = query_ref[...]
    gpos = target_side(shape, limits, query, query_t_ref, target, o_ref, w_ref)
    gpos_ref[...] = gpos
    gd = mm(target_terms(shape, limits, query, gpos, w_ref, d_scr), d_hot_t_ref[...])
    gd_mine[...] = gd[:, :half]
    gd_other[...] = gd[:, half:].astype(BF)


def target_grad(t, shape, cnt, neg, far, query, query_t, d_hot, d_hot_t):
    dim, slots = query.shape
    half = far[0].shape[1]
    width = shape[2]
    sds = jax.ShapeDtypeStruct
    return pl.pallas_call(
        functools.partial(target_kernel, t, shape),
        in_specs=[anywhere()] * 2 + [vmem()] * 6,
        out_specs=[vmem()] * 5,
        out_shape=[
            sds((dim, half), F32),
            sds((dim, half), BF),
            sds((dim, slots), BF),
            sds((width, slots), BF),
            sds((1, slots), F32),
        ],
        scratch_shapes=Limits.scratch(shape) + [pltpu.VMEM((dim, slots), F32)],
        compiler_params=params(),
        cost_estimate=cost(4 * dim * slots * (2 * half + width), 12 * dim * slots),
        name="target_grad",
    )(cnt, neg, *far, query, query_t, d_hot, d_hot_t)


def source_grad_kernel(
    t, shape, cnt_ref, neg_ref, _, o_ref, w_ref, gpos_ref, source_ref, rel_ref, s_hot_ref,
    gs_mine, gs_other, drel_ref, cnt, neg, sems,
):
    limits = Limits(t, cnt_ref, neg_ref, cnt, neg, sems)
    limits.wait()
    half = gs_mine.shape[1]
    dq = make_dquery(shape, limits, gpos_ref[...], o_ref, w_ref)
    drel_ref[...] = conj_times(dq, source_ref[...].astype(F32))
    gs = mm(conj_times(dq, rel_ref[...].astype(F32)), s_hot_ref[...], NT)
    gs_mine[...] = gs[:, :half]
    gs_other[...] = gs[:, half:].astype(BF)


def source_grad(t, shape, cnt, neg, after, target, weight, gpos, source, rel, s_hot):
    dim, slots = rel.shape
    half = s_hot.shape[0] // 2
    sds = jax.ShapeDtypeStruct
    return pl.pallas_call(
        functools.partial(source_grad_kernel, t, shape),
        in_specs=[anywhere()] * 3 + [vmem()] * 6,
        out_specs=[vmem()] * 3,
        out_shape=[sds((dim, half), F32), sds((dim, half), BF), sds((dim, slots), BF)],
        scratch_shapes=Limits.scratch(shape),
        compiler_params=params(),
        cost_estimate=cost(dim * slots, dim * slots),
        name="source_grad",
    )(cnt, neg, after, target, weight, gpos, source, rel, s_hot)


def last_kernel(
    t, shape, cnt_ref, neg_ref, far0, far1, query_ref, query_t_ref, d_hot_ref, source_ref, rel_ref,
    drel_ref, dsource_ref, dterm_ref, cnt, neg, sems, o_scr, d_scr, w_scr,
):
    limits = Limits(t, cnt_ref, neg_ref, cnt, neg, sems)
    far = jnp.concatenate([far0[...], far1[...]], axis=1)
    target = mm(far, d_hot_ref[...])
    query = query_ref[...]
    gpos = target_side(shape, limits, query, query_t_ref, target, o_scr, w_scr)
    dterm_ref[...] = target_terms(shape, limits, query, gpos, w_scr, d_scr)
    dq = make_dquery(shape, limits, gpos, o_scr, w_scr)
    drel_ref[...] = conj_times(dq, source_ref[...].astype(F32))
    dsource_ref[...] = conj_times(dq, rel_ref[...].astype(F32))


def last_terms(t, shape, cnt, neg, far, query, query_t, d_hot, source, rel):
    dim, slots = query.shape
    sds = jax.ShapeDtypeStruct
    return pl.pallas_call(
        functools.partial(last_kernel, t, shape),
        in_specs=[anywhere()] * 2 + [vmem()] * 7,
        out_specs=[vmem()] * 3,
        out_shape=[sds((dim, slots), BF)] * 3,
        scratch_shapes=Limits.scratch(shape)
        + [
            pltpu.VMEM((dim, slots), BF),
            pltpu.VMEM((dim, slots), F32),
            pltpu.VMEM((shape[2], slots), BF),
        ],
        compiler_params=params(),
        cost_estimate=cost(6 * dim * slots * shape[2], 12 * dim * slots),
        name="last_terms",
    )(cnt, neg, *far, query, query_t, d_hot, source, rel)


def both_kernel(_, dsource_ref, s_hot_ref, dterm_ref, d_hot_t_ref, gs_mine, gs_other, gd_mine, gd_other):
    half = gs_mine.shape[1]
    for terms, hot, dims, mine, other in (
        (dterm_ref, d_hot_t_ref, NN, gd_mine, gd_other),
        (dsource_ref, s_hot_ref, NT, gs_mine, gs_other),
    ):
        grad = mm(terms[...], hot[...], dims)
        mine[...] = grad[:, :half]
        other[...] = grad[:, half:].astype(BF)


def both_grads(after, dsource, s_hot, dterm, d_hot_t):
    dim, slots = dterm.shape
    half = s_hot.shape[0] // 2
    sds = jax.ShapeDtypeStruct
    return pl.pallas_call(
        both_kernel,
        in_specs=[anywhere()] + [vmem()] * 4,
        out_specs=[vmem()] * 4,
        out_shape=[sds((dim, half), F32), sds((dim, half), BF)] * 2,
        compiler_params=params(),
        cost_estimate=cost(8 * dim * slots * half, 12 * dim * slots),
        name="both_grads",
    )(after, dsource, s_hot, dterm, d_hot_t)


def update_kernel(n_grads, last, *refs):
    ent_ref, state_ref, grads = refs[0], refs[1], refs[2 : 2 + n_grads]
    grad = grads[0][...].astype(F32)
    for g in grads[1:]:
        grad = grad + g[...].astype(F32)
    dim = grad.shape[0]
    state = state_ref[...] + jnp.sum(grad * grad, axis=0, keepdims=True) / dim
    new = ent_ref[...] - grad * (learn_rate / jnp.sqrt(state))
    if last:
        refs[-1][:dim] = new
        refs[-1][dim:] = jnp.broadcast_to(state, (refs[-1].shape[0] - dim, state.shape[1]))
    else:
        refs[-3][...] = new
        refs[-2][...] = state
        refs[-1][...] = new.astype(BF)


def update(ent, state, grads, after, last=False):
    dim, half = ent.shape
    sds = jax.ShapeDtypeStruct
    outs = [sds((dim, half), F32), sds((1, half), F32), sds((dim, half), BF)]
    if last:
        outs = [sds((dim + 8, half), F32)]
    return pl.pallas_call(
        functools.partial(update_kernel, len(grads), last),
        in_specs=[vmem()] * (2 + len(grads)) + [anywhere()] * len(after),
        out_specs=[vmem()] * len(outs),
        out_shape=outs,
        compiler_params=params(),
        cost_estimate=cost(10 * dim * half, 16 * dim * half),
        name="update",
    )(ent, state, *grads, *after)


def pair_kernel(a_ref, b_ref, out_ref):
    out_ref[...] = (a_ref[...] + b_ref[...].astype(F32)).astype(out_ref.dtype)


def sum_pair(a, b, dtype=BF):
    return pl.pallas_call(
        pair_kernel,
        in_specs=[vmem()] * 2,
        out_specs=vmem(),
        out_shape=jax.ShapeDtypeStruct(a.shape, dtype),
        compiler_params=params(),
        name="sum_pair",
    )(a, b)


def held_kernel(x_ref, *refs):
    pass


def held(x, after):
    return pl.pallas_call(
        held_kernel,
        in_specs=[anywhere()] * (1 + len(after)),
        out_specs=anywhere(),
        out_shape=jax.ShapeDtypeStruct(x.shape, x.dtype),
        input_output_aliases={0: 0},
        compiler_params=params(),
        name="held",
    )(x, *after)


def whole_kernel(mine, theirs, ent_out, state_out, token):
    token[...] = jnp.zeros_like(token)
    dim, rows = ent_out.shape
    half = rows // 2
    edge = place()[2]
    for core, part in ((edge, mine), (1 - edge, theirs)):
        at = pl.ds(pl.multiple_of(core * half, half), half)
        ent_out[:, at] = part[:dim]
        state_out[:, at] = part[dim : dim + 1]


def whole_partition(mine, theirs):
    dim, half = mine.shape[0] - 8, mine.shape[1]
    return pl.pallas_call(
        whole_kernel,
        in_specs=[vmem()] * 2,
        out_specs=[vmem()] * 3,
        out_shape=[
            jax.ShapeDtypeStruct((dim, 2 * half), F32),
            jax.ShapeDtypeStruct((1, 2 * half), F32),
            jax.ShapeDtypeStruct((8, 128), F32),
        ],
        compiler_params=params(),
        name="whole_partition",
    )(mine, theirs)


def first_column(owner, core, w):
    return pl.multiple_of((2 * owner + core) * w, w)


def pieces_kernel(t, nz, same, ids_ref, drel_ref, acc_ref, *refs):
    mine, other = refs[-nz - 1 : -1], refs[-1]
    w = other.shape[2]
    z, x, edge = place()
    drel = drel_ref[...]
    for k in range(nz):
        owner = 2 * lax.bitwise_xor(z, k) + (x if same else 1 - x)
        at = [first_column(owner, core, w) for core in (edge, 1 - edge)]
        hot = jnp.concatenate([one_hot(ids_ref, t, w, lambda i, lo=lo: i - lo) for lo in at], axis=0)
        part = mm(drel, hot, NT)
        mine[k][...] = acc_ref[:, pl.ds(at[0], w)] + part[:, :w]
        other[k] = (acc_ref[:, pl.ds(at[1], w)] + part[:, w:]).astype(BF)


def pieces(t, n, same, rel_ids, drel, acc, after):
    dim, rels = acc.shape
    w = rels // (2 * n)
    sds = jax.ShapeDtypeStruct
    out = pl.pallas_call(
        functools.partial(pieces_kernel, t, n // 2, same),
        in_specs=[vmem()] * 3 + [anywhere()] * len(after),
        out_specs=[vmem()] * (n // 2 + 1),
        out_shape=[sds((dim, w), F32)] * (n // 2) + [sds((n // 2, dim, w), BF)],
        compiler_params=params(),
        cost_estimate=cost(dim * rels * drel.shape[1], 4 * dim * rels),
        name="pieces",
    )(rel_ids, drel, acc, *after)
    return out[:-1], out[-1]


def add_kernel(n, *refs):
    for k in range(n):
        refs[n + 1 + k][...] = (refs[k][...] + refs[n][k].astype(F32)).astype(BF)


def add_each(mine, theirs):
    n = len(mine)
    return pl.pallas_call(
        functools.partial(add_kernel, n),
        in_specs=[vmem()] * (n + 1),
        out_specs=[vmem()] * n,
        out_shape=[jax.ShapeDtypeStruct(x.shape, BF) for x in mine],
        compiler_params=params(),
        name="add_each",
    )(*mine, theirs)


def sum_kernel(k, count, mine, theirs, *refs):
    total = mine[...] + theirs[k].astype(F32)
    for r in refs[:count]:
        total = total + r[...].astype(F32)
    refs[-1][...] = total.astype(BF)


def sum_piece(k, mine, theirs, parts, after):
    return pl.pallas_call(
        functools.partial(sum_kernel, k, len(parts)),
        in_specs=[vmem()] * (2 + len(parts)) + [anywhere()] * len(after),
        out_specs=vmem(),
        out_shape=jax.ShapeDtypeStruct(mine.shape, BF),
        compiler_params=params(),
        name="sum_piece",
    )(mine, theirs, *parts, *after)


def stacked_kernel(*refs):
    for i in range(refs[-1].shape[0]):
        refs[-1][i] = refs[i][...]


def stacked(parts, after):
    return pl.pallas_call(
        stacked_kernel,
        in_specs=[vmem()] * len(parts) + [anywhere()] * len(after),
        out_specs=vmem(),
        out_shape=jax.ShapeDtypeStruct((len(parts), *parts[0].shape), parts[0].dtype),
        compiler_params=params(),
        name="stacked",
    )(*parts, *after)


def relnew_kernel(nz, same, ks, rel_ref, state_ref, *refs):
    mine, theirs = refs[: len(ks)], refs[len(ks)]
    rel_out, state_out, buf, sems = refs[-4:]
    w = mine[0].shape[1]
    state_out[...] = refs[len(ks) + (1 if same else 2)][...]
    z, x, edge = place()
    copies = []
    for i in range(2 * len(ks)):
        owner = 2 * lax.bitwise_xor(z, ks[i // 2]) + (x if same else 1 - x)
        at = pl.ds(first_column(owner, edge if i % 2 == 0 else 1 - edge, w), w)
        grad = (mine[i // 2][...] if i % 2 == 0 else theirs[i // 2]).astype(F32)
        state = state_ref[:, at] + jnp.sum(grad * grad, axis=0, keepdims=True) / grad.shape[0]
        state_out[:, at] = state
        buf[i] = rel_ref[:, at] - grad * (learn_rate / jnp.sqrt(state))
        copy = pltpu.make_async_copy(buf.at[i], rel_out.at[:, at], sems.at[i])
        copy.start()
        copies.append(copy)
    for copy in copies:
        copy.wait()


def relnew(nz, same, ks, relations, state, mine, theirs, before, after):
    dim, rels = relations.shape
    w = mine[0].shape[1]
    count = 2 * len(ks)
    start = [state] if before is None else list(before)
    return pl.pallas_call(
        functools.partial(relnew_kernel, nz, same, ks),
        in_specs=[vmem()] * (3 + len(ks))
        + ([anywhere()] if before else [])
        + [vmem()]
        + [anywhere()] * len(after),
        out_specs=[anywhere(), vmem()],
        out_shape=[jax.ShapeDtypeStruct((dim, rels), F32), jax.ShapeDtypeStruct((1, rels), F32)],
        input_output_aliases={3 + len(ks): 0} if before else {},
        scratch_shapes=[pltpu.VMEM((count, dim, w), F32), pltpu.SemaphoreType.DMA((count,))],
        compiler_params=params(),
        cost_estimate=cost(4 * dim * w * count, 4 * dim * w * count),
        name="relnew",
    )(relations, state, *mine, theirs, *start, *after)


def relation_update(t, rel_ids, drel, acc, relations, state, send, finish):
    n = lax.axis_size("dom")
    dim, rels = relations.shape
    if n < 4 or n & (n - 1) or rels % (256 * n):
        total = lax.psum(relsum(t, rel_ids, drel, acc, rels), ("dom", "edge"))
        state = state + jnp.mean(total * total, axis=0)
        return relations - learn_rate * total / jnp.sqrt(state)[None, :], state, finish(send(drel)[0], [])
    nz = n // 2
    mine_x, other_x = pieces(t, n, False, rel_ids, drel, acc, [])
    grads, sent = send(other_x)
    mine_s, other_s = pieces(t, n, True, rel_ids, drel, acc, [sent])
    to_x = add_each(mine_x, across(other_x))
    theirs = across(other_s)
    down = range(nz - 1, -1, -1)
    from_x = {k: swapped(to_x[k], 1) for k in down}
    turned = {
        k: sum_piece(k, mine_s[k], theirs, [from_x[k]], grads[1:] if k == 1 else [])
        for k in down[:-1]
    }
    from_z = [swapped(turned[k], 2 * k) for k in down[:-1]]
    done = finish(grads, [turned[nz - 1]])
    summed = sum_piece(0, mine_s[0], theirs, [from_x[0]] + from_z, [])
    got = [summed if k == 0 else swapped(summed, 2 * k) for k in range(nz)]
    got_x = [swapped(piece, 1) for piece in got]
    state = state.reshape(1, rels)
    ks = [0, *down[:-1]]
    mine = [got[k] for k in ks]
    new = relnew(nz, True, ks, relations, state, mine, across(stacked(mine, [done[2]])), None, [])
    mine = [got_x[k] for k in ks]
    theirs = across(stacked(mine, []))
    rel_new, state_new = relnew(nz, False, ks, relations, state, mine, theirs, new, [])
    return rel_new, state_new.reshape(rels), done


def on_device(
    entities,
    entity_state,
    relations,
    relation_state,
    src_rows,
    rel_ids,
    dst_rows,
    counts,
    neg_blocks,
):
    rounds = src_rows.shape[0]
    rels = relations.shape[1]
    shape = src_rows.shape
    cnt, neg = counts.T, neg_blocks.T
    g_mine, g_other, drel, rel16, ent, state = first_round(
        cnt, neg, src_rows, dst_rows, rel_ids, entities, entity_state.reshape(1, -1), relations
    )
    acc = relsum(0, rel_ids, drel, None, rels)
    ent, state, low = update(ent, state, [g_mine, across(g_other)], [])
    rel = relvec(1, rel_ids, rel16)
    for t in range(1, rounds):
        far = shifted(low, -t)
        own = (low, across(low))
        query, query_t, source, s_hot, d_hot, d_hot_t = source_side(t, src_rows, dst_rows, own, rel)
        far = held(far, [query, acc])
        far = (far, across(far))
        if t == rounds - 1:
            break
        gd_mine, gd_other, target, weight, gpos = target_grad(
            t, shape, cnt, neg, far, query, query_t, d_hot, d_hot_t
        )
        gd = sum_pair(gd_mine, across(gd_other))
        gs_mine, gs_other, drel = source_grad(
            t, shape, cnt, neg, gd, target, weight, gpos, source, rel, s_hot
        )
        acc = relsum(t, rel_ids, drel, acc, rels)
        rel = relvec(t + 1, rel_ids, rel16)
        grads = [sum_pair(gs_mine, shifted(gd, t), F32), across(gs_other)]
        ent, state, low = update(ent, state, grads, [rel])
    drel, dsource, dterm = last_terms(t, shape, cnt, neg, far, query, query_t, d_hot, source, rel)

    def send(after):
        gs_mine, gs_other, gd_mine, gd_other = both_grads(after, dsource, s_hot, dterm, d_hot_t)
        gd = sum_pair(gd_mine, across(gd_other))
        return [gs_mine, across(gs_other), shifted(gd, t)], gd_other

    def finish(grads, after):
        (mine,) = update(ent, state, grads, after, last=True)
        return whole_partition(mine, across(mine))

    rel_new, rel_state, done = relation_update(
        t, rel_ids, drel, acc, relations, relation_state, send, finish
    )
    return (done[0], done[1].reshape(-1), rel_new, rel_state)


def solution(mesh):
    return jax.shard_map(
        on_device,
        mesh=mesh,
        in_specs=(
            P(None, ("groups", "dom")),
            P(("groups", "dom")),
            P(None, "groups"),
            P("groups"),
            P(None, ("groups", "dom", "edge"), None),
            P(None, ("groups", "dom", "edge"), None),
            P(None, ("groups", "dom", "edge"), None),
            P(None, ("groups", "dom", "edge")),
            P(None, ("groups", "dom", "edge")),
        ),
        out_specs=(
            P(None, ("groups", "dom")),
            P(("groups", "dom")),
            P(None, "groups"),
            P("groups"),
        ),
        check_vma=False,
    )
```

```python
import functools

import jax
import jax.numpy as jnp
from jax import lax
from jax.experimental import pallas as pl
from jax.experimental.pallas import tpu as pltpu
from jax.sharding import PartitionSpec as P

learn_rate = 0.1
BF = jnp.bfloat16
F32 = jnp.float32
VMEM_LIMIT = 40 * 1024 * 1024
NN = (((1,), (0,)), ((), ()))
NT = (((1,), (1,)), ((), ()))
TN = (((0,), (0,)), ((), ()))


def mm(a, b, dims=NN):
    return lax.dot_general(a, b, dims, preferred_element_type=F32)


def vmem():
    return pl.BlockSpec(memory_space=pltpu.VMEM)


def smem():
    return pl.BlockSpec(memory_space=pltpu.SMEM)


def anywhere():
    return pl.BlockSpec(memory_space=pl.ANY)


def in_hbm(x):
    return pltpu.with_memory_space_constraint(x, pltpu.HBM)


def cost(flops, size):
    return pl.CostEstimate(flops=flops, bytes_accessed=size, transcendentals=0)


def params():
    return pltpu.CompilerParams(vmem_limit_bytes=VMEM_LIMIT)


def shifted(x, by):
    n = lax.axis_size("dom")
    return lax.ppermute(x, "dom", [(i, (i + by) % n) for i in range(n)])


def swapped(x, bits):
    n = lax.axis_size("dom")
    return lax.ppermute(x, "dom", [(i, i ^ bits) for i in range(n)])


def across(x):
    return lax.ppermute(x, "edge", [(0, 1), (1, 0)])


def one_hot(rows_ref, t, count, base):
    blocks, width = rows_ref.shape[1:]
    at = lax.broadcasted_iota(jnp.int32, (count, width), 0)
    idx = rows_ref[t]
    return jnp.concatenate(
        [
            jnp.where(at == base(idx[b : b + 1, :]), 1.0, 0.0).astype(BF)
            for b in range(blocks)
        ],
        axis=1,
    )


def relvec_kernel(t, ids_ref, rel_ref, out_ref):
    rels = rel_ref.shape[1]
    tile = min(rels, 512)
    out = None
    for lo in range(0, rels, tile):
        hot = one_hot(ids_ref, t, tile, lambda i, lo=lo: i - lo)
        part = mm(rel_ref[:, lo : lo + tile], hot)
        out = part if out is None else out + part
    out_ref[...] = out.astype(BF)


def relvec(t, rel_ids, rel16):
    width, rels = rel16.shape
    slots = rel_ids.shape[1] * rel_ids.shape[2]
    return pl.pallas_call(
        functools.partial(relvec_kernel, t),
        in_specs=[vmem()] * 2,
        out_specs=vmem(),
        out_shape=jax.ShapeDtypeStruct((width, slots), BF),
        compiler_params=params(),
        cost_estimate=cost(width * slots, width * slots),
        name="relvec",
    )(rel_ids, rel16)


def relsum_kernel(t, first, ids_ref, drel_ref, *refs):
    step = pl.program_id(0)
    out_ref = refs[-1]
    tile = out_ref.shape[1]
    hot = one_hot(ids_ref, t, tile, lambda i: i - step * tile)
    part = mm(drel_ref[...], hot, NT)
    out_ref[...] = part if first else refs[0][...] + part


def relsum(t, rel_ids, drel, acc, rels):
    width, slots = drel.shape
    tile = min(rels, 512)
    wide = pl.BlockSpec((width, tile), lambda i: (0, i))
    ins = [rel_ids, drel] + ([] if acc is None else [acc])
    return pl.pallas_call(
        functools.partial(relsum_kernel, t, acc is None),
        grid=(rels // tile,),
        in_specs=[
            pl.BlockSpec(rel_ids.shape, lambda i: (0, 0, 0)),
            pl.BlockSpec((width, slots), lambda i: (0, 0)),
        ]
        + ([] if acc is None else [wide]),
        out_specs=wide,
        out_shape=jax.ShapeDtypeStruct((width, rels), F32),
        input_output_aliases={} if acc is None else {2: 0},
        compiler_params=params(),
        cost_estimate=cost(width * slots, width * slots),
        name="relsum",
    )(*ins)


class Limits:
    scratch = lambda shape: [
        pltpu.SMEM((shape[1], shape[0]), jnp.int32),
        pltpu.SMEM((shape[1], shape[0]), jnp.int32),
        pltpu.SemaphoreType.DMA((2,)),
    ]

    def __init__(self, t, from_cnt, from_neg, cnt, neg, sems):
        self.t, self.cnt, self.neg = t, cnt, neg
        self.copies = [
            pltpu.make_async_copy(from_cnt, cnt, sems.at[0]),
            pltpu.make_async_copy(from_neg, neg, sems.at[1]),
        ]
        for copy in self.copies:
            copy.start()

    def wait(self):
        for copy in self.copies:
            copy.wait()

    def count(self, b):
        return self.cnt[b, self.t]

    def negative(self, b):
        return self.neg[b, self.t]


def place():
    dom = lax.axis_index("dom")
    return dom // 2, lax.rem(dom, 2), lax.axis_index("edge")


def localize(edge, half):
    def local(idx):
        moved = idx + edge * half
        return jnp.where(moved >= 2 * half, moved - 2 * half, moved)

    return local


def halves(x):
    hd = x.shape[0] // 2
    return x[:hd], x[hd:]


def make_query(source, rel):
    (s_re, s_im), (w_re, w_im) = halves(source), halves(rel)
    return jnp.concatenate(
        [s_re * w_re - s_im * w_im, s_re * w_im + s_im * w_re], axis=0
    ).astype(BF)


def conj_times(dq, v):
    (dq_re, dq_im), (v_re, v_im) = halves(dq), halves(v)
    return jnp.concatenate(
        [dq_re * v_re + dq_im * v_im, dq_im * v_re - dq_re * v_im], axis=0
    ).astype(BF)


def target_side(shape, limits, query, query_t, target, o_ref, w_ref):
    _, blocks, width = shape
    lanes = lambda b: pl.ds(pl.multiple_of(b * width, width), width)
    count = limits.count
    o_ref[...] = target.astype(BF)
    pos = jnp.sum(query.astype(F32) * target, axis=0, keepdims=True)
    lane = lax.broadcasted_iota(jnp.int32, (1, width), 1)
    limits.wait()
    row_i = lax.broadcasted_iota(jnp.int32, (width, width), 0)
    col_j = lax.broadcasted_iota(jnp.int32, (width, width), 1)
    for b in range(blocks):
        nb = limits.negative(b)
        neg = o_ref[:, lanes(nb)]
        at = slice(b * width, (b + 1) * width)
        scores = mm(query[:, at], neg, TN) if query_t is None else mm(query_t[at], neg)
        keep = jnp.logical_and(row_i < count(b), col_j < count(nb))
        w_ref[:, at] = jnp.where(keep, jax.nn.sigmoid(scores) / width, 0.0).astype(BF)
    valid = jnp.concatenate(
        [jnp.where(lane < count(b), 1.0, 0.0) for b in range(blocks)], axis=1
    )
    return -jax.nn.sigmoid(-pos) * valid


def target_terms(shape, limits, query, gpos, w_ref, d_ref):
    _, blocks, width = shape
    d_ref[...] = gpos * query.astype(F32)
    for b in range(blocks):
        at = slice(b * width, (b + 1) * width)
        to = pl.ds(pl.multiple_of(limits.negative(b) * width, width), width)
        d_ref[:, to] += mm(query[:, at], w_ref[:, at])
    return d_ref[...].astype(BF)


def make_dquery(shape, limits, gpos, o_ref, w_ref):
    _, blocks, width = shape
    lanes = lambda b: pl.ds(pl.multiple_of(b * width, width), width)
    out = []
    for b in range(blocks):
        nb = limits.negative(b)
        at = slice(b * width, (b + 1) * width)
        own = gpos[:, at] * o_ref[:, at].astype(F32)
        out.append(own + mm(o_ref[:, lanes(nb)], w_ref[:, at], NT))
    return jnp.concatenate(out, axis=1)


def first_kernel(
    shape, cnt_ref, neg_ref, src_ref, dst_ref, ids_ref, ent_ref, state_ref, rel_ref,
    g_mine, g_other, drel_ref, rel16_ref, ent_mine, state_mine,
    cnt, neg, lim_sems, src, dst, ids, ent, state, rel_buf, o_scr, d_scr, w_scr, in_sems, sems,
):
    rels = rel_buf.shape[1]
    tile = min(rels, 512)
    spans = range(0, rels, tile)
    inputs = [
        pltpu.make_async_copy(there, here, in_sems.at[i])
        for i, (there, here) in enumerate(
            [(src_ref.at[:1], src), (dst_ref.at[:1], dst), (ids_ref.at[:1], ids), (ent_ref, ent), (state_ref, state)]
        )
    ]
    loads = [
        pltpu.make_async_copy(
            rel_ref.at[:, lo : lo + tile], rel_buf.at[:, lo : lo + tile], sems.at[i]
        )
        for i, lo in enumerate(spans)
    ]
    for load in inputs:
        load.start()
    limits = Limits(0, cnt_ref, neg_ref, cnt, neg, lim_sems)
    for load in loads:
        load.start()
    half = ent.shape[1] // 2
    _, _, edge = place()
    local = localize(edge, half)
    inputs[0].wait()
    s_hot = one_hot(src, 0, 2 * half, local)
    inputs[1].wait()
    d_hot = one_hot(dst, 0, 2 * half, local)
    inputs[2].wait()
    ids_hot = [one_hot(ids, 0, tile, lambda i, lo=lo: i - lo) for lo in spans]
    inputs[3].wait()
    inputs[4].wait()
    mine = pl.ds(pl.multiple_of(edge * half, half), half)
    ent_mine[...] = ent[:, mine]
    state_mine[...] = state[:, mine]
    table = jnp.concatenate(
        [ent[:, pl.ds(pl.multiple_of(h * half, half), half)].astype(BF) for h in (edge, 1 - edge)],
        axis=1,
    )
    source = mm(table, s_hot)
    target = mm(table, d_hot)
    rel = None
    for load, lo, hot in zip(loads, spans, ids_hot):
        load.wait()
        low = rel_buf[:, lo : lo + tile].astype(BF)
        rel16_ref[:, lo : lo + tile] = low
        part = mm(low, hot)
        rel = part if rel is None else rel + part
    query = make_query(source, rel)
    gpos = target_side(shape, limits, query, None, target, o_scr, w_scr)
    dq = make_dquery(shape, limits, gpos, o_scr, w_scr)
    drel_ref[...] = conj_times(dq, source)
    total = mm(conj_times(dq, rel), s_hot, NT) + mm(
        target_terms(shape, limits, query, gpos, w_scr, d_scr), d_hot, NT
    )
    g_mine[...] = total[:, :half]
    g_other[...] = total[:, half:].astype(BF)


def first_round(cnt, neg, src, dst, rel_ids, entities, state, relations):
    dim, rows = entities.shape
    rels = relations.shape[1]
    _, blocks, width = src.shape
    slots = blocks * width
    sds = jax.ShapeDtypeStruct
    return pl.pallas_call(
        functools.partial(first_kernel, src.shape),
        in_specs=[anywhere()] * 8,
        out_specs=[vmem()] * 6,
        out_shape=[
            sds((dim, rows // 2), F32),
            sds((dim, rows // 2), BF),
            sds((dim, slots), BF),
            sds((dim, rels), BF),
            sds((dim, rows // 2), F32),
            sds((1, rows // 2), F32),
        ],
        scratch_shapes=Limits.scratch(src.shape)
        + [
            pltpu.VMEM((1, blocks, width), jnp.int32),
            pltpu.VMEM((1, blocks, width), jnp.int32),
            pltpu.VMEM((1, blocks, width), jnp.int32),
            pltpu.VMEM((dim, rows), F32),
            pltpu.VMEM((1, rows), F32),
            pltpu.VMEM((dim, rels), F32),
            pltpu.VMEM((dim, slots), BF),
            pltpu.VMEM((dim, slots), F32),
            pltpu.VMEM((width, slots), BF),
            pltpu.SemaphoreType.DMA((5,)),
            pltpu.SemaphoreType.DMA((-(-rels // min(rels, 512)),)),
        ],
        compiler_params=params(),
        cost_estimate=cost(2 * dim * slots * (rels + 4 * rows), 8 * dim * rels),
        name="first_round",
    )(*(in_hbm(x) for x in (cnt, neg, src, dst, rel_ids, entities, state, relations)))


def source_kernel(
    t, src_ref, dst_ref, own0, own1, rel_ref,
    query_ref, query_t_ref, source_ref, s_hot_ref, d_hot_ref, d_hot_t_ref,
):
    half = own0.shape[1]
    local = localize(place()[2], half)
    s_hot = one_hot(src_ref, t, 2 * half, local)
    d_hot = one_hot(dst_ref, t, 2 * half, local)
    s_hot_ref[...] = s_hot
    d_hot_ref[...] = d_hot
    d_hot_t_ref[...] = d_hot.T
    source = mm(jnp.concatenate([own0[...], own1[...]], axis=1), s_hot)
    source_ref[...] = source.astype(BF)
    query = make_query(source, rel_ref[...].astype(F32))
    query_ref[...] = query
    query_t_ref[...] = query.T


def source_side(t, src, dst, own, rel):
    dim, slots = rel.shape
    rows = 2 * own[0].shape[1]
    sds = lambda *shape: jax.ShapeDtypeStruct(shape, BF)
    return pl.pallas_call(
        functools.partial(source_kernel, t),
        in_specs=[vmem()] * 5,
        out_specs=[vmem()] * 6,
        out_shape=[
            sds(dim, slots), sds(slots, dim), sds(dim, slots),
            sds(rows, slots), sds(rows, slots), sds(slots, rows),
        ],
        compiler_params=params(),
        cost_estimate=cost(dim * slots, dim * slots),
        name="source_side",
    )(src, dst, *own, rel)


def target_kernel(
    t, shape, cnt_ref, neg_ref, far0, far1, query_ref, query_t_ref, d_hot_ref, d_hot_t_ref,
    gd_mine, gd_other, o_ref, w_ref, gpos_ref, cnt, neg, sems, d_scr,
):
    limits = Limits(t, cnt_ref, neg_ref, cnt, neg, sems)
    half = far0.shape[1]
    far = jnp.concatenate([far0[...], far1[...]], axis=1)
    target = mm(far, d_hot_ref[...])
    query = query_ref[...]
    gpos = target_side(shape, limits, query, query_t_ref, target, o_ref, w_ref)
    gpos_ref[...] = gpos
    gd = mm(target_terms(shape, limits, query, gpos, w_ref, d_scr), d_hot_t_ref[...])
    gd_mine[...] = gd[:, :half]
    gd_other[...] = gd[:, half:].astype(BF)


def target_grad(t, shape, cnt, neg, far, query, query_t, d_hot, d_hot_t):
    dim, slots = query.shape
    half = far[0].shape[1]
    width = shape[2]
    sds = jax.ShapeDtypeStruct
    return pl.pallas_call(
        functools.partial(target_kernel, t, shape),
        in_specs=[anywhere()] * 2 + [vmem()] * 6,
        out_specs=[vmem()] * 5,
        out_shape=[
            sds((dim, half), F32),
            sds((dim, half), BF),
            sds((dim, slots), BF),
            sds((width, slots), BF),
            sds((1, slots), F32),
        ],
        scratch_shapes=Limits.scratch(shape) + [pltpu.VMEM((dim, slots), F32)],
        compiler_params=params(),
        cost_estimate=cost(4 * dim * slots * (2 * half + width), 12 * dim * slots),
        name="target_grad",
    )(cnt, neg, *far, query, query_t, d_hot, d_hot_t)


def source_grad_kernel(
    t, shape, cnt_ref, neg_ref, _, o_ref, w_ref, gpos_ref, source_ref, rel_ref, s_hot_ref,
    gs_mine, gs_other, drel_ref, cnt, neg, sems,
):
    limits = Limits(t, cnt_ref, neg_ref, cnt, neg, sems)
    limits.wait()
    half = gs_mine.shape[1]
    dq = make_dquery(shape, limits, gpos_ref[...], o_ref, w_ref)
    drel_ref[...] = conj_times(dq, source_ref[...].astype(F32))
    gs = mm(conj_times(dq, rel_ref[...].astype(F32)), s_hot_ref[...], NT)
    gs_mine[...] = gs[:, :half]
    gs_other[...] = gs[:, half:].astype(BF)


def source_grad(t, shape, cnt, neg, after, target, weight, gpos, source, rel, s_hot):
    dim, slots = rel.shape
    half = s_hot.shape[0] // 2
    sds = jax.ShapeDtypeStruct
    return pl.pallas_call(
        functools.partial(source_grad_kernel, t, shape),
        in_specs=[anywhere()] * 3 + [vmem()] * 6,
        out_specs=[vmem()] * 3,
        out_shape=[sds((dim, half), F32), sds((dim, half), BF), sds((dim, slots), BF)],
        scratch_shapes=Limits.scratch(shape),
        compiler_params=params(),
        cost_estimate=cost(dim * slots, dim * slots),
        name="source_grad",
    )(cnt, neg, after, target, weight, gpos, source, rel, s_hot)


def last_kernel(
    t, shape, cnt_ref, neg_ref, far0, far1, query_ref, query_t_ref, d_hot_ref, source_ref, rel_ref,
    drel_ref, dsource_ref, dterm_ref, cnt, neg, sems, o_scr, d_scr, w_scr,
):
    limits = Limits(t, cnt_ref, neg_ref, cnt, neg, sems)
    far = jnp.concatenate([far0[...], far1[...]], axis=1)
    target = mm(far, d_hot_ref[...])
    query = query_ref[...]
    gpos = target_side(shape, limits, query, query_t_ref, target, o_scr, w_scr)
    dterm_ref[...] = target_terms(shape, limits, query, gpos, w_scr, d_scr)
    dq = make_dquery(shape, limits, gpos, o_scr, w_scr)
    drel_ref[...] = conj_times(dq, source_ref[...].astype(F32))
    dsource_ref[...] = conj_times(dq, rel_ref[...].astype(F32))


def last_terms(t, shape, cnt, neg, far, query, query_t, d_hot, source, rel):
    dim, slots = query.shape
    sds = jax.ShapeDtypeStruct
    return pl.pallas_call(
        functools.partial(last_kernel, t, shape),
        in_specs=[anywhere()] * 2 + [vmem()] * 7,
        out_specs=[vmem()] * 3,
        out_shape=[sds((dim, slots), BF)] * 3,
        scratch_shapes=Limits.scratch(shape)
        + [
            pltpu.VMEM((dim, slots), BF),
            pltpu.VMEM((dim, slots), F32),
            pltpu.VMEM((shape[2], slots), BF),
        ],
        compiler_params=params(),
        cost_estimate=cost(6 * dim * slots * shape[2], 12 * dim * slots),
        name="last_terms",
    )(cnt, neg, *far, query, query_t, d_hot, source, rel)


def both_kernel(_, dsource_ref, s_hot_ref, dterm_ref, d_hot_t_ref, gs_mine, gs_other, gd_mine, gd_other):
    half = gs_mine.shape[1]
    for terms, hot, dims, mine, other in (
        (dterm_ref, d_hot_t_ref, NN, gd_mine, gd_other),
        (dsource_ref, s_hot_ref, NT, gs_mine, gs_other),
    ):
        grad = mm(terms[...], hot[...], dims)
        mine[...] = grad[:, :half]
        other[...] = grad[:, half:].astype(BF)


def both_grads(after, dsource, s_hot, dterm, d_hot_t):
    dim, slots = dterm.shape
    half = s_hot.shape[0] // 2
    sds = jax.ShapeDtypeStruct
    return pl.pallas_call(
        both_kernel,
        in_specs=[anywhere()] + [vmem()] * 4,
        out_specs=[vmem()] * 4,
        out_shape=[sds((dim, half), F32), sds((dim, half), BF)] * 2,
        compiler_params=params(),
        cost_estimate=cost(8 * dim * slots * half, 12 * dim * slots),
        name="both_grads",
    )(after, dsource, s_hot, dterm, d_hot_t)


def update_kernel(n_grads, last, *refs):
    ent_ref, state_ref, grads = refs[0], refs[1], refs[2 : 2 + n_grads]
    grad = grads[0][...].astype(F32)
    for g in grads[1:]:
        grad = grad + g[...].astype(F32)
    dim = grad.shape[0]
    state = state_ref[...] + jnp.sum(grad * grad, axis=0, keepdims=True) / dim
    new = ent_ref[...] - grad * (learn_rate / jnp.sqrt(state))
    if last:
        refs[-1][:dim] = new
        refs[-1][dim:] = jnp.broadcast_to(state, (refs[-1].shape[0] - dim, state.shape[1]))
    else:
        refs[-3][...] = new
        refs[-2][...] = state
        refs[-1][...] = new.astype(BF)


def update(ent, state, grads, after, last=False):
    dim, half = ent.shape
    sds = jax.ShapeDtypeStruct
    outs = [sds((dim, half), F32), sds((1, half), F32), sds((dim, half), BF)]
    if last:
        outs = [sds((dim + 8, half), F32)]
    return pl.pallas_call(
        functools.partial(update_kernel, len(grads), last),
        in_specs=[vmem()] * (2 + len(grads)) + [anywhere()] * len(after),
        out_specs=[vmem()] * len(outs),
        out_shape=outs,
        compiler_params=params(),
        cost_estimate=cost(10 * dim * half, 16 * dim * half),
        name="update",
    )(ent, state, *grads, *after)


def pair_kernel(a_ref, b_ref, out_ref):
    out_ref[...] = (a_ref[...] + b_ref[...].astype(F32)).astype(out_ref.dtype)


def sum_pair(a, b, dtype=BF):
    return pl.pallas_call(
        pair_kernel,
        in_specs=[vmem()] * 2,
        out_specs=vmem(),
        out_shape=jax.ShapeDtypeStruct(a.shape, dtype),
        compiler_params=params(),
        name="sum_pair",
    )(a, b)


def held_kernel(x_ref, *refs):
    pass


def held(x, after):
    return pl.pallas_call(
        held_kernel,
        in_specs=[anywhere()] * (1 + len(after)),
        out_specs=anywhere(),
        out_shape=jax.ShapeDtypeStruct(x.shape, x.dtype),
        input_output_aliases={0: 0},
        compiler_params=params(),
        name="held",
    )(x, *after)


def whole_kernel(mine, theirs, ent_out, state_out, token):
    token[...] = jnp.zeros_like(token)
    dim, rows = ent_out.shape
    half = rows // 2
    edge = place()[2]
    for core, part in ((edge, mine), (1 - edge, theirs)):
        at = pl.ds(pl.multiple_of(core * half, half), half)
        ent_out[:, at] = part[:dim]
        state_out[:, at] = part[dim : dim + 1]


def whole_partition(mine, theirs):
    dim, half = mine.shape[0] - 8, mine.shape[1]
    return pl.pallas_call(
        whole_kernel,
        in_specs=[vmem()] * 2,
        out_specs=[vmem()] * 3,
        out_shape=[
            jax.ShapeDtypeStruct((dim, 2 * half), F32),
            jax.ShapeDtypeStruct((1, 2 * half), F32),
            jax.ShapeDtypeStruct((8, 128), F32),
        ],
        compiler_params=params(),
        name="whole_partition",
    )(mine, theirs)


def first_column(owner, core, w):
    return pl.multiple_of((2 * owner + core) * w, w)


def pieces_kernel(t, nz, same, ids_ref, drel_ref, acc_ref, *refs):
    mine, other = refs[-nz - 1 : -1], refs[-1]
    w = other.shape[2]
    z, x, edge = place()
    drel = drel_ref[...]
    for k in range(nz):
        owner = 2 * lax.bitwise_xor(z, k) + (x if same else 1 - x)
        at = [first_column(owner, core, w) for core in (edge, 1 - edge)]
        hot = jnp.concatenate([one_hot(ids_ref, t, w, lambda i, lo=lo: i - lo) for lo in at], axis=0)
        part = mm(drel, hot, NT)
        mine[k][...] = acc_ref[:, pl.ds(at[0], w)] + part[:, :w]
        other[k] = (acc_ref[:, pl.ds(at[1], w)] + part[:, w:]).astype(BF)


def pieces(t, n, same, rel_ids, drel, acc, after):
    dim, rels = acc.shape
    w = rels // (2 * n)
    sds = jax.ShapeDtypeStruct
    out = pl.pallas_call(
        functools.partial(pieces_kernel, t, n // 2, same),
        in_specs=[vmem()] * 3 + [anywhere()] * len(after),
        out_specs=[vmem()] * (n // 2 + 1),
        out_shape=[sds((dim, w), F32)] * (n // 2) + [sds((n // 2, dim, w), BF)],
        compiler_params=params(),
        cost_estimate=cost(dim * rels * drel.shape[1], 4 * dim * rels),
        name="pieces",
    )(rel_ids, drel, acc, *after)
    return out[:-1], out[-1]


def add_kernel(n, *refs):
    for k in range(n):
        refs[n + 1 + k][...] = (refs[k][...] + refs[n][k].astype(F32)).astype(BF)


def add_each(mine, theirs):
    n = len(mine)
    return pl.pallas_call(
        functools.partial(add_kernel, n),
        in_specs=[vmem()] * (n + 1),
        out_specs=[vmem()] * n,
        out_shape=[jax.ShapeDtypeStruct(x.shape, BF) for x in mine],
        compiler_params=params(),
        name="add_each",
    )(*mine, theirs)


def sum_kernel(k, count, mine, theirs, *refs):
    total = mine[...] + theirs[k].astype(F32)
    for r in refs[:count]:
        total = total + r[...].astype(F32)
    refs[-1][...] = total.astype(BF)


def sum_piece(k, mine, theirs, parts, after):
    return pl.pallas_call(
        functools.partial(sum_kernel, k, len(parts)),
        in_specs=[vmem()] * (2 + len(parts)) + [anywhere()] * len(after),
        out_specs=vmem(),
        out_shape=jax.ShapeDtypeStruct(mine.shape, BF),
        compiler_params=params(),
        name="sum_piece",
    )(mine, theirs, *parts, *after)


def stacked_kernel(*refs):
    for i in range(refs[-1].shape[0]):
        refs[-1][i] = refs[i][...]


def stacked(parts, after):
    return pl.pallas_call(
        stacked_kernel,
        in_specs=[vmem()] * len(parts) + [anywhere()] * len(after),
        out_specs=vmem(),
        out_shape=jax.ShapeDtypeStruct((len(parts), *parts[0].shape), parts[0].dtype),
        compiler_params=params(),
        name="stacked",
    )(*parts, *after)


def relnew_kernel(nz, same, ks, rel_ref, state_ref, *refs):
    mine, theirs = refs[: len(ks)], refs[len(ks)]
    rel_out, state_out, buf, sems = refs[-4:]
    w = mine[0].shape[1]
    state_out[...] = refs[len(ks) + (1 if same else 2)][...]
    z, x, edge = place()
    copies = []
    for i in range(2 * len(ks)):
        owner = 2 * lax.bitwise_xor(z, ks[i // 2]) + (x if same else 1 - x)
        at = pl.ds(first_column(owner, edge if i % 2 == 0 else 1 - edge, w), w)
        grad = (mine[i // 2][...] if i % 2 == 0 else theirs[i // 2]).astype(F32)
        state = state_ref[:, at] + jnp.sum(grad * grad, axis=0, keepdims=True) / grad.shape[0]
        state_out[:, at] = state
        buf[i] = rel_ref[:, at] - grad * (learn_rate / jnp.sqrt(state))
        copy = pltpu.make_async_copy(buf.at[i], rel_out.at[:, at], sems.at[i])
        copy.start()
        copies.append(copy)
    for copy in copies:
        copy.wait()


def relnew(nz, same, ks, relations, state, mine, theirs, before, after):
    dim, rels = relations.shape
    w = mine[0].shape[1]
    count = 2 * len(ks)
    start = [state] if before is None else list(before)
    return pl.pallas_call(
        functools.partial(relnew_kernel, nz, same, ks),
        in_specs=[vmem()] * (3 + len(ks))
        + ([anywhere()] if before else [])
        + [vmem()]
        + [anywhere()] * len(after),
        out_specs=[anywhere(), vmem()],
        out_shape=[jax.ShapeDtypeStruct((dim, rels), F32), jax.ShapeDtypeStruct((1, rels), F32)],
        input_output_aliases={3 + len(ks): 0} if before else {},
        scratch_shapes=[pltpu.VMEM((count, dim, w), F32), pltpu.SemaphoreType.DMA((count,))],
        compiler_params=params(),
        cost_estimate=cost(4 * dim * w * count, 4 * dim * w * count),
        name="relnew",
    )(relations, state, *mine, theirs, *start, *after)


def relation_update(t, rel_ids, drel, acc, relations, state, send, finish):
    n = lax.axis_size("dom")
    dim, rels = relations.shape
    if n < 4 or n & (n - 1) or rels % (256 * n):
        total = lax.psum(relsum(t, rel_ids, drel, acc, rels), ("dom", "edge"))
        state = state + jnp.mean(total * total, axis=0)
        return relations - learn_rate * total / jnp.sqrt(state)[None, :], state, finish(send(drel)[0], [])
    nz = n // 2
    mine_x, other_x = pieces(t, n, False, rel_ids, drel, acc, [])
    grads, sent = send(other_x)
    mine_s, other_s = pieces(t, n, True, rel_ids, drel, acc, [sent])
    to_x = add_each(mine_x, across(other_x))
    theirs = across(other_s)
    down = range(nz - 1, -1, -1)
    from_x = {k: swapped(to_x[k], 1) for k in down}
    turned = {
        k: sum_piece(k, mine_s[k], theirs, [from_x[k]], grads[1:] if k == nz - 1 else [])
        for k in down[:-1]
    }
    from_z = [swapped(turned[k], 2 * k) for k in down[:-1]]
    done = finish(grads, [turned[nz - 1]])
    summed = sum_piece(0, mine_s[0], theirs, [from_x[0]] + from_z, [])
    got = [summed if k == 0 else swapped(summed, 2 * k) for k in range(nz)]
    got_x = [swapped(piece, 1) for piece in got]
    state = state.reshape(1, rels)
    ks = [0, *down[:-1]]
    mine = [got[k] for k in ks]
    new = relnew(nz, True, ks, relations, state, mine, across(stacked(mine, [done[2]])), None, [])
    mine = [got_x[k] for k in ks]
    theirs = across(stacked(mine, []))
    rel_new, state_new = relnew(nz, False, ks, relations, state, mine, theirs, new, [])
    return rel_new, state_new.reshape(rels), done


def on_device(
    entities,
    entity_state,
    relations,
    relation_state,
    src_rows,
    rel_ids,
    dst_rows,
    counts,
    neg_blocks,
):
    rounds = src_rows.shape[0]
    rels = relations.shape[1]
    shape = src_rows.shape
    cnt, neg = counts.T, neg_blocks.T
    g_mine, g_other, drel, rel16, ent, state = first_round(
        cnt, neg, src_rows, dst_rows, rel_ids, entities, entity_state.reshape(1, -1), relations
    )
    acc = relsum(0, rel_ids, drel, None, rels)
    ent, state, low = update(ent, state, [g_mine, across(g_other)], [])
    rel = relvec(1, rel_ids, rel16)
    for t in range(1, rounds):
        far = shifted(low, -t)
        own = (low, across(low))
        query, query_t, source, s_hot, d_hot, d_hot_t = source_side(t, src_rows, dst_rows, own, rel)
        far = held(far, [query, acc])
        far = (far, across(far))
        if t == rounds - 1:
            break
        gd_mine, gd_other, target, weight, gpos = target_grad(
            t, shape, cnt, neg, far, query, query_t, d_hot, d_hot_t
        )
        gd = sum_pair(gd_mine, across(gd_other))
        gs_mine, gs_other, drel = source_grad(
            t, shape, cnt, neg, gd, target, weight, gpos, source, rel, s_hot
        )
        acc = relsum(t, rel_ids, drel, acc, rels)
        rel = relvec(t + 1, rel_ids, rel16)
        grads = [sum_pair(gs_mine, shifted(gd, t), F32), across(gs_other)]
        ent, state, low = update(ent, state, grads, [rel])
    drel, dsource, dterm = last_terms(t, shape, cnt, neg, far, query, query_t, d_hot, source, rel)

    def send(after):
        gs_mine, gs_other, gd_mine, gd_other = both_grads(after, dsource, s_hot, dterm, d_hot_t)
        gd = sum_pair(gd_mine, across(gd_other))
        return [gs_mine, across(gs_other), shifted(gd, t)], gd_other

    def finish(grads, after):
        (mine,) = update(ent, state, grads, after, last=True)
        return whole_partition(mine, across(mine))

    rel_new, rel_state, done = relation_update(
        t, rel_ids, drel, acc, relations, relation_state, send, finish
    )
    return (done[0], done[1].reshape(-1), rel_new, rel_state)


def solution(mesh):
    return jax.shard_map(
        on_device,
        mesh=mesh,
        in_specs=(
            P(None, ("groups", "dom")),
            P(("groups", "dom")),
            P(None, "groups"),
            P("groups"),
            P(None, ("groups", "dom", "edge"), None),
            P(None, ("groups", "dom", "edge"), None),
            P(None, ("groups", "dom", "edge"), None),
            P(None, ("groups", "dom", "edge")),
            P(None, ("groups", "dom", "edge")),
        ),
        out_specs=(
            P(None, ("groups", "dom")),
            P(("groups", "dom")),
            P(None, "groups"),
            P("groups"),
        ),
        check_vma=False,
    )
```

```python
import functools

import jax
import jax.numpy as jnp
from jax import lax
from jax.experimental import pallas as pl
from jax.experimental.pallas import tpu as pltpu
from jax.sharding import PartitionSpec as P

learn_rate = 0.1
BF = jnp.bfloat16
F32 = jnp.float32
VMEM_LIMIT = 24 * 1024 * 1024
NN = (((1,), (0,)), ((), ()))
NT = (((1,), (1,)), ((), ()))
TN = (((0,), (0,)), ((), ()))


def mm(a, b, dims=NN):
    return lax.dot_general(a, b, dims, preferred_element_type=F32)


def vmem():
    return pl.BlockSpec(memory_space=pltpu.VMEM)


def smem():
    return pl.BlockSpec(memory_space=pltpu.SMEM)


def anywhere():
    return pl.BlockSpec(memory_space=pl.ANY)


def in_hbm(x):
    return pltpu.with_memory_space_constraint(x, pltpu.HBM)


def cost(flops, size):
    return pl.CostEstimate(flops=flops, bytes_accessed=size, transcendentals=0)


def params():
    return pltpu.CompilerParams(vmem_limit_bytes=VMEM_LIMIT)


def shifted(x, by):
    n = lax.axis_size("dom")
    return lax.ppermute(x, "dom", [(i, (i + by) % n) for i in range(n)])


def swapped(x, bits):
    n = lax.axis_size("dom")
    return lax.ppermute(x, "dom", [(i, i ^ bits) for i in range(n)])


def across(x):
    return lax.ppermute(x, "edge", [(0, 1), (1, 0)])


def one_hot(rows_ref, t, count, base):
    blocks, width = rows_ref.shape[1:]
    at = lax.broadcasted_iota(jnp.int32, (count, width), 0)
    idx = rows_ref[t]
    return jnp.concatenate(
        [
            jnp.where(at == base(idx[b : b + 1, :]), 1.0, 0.0).astype(BF)
            for b in range(blocks)
        ],
        axis=1,
    )


def relvec_kernel(t, ids_ref, rel_ref, out_ref):
    rels = rel_ref.shape[1]
    tile = min(rels, 512)
    out = None
    for lo in range(0, rels, tile):
        hot = one_hot(ids_ref, t, tile, lambda i, lo=lo: i - lo)
        part = mm(rel_ref[:, lo : lo + tile], hot)
        out = part if out is None else out + part
    out_ref[...] = out.astype(BF)


def relvec(t, rel_ids, rel16):
    width, rels = rel16.shape
    slots = rel_ids.shape[1] * rel_ids.shape[2]
    return pl.pallas_call(
        functools.partial(relvec_kernel, t),
        in_specs=[vmem()] * 2,
        out_specs=vmem(),
        out_shape=jax.ShapeDtypeStruct((width, slots), BF),
        compiler_params=params(),
        cost_estimate=cost(width * slots, width * slots),
        name="relvec",
    )(rel_ids, rel16)


def relsum_kernel(t, first, ids_ref, drel_ref, *refs):
    step = pl.program_id(0)
    out_ref = refs[-1]
    tile = out_ref.shape[1]
    hot = one_hot(ids_ref, t, tile, lambda i: i - step * tile)
    part = mm(drel_ref[...], hot, NT)
    out_ref[...] = part if first else refs[0][...] + part


def relsum(t, rel_ids, drel, acc, rels):
    width, slots = drel.shape
    tile = min(rels, 512)
    wide = pl.BlockSpec((width, tile), lambda i: (0, i))
    ins = [rel_ids, drel] + ([] if acc is None else [acc])
    return pl.pallas_call(
        functools.partial(relsum_kernel, t, acc is None),
        grid=(rels // tile,),
        in_specs=[
            pl.BlockSpec(rel_ids.shape, lambda i: (0, 0, 0)),
            pl.BlockSpec((width, slots), lambda i: (0, 0)),
        ]
        + ([] if acc is None else [wide]),
        out_specs=wide,
        out_shape=jax.ShapeDtypeStruct((width, rels), F32),
        input_output_aliases={} if acc is None else {2: 0},
        compiler_params=params(),
        cost_estimate=cost(width * slots, width * slots),
        name="relsum",
    )(*ins)


class Limits:
    scratch = lambda shape: [
        pltpu.SMEM((shape[1], shape[0]), jnp.int32),
        pltpu.SMEM((shape[1], shape[0]), jnp.int32),
        pltpu.SemaphoreType.DMA((2,)),
    ]

    def __init__(self, t, from_cnt, from_neg, cnt, neg, sems):
        self.t, self.cnt, self.neg = t, cnt, neg
        self.copies = [
            pltpu.make_async_copy(from_cnt, cnt, sems.at[0]),
            pltpu.make_async_copy(from_neg, neg, sems.at[1]),
        ]
        for copy in self.copies:
            copy.start()

    def wait(self):
        for copy in self.copies:
            copy.wait()

    def count(self, b):
        return self.cnt[b, self.t]

    def negative(self, b):
        return self.neg[b, self.t]


def place():
    dom = lax.axis_index("dom")
    return dom // 2, lax.rem(dom, 2), lax.axis_index("edge")


def localize(edge, half):
    def local(idx):
        moved = idx + edge * half
        return jnp.where(moved >= 2 * half, moved - 2 * half, moved)

    return local


def halves(x):
    hd = x.shape[0] // 2
    return x[:hd], x[hd:]


def make_query(source, rel):
    (s_re, s_im), (w_re, w_im) = halves(source), halves(rel)
    return jnp.concatenate(
        [s_re * w_re - s_im * w_im, s_re * w_im + s_im * w_re], axis=0
    ).astype(BF)


def conj_times(dq, v):
    (dq_re, dq_im), (v_re, v_im) = halves(dq), halves(v)
    return jnp.concatenate(
        [dq_re * v_re + dq_im * v_im, dq_im * v_re - dq_re * v_im], axis=0
    ).astype(BF)


def positive_factors(shape, limits, query, target):
    _, blocks, width = shape
    pos = jnp.sum(query.astype(F32) * target, axis=0, keepdims=True)
    lane = lax.broadcasted_iota(jnp.int32, (1, width), 1)
    valid = jnp.concatenate(
        [jnp.where(lane < limits.count(b), 1.0, 0.0) for b in range(blocks)], axis=1
    )
    return -jax.nn.sigmoid(-pos) * valid


def target_side(shape, limits, query, query_t, target, o_ref, w_ref):
    _, blocks, width = shape
    lanes = lambda b: pl.ds(pl.multiple_of(b * width, width), width)
    count = limits.count
    o_ref[...] = target.astype(BF)
    limits.wait()
    gpos = positive_factors(shape, limits, query, target)
    row_i = lax.broadcasted_iota(jnp.int32, (width, width), 0)
    col_j = lax.broadcasted_iota(jnp.int32, (width, width), 1)
    for b in range(blocks):
        nb = limits.negative(b)
        neg = o_ref[:, lanes(nb)]
        at = slice(b * width, (b + 1) * width)
        scores = mm(query[:, at], neg, TN) if query_t is None else mm(query_t[at], neg)
        keep = jnp.logical_and(row_i < count(b), col_j < count(nb))
        w_ref[:, at] = jnp.where(keep, jax.nn.sigmoid(scores) / width, 0.0).astype(BF)
    return gpos


def target_terms(shape, limits, query, gpos, w_ref, d_ref):
    _, blocks, width = shape
    d_ref[...] = gpos * query.astype(F32)
    for b in range(blocks):
        at = slice(b * width, (b + 1) * width)
        to = pl.ds(pl.multiple_of(limits.negative(b) * width, width), width)
        d_ref[:, to] += mm(query[:, at], w_ref[:, at])
    return d_ref[...].astype(BF)


def make_dquery(shape, limits, gpos, o_ref, w_ref):
    _, blocks, width = shape
    lanes = lambda b: pl.ds(pl.multiple_of(b * width, width), width)
    out = []
    for b in range(blocks):
        nb = limits.negative(b)
        at = slice(b * width, (b + 1) * width)
        own = gpos[:, at] * o_ref[:, at].astype(F32)
        out.append(own + mm(o_ref[:, lanes(nb)], w_ref[:, at], NT))
    return jnp.concatenate(out, axis=1)


def first_kernel(
    shape, cnt_ref, neg_ref, src_ref, dst_ref, ids_ref, ent_ref, state_ref, rel_ref,
    g_mine, g_other, drel_ref, rel16_ref, ent_mine, state_mine,
    cnt, neg, lim_sems, src, dst, ids, ent, state, rel_buf, o_scr, d_scr, w_scr, in_sems, sems,
):
    rels = rel_buf.shape[1]
    tile = min(rels, 512)
    spans = range(0, rels, tile)
    inputs = [
        pltpu.make_async_copy(there, here, in_sems.at[i])
        for i, (there, here) in enumerate(
            [(src_ref.at[:1], src), (dst_ref.at[:1], dst), (ids_ref.at[:1], ids), (ent_ref, ent), (state_ref, state)]
        )
    ]
    loads = [
        pltpu.make_async_copy(
            rel_ref.at[:, lo : lo + tile], rel_buf.at[:, lo : lo + tile], sems.at[i]
        )
        for i, lo in enumerate(spans)
    ]
    for load in inputs:
        load.start()
    limits = Limits(0, cnt_ref, neg_ref, cnt, neg, lim_sems)
    for load in loads:
        load.start()
    half = ent.shape[1] // 2
    _, _, edge = place()
    local = localize(edge, half)
    inputs[0].wait()
    s_hot = one_hot(src, 0, 2 * half, local)
    inputs[1].wait()
    d_hot = one_hot(dst, 0, 2 * half, local)
    inputs[2].wait()
    ids_hot = [one_hot(ids, 0, tile, lambda i, lo=lo: i - lo) for lo in spans]
    inputs[3].wait()
    inputs[4].wait()
    mine = pl.ds(pl.multiple_of(edge * half, half), half)
    ent_mine[...] = ent[:, mine]
    state_mine[...] = state[:, mine]
    table = jnp.concatenate(
        [ent[:, pl.ds(pl.multiple_of(h * half, half), half)].astype(BF) for h in (edge, 1 - edge)],
        axis=1,
    )
    source = mm(table, s_hot)
    target = mm(table, d_hot)
    rel = None
    for load, lo, hot in zip(loads, spans, ids_hot):
        load.wait()
        low = rel_buf[:, lo : lo + tile].astype(BF)
        rel16_ref[:, lo : lo + tile] = low
        part = mm(low, hot)
        rel = part if rel is None else rel + part
    query = make_query(source, rel)
    gpos = target_side(shape, limits, query, None, target, o_scr, w_scr)
    dq = make_dquery(shape, limits, gpos, o_scr, w_scr)
    drel_ref[...] = conj_times(dq, source)
    total = mm(conj_times(dq, rel), s_hot, NT) + mm(
        target_terms(shape, limits, query, gpos, w_scr, d_scr), d_hot, NT
    )
    g_mine[...] = total[:, :half]
    g_other[...] = total[:, half:].astype(BF)


def first_round(cnt, neg, src, dst, rel_ids, entities, state, relations):
    dim, rows = entities.shape
    rels = relations.shape[1]
    _, blocks, width = src.shape
    slots = blocks * width
    sds = jax.ShapeDtypeStruct
    return pl.pallas_call(
        functools.partial(first_kernel, src.shape),
        in_specs=[anywhere()] * 8,
        out_specs=[vmem()] * 6,
        out_shape=[
            sds((dim, rows // 2), F32),
            sds((dim, rows // 2), BF),
            sds((dim, slots), BF),
            sds((dim, rels), BF),
            sds((dim, rows // 2), F32),
            sds((1, rows // 2), F32),
        ],
        scratch_shapes=Limits.scratch(src.shape)
        + [
            pltpu.VMEM((1, blocks, width), jnp.int32),
            pltpu.VMEM((1, blocks, width), jnp.int32),
            pltpu.VMEM((1, blocks, width), jnp.int32),
            pltpu.VMEM((dim, rows), F32),
            pltpu.VMEM((1, rows), F32),
            pltpu.VMEM((dim, rels), F32),
            pltpu.VMEM((dim, slots), BF),
            pltpu.VMEM((dim, slots), F32),
            pltpu.VMEM((width, slots), BF),
            pltpu.SemaphoreType.DMA((5,)),
            pltpu.SemaphoreType.DMA((-(-rels // min(rels, 512)),)),
        ],
        compiler_params=params(),
        cost_estimate=cost(2 * dim * slots * (rels + 4 * rows), 8 * dim * rels),
        name="first_round",
    )(*(in_hbm(x) for x in (cnt, neg, src, dst, rel_ids, entities, state, relations)))


def source_kernel(
    t, shape, cnt_ref, neg_ref, src_ref, dst_ref, own0, own1, rel_ref,
    query_ref, query_t_ref, source_ref, s_hot_ref, d_hot_ref, d_hot_t_ref,
    n_hot_ref, n_hot_t_ref, mask_ref, valid_ref, cnt, neg, sems,
):
    limits = Limits(t, cnt_ref, neg_ref, cnt, neg, sems)
    _, blocks, width = shape
    half = own0.shape[1]
    local = localize(place()[2], half)
    s_hot = one_hot(src_ref, t, 2 * half, local)
    d_hot = one_hot(dst_ref, t, 2 * half, local)
    s_hot_ref[...] = s_hot
    d_hot_ref[...] = d_hot
    d_hot_t_ref[...] = d_hot.T
    source = mm(jnp.concatenate([own0[...], own1[...]], axis=1), s_hot)
    source_ref[...] = source.astype(BF)
    query = make_query(source, rel_ref[...].astype(F32))
    query_ref[...] = query
    query_t_ref[...] = query.T
    limits.wait()
    row_i = lax.broadcasted_iota(jnp.int32, (width, width), 0)
    col_j = lax.broadcasted_iota(jnp.int32, (width, width), 1)
    slot = lax.broadcasted_iota(jnp.int32, (width, 1), 0)
    for b in range(blocks):
        nb = limits.negative(b)
        at = slice(b * width, (b + 1) * width)
        there = pl.ds(pl.multiple_of(nb * width, width), width)
        n_hot_ref[:, at] = d_hot_ref[:, there]
        n_hot_t_ref[at] = d_hot_t_ref[there, :]
        keep = jnp.logical_and(row_i < limits.count(b), col_j < limits.count(nb))
        mask_ref[:, at] = jnp.where(keep, 1.0 / width, 0.0)
        valid_ref[at] = jnp.where(slot < limits.count(b), 1.0, 0.0)


def source_side(t, shape, cnt, neg, src, dst, own, rel):
    dim, slots = rel.shape
    width = shape[2]
    rows = 2 * own[0].shape[1]
    sds = lambda *shape: jax.ShapeDtypeStruct(shape, BF)
    return pl.pallas_call(
        functools.partial(source_kernel, t, shape),
        in_specs=[anywhere()] * 2 + [vmem()] * 5,
        out_specs=[vmem()] * 10,
        out_shape=[
            sds(dim, slots), sds(slots, dim), sds(dim, slots),
            sds(rows, slots), sds(rows, slots), sds(slots, rows),
            sds(rows, slots), sds(slots, rows),
            jax.ShapeDtypeStruct((width, slots), F32),
            jax.ShapeDtypeStruct((slots, 1), F32),
        ],
        scratch_shapes=Limits.scratch(shape),
        compiler_params=params(),
        cost_estimate=cost(dim * slots, dim * slots),
        name="source_side",
    )(cnt, neg, src, dst, *own, rel)


def near_kernel(query_t_ref, far0, out_ref):
    out_ref[...] = mm(query_t_ref[...], far0[...])


def near_products(query_t, far0):
    slots, half = query_t.shape[0], far0.shape[1]
    return pl.pallas_call(
        near_kernel,
        in_specs=[vmem()] * 2,
        out_specs=vmem(),
        out_shape=jax.ShapeDtypeStruct((slots, half), F32),
        compiler_params=params(),
        cost_estimate=cost(slots * half, slots * half),
        name="near_products",
    )(query_t, far0)


def target_kernel(
    near, far1, query_ref, query_t_ref, d_hot_t_ref, n_hot_ref, n_hot_t_ref, mask_ref, valid_ref,
    gd_mine, gd_other, w_ref,
):
    width, slots = mask_ref.shape
    half = far1.shape[1]
    products = jnp.concatenate([near[...], mm(query_t_ref[...], far1[...])], axis=1)
    high = products.astype(BF)
    low = (products - high.astype(F32)).astype(BF)
    d_hot_t = d_hot_t_ref[...].astype(F32)
    pos = jnp.sum(products * d_hot_t, axis=1, keepdims=True)
    gpos = -jax.nn.sigmoid(-pos) * valid_ref[...]
    factors = []
    for lo in range(0, slots, width):
        at = slice(lo, lo + width)
        n_hot = n_hot_ref[:, at]
        scores = mm(high[at], n_hot) + mm(low[at], n_hot)
        weight = (jax.nn.sigmoid(scores) * mask_ref[:, at]).astype(BF)
        w_ref[:, at] = weight
        factors.append(gpos[at] * d_hot_t[at] + mm(weight, n_hot_t_ref[at]))
    gd = mm(query_ref[...], jnp.concatenate(factors, axis=0).astype(BF))
    gd_mine[...] = gd[:, :half]
    gd_other[...] = gd[:, half:].astype(BF)


def target_grad(near, far1, query, query_t, d_hot_t, n_hot, n_hot_t, mask, valid):
    dim, slots = query.shape
    half = far1.shape[1]
    sds = jax.ShapeDtypeStruct
    return pl.pallas_call(
        target_kernel,
        in_specs=[vmem()] * 9,
        out_specs=[vmem()] * 3,
        out_shape=[sds((dim, half), F32), sds((dim, half), BF), sds(mask.shape, BF)],
        compiler_params=params(),
        cost_estimate=cost(4 * dim * slots * half, 12 * dim * slots),
        name="target_grad",
    )(near, far1, query, query_t, d_hot_t, n_hot, n_hot_t, mask, valid)


def source_grad_kernel(
    t, shape, cnt_ref, neg_ref, _, far0, far1, d_hot_ref, query_ref, w_ref, source_ref, rel_ref, s_hot_ref,
    gs_mine, gs_other, drel_ref, cnt, neg, sems, o_scr,
):
    limits = Limits(t, cnt_ref, neg_ref, cnt, neg, sems)
    half = gs_mine.shape[1]
    target = mm(jnp.concatenate([far0[...], far1[...]], axis=1), d_hot_ref[...])
    o_scr[...] = target.astype(BF)
    limits.wait()
    gpos = positive_factors(shape, limits, query_ref[...], target)
    dq = make_dquery(shape, limits, gpos, o_scr, w_ref)
    drel_ref[...] = conj_times(dq, source_ref[...].astype(F32))
    gs = mm(conj_times(dq, rel_ref[...].astype(F32)), s_hot_ref[...], NT)
    gs_mine[...] = gs[:, :half]
    gs_other[...] = gs[:, half:].astype(BF)


def source_grad(t, shape, cnt, neg, after, far, d_hot, query, weight, source, rel, s_hot):
    dim, slots = rel.shape
    half = s_hot.shape[0] // 2
    sds = jax.ShapeDtypeStruct
    return pl.pallas_call(
        functools.partial(source_grad_kernel, t, shape),
        in_specs=[anywhere()] * 3 + [vmem()] * 8,
        out_specs=[vmem()] * 3,
        out_shape=[sds((dim, half), F32), sds((dim, half), BF), sds((dim, slots), BF)],
        scratch_shapes=Limits.scratch(shape) + [pltpu.VMEM((dim, slots), BF)],
        compiler_params=params(),
        cost_estimate=cost(dim * slots, dim * slots),
        name="source_grad",
    )(cnt, neg, after, *far, d_hot, query, weight, source, rel, s_hot)


def last_kernel(
    t, shape, cnt_ref, neg_ref, far0, far1, query_ref, query_t_ref, d_hot_ref, source_ref, rel_ref,
    drel_ref, dsource_ref, dterm_ref, cnt, neg, sems, o_scr, d_scr, w_scr,
):
    limits = Limits(t, cnt_ref, neg_ref, cnt, neg, sems)
    far = jnp.concatenate([far0[...], far1[...]], axis=1)
    target = mm(far, d_hot_ref[...])
    query = query_ref[...]
    gpos = target_side(shape, limits, query, query_t_ref, target, o_scr, w_scr)
    dterm_ref[...] = target_terms(shape, limits, query, gpos, w_scr, d_scr)
    dq = make_dquery(shape, limits, gpos, o_scr, w_scr)
    drel_ref[...] = conj_times(dq, source_ref[...].astype(F32))
    dsource_ref[...] = conj_times(dq, rel_ref[...].astype(F32))


def last_terms(t, shape, cnt, neg, far, query, query_t, d_hot, source, rel):
    dim, slots = query.shape
    sds = jax.ShapeDtypeStruct
    return pl.pallas_call(
        functools.partial(last_kernel, t, shape),
        in_specs=[anywhere()] * 2 + [vmem()] * 7,
        out_specs=[vmem()] * 3,
        out_shape=[sds((dim, slots), BF)] * 3,
        scratch_shapes=Limits.scratch(shape)
        + [
            pltpu.VMEM((dim, slots), BF),
            pltpu.VMEM((dim, slots), F32),
            pltpu.VMEM((shape[2], slots), BF),
        ],
        compiler_params=params(),
        cost_estimate=cost(6 * dim * slots * shape[2], 12 * dim * slots),
        name="last_terms",
    )(cnt, neg, *far, query, query_t, d_hot, source, rel)


def both_kernel(_, dsource_ref, s_hot_ref, dterm_ref, d_hot_t_ref, gs_mine, gs_other, gd_mine, gd_other):
    half = gs_mine.shape[1]
    for terms, hot, dims, mine, other in (
        (dterm_ref, d_hot_t_ref, NN, gd_mine, gd_other),
        (dsource_ref, s_hot_ref, NT, gs_mine, gs_other),
    ):
        grad = mm(terms[...], hot[...], dims)
        mine[...] = grad[:, :half]
        other[...] = grad[:, half:].astype(BF)


def both_grads(after, dsource, s_hot, dterm, d_hot_t):
    dim, slots = dterm.shape
    half = s_hot.shape[0] // 2
    sds = jax.ShapeDtypeStruct
    return pl.pallas_call(
        both_kernel,
        in_specs=[anywhere()] + [vmem()] * 4,
        out_specs=[vmem()] * 4,
        out_shape=[sds((dim, half), F32), sds((dim, half), BF)] * 2,
        compiler_params=params(),
        cost_estimate=cost(8 * dim * slots * half, 12 * dim * slots),
        name="both_grads",
    )(after, dsource, s_hot, dterm, d_hot_t)


def update_kernel(n_grads, last, *refs):
    ent_ref, state_ref, grads = refs[0], refs[1], refs[2 : 2 + n_grads]
    grad = grads[0][...].astype(F32)
    for g in grads[1:]:
        grad = grad + g[...].astype(F32)
    dim = grad.shape[0]
    state = state_ref[...] + jnp.sum(grad * grad, axis=0, keepdims=True) / dim
    new = ent_ref[...] - grad * (learn_rate / jnp.sqrt(state))
    if last:
        refs[-1][:dim] = new
        refs[-1][dim:] = jnp.broadcast_to(state, (refs[-1].shape[0] - dim, state.shape[1]))
    else:
        refs[-3][...] = new
        refs[-2][...] = state
        refs[-1][...] = new.astype(BF)


def update(ent, state, grads, after, last=False):
    dim, half = ent.shape
    sds = jax.ShapeDtypeStruct
    outs = [sds((dim, half), F32), sds((1, half), F32), sds((dim, half), BF)]
    if last:
        outs = [sds((dim + 8, half), F32)]
    return pl.pallas_call(
        functools.partial(update_kernel, len(grads), last),
        in_specs=[vmem()] * (2 + len(grads)) + [anywhere()] * len(after),
        out_specs=[vmem()] * len(outs),
        out_shape=outs,
        compiler_params=params(),
        cost_estimate=cost(10 * dim * half, 16 * dim * half),
        name="update",
    )(ent, state, *grads, *after)


def pair_kernel(a_ref, b_ref, out_ref):
    out_ref[...] = (a_ref[...] + b_ref[...].astype(F32)).astype(out_ref.dtype)


def sum_pair(a, b, dtype=BF):
    return pl.pallas_call(
        pair_kernel,
        in_specs=[vmem()] * 2,
        out_specs=vmem(),
        out_shape=jax.ShapeDtypeStruct(a.shape, dtype),
        compiler_params=params(),
        name="sum_pair",
    )(a, b)


def held_kernel(x_ref, *refs):
    pass


def held(x, after):
    return pl.pallas_call(
        held_kernel,
        in_specs=[anywhere()] * (1 + len(after)),
        out_specs=anywhere(),
        out_shape=jax.ShapeDtypeStruct(x.shape, x.dtype),
        input_output_aliases={0: 0},
        compiler_params=params(),
        name="held",
    )(x, *after)


def whole_kernel(mine, theirs, ent_out, state_out, token):
    token[...] = jnp.zeros_like(token)
    dim, rows = ent_out.shape
    half = rows // 2
    edge = place()[2]
    for core, part in ((edge, mine), (1 - edge, theirs)):
        at = pl.ds(pl.multiple_of(core * half, half), half)
        ent_out[:, at] = part[:dim]
        state_out[:, at] = part[dim : dim + 1]


def whole_partition(mine, theirs):
    dim, half = mine.shape[0] - 8, mine.shape[1]
    return pl.pallas_call(
        whole_kernel,
        in_specs=[vmem()] * 2,
        out_specs=[vmem()] * 3,
        out_shape=[
            jax.ShapeDtypeStruct((dim, 2 * half), F32),
            jax.ShapeDtypeStruct((1, 2 * half), F32),
            jax.ShapeDtypeStruct((8, 128), F32),
        ],
        compiler_params=params(),
        name="whole_partition",
    )(mine, theirs)


def first_column(owner, core, w):
    return pl.multiple_of((2 * owner + core) * w, w)


def pieces_kernel(t, nz, same, ids_ref, drel_ref, acc_ref, *refs):
    mine, other = refs[-nz - 1 : -1], refs[-1]
    w = other.shape[2]
    z, x, edge = place()
    drel = drel_ref[...]
    for k in range(nz):
        owner = 2 * lax.bitwise_xor(z, k) + (x if same else 1 - x)
        at = [first_column(owner, core, w) for core in (edge, 1 - edge)]
        hot = jnp.concatenate([one_hot(ids_ref, t, w, lambda i, lo=lo: i - lo) for lo in at], axis=0)
        part = mm(drel, hot, NT)
        mine[k][...] = acc_ref[:, pl.ds(at[0], w)] + part[:, :w]
        other[k] = (acc_ref[:, pl.ds(at[1], w)] + part[:, w:]).astype(BF)


def pieces(t, n, same, rel_ids, drel, acc, after):
    dim, rels = acc.shape
    w = rels // (2 * n)
    sds = jax.ShapeDtypeStruct
    out = pl.pallas_call(
        functools.partial(pieces_kernel, t, n // 2, same),
        in_specs=[vmem()] * 3 + [anywhere()] * len(after),
        out_specs=[vmem()] * (n // 2 + 1),
        out_shape=[sds((dim, w), F32)] * (n // 2) + [sds((n // 2, dim, w), BF)],
        compiler_params=params(),
        cost_estimate=cost(dim * rels * drel.shape[1], 4 * dim * rels),
        name="pieces",
    )(rel_ids, drel, acc, *after)
    return out[:-1], out[-1]


def add_kernel(n, *refs):
    for k in range(n):
        refs[n + 1 + k][...] = (refs[k][...] + refs[n][k].astype(F32)).astype(BF)


def add_each(mine, theirs):
    n = len(mine)
    return pl.pallas_call(
        functools.partial(add_kernel, n),
        in_specs=[vmem()] * (n + 1),
        out_specs=[vmem()] * n,
        out_shape=[jax.ShapeDtypeStruct(x.shape, BF) for x in mine],
        compiler_params=params(),
        name="add_each",
    )(*mine, theirs)


def sum_kernel(k, count, mine, theirs, *refs):
    total = mine[...] + theirs[k].astype(F32)
    for r in refs[:count]:
        total = total + r[...].astype(F32)
    refs[-1][...] = total.astype(BF)


def sum_piece(k, mine, theirs, parts, after):
    return pl.pallas_call(
        functools.partial(sum_kernel, k, len(parts)),
        in_specs=[vmem()] * (2 + len(parts)) + [anywhere()] * len(after),
        out_specs=vmem(),
        out_shape=jax.ShapeDtypeStruct(mine.shape, BF),
        compiler_params=params(),
        name="sum_piece",
    )(mine, theirs, *parts, *after)


def stacked_kernel(*refs):
    for i in range(refs[-1].shape[0]):
        refs[-1][i] = refs[i][...]


def stacked(parts, after):
    return pl.pallas_call(
        stacked_kernel,
        in_specs=[vmem()] * len(parts) + [anywhere()] * len(after),
        out_specs=vmem(),
        out_shape=jax.ShapeDtypeStruct((len(parts), *parts[0].shape), parts[0].dtype),
        compiler_params=params(),
        name="stacked",
    )(*parts, *after)


def relnew_kernel(nz, same, ks, rel_ref, state_ref, *refs):
    mine, theirs = refs[: len(ks)], refs[len(ks)]
    rel_out, state_out, buf, sems = refs[-4:]
    w = mine[0].shape[1]
    state_out[...] = refs[len(ks) + (1 if same else 2)][...]
    z, x, edge = place()
    copies = []
    for i in range(2 * len(ks)):
        owner = 2 * lax.bitwise_xor(z, ks[i // 2]) + (x if same else 1 - x)
        at = pl.ds(first_column(owner, edge if i % 2 == 0 else 1 - edge, w), w)
        grad = (mine[i // 2][...] if i % 2 == 0 else theirs[i // 2]).astype(F32)
        state = state_ref[:, at] + jnp.sum(grad * grad, axis=0, keepdims=True) / grad.shape[0]
        state_out[:, at] = state
        buf[i] = rel_ref[:, at] - grad * (learn_rate / jnp.sqrt(state))
        copy = pltpu.make_async_copy(buf.at[i], rel_out.at[:, at], sems.at[i])
        copy.start()
        copies.append(copy)
    for copy in copies:
        copy.wait()


def relnew(nz, same, ks, relations, state, mine, theirs, before, after):
    dim, rels = relations.shape
    w = mine[0].shape[1]
    count = 2 * len(ks)
    start = [state] if before is None else list(before)
    return pl.pallas_call(
        functools.partial(relnew_kernel, nz, same, ks),
        in_specs=[vmem()] * (3 + len(ks))
        + ([anywhere()] if before else [])
        + [vmem()]
        + [anywhere()] * len(after),
        out_specs=[anywhere(), vmem()],
        out_shape=[jax.ShapeDtypeStruct((dim, rels), F32), jax.ShapeDtypeStruct((1, rels), F32)],
        input_output_aliases={3 + len(ks): 0} if before else {},
        scratch_shapes=[pltpu.VMEM((count, dim, w), F32), pltpu.SemaphoreType.DMA((count,))],
        compiler_params=params(),
        cost_estimate=cost(4 * dim * w * count, 4 * dim * w * count),
        name="relnew",
    )(relations, state, *mine, theirs, *start, *after)


def relation_update(t, rel_ids, drel, acc, relations, state, send, finish):
    n = lax.axis_size("dom")
    dim, rels = relations.shape
    if n < 4 or n & (n - 1) or rels % (256 * n):
        total = lax.psum(relsum(t, rel_ids, drel, acc, rels), ("dom", "edge"))
        state = state + jnp.mean(total * total, axis=0)
        return relations - learn_rate * total / jnp.sqrt(state)[None, :], state, finish(send(drel), [])
    nz = n // 2
    mine_x, other_x = pieces(t, n, False, rel_ids, drel, acc, [])
    grads = send(other_x)
    mine_s, other_s = pieces(t, n, True, rel_ids, drel, acc, [other_x])
    to_x = add_each(mine_x, across(other_x))
    theirs = across(other_s)
    down = range(nz - 1, -1, -1)
    from_x = {k: swapped(to_x[k], 1) for k in down}
    turned = {
        k: sum_piece(k, mine_s[k], theirs, [from_x[k]], grads[1:2] if k == nz - 1 else [])
        for k in down[:-1]
    }
    from_z = [swapped(turned[k], 2 * k) for k in down[:-1]]
    done = finish(grads, [turned[nz - 1]])
    summed = sum_piece(0, mine_s[0], theirs, [from_x[0]] + from_z, [])
    got = [summed if k == 0 else swapped(summed, 2 * k) for k in range(nz)]
    got_x = [swapped(piece, 1) for piece in got]
    state = state.reshape(1, rels)
    ks = [0, *down[:-1]]
    mine = [got[k] for k in ks]
    new = relnew(nz, True, ks, relations, state, mine, across(stacked(mine, [done[2]])), None, [])
    mine = [got_x[k] for k in ks]
    theirs = across(stacked(mine, []))
    rel_new, state_new = relnew(nz, False, ks, relations, state, mine, theirs, new, [])
    return rel_new, state_new.reshape(rels), done


def on_device(
    entities,
    entity_state,
    relations,
    relation_state,
    src_rows,
    rel_ids,
    dst_rows,
    counts,
    neg_blocks,
):
    rounds = src_rows.shape[0]
    rels = relations.shape[1]
    shape = src_rows.shape
    cnt, neg = counts.T, neg_blocks.T
    g_mine, g_other, drel, rel16, ent, state = first_round(
        cnt, neg, src_rows, dst_rows, rel_ids, entities, entity_state.reshape(1, -1), relations
    )
    acc = relsum(0, rel_ids, drel, None, rels)
    ent, state, low = update(ent, state, [g_mine, across(g_other)], [])
    rel = relvec(1, rel_ids, rel16)
    for t in range(1, rounds):
        far = shifted(low, -t)
        own = (low, across(low))
        query, query_t, source, s_hot, d_hot, d_hot_t, *negatives = source_side(
            t, shape, cnt, neg, src_rows, dst_rows, own, rel
        )
        far = held(far, [query, acc])
        far = (far, across(far))
        if t == rounds - 1:
            break
        near = near_products(query_t, far[0])
        gd_mine, gd_other, weight = target_grad(near, far[1], query, query_t, d_hot_t, *negatives)
        gd = sum_pair(gd_mine, across(gd_other))
        gs_mine, gs_other, drel = source_grad(
            t, shape, cnt, neg, gd, far, d_hot, query, weight, source, rel, s_hot
        )
        acc = relsum(t, rel_ids, drel, acc, rels)
        rel = relvec(t + 1, rel_ids, rel16)
        grads = [sum_pair(gs_mine, shifted(gd, t), F32), across(gs_other)]
        ent, state, low = update(ent, state, grads, [rel])
    drel, dsource, dterm = last_terms(t, shape, cnt, neg, far, query, query_t, d_hot, source, rel)

    def send(after):
        gs_mine, gs_other, gd_mine, gd_other = both_grads(after, dsource, s_hot, dterm, d_hot_t)
        gd = sum_pair(gd_mine, across(gd_other))
        return [gs_mine, across(gs_other), shifted(gd, t)]

    def finish(grads, after):
        (mine,) = update(ent, state, grads, after, last=True)
        return whole_partition(mine, across(mine))

    rel_new, rel_state, done = relation_update(
        t, rel_ids, drel, acc, relations, relation_state, send, finish
    )
    return (done[0], done[1].reshape(-1), rel_new, rel_state)


def solution(mesh):
    return jax.shard_map(
        on_device,
        mesh=mesh,
        in_specs=(
            P(None, ("groups", "dom")),
            P(("groups", "dom")),
            P(None, "groups"),
            P("groups"),
            P(None, ("groups", "dom", "edge"), None),
            P(None, ("groups", "dom", "edge"), None),
            P(None, ("groups", "dom", "edge"), None),
            P(None, ("groups", "dom", "edge")),
            P(None, ("groups", "dom", "edge")),
        ),
        out_specs=(
            P(None, ("groups", "dom")),
            P(("groups", "dom")),
            P(None, "groups"),
            P("groups"),
        ),
        check_vma=False,
    )
```

```python
import functools

import jax
import jax.numpy as jnp
from jax import lax
from jax.experimental import pallas as pl
from jax.experimental.pallas import tpu as pltpu
from jax.sharding import PartitionSpec as P

learn_rate = 0.1
BF = jnp.bfloat16
F32 = jnp.float32
VMEM_LIMIT = 24 * 1024 * 1024
NN = (((1,), (0,)), ((), ()))
NT = (((1,), (1,)), ((), ()))
TN = (((0,), (0,)), ((), ()))


def mm(a, b, dims=NN):
    return lax.dot_general(a, b, dims, preferred_element_type=F32)


def vmem():
    return pl.BlockSpec(memory_space=pltpu.VMEM)


def smem():
    return pl.BlockSpec(memory_space=pltpu.SMEM)


def anywhere():
    return pl.BlockSpec(memory_space=pl.ANY)


def in_hbm(x):
    return pltpu.with_memory_space_constraint(x, pltpu.HBM)


def cost(flops, size):
    return pl.CostEstimate(flops=flops, bytes_accessed=size, transcendentals=0)


def params():
    return pltpu.CompilerParams(vmem_limit_bytes=VMEM_LIMIT)


def shifted(x, by):
    n = lax.axis_size("dom")
    return lax.ppermute(x, "dom", [(i, (i + by) % n) for i in range(n)])


def swapped(x, bits):
    n = lax.axis_size("dom")
    return lax.ppermute(x, "dom", [(i, i ^ bits) for i in range(n)])


def across(x):
    return lax.ppermute(x, "edge", [(0, 1), (1, 0)])


def one_hot(rows_ref, t, count, base):
    blocks, width = rows_ref.shape[1:]
    at = lax.broadcasted_iota(jnp.int32, (count, width), 0)
    idx = rows_ref[t]
    return jnp.concatenate(
        [
            jnp.where(at == base(idx[b : b + 1, :]), 1.0, 0.0).astype(BF)
            for b in range(blocks)
        ],
        axis=1,
    )


def relvec_kernel(t, ids_ref, rel_ref, out_ref):
    rels = rel_ref.shape[1]
    tile = min(rels, 512)
    out = None
    for lo in range(0, rels, tile):
        hot = one_hot(ids_ref, t, tile, lambda i, lo=lo: i - lo)
        part = mm(rel_ref[:, lo : lo + tile], hot)
        out = part if out is None else out + part
    out_ref[...] = out.astype(BF)


def relvec(t, rel_ids, rel16):
    width, rels = rel16.shape
    slots = rel_ids.shape[1] * rel_ids.shape[2]
    return pl.pallas_call(
        functools.partial(relvec_kernel, t),
        in_specs=[vmem()] * 2,
        out_specs=vmem(),
        out_shape=jax.ShapeDtypeStruct((width, slots), BF),
        compiler_params=params(),
        cost_estimate=cost(width * slots, width * slots),
        name="relvec",
    )(rel_ids, rel16)


def relsum_kernel(t, first, ids_ref, drel_ref, *refs):
    step = pl.program_id(0)
    out_ref = refs[-1]
    tile = out_ref.shape[1]
    hot = one_hot(ids_ref, t, tile, lambda i: i - step * tile)
    part = mm(drel_ref[...], hot, NT)
    out_ref[...] = part if first else refs[0][...] + part


def relsum(t, rel_ids, drel, acc, rels):
    width, slots = drel.shape
    tile = min(rels, 512)
    wide = pl.BlockSpec((width, tile), lambda i: (0, i))
    ins = [rel_ids, drel] + ([] if acc is None else [acc])
    return pl.pallas_call(
        functools.partial(relsum_kernel, t, acc is None),
        grid=(rels // tile,),
        in_specs=[
            pl.BlockSpec(rel_ids.shape, lambda i: (0, 0, 0)),
            pl.BlockSpec((width, slots), lambda i: (0, 0)),
        ]
        + ([] if acc is None else [wide]),
        out_specs=wide,
        out_shape=jax.ShapeDtypeStruct((width, rels), F32),
        input_output_aliases={} if acc is None else {2: 0},
        compiler_params=params(),
        cost_estimate=cost(width * slots, width * slots),
        name="relsum",
    )(*ins)


class Limits:
    scratch = lambda shape: [
        pltpu.SMEM((shape[1], shape[0]), jnp.int32),
        pltpu.SMEM((shape[1], shape[0]), jnp.int32),
        pltpu.SemaphoreType.DMA((2,)),
    ]

    def __init__(self, t, from_cnt, from_neg, cnt, neg, sems):
        self.t, self.cnt, self.neg = t, cnt, neg
        self.copies = [
            pltpu.make_async_copy(from_cnt, cnt, sems.at[0]),
            pltpu.make_async_copy(from_neg, neg, sems.at[1]),
        ]
        for copy in self.copies:
            copy.start()

    def wait(self):
        for copy in self.copies:
            copy.wait()

    def count(self, b):
        return self.cnt[b, self.t]

    def negative(self, b):
        return self.neg[b, self.t]


def place():
    dom = lax.axis_index("dom")
    return dom // 2, lax.rem(dom, 2), lax.axis_index("edge")


def localize(edge, half):
    def local(idx):
        moved = idx + edge * half
        return jnp.where(moved >= 2 * half, moved - 2 * half, moved)

    return local


def halves(x):
    hd = x.shape[0] // 2
    return x[:hd], x[hd:]


def make_query(source, rel):
    (s_re, s_im), (w_re, w_im) = halves(source), halves(rel)
    return jnp.concatenate(
        [s_re * w_re - s_im * w_im, s_re * w_im + s_im * w_re], axis=0
    ).astype(BF)


def conj_times(dq, v):
    (dq_re, dq_im), (v_re, v_im) = halves(dq), halves(v)
    return jnp.concatenate(
        [dq_re * v_re + dq_im * v_im, dq_im * v_re - dq_re * v_im], axis=0
    ).astype(BF)


def positive_factors(shape, limits, query, target):
    _, blocks, width = shape
    pos = jnp.sum(query.astype(F32) * target, axis=0, keepdims=True)
    lane = lax.broadcasted_iota(jnp.int32, (1, width), 1)
    valid = jnp.concatenate(
        [jnp.where(lane < limits.count(b), 1.0, 0.0) for b in range(blocks)], axis=1
    )
    return -jax.nn.sigmoid(-pos) * valid


def target_side(shape, limits, query, query_t, target, o_ref, w_ref):
    _, blocks, width = shape
    lanes = lambda b: pl.ds(pl.multiple_of(b * width, width), width)
    count = limits.count
    o_ref[...] = target.astype(BF)
    limits.wait()
    gpos = positive_factors(shape, limits, query, target)
    row_i = lax.broadcasted_iota(jnp.int32, (width, width), 0)
    col_j = lax.broadcasted_iota(jnp.int32, (width, width), 1)
    for b in range(blocks):
        nb = limits.negative(b)
        neg = o_ref[:, lanes(nb)]
        at = slice(b * width, (b + 1) * width)
        scores = mm(query[:, at], neg, TN) if query_t is None else mm(query_t[at], neg)
        keep = jnp.logical_and(row_i < count(b), col_j < count(nb))
        w_ref[:, at] = jnp.where(keep, jax.nn.sigmoid(scores) / width, 0.0).astype(BF)
    return gpos


def target_terms(shape, limits, query, gpos, w_ref, d_ref):
    _, blocks, width = shape
    d_ref[...] = gpos * query.astype(F32)
    for b in range(blocks):
        at = slice(b * width, (b + 1) * width)
        to = pl.ds(pl.multiple_of(limits.negative(b) * width, width), width)
        d_ref[:, to] += mm(query[:, at], w_ref[:, at])
    return d_ref[...].astype(BF)


def make_dquery(shape, limits, gpos, o_ref, w_ref):
    _, blocks, width = shape
    lanes = lambda b: pl.ds(pl.multiple_of(b * width, width), width)
    out = []
    for b in range(blocks):
        nb = limits.negative(b)
        at = slice(b * width, (b + 1) * width)
        own = gpos[:, at] * o_ref[:, at].astype(F32)
        out.append(own + mm(o_ref[:, lanes(nb)], w_ref[:, at], NT))
    return jnp.concatenate(out, axis=1)


def first_kernel(
    shape, cnt_ref, neg_ref, src_ref, dst_ref, ids_ref, ent_ref, state_ref, rel_ref,
    g_mine, g_other, drel_ref, rel16_ref, ent_mine, state_mine,
    cnt, neg, lim_sems, src, dst, ids, ent, state, rel_buf, o_scr, d_scr, w_scr, in_sems, sems,
):
    rels = rel_buf.shape[1]
    tile = min(rels, 512)
    spans = range(0, rels, tile)
    inputs = [
        pltpu.make_async_copy(there, here, in_sems.at[i])
        for i, (there, here) in enumerate(
            [(src_ref.at[:1], src), (dst_ref.at[:1], dst), (ids_ref.at[:1], ids), (ent_ref, ent), (state_ref, state)]
        )
    ]
    loads = [
        pltpu.make_async_copy(
            rel_ref.at[:, lo : lo + tile], rel_buf.at[:, lo : lo + tile], sems.at[i]
        )
        for i, lo in enumerate(spans)
    ]
    for load in inputs:
        load.start()
    limits = Limits(0, cnt_ref, neg_ref, cnt, neg, lim_sems)
    for load in loads:
        load.start()
    half = ent.shape[1] // 2
    _, _, edge = place()
    local = localize(edge, half)
    inputs[0].wait()
    s_hot = one_hot(src, 0, 2 * half, local)
    inputs[1].wait()
    d_hot = one_hot(dst, 0, 2 * half, local)
    inputs[2].wait()
    ids_hot = [one_hot(ids, 0, tile, lambda i, lo=lo: i - lo) for lo in spans]
    inputs[3].wait()
    inputs[4].wait()
    mine = pl.ds(pl.multiple_of(edge * half, half), half)
    ent_mine[...] = ent[:, mine]
    state_mine[...] = state[:, mine]
    table = jnp.concatenate(
        [ent[:, pl.ds(pl.multiple_of(h * half, half), half)].astype(BF) for h in (edge, 1 - edge)],
        axis=1,
    )
    source = mm(table, s_hot)
    target = mm(table, d_hot)
    rel = None
    for load, lo, hot in zip(loads, spans, ids_hot):
        load.wait()
        low = rel_buf[:, lo : lo + tile].astype(BF)
        rel16_ref[:, lo : lo + tile] = low
        part = mm(low, hot)
        rel = part if rel is None else rel + part
    query = make_query(source, rel)
    gpos = target_side(shape, limits, query, None, target, o_scr, w_scr)
    dq = make_dquery(shape, limits, gpos, o_scr, w_scr)
    drel_ref[...] = conj_times(dq, source)
    total = mm(conj_times(dq, rel), s_hot, NT) + mm(
        target_terms(shape, limits, query, gpos, w_scr, d_scr), d_hot, NT
    )
    g_mine[...] = total[:, :half]
    g_other[...] = total[:, half:].astype(BF)


def first_round(cnt, neg, src, dst, rel_ids, entities, state, relations):
    dim, rows = entities.shape
    rels = relations.shape[1]
    _, blocks, width = src.shape
    slots = blocks * width
    sds = jax.ShapeDtypeStruct
    return pl.pallas_call(
        functools.partial(first_kernel, src.shape),
        in_specs=[anywhere()] * 8,
        out_specs=[vmem()] * 6,
        out_shape=[
            sds((dim, rows // 2), F32),
            sds((dim, rows // 2), BF),
            sds((dim, slots), BF),
            sds((dim, rels), BF),
            sds((dim, rows // 2), F32),
            sds((1, rows // 2), F32),
        ],
        scratch_shapes=Limits.scratch(src.shape)
        + [
            pltpu.VMEM((1, blocks, width), jnp.int32),
            pltpu.VMEM((1, blocks, width), jnp.int32),
            pltpu.VMEM((1, blocks, width), jnp.int32),
            pltpu.VMEM((dim, rows), F32),
            pltpu.VMEM((1, rows), F32),
            pltpu.VMEM((dim, rels), F32),
            pltpu.VMEM((dim, slots), BF),
            pltpu.VMEM((dim, slots), F32),
            pltpu.VMEM((width, slots), BF),
            pltpu.SemaphoreType.DMA((5,)),
            pltpu.SemaphoreType.DMA((-(-rels // min(rels, 512)),)),
        ],
        compiler_params=params(),
        cost_estimate=cost(2 * dim * slots * (rels + 4 * rows), 8 * dim * rels),
        name="first_round",
    )(*(in_hbm(x) for x in (cnt, neg, src, dst, rel_ids, entities, state, relations)))


def source_kernel(
    t, shape, cnt_ref, neg_ref, src_ref, dst_ref, own0, own1, rel_ref,
    query_ref, query_t_ref, source_ref, s_hot_ref, d_hot_ref, d_hot_t_ref,
    v_hot_t_ref, n_hot_ref, n_hot_t_ref, mask_ref, cnt, neg, sems,
):
    limits = Limits(t, cnt_ref, neg_ref, cnt, neg, sems)
    _, blocks, width = shape
    half = own0.shape[1]
    local = localize(place()[2], half)
    s_hot = one_hot(src_ref, t, 2 * half, local)
    d_hot = one_hot(dst_ref, t, 2 * half, local)
    s_hot_ref[...] = s_hot
    d_hot_ref[...] = d_hot
    d_hot_t_ref[...] = d_hot.T
    source = mm(jnp.concatenate([own0[...], own1[...]], axis=1), s_hot)
    source_ref[...] = source.astype(BF)
    query = make_query(source, rel_ref[...].astype(F32))
    query_ref[...] = query
    query_t_ref[...] = query.T
    limits.wait()
    row_i = lax.broadcasted_iota(jnp.int32, (width, width), 0)
    col_j = lax.broadcasted_iota(jnp.int32, (width, width), 1)
    slot = lax.broadcasted_iota(jnp.int32, (width, 2 * half), 0)
    for b in range(blocks):
        nb = limits.negative(b)
        at = slice(b * width, (b + 1) * width)
        there = pl.ds(pl.multiple_of(nb * width, width), width)
        n_hot_ref[:, at] = d_hot_ref[:, there]
        n_hot_t_ref[at] = d_hot_t_ref[there, :]
        keep = jnp.logical_and(row_i < limits.count(b), col_j < limits.count(nb))
        mask_ref[:, at] = jnp.where(keep, 1.0 / width, 0.0)
        hot = d_hot_t_ref[at].astype(F32)
        v_hot_t_ref[at] = jnp.where(slot < limits.count(b), hot, 0.0).astype(BF)


def source_side(t, shape, cnt, neg, src, dst, own, rel):
    dim, slots = rel.shape
    width = shape[2]
    rows = 2 * own[0].shape[1]
    sds = lambda *shape: jax.ShapeDtypeStruct(shape, BF)
    return pl.pallas_call(
        functools.partial(source_kernel, t, shape),
        in_specs=[anywhere()] * 2 + [vmem()] * 5,
        out_specs=[vmem()] * 10,
        out_shape=[
            sds(dim, slots), sds(slots, dim), sds(dim, slots),
            sds(rows, slots), sds(rows, slots), sds(slots, rows),
            sds(slots, rows), sds(rows, slots), sds(slots, rows),
            jax.ShapeDtypeStruct((width, slots), F32),
        ],
        scratch_shapes=Limits.scratch(shape),
        compiler_params=params(),
        cost_estimate=cost(dim * slots, dim * slots),
        name="source_side",
    )(cnt, neg, src, dst, *own, rel)


def near_kernel(query_t_ref, far0, out_ref):
    out_ref[...] = mm(query_t_ref[...], far0[...])


def near_products(query_t, far0):
    slots, half = query_t.shape[0], far0.shape[1]
    return pl.pallas_call(
        near_kernel,
        in_specs=[vmem()] * 2,
        out_specs=vmem(),
        out_shape=jax.ShapeDtypeStruct((slots, half), F32),
        compiler_params=params(),
        cost_estimate=cost(slots * half, slots * half),
        name="near_products",
    )(query_t, far0)


def target_kernel(
    near, far1, query_ref, query_t_ref, v_hot_t_ref, n_hot_ref, n_hot_t_ref, mask_ref,
    gd_mine, gd_other, w_ref,
):
    width, slots = mask_ref.shape
    half = far1.shape[1]
    products = jnp.concatenate([near[...], mm(query_t_ref[...], far1[...])], axis=1)
    high = products.astype(BF)
    low = (products - high.astype(F32)).astype(BF)
    factors = []
    for lo in range(0, slots, width):
        at = slice(lo, lo + width)
        n_hot = n_hot_ref[:, at]
        scores = mm(high[at], n_hot) + mm(low[at], n_hot)
        weight = (jax.nn.sigmoid(scores) * mask_ref[:, at]).astype(BF)
        w_ref[:, at] = weight
        positive = jax.nn.sigmoid(-products[at]) * v_hot_t_ref[at].astype(F32)
        factors.append((mm(weight, n_hot_t_ref[at]) - positive).astype(BF))
    gd = mm(query_ref[...], jnp.concatenate(factors, axis=0))
    gd_mine[...] = gd[:, :half]
    gd_other[...] = gd[:, half:].astype(BF)


def target_grad(near, far1, query, query_t, v_hot_t, n_hot, n_hot_t, mask):
    dim, slots = query.shape
    half = far1.shape[1]
    sds = jax.ShapeDtypeStruct
    return pl.pallas_call(
        target_kernel,
        in_specs=[vmem()] * 8,
        out_specs=[vmem()] * 3,
        out_shape=[sds((dim, half), F32), sds((dim, half), BF), sds(mask.shape, BF)],
        compiler_params=params(),
        cost_estimate=cost(4 * dim * slots * half, 12 * dim * slots),
        name="target_grad",
    )(near, far1, query, query_t, v_hot_t, n_hot, n_hot_t, mask)


def source_grad_kernel(
    t, shape, cnt_ref, neg_ref, _, far0, far1, d_hot_ref, query_ref, w_ref, source_ref, rel_ref, s_hot_ref,
    gs_mine, gs_other, drel_ref, cnt, neg, sems, o_scr,
):
    limits = Limits(t, cnt_ref, neg_ref, cnt, neg, sems)
    half = gs_mine.shape[1]
    target = mm(jnp.concatenate([far0[...], far1[...]], axis=1), d_hot_ref[...])
    o_scr[...] = target.astype(BF)
    limits.wait()
    gpos = positive_factors(shape, limits, query_ref[...], target)
    dq = make_dquery(shape, limits, gpos, o_scr, w_ref)
    drel_ref[...] = conj_times(dq, source_ref[...].astype(F32))
    gs = mm(conj_times(dq, rel_ref[...].astype(F32)), s_hot_ref[...], NT)
    gs_mine[...] = gs[:, :half]
    gs_other[...] = gs[:, half:].astype(BF)


def source_grad(t, shape, cnt, neg, after, far, d_hot, query, weight, source, rel, s_hot):
    dim, slots = rel.shape
    half = s_hot.shape[0] // 2
    sds = jax.ShapeDtypeStruct
    return pl.pallas_call(
        functools.partial(source_grad_kernel, t, shape),
        in_specs=[anywhere()] * 3 + [vmem()] * 8,
        out_specs=[vmem()] * 3,
        out_shape=[sds((dim, half), F32), sds((dim, half), BF), sds((dim, slots), BF)],
        scratch_shapes=Limits.scratch(shape) + [pltpu.VMEM((dim, slots), BF)],
        compiler_params=params(),
        cost_estimate=cost(dim * slots, dim * slots),
        name="source_grad",
    )(cnt, neg, after, *far, d_hot, query, weight, source, rel, s_hot)


def last_kernel(
    t, shape, cnt_ref, neg_ref, far0, far1, query_ref, query_t_ref, d_hot_ref, source_ref, rel_ref,
    drel_ref, dsource_ref, dterm_ref, cnt, neg, sems, o_scr, d_scr, w_scr,
):
    limits = Limits(t, cnt_ref, neg_ref, cnt, neg, sems)
    far = jnp.concatenate([far0[...], far1[...]], axis=1)
    target = mm(far, d_hot_ref[...])
    query = query_ref[...]
    gpos = target_side(shape, limits, query, query_t_ref, target, o_scr, w_scr)
    dterm_ref[...] = target_terms(shape, limits, query, gpos, w_scr, d_scr)
    dq = make_dquery(shape, limits, gpos, o_scr, w_scr)
    drel_ref[...] = conj_times(dq, source_ref[...].astype(F32))
    dsource_ref[...] = conj_times(dq, rel_ref[...].astype(F32))


def last_terms(t, shape, cnt, neg, far, query, query_t, d_hot, source, rel):
    dim, slots = query.shape
    sds = jax.ShapeDtypeStruct
    return pl.pallas_call(
        functools.partial(last_kernel, t, shape),
        in_specs=[anywhere()] * 2 + [vmem()] * 7,
        out_specs=[vmem()] * 3,
        out_shape=[sds((dim, slots), BF)] * 3,
        scratch_shapes=Limits.scratch(shape)
        + [
            pltpu.VMEM((dim, slots), BF),
            pltpu.VMEM((dim, slots), F32),
            pltpu.VMEM((shape[2], slots), BF),
        ],
        compiler_params=params(),
        cost_estimate=cost(6 * dim * slots * shape[2], 12 * dim * slots),
        name="last_terms",
    )(cnt, neg, *far, query, query_t, d_hot, source, rel)


def both_kernel(_, dsource_ref, s_hot_ref, dterm_ref, d_hot_t_ref, gs_mine, gs_other, gd_mine, gd_other):
    half = gs_mine.shape[1]
    for terms, hot, dims, mine, other in (
        (dterm_ref, d_hot_t_ref, NN, gd_mine, gd_other),
        (dsource_ref, s_hot_ref, NT, gs_mine, gs_other),
    ):
        grad = mm(terms[...], hot[...], dims)
        mine[...] = grad[:, :half]
        other[...] = grad[:, half:].astype(BF)


def both_grads(after, dsource, s_hot, dterm, d_hot_t):
    dim, slots = dterm.shape
    half = s_hot.shape[0] // 2
    sds = jax.ShapeDtypeStruct
    return pl.pallas_call(
        both_kernel,
        in_specs=[anywhere()] + [vmem()] * 4,
        out_specs=[vmem()] * 4,
        out_shape=[sds((dim, half), F32), sds((dim, half), BF)] * 2,
        compiler_params=params(),
        cost_estimate=cost(8 * dim * slots * half, 12 * dim * slots),
        name="both_grads",
    )(after, dsource, s_hot, dterm, d_hot_t)


def update_kernel(n_grads, last, *refs):
    ent_ref, state_ref, grads = refs[0], refs[1], refs[2 : 2 + n_grads]
    grad = grads[0][...].astype(F32)
    for g in grads[1:]:
        grad = grad + g[...].astype(F32)
    dim = grad.shape[0]
    state = state_ref[...] + jnp.sum(grad * grad, axis=0, keepdims=True) / dim
    new = ent_ref[...] - grad * (learn_rate / jnp.sqrt(state))
    if last:
        refs[-1][:dim] = new
        refs[-1][dim:] = jnp.broadcast_to(state, (refs[-1].shape[0] - dim, state.shape[1]))
    else:
        refs[-3][...] = new
        refs[-2][...] = state
        refs[-1][...] = new.astype(BF)


def update(ent, state, grads, after, last=False):
    dim, half = ent.shape
    sds = jax.ShapeDtypeStruct
    outs = [sds((dim, half), F32), sds((1, half), F32), sds((dim, half), BF)]
    if last:
        outs = [sds((dim + 8, half), F32)]
    return pl.pallas_call(
        functools.partial(update_kernel, len(grads), last),
        in_specs=[vmem()] * (2 + len(grads)) + [anywhere()] * len(after),
        out_specs=[vmem()] * len(outs),
        out_shape=outs,
        compiler_params=params(),
        cost_estimate=cost(10 * dim * half, 16 * dim * half),
        name="update",
    )(ent, state, *grads, *after)


def pair_kernel(a_ref, b_ref, out_ref):
    out_ref[...] = (a_ref[...] + b_ref[...].astype(F32)).astype(out_ref.dtype)


def sum_pair(a, b, dtype=BF):
    return pl.pallas_call(
        pair_kernel,
        in_specs=[vmem()] * 2,
        out_specs=vmem(),
        out_shape=jax.ShapeDtypeStruct(a.shape, dtype),
        compiler_params=params(),
        name="sum_pair",
    )(a, b)


def held_kernel(x_ref, *refs):
    pass


def held(x, after):
    return pl.pallas_call(
        held_kernel,
        in_specs=[anywhere()] * (1 + len(after)),
        out_specs=anywhere(),
        out_shape=jax.ShapeDtypeStruct(x.shape, x.dtype),
        input_output_aliases={0: 0},
        compiler_params=params(),
        name="held",
    )(x, *after)


def whole_kernel(mine, theirs, ent_out, state_out, token):
    token[...] = jnp.zeros_like(token)
    dim, rows = ent_out.shape
    half = rows // 2
    edge = place()[2]
    for core, part in ((edge, mine), (1 - edge, theirs)):
        at = pl.ds(pl.multiple_of(core * half, half), half)
        ent_out[:, at] = part[:dim]
        state_out[:, at] = part[dim : dim + 1]


def whole_partition(mine, theirs):
    dim, half = mine.shape[0] - 8, mine.shape[1]
    return pl.pallas_call(
        whole_kernel,
        in_specs=[vmem()] * 2,
        out_specs=[vmem()] * 3,
        out_shape=[
            jax.ShapeDtypeStruct((dim, 2 * half), F32),
            jax.ShapeDtypeStruct((1, 2 * half), F32),
            jax.ShapeDtypeStruct((8, 128), F32),
        ],
        compiler_params=params(),
        name="whole_partition",
    )(mine, theirs)


def first_column(owner, core, w):
    return pl.multiple_of((2 * owner + core) * w, w)


def pieces_kernel(t, nz, same, ids_ref, drel_ref, acc_ref, *refs):
    mine, other = refs[-nz - 1 : -1], refs[-1]
    w = other.shape[2]
    z, x, edge = place()
    drel = drel_ref[...]
    for k in range(nz):
        owner = 2 * lax.bitwise_xor(z, k) + (x if same else 1 - x)
        at = [first_column(owner, core, w) for core in (edge, 1 - edge)]
        hot = jnp.concatenate([one_hot(ids_ref, t, w, lambda i, lo=lo: i - lo) for lo in at], axis=0)
        part = mm(drel, hot, NT)
        mine[k][...] = acc_ref[:, pl.ds(at[0], w)] + part[:, :w]
        other[k] = (acc_ref[:, pl.ds(at[1], w)] + part[:, w:]).astype(BF)


def pieces(t, n, same, rel_ids, drel, acc, after):
    dim, rels = acc.shape
    w = rels // (2 * n)
    sds = jax.ShapeDtypeStruct
    out = pl.pallas_call(
        functools.partial(pieces_kernel, t, n // 2, same),
        in_specs=[vmem()] * 3 + [anywhere()] * len(after),
        out_specs=[vmem()] * (n // 2 + 1),
        out_shape=[sds((dim, w), F32)] * (n // 2) + [sds((n // 2, dim, w), BF)],
        compiler_params=params(),
        cost_estimate=cost(dim * rels * drel.shape[1], 4 * dim * rels),
        name="pieces",
    )(rel_ids, drel, acc, *after)
    return out[:-1], out[-1]


def add_kernel(n, *refs):
    for k in range(n):
        refs[n + 1 + k][...] = (refs[k][...] + refs[n][k].astype(F32)).astype(BF)


def add_each(mine, theirs):
    n = len(mine)
    return pl.pallas_call(
        functools.partial(add_kernel, n),
        in_specs=[vmem()] * (n + 1),
        out_specs=[vmem()] * n,
        out_shape=[jax.ShapeDtypeStruct(x.shape, BF) for x in mine],
        compiler_params=params(),
        name="add_each",
    )(*mine, theirs)


def sum_kernel(k, count, mine, theirs, *refs):
    total = mine[...] + theirs[k].astype(F32)
    for r in refs[:count]:
        total = total + r[...].astype(F32)
    refs[-1][...] = total.astype(BF)


def sum_piece(k, mine, theirs, parts, after):
    return pl.pallas_call(
        functools.partial(sum_kernel, k, len(parts)),
        in_specs=[vmem()] * (2 + len(parts)) + [anywhere()] * len(after),
        out_specs=vmem(),
        out_shape=jax.ShapeDtypeStruct(mine.shape, BF),
        compiler_params=params(),
        name="sum_piece",
    )(mine, theirs, *parts, *after)


def stacked_kernel(*refs):
    for i in range(refs[-1].shape[0]):
        refs[-1][i] = refs[i][...]


def stacked(parts, after):
    return pl.pallas_call(
        stacked_kernel,
        in_specs=[vmem()] * len(parts) + [anywhere()] * len(after),
        out_specs=vmem(),
        out_shape=jax.ShapeDtypeStruct((len(parts), *parts[0].shape), parts[0].dtype),
        compiler_params=params(),
        name="stacked",
    )(*parts, *after)


def relnew_kernel(nz, same, ks, rel_ref, state_ref, *refs):
    mine, theirs = refs[: len(ks)], refs[len(ks)]
    rel_out, state_out, buf, sems = refs[-4:]
    w = mine[0].shape[1]
    state_out[...] = refs[len(ks) + (1 if same else 2)][...]
    z, x, edge = place()
    copies = []
    for i in range(2 * len(ks)):
        owner = 2 * lax.bitwise_xor(z, ks[i // 2]) + (x if same else 1 - x)
        at = pl.ds(first_column(owner, edge if i % 2 == 0 else 1 - edge, w), w)
        grad = (mine[i // 2][...] if i % 2 == 0 else theirs[i // 2]).astype(F32)
        state = state_ref[:, at] + jnp.sum(grad * grad, axis=0, keepdims=True) / grad.shape[0]
        state_out[:, at] = state
        buf[i] = rel_ref[:, at] - grad * (learn_rate / jnp.sqrt(state))
        copy = pltpu.make_async_copy(buf.at[i], rel_out.at[:, at], sems.at[i])
        copy.start()
        copies.append(copy)
    for copy in copies:
        copy.wait()


def relnew(nz, same, ks, relations, state, mine, theirs, before, after):
    dim, rels = relations.shape
    w = mine[0].shape[1]
    count = 2 * len(ks)
    start = [state] if before is None else list(before)
    return pl.pallas_call(
        functools.partial(relnew_kernel, nz, same, ks),
        in_specs=[vmem()] * (3 + len(ks))
        + ([anywhere()] if before else [])
        + [vmem()]
        + [anywhere()] * len(after),
        out_specs=[anywhere(), vmem()],
        out_shape=[jax.ShapeDtypeStruct((dim, rels), F32), jax.ShapeDtypeStruct((1, rels), F32)],
        input_output_aliases={3 + len(ks): 0} if before else {},
        scratch_shapes=[pltpu.VMEM((count, dim, w), F32), pltpu.SemaphoreType.DMA((count,))],
        compiler_params=params(),
        cost_estimate=cost(4 * dim * w * count, 4 * dim * w * count),
        name="relnew",
    )(relations, state, *mine, theirs, *start, *after)


def relation_update(t, rel_ids, drel, acc, relations, state, send, finish):
    n = lax.axis_size("dom")
    dim, rels = relations.shape
    if n < 4 or n & (n - 1) or rels % (256 * n):
        total = lax.psum(relsum(t, rel_ids, drel, acc, rels), ("dom", "edge"))
        state = state + jnp.mean(total * total, axis=0)
        return relations - learn_rate * total / jnp.sqrt(state)[None, :], state, finish(send(drel), [])
    nz = n // 2
    mine_x, other_x = pieces(t, n, False, rel_ids, drel, acc, [])
    grads = send(other_x)
    mine_s, other_s = pieces(t, n, True, rel_ids, drel, acc, [other_x])
    to_x = add_each(mine_x, across(other_x))
    theirs = across(other_s)
    down = range(nz - 1, -1, -1)
    from_x = {k: swapped(to_x[k], 1) for k in down}
    turned = {
        k: sum_piece(k, mine_s[k], theirs, [from_x[k]], grads[1:2] if k == nz - 1 else [])
        for k in down[:-1]
    }
    from_z = [swapped(turned[k], 2 * k) for k in down[:-1]]
    done = finish(grads, [turned[nz - 1]])
    summed = sum_piece(0, mine_s[0], theirs, [from_x[0]] + from_z, [])
    got = [summed if k == 0 else swapped(summed, 2 * k) for k in range(nz)]
    got_x = [swapped(piece, 1) for piece in got]
    state = state.reshape(1, rels)
    ks = [0, *down[:-1]]
    mine = [got[k] for k in ks]
    new = relnew(nz, True, ks, relations, state, mine, across(stacked(mine, [done[2]])), None, [])
    mine = [got_x[k] for k in ks]
    theirs = across(stacked(mine, []))
    rel_new, state_new = relnew(nz, False, ks, relations, state, mine, theirs, new, [])
    return rel_new, state_new.reshape(rels), done


def on_device(
    entities,
    entity_state,
    relations,
    relation_state,
    src_rows,
    rel_ids,
    dst_rows,
    counts,
    neg_blocks,
):
    rounds = src_rows.shape[0]
    rels = relations.shape[1]
    shape = src_rows.shape
    cnt, neg = counts.T, neg_blocks.T
    g_mine, g_other, drel, rel16, ent, state = first_round(
        cnt, neg, src_rows, dst_rows, rel_ids, entities, entity_state.reshape(1, -1), relations
    )
    acc = relsum(0, rel_ids, drel, None, rels)
    ent, state, low = update(ent, state, [g_mine, across(g_other)], [])
    rel = relvec(1, rel_ids, rel16)
    for t in range(1, rounds):
        far = shifted(low, -t)
        own = (low, across(low))
        query, query_t, source, s_hot, d_hot, d_hot_t, *negatives = source_side(
            t, shape, cnt, neg, src_rows, dst_rows, own, rel
        )
        far = held(far, [query, acc])
        far = (far, across(far))
        if t == rounds - 1:
            break
        near = near_products(query_t, far[0])
        gd_mine, gd_other, weight = target_grad(near, far[1], query, query_t, *negatives)
        gd = sum_pair(gd_mine, across(gd_other))
        gs_mine, gs_other, drel = source_grad(
            t, shape, cnt, neg, gd, far, d_hot, query, weight, source, rel, s_hot
        )
        acc = relsum(t, rel_ids, drel, acc, rels)
        rel = relvec(t + 1, rel_ids, rel16)
        grads = [sum_pair(gs_mine, shifted(gd, t), F32), across(gs_other)]
        ent, state, low = update(ent, state, grads, [rel])
    drel, dsource, dterm = last_terms(t, shape, cnt, neg, far, query, query_t, d_hot, source, rel)

    def send(after):
        gs_mine, gs_other, gd_mine, gd_other = both_grads(after, dsource, s_hot, dterm, d_hot_t)
        gd = sum_pair(gd_mine, across(gd_other))
        return [gs_mine, across(gs_other), shifted(gd, t)]

    def finish(grads, after):
        (mine,) = update(ent, state, grads, after, last=True)
        return whole_partition(mine, across(mine))

    rel_new, rel_state, done = relation_update(
        t, rel_ids, drel, acc, relations, relation_state, send, finish
    )
    return (done[0], done[1].reshape(-1), rel_new, rel_state)


def solution(mesh):
    return jax.shard_map(
        on_device,
        mesh=mesh,
        in_specs=(
            P(None, ("groups", "dom")),
            P(("groups", "dom")),
            P(None, "groups"),
            P("groups"),
            P(None, ("groups", "dom", "edge"), None),
            P(None, ("groups", "dom", "edge"), None),
            P(None, ("groups", "dom", "edge"), None),
            P(None, ("groups", "dom", "edge")),
            P(None, ("groups", "dom", "edge")),
        ),
        out_specs=(
            P(None, ("groups", "dom")),
            P(("groups", "dom")),
            P(None, "groups"),
            P("groups"),
        ),
        check_vma=False,
    )
```

```python
import functools

import jax
import jax.numpy as jnp
from jax import lax
from jax.experimental import pallas as pl
from jax.experimental.pallas import tpu as pltpu
from jax.sharding import PartitionSpec as P

learn_rate = 0.1
BF = jnp.bfloat16
F32 = jnp.float32
VMEM_LIMIT = 24 * 1024 * 1024
NN = (((1,), (0,)), ((), ()))
NT = (((1,), (1,)), ((), ()))
TN = (((0,), (0,)), ((), ()))


def mm(a, b, dims=NN):
    return lax.dot_general(a, b, dims, preferred_element_type=F32)


def vmem():
    return pl.BlockSpec(memory_space=pltpu.VMEM)


def smem():
    return pl.BlockSpec(memory_space=pltpu.SMEM)


def anywhere():
    return pl.BlockSpec(memory_space=pl.ANY)


def in_hbm(x):
    return pltpu.with_memory_space_constraint(x, pltpu.HBM)


def cost(flops, size):
    return pl.CostEstimate(flops=flops, bytes_accessed=size, transcendentals=0)


def params():
    return pltpu.CompilerParams(vmem_limit_bytes=VMEM_LIMIT)


def shifted(x, by):
    n = lax.axis_size("dom")
    return lax.ppermute(x, "dom", [(i, (i + by) % n) for i in range(n)])


def swapped(x, bits):
    n = lax.axis_size("dom")
    return lax.ppermute(x, "dom", [(i, i ^ bits) for i in range(n)])


def across(x):
    return lax.ppermute(x, "edge", [(0, 1), (1, 0)])


def one_hot(rows_ref, t, count, base):
    blocks, width = rows_ref.shape[1:]
    at = lax.broadcasted_iota(jnp.int32, (count, width), 0)
    idx = rows_ref[t]
    return jnp.concatenate(
        [
            jnp.where(at == base(idx[b : b + 1, :]), 1.0, 0.0).astype(BF)
            for b in range(blocks)
        ],
        axis=1,
    )


def relvec_kernel(t, ids_ref, rel_ref, out_ref):
    rels = rel_ref.shape[1]
    tile = min(rels, 512)
    out = None
    for lo in range(0, rels, tile):
        hot = one_hot(ids_ref, t, tile, lambda i, lo=lo: i - lo)
        part = mm(rel_ref[:, lo : lo + tile], hot)
        out = part if out is None else out + part
    out_ref[...] = out.astype(BF)


def relvec(t, rel_ids, rel16):
    width, rels = rel16.shape
    slots = rel_ids.shape[1] * rel_ids.shape[2]
    return pl.pallas_call(
        functools.partial(relvec_kernel, t),
        in_specs=[vmem()] * 2,
        out_specs=vmem(),
        out_shape=jax.ShapeDtypeStruct((width, slots), BF),
        compiler_params=params(),
        cost_estimate=cost(width * slots, width * slots),
        name="relvec",
    )(rel_ids, rel16)


def relsum_kernel(t, first, ids_ref, drel_ref, *refs):
    step = pl.program_id(0)
    out_ref = refs[-1]
    tile = out_ref.shape[1]
    hot = one_hot(ids_ref, t, tile, lambda i: i - step * tile)
    part = mm(drel_ref[...], hot, NT)
    out_ref[...] = part if first else refs[0][...] + part


def relsum(t, rel_ids, drel, acc, rels):
    width, slots = drel.shape
    tile = min(rels, 512)
    wide = pl.BlockSpec((width, tile), lambda i: (0, i))
    ins = [rel_ids, drel] + ([] if acc is None else [acc])
    return pl.pallas_call(
        functools.partial(relsum_kernel, t, acc is None),
        grid=(rels // tile,),
        in_specs=[
            pl.BlockSpec(rel_ids.shape, lambda i: (0, 0, 0)),
            pl.BlockSpec((width, slots), lambda i: (0, 0)),
        ]
        + ([] if acc is None else [wide]),
        out_specs=wide,
        out_shape=jax.ShapeDtypeStruct((width, rels), F32),
        input_output_aliases={} if acc is None else {2: 0},
        compiler_params=params(),
        cost_estimate=cost(width * slots, width * slots),
        name="relsum",
    )(*ins)


class Limits:
    scratch = lambda shape: [
        pltpu.SMEM((shape[1], shape[0]), jnp.int32),
        pltpu.SMEM((shape[1], shape[0]), jnp.int32),
        pltpu.SemaphoreType.DMA((2,)),
    ]

    def __init__(self, t, from_cnt, from_neg, cnt, neg, sems):
        self.t, self.cnt, self.neg = t, cnt, neg
        self.copies = [
            pltpu.make_async_copy(from_cnt, cnt, sems.at[0]),
            pltpu.make_async_copy(from_neg, neg, sems.at[1]),
        ]
        for copy in self.copies:
            copy.start()

    def wait(self):
        for copy in self.copies:
            copy.wait()

    def count(self, b):
        return self.cnt[b, self.t]

    def negative(self, b):
        return self.neg[b, self.t]


def place():
    dom = lax.axis_index("dom")
    return dom // 2, lax.rem(dom, 2), lax.axis_index("edge")


def localize(edge, half):
    def local(idx):
        moved = idx + edge * half
        return jnp.where(moved >= 2 * half, moved - 2 * half, moved)

    return local


def halves(x):
    hd = x.shape[0] // 2
    return x[:hd], x[hd:]


def make_query(source, rel):
    (s_re, s_im), (w_re, w_im) = halves(source), halves(rel)
    return jnp.concatenate(
        [s_re * w_re - s_im * w_im, s_re * w_im + s_im * w_re], axis=0
    ).astype(BF)


def conj_times(dq, v):
    (dq_re, dq_im), (v_re, v_im) = halves(dq), halves(v)
    return jnp.concatenate(
        [dq_re * v_re + dq_im * v_im, dq_im * v_re - dq_re * v_im], axis=0
    ).astype(BF)


def positive_factors(shape, limits, query, target):
    _, blocks, width = shape
    pos = jnp.sum(query.astype(F32) * target, axis=0, keepdims=True)
    lane = lax.broadcasted_iota(jnp.int32, (1, width), 1)
    valid = jnp.concatenate(
        [jnp.where(lane < limits.count(b), 1.0, 0.0) for b in range(blocks)], axis=1
    )
    return -jax.nn.sigmoid(-pos) * valid


def target_side(shape, limits, query, query_t, target, o_ref, w_ref):
    _, blocks, width = shape
    lanes = lambda b: pl.ds(pl.multiple_of(b * width, width), width)
    count = limits.count
    o_ref[...] = target.astype(BF)
    limits.wait()
    gpos = positive_factors(shape, limits, query, target)
    row_i = lax.broadcasted_iota(jnp.int32, (width, width), 0)
    col_j = lax.broadcasted_iota(jnp.int32, (width, width), 1)
    for b in range(blocks):
        nb = limits.negative(b)
        neg = o_ref[:, lanes(nb)]
        at = slice(b * width, (b + 1) * width)
        scores = mm(query[:, at], neg, TN) if query_t is None else mm(query_t[at], neg)
        keep = jnp.logical_and(row_i < count(b), col_j < count(nb))
        w_ref[:, at] = jnp.where(keep, jax.nn.sigmoid(scores) / width, 0.0).astype(BF)
    return gpos


def target_terms(shape, limits, query, gpos, w_ref, d_ref):
    _, blocks, width = shape
    d_ref[...] = gpos * query.astype(F32)
    for b in range(blocks):
        at = slice(b * width, (b + 1) * width)
        to = pl.ds(pl.multiple_of(limits.negative(b) * width, width), width)
        d_ref[:, to] += mm(query[:, at], w_ref[:, at])
    return d_ref[...].astype(BF)


def make_dquery(shape, limits, gpos, o_ref, w_ref):
    _, blocks, width = shape
    lanes = lambda b: pl.ds(pl.multiple_of(b * width, width), width)
    out = []
    for b in range(blocks):
        nb = limits.negative(b)
        at = slice(b * width, (b + 1) * width)
        own = gpos[:, at] * o_ref[:, at].astype(F32)
        out.append(own + mm(o_ref[:, lanes(nb)], w_ref[:, at], NT))
    return jnp.concatenate(out, axis=1)


def first_kernel(
    shape, cnt_ref, neg_ref, src_ref, dst_ref, ids_ref, ent_ref, state_ref, rel_ref,
    g_mine, g_other, drel_ref, rel16_ref, ent_mine, state_mine,
    cnt, neg, lim_sems, src, dst, ids, ent, state, rel_buf, o_scr, d_scr, w_scr, in_sems, sems,
):
    rels = rel_buf.shape[1]
    tile = min(rels, 512)
    spans = range(0, rels, tile)
    inputs = [
        pltpu.make_async_copy(there, here, in_sems.at[i])
        for i, (there, here) in enumerate(
            [(src_ref.at[:1], src), (dst_ref.at[:1], dst), (ids_ref.at[:1], ids), (ent_ref, ent), (state_ref, state)]
        )
    ]
    loads = [
        pltpu.make_async_copy(
            rel_ref.at[:, lo : lo + tile], rel_buf.at[:, lo : lo + tile], sems.at[i]
        )
        for i, lo in enumerate(spans)
    ]
    for load in inputs:
        load.start()
    limits = Limits(0, cnt_ref, neg_ref, cnt, neg, lim_sems)
    for load in loads:
        load.start()
    half = ent.shape[1] // 2
    _, _, edge = place()
    local = localize(edge, half)
    inputs[0].wait()
    s_hot = one_hot(src, 0, 2 * half, local)
    inputs[1].wait()
    d_hot = one_hot(dst, 0, 2 * half, local)
    inputs[2].wait()
    ids_hot = [one_hot(ids, 0, tile, lambda i, lo=lo: i - lo) for lo in spans]
    inputs[3].wait()
    inputs[4].wait()
    mine = pl.ds(pl.multiple_of(edge * half, half), half)
    ent_mine[...] = ent[:, mine]
    state_mine[...] = state[:, mine]
    table = jnp.concatenate(
        [ent[:, pl.ds(pl.multiple_of(h * half, half), half)].astype(BF) for h in (edge, 1 - edge)],
        axis=1,
    )
    source = mm(table, s_hot)
    target = mm(table, d_hot)
    rel = None
    for load, lo, hot in zip(loads, spans, ids_hot):
        load.wait()
        low = rel_buf[:, lo : lo + tile].astype(BF)
        rel16_ref[:, lo : lo + tile] = low
        part = mm(low, hot)
        rel = part if rel is None else rel + part
    query = make_query(source, rel)
    gpos = target_side(shape, limits, query, None, target, o_scr, w_scr)
    dq = make_dquery(shape, limits, gpos, o_scr, w_scr)
    drel_ref[...] = conj_times(dq, source)
    total = mm(conj_times(dq, rel), s_hot, NT) + mm(
        target_terms(shape, limits, query, gpos, w_scr, d_scr), d_hot, NT
    )
    g_mine[...] = total[:, :half]
    g_other[...] = total[:, half:].astype(BF)


def first_round(cnt, neg, src, dst, rel_ids, entities, state, relations):
    dim, rows = entities.shape
    rels = relations.shape[1]
    _, blocks, width = src.shape
    slots = blocks * width
    sds = jax.ShapeDtypeStruct
    return pl.pallas_call(
        functools.partial(first_kernel, src.shape),
        in_specs=[anywhere()] * 8,
        out_specs=[vmem()] * 6,
        out_shape=[
            sds((dim, rows // 2), F32),
            sds((dim, rows // 2), BF),
            sds((dim, slots), BF),
            sds((dim, rels), BF),
            sds((dim, rows // 2), F32),
            sds((1, rows // 2), F32),
        ],
        scratch_shapes=Limits.scratch(src.shape)
        + [
            pltpu.VMEM((1, blocks, width), jnp.int32),
            pltpu.VMEM((1, blocks, width), jnp.int32),
            pltpu.VMEM((1, blocks, width), jnp.int32),
            pltpu.VMEM((dim, rows), F32),
            pltpu.VMEM((1, rows), F32),
            pltpu.VMEM((dim, rels), F32),
            pltpu.VMEM((dim, slots), BF),
            pltpu.VMEM((dim, slots), F32),
            pltpu.VMEM((width, slots), BF),
            pltpu.SemaphoreType.DMA((5,)),
            pltpu.SemaphoreType.DMA((-(-rels // min(rels, 512)),)),
        ],
        compiler_params=params(),
        cost_estimate=cost(2 * dim * slots * (rels + 4 * rows), 8 * dim * rels),
        name="first_round",
    )(*(in_hbm(x) for x in (cnt, neg, src, dst, rel_ids, entities, state, relations)))


def source_kernel(t, shape, last, cnt_ref, neg_ref, src_ref, dst_ref, own0, own1, rel_ref, *refs):
    query_ref, query_t_ref, source_ref, s_hot_ref, d_hot_ref = refs[:5]
    if last:
        (d_hot_t_ref,) = refs[5:]
    else:
        v_hot_t_ref, n_hot_ref, n_hot_t_ref, mask_ref, cnt, neg, sems, d_hot_t_ref = refs[5:]
        limits = Limits(t, cnt_ref, neg_ref, cnt, neg, sems)
    _, blocks, width = shape
    half = own0.shape[1]
    local = localize(place()[2], half)
    s_hot = one_hot(src_ref, t, 2 * half, local)
    d_hot = one_hot(dst_ref, t, 2 * half, local)
    s_hot_ref[...] = s_hot
    d_hot_ref[...] = d_hot
    d_hot_t_ref[...] = d_hot.T
    source = mm(jnp.concatenate([own0[...], own1[...]], axis=1), s_hot)
    source_ref[...] = source.astype(BF)
    query = make_query(source, rel_ref[...].astype(F32))
    query_ref[...] = query
    query_t_ref[...] = query.T
    if last:
        return
    limits.wait()
    row_i = lax.broadcasted_iota(jnp.int32, (width, width), 0)
    col_j = lax.broadcasted_iota(jnp.int32, (width, width), 1)
    slot = lax.broadcasted_iota(jnp.int32, (width, 2 * half), 0)
    for b in range(blocks):
        nb = limits.negative(b)
        at = slice(b * width, (b + 1) * width)
        there = pl.ds(pl.multiple_of(nb * width, width), width)
        n_hot_ref[:, at] = d_hot_ref[:, there]
        n_hot_t_ref[at] = d_hot_t_ref[there, :]
        keep = jnp.logical_and(row_i < limits.count(b), col_j < limits.count(nb))
        mask_ref[:, at] = jnp.where(keep, 1.0 / width, 0.0)
        hot = d_hot_t_ref[at].astype(F32)
        v_hot_t_ref[at] = jnp.where(slot < limits.count(b), hot, 0.0).astype(BF)


def source_side(t, shape, cnt, neg, src, dst, own, rel):
    dim, slots = rel.shape
    width = shape[2]
    rows = 2 * own[0].shape[1]
    last = t == shape[0] - 1
    sds = lambda *shape: jax.ShapeDtypeStruct(shape, BF)
    outs = [sds(dim, slots), sds(slots, dim), sds(dim, slots), sds(rows, slots), sds(rows, slots)]
    if last:
        outs += [sds(slots, rows)]
    else:
        outs += [sds(slots, rows), sds(rows, slots), sds(slots, rows)]
        outs += [jax.ShapeDtypeStruct((width, slots), F32)]
    return pl.pallas_call(
        functools.partial(source_kernel, t, shape, last),
        in_specs=[anywhere()] * 2 + [vmem()] * 5,
        out_specs=[vmem()] * len(outs),
        out_shape=outs,
        scratch_shapes=[] if last else Limits.scratch(shape) + [pltpu.VMEM((slots, rows), BF)],
        compiler_params=params(),
        cost_estimate=cost(dim * slots, dim * slots),
        name="source_side",
    )(cnt, neg, src, dst, *own, rel)


def near_kernel(query_t_ref, far0, out_ref):
    out_ref[...] = mm(query_t_ref[...], far0[...])


def near_products(query_t, far0):
    slots, half = query_t.shape[0], far0.shape[1]
    return pl.pallas_call(
        near_kernel,
        in_specs=[vmem()] * 2,
        out_specs=vmem(),
        out_shape=jax.ShapeDtypeStruct((slots, half), F32),
        compiler_params=params(),
        cost_estimate=cost(slots * half, slots * half),
        name="near_products",
    )(query_t, far0)


def target_kernel(
    near, far1, query_ref, query_t_ref, v_hot_t_ref, n_hot_ref, n_hot_t_ref, mask_ref,
    gd_mine, gd_other, w_ref,
):
    width, slots = mask_ref.shape
    half = far1.shape[1]
    products = jnp.concatenate([near[...], mm(query_t_ref[...], far1[...])], axis=1)
    high = products.astype(BF)
    low = (products - high.astype(F32)).astype(BF)
    factors = []
    for lo in range(0, slots, width):
        at = slice(lo, lo + width)
        n_hot = n_hot_ref[:, at]
        scores = mm(high[at], n_hot) + mm(low[at], n_hot)
        weight = (jax.nn.sigmoid(scores) * mask_ref[:, at]).astype(BF)
        w_ref[:, at] = weight
        positive = jax.nn.sigmoid(-products[at]) * v_hot_t_ref[at].astype(F32)
        factors.append((mm(weight, n_hot_t_ref[at]) - positive).astype(BF))
    gd = mm(query_ref[...], jnp.concatenate(factors, axis=0))
    gd_mine[...] = gd[:, :half]
    gd_other[...] = gd[:, half:].astype(BF)


def target_grad(near, far1, query, query_t, v_hot_t, n_hot, n_hot_t, mask):
    dim, slots = query.shape
    half = far1.shape[1]
    sds = jax.ShapeDtypeStruct
    return pl.pallas_call(
        target_kernel,
        in_specs=[vmem()] * 8,
        out_specs=[vmem()] * 3,
        out_shape=[sds((dim, half), F32), sds((dim, half), BF), sds(mask.shape, BF)],
        compiler_params=params(),
        cost_estimate=cost(4 * dim * slots * half, 12 * dim * slots),
        name="target_grad",
    )(near, far1, query, query_t, v_hot_t, n_hot, n_hot_t, mask)


def source_grad_kernel(
    t, shape, cnt_ref, neg_ref, _, far0, far1, d_hot_ref, query_ref, w_ref, source_ref, rel_ref, s_hot_ref,
    gs_mine, gs_other, drel_ref, cnt, neg, sems, o_scr,
):
    limits = Limits(t, cnt_ref, neg_ref, cnt, neg, sems)
    half = gs_mine.shape[1]
    target = mm(jnp.concatenate([far0[...], far1[...]], axis=1), d_hot_ref[...])
    o_scr[...] = target.astype(BF)
    limits.wait()
    gpos = positive_factors(shape, limits, query_ref[...], target)
    dq = make_dquery(shape, limits, gpos, o_scr, w_ref)
    drel_ref[...] = conj_times(dq, source_ref[...].astype(F32))
    gs = mm(conj_times(dq, rel_ref[...].astype(F32)), s_hot_ref[...], NT)
    gs_mine[...] = gs[:, :half]
    gs_other[...] = gs[:, half:].astype(BF)


def source_grad(t, shape, cnt, neg, after, far, d_hot, query, weight, source, rel, s_hot):
    dim, slots = rel.shape
    half = s_hot.shape[0] // 2
    sds = jax.ShapeDtypeStruct
    return pl.pallas_call(
        functools.partial(source_grad_kernel, t, shape),
        in_specs=[anywhere()] * 3 + [vmem()] * 8,
        out_specs=[vmem()] * 3,
        out_shape=[sds((dim, half), F32), sds((dim, half), BF), sds((dim, slots), BF)],
        scratch_shapes=Limits.scratch(shape) + [pltpu.VMEM((dim, slots), BF)],
        compiler_params=params(),
        cost_estimate=cost(dim * slots, dim * slots),
        name="source_grad",
    )(cnt, neg, after, *far, d_hot, query, weight, source, rel, s_hot)


def last_kernel(
    t, shape, cnt_ref, neg_ref, far0, far1, query_ref, query_t_ref, d_hot_ref, source_ref, rel_ref,
    drel_ref, dsource_ref, dterm_ref, cnt, neg, sems, o_scr, d_scr, w_scr,
):
    limits = Limits(t, cnt_ref, neg_ref, cnt, neg, sems)
    far = jnp.concatenate([far0[...], far1[...]], axis=1)
    target = mm(far, d_hot_ref[...])
    query = query_ref[...]
    gpos = target_side(shape, limits, query, query_t_ref, target, o_scr, w_scr)
    dterm_ref[...] = target_terms(shape, limits, query, gpos, w_scr, d_scr)
    dq = make_dquery(shape, limits, gpos, o_scr, w_scr)
    drel_ref[...] = conj_times(dq, source_ref[...].astype(F32))
    dsource_ref[...] = conj_times(dq, rel_ref[...].astype(F32))


def last_terms(t, shape, cnt, neg, far, query, query_t, d_hot, source, rel):
    dim, slots = query.shape
    sds = jax.ShapeDtypeStruct
    return pl.pallas_call(
        functools.partial(last_kernel, t, shape),
        in_specs=[anywhere()] * 2 + [vmem()] * 7,
        out_specs=[vmem()] * 3,
        out_shape=[sds((dim, slots), BF)] * 3,
        scratch_shapes=Limits.scratch(shape)
        + [
            pltpu.VMEM((dim, slots), BF),
            pltpu.VMEM((dim, slots), F32),
            pltpu.VMEM((shape[2], slots), BF),
        ],
        compiler_params=params(),
        cost_estimate=cost(6 * dim * slots * shape[2], 12 * dim * slots),
        name="last_terms",
    )(cnt, neg, *far, query, query_t, d_hot, source, rel)


def both_kernel(_, dsource_ref, s_hot_ref, dterm_ref, d_hot_t_ref, gs_mine, gs_other, gd_mine, gd_other):
    half = gs_mine.shape[1]
    for terms, hot, dims, mine, other in (
        (dterm_ref, d_hot_t_ref, NN, gd_mine, gd_other),
        (dsource_ref, s_hot_ref, NT, gs_mine, gs_other),
    ):
        grad = mm(terms[...], hot[...], dims)
        mine[...] = grad[:, :half]
        other[...] = grad[:, half:].astype(BF)


def both_grads(after, dsource, s_hot, dterm, d_hot_t):
    dim, slots = dterm.shape
    half = s_hot.shape[0] // 2
    sds = jax.ShapeDtypeStruct
    return pl.pallas_call(
        both_kernel,
        in_specs=[anywhere()] + [vmem()] * 4,
        out_specs=[vmem()] * 4,
        out_shape=[sds((dim, half), F32), sds((dim, half), BF)] * 2,
        compiler_params=params(),
        cost_estimate=cost(8 * dim * slots * half, 12 * dim * slots),
        name="both_grads",
    )(after, dsource, s_hot, dterm, d_hot_t)


def update_kernel(n_grads, last, *refs):
    ent_ref, state_ref, grads = refs[0], refs[1], refs[2 : 2 + n_grads]
    grad = grads[0][...].astype(F32)
    for g in grads[1:]:
        grad = grad + g[...].astype(F32)
    dim = grad.shape[0]
    state = state_ref[...] + jnp.sum(grad * grad, axis=0, keepdims=True) / dim
    new = ent_ref[...] - grad * (learn_rate / jnp.sqrt(state))
    if last:
        refs[-1][:dim] = new
        refs[-1][dim:] = jnp.broadcast_to(state, (refs[-1].shape[0] - dim, state.shape[1]))
    else:
        refs[-3][...] = new
        refs[-2][...] = state
        refs[-1][...] = new.astype(BF)


def update(ent, state, grads, after, last=False):
    dim, half = ent.shape
    sds = jax.ShapeDtypeStruct
    outs = [sds((dim, half), F32), sds((1, half), F32), sds((dim, half), BF)]
    if last:
        outs = [sds((dim + 8, half), F32)]
    return pl.pallas_call(
        functools.partial(update_kernel, len(grads), last),
        in_specs=[vmem()] * (2 + len(grads)) + [anywhere()] * len(after),
        out_specs=[vmem()] * len(outs),
        out_shape=outs,
        compiler_params=params(),
        cost_estimate=cost(10 * dim * half, 16 * dim * half),
        name="update",
    )(ent, state, *grads, *after)


def pair_kernel(a_ref, b_ref, out_ref):
    out_ref[...] = (a_ref[...] + b_ref[...].astype(F32)).astype(out_ref.dtype)


def sum_pair(a, b, dtype=BF):
    return pl.pallas_call(
        pair_kernel,
        in_specs=[vmem()] * 2,
        out_specs=vmem(),
        out_shape=jax.ShapeDtypeStruct(a.shape, dtype),
        compiler_params=params(),
        name="sum_pair",
    )(a, b)


def held_kernel(x_ref, *refs):
    pass


def held(x, after):
    return pl.pallas_call(
        held_kernel,
        in_specs=[anywhere()] * (1 + len(after)),
        out_specs=anywhere(),
        out_shape=jax.ShapeDtypeStruct(x.shape, x.dtype),
        input_output_aliases={0: 0},
        compiler_params=params(),
        name="held",
    )(x, *after)


def whole_kernel(mine, theirs, ent_out, state_out, token):
    token[...] = jnp.zeros_like(token)
    dim, rows = ent_out.shape
    half = rows // 2
    edge = place()[2]
    for core, part in ((edge, mine), (1 - edge, theirs)):
        at = pl.ds(pl.multiple_of(core * half, half), half)
        ent_out[:, at] = part[:dim]
        state_out[:, at] = part[dim : dim + 1]


def whole_partition(mine, theirs):
    dim, half = mine.shape[0] - 8, mine.shape[1]
    return pl.pallas_call(
        whole_kernel,
        in_specs=[vmem()] * 2,
        out_specs=[vmem()] * 3,
        out_shape=[
            jax.ShapeDtypeStruct((dim, 2 * half), F32),
            jax.ShapeDtypeStruct((1, 2 * half), F32),
            jax.ShapeDtypeStruct((8, 128), F32),
        ],
        compiler_params=params(),
        name="whole_partition",
    )(mine, theirs)


def first_column(owner, core, w):
    return pl.multiple_of((2 * owner + core) * w, w)


def pieces_kernel(t, nz, same, ids_ref, drel_ref, acc_ref, *refs):
    mine, other = refs[-nz - 1 : -1], refs[-1]
    w = other.shape[2]
    z, x, edge = place()
    drel = drel_ref[...]
    for k in range(nz):
        owner = 2 * lax.bitwise_xor(z, k) + (x if same else 1 - x)
        at = [first_column(owner, core, w) for core in (edge, 1 - edge)]
        hot = jnp.concatenate([one_hot(ids_ref, t, w, lambda i, lo=lo: i - lo) for lo in at], axis=0)
        part = mm(drel, hot, NT)
        mine[k][...] = acc_ref[:, pl.ds(at[0], w)] + part[:, :w]
        other[k] = (acc_ref[:, pl.ds(at[1], w)] + part[:, w:]).astype(BF)


def pieces(t, n, same, rel_ids, drel, acc, after):
    dim, rels = acc.shape
    w = rels // (2 * n)
    sds = jax.ShapeDtypeStruct
    out = pl.pallas_call(
        functools.partial(pieces_kernel, t, n // 2, same),
        in_specs=[vmem()] * 3 + [anywhere()] * len(after),
        out_specs=[vmem()] * (n // 2 + 1),
        out_shape=[sds((dim, w), F32)] * (n // 2) + [sds((n // 2, dim, w), BF)],
        compiler_params=params(),
        cost_estimate=cost(dim * rels * drel.shape[1], 4 * dim * rels),
        name="pieces",
    )(rel_ids, drel, acc, *after)
    return out[:-1], out[-1]


def add_kernel(n, *refs):
    for k in range(n):
        refs[n + 1 + k][...] = (refs[k][...] + refs[n][k].astype(F32)).astype(BF)


def add_each(mine, theirs):
    n = len(mine)
    return pl.pallas_call(
        functools.partial(add_kernel, n),
        in_specs=[vmem()] * (n + 1),
        out_specs=[vmem()] * n,
        out_shape=[jax.ShapeDtypeStruct(x.shape, BF) for x in mine],
        compiler_params=params(),
        name="add_each",
    )(*mine, theirs)


def sum_kernel(k, count, mine, theirs, *refs):
    total = mine[...] + theirs[k].astype(F32)
    for r in refs[:count]:
        total = total + r[...].astype(F32)
    refs[-1][...] = total.astype(BF)


def sum_piece(k, mine, theirs, parts, after):
    return pl.pallas_call(
        functools.partial(sum_kernel, k, len(parts)),
        in_specs=[vmem()] * (2 + len(parts)) + [anywhere()] * len(after),
        out_specs=vmem(),
        out_shape=jax.ShapeDtypeStruct(mine.shape, BF),
        compiler_params=params(),
        name="sum_piece",
    )(mine, theirs, *parts, *after)


def stacked_kernel(*refs):
    for i in range(refs[-1].shape[0]):
        refs[-1][i] = refs[i][...]


def stacked(parts, after):
    return pl.pallas_call(
        stacked_kernel,
        in_specs=[vmem()] * len(parts) + [anywhere()] * len(after),
        out_specs=vmem(),
        out_shape=jax.ShapeDtypeStruct((len(parts), *parts[0].shape), parts[0].dtype),
        compiler_params=params(),
        name="stacked",
    )(*parts, *after)


def relnew_kernel(nz, kinds, count, first, rel_ref, state_ref, *refs):
    arrays = refs[:count]
    rel_out, state_out, buf, sems = refs[-4:]
    w = buf.shape[2]
    state_out[...] = refs[count + (0 if first else 1)][...]
    z, x, edge = place()
    copies = []
    for i, (k, same, own, source, index) in enumerate(kinds):
        owner = 2 * lax.bitwise_xor(z, k) + (x if same else 1 - x)
        at = pl.ds(first_column(owner, edge if own else 1 - edge, w), w)
        grad = (arrays[source][...] if index is None else arrays[source][index]).astype(F32)
        state = state_ref[:, at] + jnp.sum(grad * grad, axis=0, keepdims=True) / grad.shape[0]
        state_out[:, at] = state
        buf[i] = rel_ref[:, at] - grad * (learn_rate / jnp.sqrt(state))
        copy = pltpu.make_async_copy(buf.at[i], rel_out.at[:, at], sems.at[i])
        copy.start()
        copies.append(copy)
    for copy in copies:
        copy.wait()


def relnew(nz, relations, state, groups, before, after):
    dim, rels = relations.shape
    w = rels // (4 * nz)
    kinds, arrays = [], []
    for ks, same, own, parts in groups:
        one = not isinstance(parts, list)
        for i, k in enumerate(ks):
            kinds.append((k, same, own, len(arrays) + (0 if one else i), i if one else None))
        arrays += [parts] if one else parts
    count = len(kinds)
    start = [state] if before is None else list(before)
    return pl.pallas_call(
        functools.partial(relnew_kernel, nz, tuple(kinds), len(arrays), before is None),
        in_specs=[vmem()] * (2 + len(arrays))
        + ([anywhere()] if before else [])
        + [vmem()]
        + [anywhere()] * len(after),
        out_specs=[anywhere(), vmem()],
        out_shape=[jax.ShapeDtypeStruct((dim, rels), F32), jax.ShapeDtypeStruct((1, rels), F32)],
        input_output_aliases={2 + len(arrays): 0} if before else {},
        scratch_shapes=[pltpu.VMEM((count, dim, w), F32), pltpu.SemaphoreType.DMA((count,))],
        compiler_params=params(),
        cost_estimate=cost(dim, dim),
        name="relnew",
    )(relations, state, *arrays, *start, *after)


def relation_update(t, rel_ids, drel, acc, relations, state, send, finish):
    n = lax.axis_size("dom")
    dim, rels = relations.shape
    if n < 4 or n & (n - 1) or rels % (256 * n):
        total = lax.psum(relsum(t, rel_ids, drel, acc, rels), ("dom", "edge"))
        state = state + jnp.mean(total * total, axis=0)
        return relations - learn_rate * total / jnp.sqrt(state)[None, :], state, finish(send(drel), [])
    nz = n // 2
    mine_x, other_x = pieces(t, n, False, rel_ids, drel, acc, [])
    grads = send(other_x)
    mine_s, other_s = pieces(t, n, True, rel_ids, drel, acc, [other_x])
    to_x = add_each(mine_x, across(other_x))
    theirs = across(other_s)
    down = range(nz - 1, -1, -1)
    from_x = {k: swapped(to_x[k], 1) for k in down}
    turned = {
        k: sum_piece(k, mine_s[k], theirs, [from_x[k]], grads[1:2] if k == nz - 1 else [])
        for k in down[:-1]
    }
    from_z = [swapped(turned[k], 2 * k) for k in down[:-1]]
    done = finish(grads, [turned[nz - 1]])
    summed = sum_piece(0, mine_s[0], theirs, [from_x[0]] + from_z, [])
    got = [summed if k == 0 else swapped(summed, 2 * k) for k in range(nz)]
    got_x = [swapped(piece, 1) for piece in got]
    state = state.reshape(1, rels)
    ks = [0, *down[:-1]]
    mine = [got[k] for k in ks]
    mine_x = [got_x[k] for k in ks]
    there = across(stacked(mine, [done[2]]))
    new = relnew(nz, relations, state, [(ks, True, True, mine)], None, [])
    there_x = across(stacked(mine_x, [new[1]]))
    groups = [(ks, True, False, there), (ks, False, True, mine_x)]
    new = relnew(nz, relations, state, groups, new, [])
    rel_new, state_new = relnew(nz, relations, state, [(ks, False, False, there_x)], new, [])
    return rel_new, state_new.reshape(rels), done


def on_device(
    entities,
    entity_state,
    relations,
    relation_state,
    src_rows,
    rel_ids,
    dst_rows,
    counts,
    neg_blocks,
):
    rounds = src_rows.shape[0]
    rels = relations.shape[1]
    shape = src_rows.shape
    cnt, neg = counts.T, neg_blocks.T
    g_mine, g_other, drel, rel16, ent, state = first_round(
        cnt, neg, src_rows, dst_rows, rel_ids, entities, entity_state.reshape(1, -1), relations
    )
    acc = relsum(0, rel_ids, drel, None, rels)
    ent, state, low = update(ent, state, [g_mine, across(g_other)], [])
    rel = relvec(1, rel_ids, rel16)
    for t in range(1, rounds):
        far = shifted(low, -t)
        own = (low, across(low))
        query, query_t, source, s_hot, d_hot, *hots = source_side(
            t, shape, cnt, neg, src_rows, dst_rows, own, rel
        )
        far = held(far, [query, acc])
        far = (far, across(far))
        if t == rounds - 1:
            break
        near = near_products(query_t, far[0])
        gd_mine, gd_other, weight = target_grad(near, far[1], query, query_t, *hots)
        gd = sum_pair(gd_mine, across(gd_other))
        gs_mine, gs_other, drel = source_grad(
            t, shape, cnt, neg, gd, far, d_hot, query, weight, source, rel, s_hot
        )
        acc = relsum(t, rel_ids, drel, acc, rels)
        rel = relvec(t + 1, rel_ids, rel16)
        grads = [sum_pair(gs_mine, shifted(gd, t), F32), across(gs_other)]
        ent, state, low = update(ent, state, grads, [rel])
    drel, dsource, dterm = last_terms(t, shape, cnt, neg, far, query, query_t, d_hot, source, rel)

    def send(after):
        gs_mine, gs_other, gd_mine, gd_other = both_grads(after, dsource, s_hot, dterm, hots[0])
        gd = sum_pair(gd_mine, across(gd_other))
        return [gs_mine, across(gs_other), shifted(gd, t)]

    def finish(grads, after):
        (mine,) = update(ent, state, grads, after, last=True)
        return whole_partition(mine, across(mine))

    rel_new, rel_state, done = relation_update(
        t, rel_ids, drel, acc, relations, relation_state, send, finish
    )
    return (done[0], done[1].reshape(-1), rel_new, rel_state)


def solution(mesh):
    return jax.shard_map(
        on_device,
        mesh=mesh,
        in_specs=(
            P(None, ("groups", "dom")),
            P(("groups", "dom")),
            P(None, "groups"),
            P("groups"),
            P(None, ("groups", "dom", "edge"), None),
            P(None, ("groups", "dom", "edge"), None),
            P(None, ("groups", "dom", "edge"), None),
            P(None, ("groups", "dom", "edge")),
            P(None, ("groups", "dom", "edge")),
        ),
        out_specs=(
            P(None, ("groups", "dom")),
            P(("groups", "dom")),
            P(None, "groups"),
            P("groups"),
        ),
        check_vma=False,
    )
```

```python
import functools

import jax
import jax.numpy as jnp
from jax import lax
from jax.experimental import pallas as pl
from jax.experimental.pallas import tpu as pltpu
from jax.sharding import PartitionSpec as P

learn_rate = 0.1
BF = jnp.bfloat16
F32 = jnp.float32
VMEM_LIMIT = 24 * 1024 * 1024
NN = (((1,), (0,)), ((), ()))
NT = (((1,), (1,)), ((), ()))
TN = (((0,), (0,)), ((), ()))


def mm(a, b, dims=NN):
    return lax.dot_general(a, b, dims, preferred_element_type=F32)


def vmem():
    return pl.BlockSpec(memory_space=pltpu.VMEM)


def smem():
    return pl.BlockSpec(memory_space=pltpu.SMEM)


def anywhere():
    return pl.BlockSpec(memory_space=pl.ANY)


def in_hbm(x):
    return pltpu.with_memory_space_constraint(x, pltpu.HBM)


def cost(flops, size):
    return pl.CostEstimate(flops=flops, bytes_accessed=size, transcendentals=0)


def params():
    return pltpu.CompilerParams(vmem_limit_bytes=VMEM_LIMIT)


def shifted(x, by):
    n = lax.axis_size("dom")
    return lax.ppermute(x, "dom", [(i, (i + by) % n) for i in range(n)])


def swapped(x, bits):
    n = lax.axis_size("dom")
    return lax.ppermute(x, "dom", [(i, i ^ bits) for i in range(n)])


def across(x):
    return lax.ppermute(x, "edge", [(0, 1), (1, 0)])


def one_hot(rows_ref, t, count, base):
    blocks, width = rows_ref.shape[1:]
    at = lax.broadcasted_iota(jnp.int32, (count, width), 0)
    idx = rows_ref[t]
    return jnp.concatenate(
        [
            jnp.where(at == base(idx[b : b + 1, :]), 1.0, 0.0).astype(BF)
            for b in range(blocks)
        ],
        axis=1,
    )


def relvec_kernel(t, ids_ref, rel_ref, out_ref):
    rels = rel_ref.shape[1]
    tile = min(rels, 512)
    out = None
    for lo in range(0, rels, tile):
        hot = one_hot(ids_ref, t, tile, lambda i, lo=lo: i - lo)
        part = mm(rel_ref[:, lo : lo + tile], hot)
        out = part if out is None else out + part
    out_ref[...] = out.astype(BF)


def relvec(t, rel_ids, rel16):
    width, rels = rel16.shape
    slots = rel_ids.shape[1] * rel_ids.shape[2]
    return pl.pallas_call(
        functools.partial(relvec_kernel, t),
        in_specs=[vmem()] * 2,
        out_specs=vmem(),
        out_shape=jax.ShapeDtypeStruct((width, slots), BF),
        compiler_params=params(),
        cost_estimate=cost(width * slots, width * slots),
        name="relvec",
    )(rel_ids, rel16)


def relsum_kernel(t, first, ids_ref, drel_ref, *refs):
    step = pl.program_id(0)
    out_ref = refs[-1]
    tile = out_ref.shape[1]
    hot = one_hot(ids_ref, t, tile, lambda i: i - step * tile)
    part = mm(drel_ref[...], hot, NT)
    out_ref[...] = part if first else refs[0][...] + part


def relsum(t, rel_ids, drel, acc, rels):
    width, slots = drel.shape
    tile = min(rels, 512)
    wide = pl.BlockSpec((width, tile), lambda i: (0, i))
    ins = [rel_ids, drel] + ([] if acc is None else [acc])
    return pl.pallas_call(
        functools.partial(relsum_kernel, t, acc is None),
        grid=(rels // tile,),
        in_specs=[
            pl.BlockSpec(rel_ids.shape, lambda i: (0, 0, 0)),
            pl.BlockSpec((width, slots), lambda i: (0, 0)),
        ]
        + ([] if acc is None else [wide]),
        out_specs=wide,
        out_shape=jax.ShapeDtypeStruct((width, rels), F32),
        input_output_aliases={} if acc is None else {2: 0},
        compiler_params=params(),
        cost_estimate=cost(width * slots, width * slots),
        name="relsum",
    )(*ins)


class Limits:
    scratch = lambda shape: [
        pltpu.SMEM((shape[1], shape[0]), jnp.int32),
        pltpu.SMEM((shape[1], shape[0]), jnp.int32),
        pltpu.SemaphoreType.DMA((2,)),
    ]

    def __init__(self, t, from_cnt, from_neg, cnt, neg, sems):
        self.t, self.cnt, self.neg = t, cnt, neg
        self.copies = [
            pltpu.make_async_copy(from_cnt, cnt, sems.at[0]),
            pltpu.make_async_copy(from_neg, neg, sems.at[1]),
        ]
        for copy in self.copies:
            copy.start()

    def wait(self):
        for copy in self.copies:
            copy.wait()

    def count(self, b):
        return self.cnt[b, self.t]

    def negative(self, b):
        return self.neg[b, self.t]


def place():
    dom = lax.axis_index("dom")
    return dom // 2, lax.rem(dom, 2), lax.axis_index("edge")


def localize(edge, half):
    def local(idx):
        moved = idx + edge * half
        return jnp.where(moved >= 2 * half, moved - 2 * half, moved)

    return local


def halves(x):
    hd = x.shape[0] // 2
    return x[:hd], x[hd:]


def make_query(source, rel):
    (s_re, s_im), (w_re, w_im) = halves(source), halves(rel)
    return jnp.concatenate(
        [s_re * w_re - s_im * w_im, s_re * w_im + s_im * w_re], axis=0
    ).astype(BF)


def conj_times(dq, v):
    (dq_re, dq_im), (v_re, v_im) = halves(dq), halves(v)
    return jnp.concatenate(
        [dq_re * v_re + dq_im * v_im, dq_im * v_re - dq_re * v_im], axis=0
    ).astype(BF)


def positive_factors(shape, limits, query, target):
    _, blocks, width = shape
    pos = jnp.sum(query.astype(F32) * target, axis=0, keepdims=True)
    lane = lax.broadcasted_iota(jnp.int32, (1, width), 1)
    valid = jnp.concatenate(
        [jnp.where(lane < limits.count(b), 1.0, 0.0) for b in range(blocks)], axis=1
    )
    return -jax.nn.sigmoid(-pos) * valid


def target_side(shape, limits, query, query_t, target, o_ref, w_ref):
    _, blocks, width = shape
    lanes = lambda b: pl.ds(pl.multiple_of(b * width, width), width)
    count = limits.count
    o_ref[...] = target.astype(BF)
    limits.wait()
    gpos = positive_factors(shape, limits, query, target)
    row_i = lax.broadcasted_iota(jnp.int32, (width, width), 0)
    col_j = lax.broadcasted_iota(jnp.int32, (width, width), 1)
    for b in range(blocks):
        nb = limits.negative(b)
        neg = o_ref[:, lanes(nb)]
        at = slice(b * width, (b + 1) * width)
        scores = mm(query[:, at], neg, TN) if query_t is None else mm(query_t[at], neg)
        keep = jnp.logical_and(row_i < count(b), col_j < count(nb))
        w_ref[:, at] = jnp.where(keep, jax.nn.sigmoid(scores) / width, 0.0).astype(BF)
    return gpos


def target_terms(shape, limits, query, gpos, w_ref, d_ref):
    _, blocks, width = shape
    d_ref[...] = gpos * query.astype(F32)
    for b in range(blocks):
        at = slice(b * width, (b + 1) * width)
        to = pl.ds(pl.multiple_of(limits.negative(b) * width, width), width)
        d_ref[:, to] += mm(query[:, at], w_ref[:, at])
    return d_ref[...].astype(BF)


def make_dquery(shape, limits, gpos, o_ref, w_ref):
    _, blocks, width = shape
    lanes = lambda b: pl.ds(pl.multiple_of(b * width, width), width)
    out = []
    for b in range(blocks):
        nb = limits.negative(b)
        at = slice(b * width, (b + 1) * width)
        own = gpos[:, at] * o_ref[:, at].astype(F32)
        out.append(own + mm(o_ref[:, lanes(nb)], w_ref[:, at], NT))
    return jnp.concatenate(out, axis=1)


def first_kernel(
    shape, cnt_ref, neg_ref, src_ref, dst_ref, ids_ref, ent_ref, state_ref, rel_ref,
    g_mine, g_other, drel_ref, rel16_ref, ent_mine, state_mine,
    cnt, neg, lim_sems, src, dst, ids, ent, state, rel_buf, o_scr, d_scr, w_scr, in_sems, sems,
):
    rels = rel_buf.shape[1]
    tile = min(rels, 512)
    spans = range(0, rels, tile)
    inputs = [
        pltpu.make_async_copy(there, here, in_sems.at[i])
        for i, (there, here) in enumerate(
            [(src_ref.at[:1], src), (dst_ref.at[:1], dst), (ids_ref.at[:1], ids), (ent_ref, ent), (state_ref, state)]
        )
    ]
    loads = [
        pltpu.make_async_copy(
            rel_ref.at[:, lo : lo + tile], rel_buf.at[:, lo : lo + tile], sems.at[i]
        )
        for i, lo in enumerate(spans)
    ]
    for load in inputs:
        load.start()
    limits = Limits(0, cnt_ref, neg_ref, cnt, neg, lim_sems)
    for load in loads:
        load.start()
    half = ent.shape[1] // 2
    _, _, edge = place()
    local = localize(edge, half)
    inputs[0].wait()
    s_hot = one_hot(src, 0, 2 * half, local)
    inputs[1].wait()
    d_hot = one_hot(dst, 0, 2 * half, local)
    inputs[2].wait()
    ids_hot = [one_hot(ids, 0, tile, lambda i, lo=lo: i - lo) for lo in spans]
    inputs[3].wait()
    inputs[4].wait()
    mine = pl.ds(pl.multiple_of(edge * half, half), half)
    ent_mine[...] = ent[:, mine]
    state_mine[...] = state[:, mine]
    table = jnp.concatenate(
        [ent[:, pl.ds(pl.multiple_of(h * half, half), half)].astype(BF) for h in (edge, 1 - edge)],
        axis=1,
    )
    source = mm(table, s_hot)
    target = mm(table, d_hot)
    rel = None
    for load, lo, hot in zip(loads, spans, ids_hot):
        load.wait()
        low = rel_buf[:, lo : lo + tile].astype(BF)
        rel16_ref[:, lo : lo + tile] = low
        part = mm(low, hot)
        rel = part if rel is None else rel + part
    query = make_query(source, rel)
    gpos = target_side(shape, limits, query, None, target, o_scr, w_scr)
    dq = make_dquery(shape, limits, gpos, o_scr, w_scr)
    drel_ref[...] = conj_times(dq, source)
    total = mm(conj_times(dq, rel), s_hot, NT) + mm(
        target_terms(shape, limits, query, gpos, w_scr, d_scr), d_hot, NT
    )
    g_mine[...] = total[:, :half]
    g_other[...] = total[:, half:].astype(BF)


def first_round(cnt, neg, src, dst, rel_ids, entities, state, relations):
    dim, rows = entities.shape
    rels = relations.shape[1]
    _, blocks, width = src.shape
    slots = blocks * width
    sds = jax.ShapeDtypeStruct
    return pl.pallas_call(
        functools.partial(first_kernel, src.shape),
        in_specs=[anywhere()] * 8,
        out_specs=[vmem()] * 6,
        out_shape=[
            sds((dim, rows // 2), F32),
            sds((dim, rows // 2), BF),
            sds((dim, slots), BF),
            sds((dim, rels), BF),
            sds((dim, rows // 2), F32),
            sds((1, rows // 2), F32),
        ],
        scratch_shapes=Limits.scratch(src.shape)
        + [
            pltpu.VMEM((1, blocks, width), jnp.int32),
            pltpu.VMEM((1, blocks, width), jnp.int32),
            pltpu.VMEM((1, blocks, width), jnp.int32),
            pltpu.VMEM((dim, rows), F32),
            pltpu.VMEM((1, rows), F32),
            pltpu.VMEM((dim, rels), F32),
            pltpu.VMEM((dim, slots), BF),
            pltpu.VMEM((dim, slots), F32),
            pltpu.VMEM((width, slots), BF),
            pltpu.SemaphoreType.DMA((5,)),
            pltpu.SemaphoreType.DMA((-(-rels // min(rels, 512)),)),
        ],
        compiler_params=params(),
        cost_estimate=cost(2 * dim * slots * (rels + 4 * rows), 8 * dim * rels),
        name="first_round",
    )(*(in_hbm(x) for x in (cnt, neg, src, dst, rel_ids, entities, state, relations)))


def source_kernel(t, shape, last, cnt_ref, neg_ref, src_ref, dst_ref, own0, own1, rel_ref, *refs):
    query_ref, query_t_ref, source_ref, s_hot_ref, d_hot_ref = refs[:5]
    if last:
        (d_hot_t_ref,) = refs[5:]
    else:
        v_hot_t_ref, n_hot_ref, n_hot_t_ref, mask_ref, cnt, neg, sems, d_hot_t_ref = refs[5:]
        limits = Limits(t, cnt_ref, neg_ref, cnt, neg, sems)
    _, blocks, width = shape
    half = own0.shape[1]
    local = localize(place()[2], half)
    s_hot = one_hot(src_ref, t, 2 * half, local)
    d_hot = one_hot(dst_ref, t, 2 * half, local)
    s_hot_ref[...] = s_hot
    d_hot_ref[...] = d_hot
    d_hot_t_ref[...] = d_hot.T
    source = mm(jnp.concatenate([own0[...], own1[...]], axis=1), s_hot)
    source_ref[...] = source.astype(BF)
    query = make_query(source, rel_ref[...].astype(F32))
    query_ref[...] = query
    query_t_ref[...] = query.T
    if last:
        return
    limits.wait()
    row_i = lax.broadcasted_iota(jnp.int32, (width, width), 0)
    col_j = lax.broadcasted_iota(jnp.int32, (width, width), 1)
    slot = lax.broadcasted_iota(jnp.int32, (width, 2 * half), 0)
    for b in range(blocks):
        nb = limits.negative(b)
        at = slice(b * width, (b + 1) * width)
        there = pl.ds(pl.multiple_of(nb * width, width), width)
        n_hot_ref[:, at] = d_hot_ref[:, there]
        n_hot_t_ref[at] = d_hot_t_ref[there, :]
        keep = jnp.logical_and(row_i < limits.count(b), col_j < limits.count(nb))
        mask_ref[:, at] = jnp.where(keep, 1.0 / width, 0.0)
        hot = d_hot_t_ref[at].astype(F32)
        v_hot_t_ref[at] = jnp.where(slot < limits.count(b), hot, 0.0).astype(BF)


def source_side(t, shape, cnt, neg, src, dst, own, rel):
    dim, slots = rel.shape
    width = shape[2]
    rows = 2 * own[0].shape[1]
    last = t == shape[0] - 1
    sds = lambda *shape: jax.ShapeDtypeStruct(shape, BF)
    outs = [sds(dim, slots), sds(slots, dim), sds(dim, slots), sds(rows, slots), sds(rows, slots)]
    if last:
        outs += [sds(slots, rows)]
    else:
        outs += [sds(slots, rows), sds(rows, slots), sds(slots, rows)]
        outs += [jax.ShapeDtypeStruct((width, slots), F32)]
    return pl.pallas_call(
        functools.partial(source_kernel, t, shape, last),
        in_specs=[anywhere()] * 2 + [vmem()] * 5,
        out_specs=[vmem()] * len(outs),
        out_shape=outs,
        scratch_shapes=[] if last else Limits.scratch(shape) + [pltpu.VMEM((slots, rows), BF)],
        compiler_params=params(),
        cost_estimate=cost(dim * slots, dim * slots),
        name="source_side",
    )(cnt, neg, src, dst, *own, rel)


def near_kernel(query_t_ref, far0, out_ref):
    out_ref[...] = mm(query_t_ref[...], far0[...])


def near_products(query_t, far0):
    slots, half = query_t.shape[0], far0.shape[1]
    return pl.pallas_call(
        near_kernel,
        in_specs=[vmem()] * 2,
        out_specs=vmem(),
        out_shape=jax.ShapeDtypeStruct((slots, half), F32),
        compiler_params=params(),
        cost_estimate=cost(slots * half, slots * half),
        name="near_products",
    )(query_t, far0)


def target_kernel(
    near, far1, query_ref, query_t_ref, v_hot_t_ref, n_hot_ref, n_hot_t_ref, mask_ref,
    gd_mine, gd_other, w_ref,
):
    width, slots = mask_ref.shape
    half = far1.shape[1]
    products = jnp.concatenate([near[...], mm(query_t_ref[...], far1[...])], axis=1)
    high = products.astype(BF)
    low = (products - high.astype(F32)).astype(BF)
    factors = []
    for lo in range(0, slots, width):
        at = slice(lo, lo + width)
        n_hot = n_hot_ref[:, at]
        scores = mm(high[at], n_hot) + mm(low[at], n_hot)
        weight = (jax.nn.sigmoid(scores) * mask_ref[:, at]).astype(BF)
        w_ref[:, at] = weight
        positive = jax.nn.sigmoid(-products[at]) * v_hot_t_ref[at].astype(F32)
        factors.append((mm(weight, n_hot_t_ref[at]) - positive).astype(BF))
    gd = mm(query_ref[...], jnp.concatenate(factors, axis=0))
    gd_mine[...] = gd[:, :half]
    gd_other[...] = gd[:, half:].astype(BF)


def target_grad(near, far1, query, query_t, v_hot_t, n_hot, n_hot_t, mask):
    dim, slots = query.shape
    half = far1.shape[1]
    sds = jax.ShapeDtypeStruct
    return pl.pallas_call(
        target_kernel,
        in_specs=[vmem()] * 8,
        out_specs=[vmem()] * 3,
        out_shape=[sds((dim, half), F32), sds((dim, half), BF), sds(mask.shape, BF)],
        compiler_params=params(),
        cost_estimate=cost(4 * dim * slots * half, 12 * dim * slots),
        name="target_grad",
    )(near, far1, query, query_t, v_hot_t, n_hot, n_hot_t, mask)


def source_grad_kernel(
    t, shape, cnt_ref, neg_ref, _, far0, far1, d_hot_ref, query_ref, w_ref, source_ref, rel_ref, s_hot_ref,
    gs_mine, gs_other, drel_ref, cnt, neg, sems, o_scr,
):
    limits = Limits(t, cnt_ref, neg_ref, cnt, neg, sems)
    half = gs_mine.shape[1]
    target = mm(jnp.concatenate([far0[...], far1[...]], axis=1), d_hot_ref[...])
    o_scr[...] = target.astype(BF)
    limits.wait()
    gpos = positive_factors(shape, limits, query_ref[...], target)
    dq = make_dquery(shape, limits, gpos, o_scr, w_ref)
    drel_ref[...] = conj_times(dq, source_ref[...].astype(F32))
    gs = mm(conj_times(dq, rel_ref[...].astype(F32)), s_hot_ref[...], NT)
    gs_mine[...] = gs[:, :half]
    gs_other[...] = gs[:, half:].astype(BF)


def source_grad(t, shape, cnt, neg, after, far, d_hot, query, weight, source, rel, s_hot):
    dim, slots = rel.shape
    half = s_hot.shape[0] // 2
    sds = jax.ShapeDtypeStruct
    return pl.pallas_call(
        functools.partial(source_grad_kernel, t, shape),
        in_specs=[anywhere()] * 3 + [vmem()] * 8,
        out_specs=[vmem()] * 3,
        out_shape=[sds((dim, half), F32), sds((dim, half), BF), sds((dim, slots), BF)],
        scratch_shapes=Limits.scratch(shape) + [pltpu.VMEM((dim, slots), BF)],
        compiler_params=params(),
        cost_estimate=cost(dim * slots, dim * slots),
        name="source_grad",
    )(cnt, neg, after, *far, d_hot, query, weight, source, rel, s_hot)


def last_kernel(
    t, shape, cnt_ref, neg_ref, far0, far1, query_ref, query_t_ref, d_hot_ref, source_ref, rel_ref,
    drel_ref, dsource_ref, dterm_ref, cnt, neg, sems, o_scr, d_scr, w_scr,
):
    limits = Limits(t, cnt_ref, neg_ref, cnt, neg, sems)
    far = jnp.concatenate([far0[...], far1[...]], axis=1)
    target = mm(far, d_hot_ref[...])
    query = query_ref[...]
    gpos = target_side(shape, limits, query, query_t_ref, target, o_scr, w_scr)
    dterm_ref[...] = target_terms(shape, limits, query, gpos, w_scr, d_scr)
    dq = make_dquery(shape, limits, gpos, o_scr, w_scr)
    drel_ref[...] = conj_times(dq, source_ref[...].astype(F32))
    dsource_ref[...] = conj_times(dq, rel_ref[...].astype(F32))


def last_terms(t, shape, cnt, neg, far, query, query_t, d_hot, source, rel):
    dim, slots = query.shape
    sds = jax.ShapeDtypeStruct
    return pl.pallas_call(
        functools.partial(last_kernel, t, shape),
        in_specs=[anywhere()] * 2 + [vmem()] * 7,
        out_specs=[vmem()] * 3,
        out_shape=[sds((dim, slots), BF)] * 3,
        scratch_shapes=Limits.scratch(shape)
        + [
            pltpu.VMEM((dim, slots), BF),
            pltpu.VMEM((dim, slots), F32),
            pltpu.VMEM((shape[2], slots), BF),
        ],
        compiler_params=params(),
        cost_estimate=cost(6 * dim * slots * shape[2], 12 * dim * slots),
        name="last_terms",
    )(cnt, neg, *far, query, query_t, d_hot, source, rel)


def both_kernel(_, dsource_ref, s_hot_ref, dterm_ref, d_hot_t_ref, gs_mine, gs_other, gd_mine, gd_other):
    half = gs_mine.shape[1]
    for terms, hot, dims, mine, other in (
        (dterm_ref, d_hot_t_ref, NN, gd_mine, gd_other),
        (dsource_ref, s_hot_ref, NT, gs_mine, gs_other),
    ):
        grad = mm(terms[...], hot[...], dims)
        mine[...] = grad[:, :half]
        other[...] = grad[:, half:].astype(BF)


def both_grads(after, dsource, s_hot, dterm, d_hot_t):
    dim, slots = dterm.shape
    half = s_hot.shape[0] // 2
    sds = jax.ShapeDtypeStruct
    return pl.pallas_call(
        both_kernel,
        in_specs=[anywhere()] + [vmem()] * 4,
        out_specs=[vmem()] * 4,
        out_shape=[sds((dim, half), F32), sds((dim, half), BF)] * 2,
        compiler_params=params(),
        cost_estimate=cost(8 * dim * slots * half, 12 * dim * slots),
        name="both_grads",
    )(after, dsource, s_hot, dterm, d_hot_t)


def update_kernel(n_grads, last, *refs):
    ent_ref, state_ref, grads = refs[0], refs[1], refs[2 : 2 + n_grads]
    grad = grads[0][...].astype(F32)
    for g in grads[1:]:
        grad = grad + g[...].astype(F32)
    dim = grad.shape[0]
    state = state_ref[...] + jnp.sum(grad * grad, axis=0, keepdims=True) / dim
    new = ent_ref[...] - grad * (learn_rate / jnp.sqrt(state))
    if last:
        refs[-1][:dim] = new
        refs[-1][dim:] = jnp.broadcast_to(state, (refs[-1].shape[0] - dim, state.shape[1]))
    else:
        refs[-3][...] = new
        refs[-2][...] = state
        refs[-1][...] = new.astype(BF)


def update(ent, state, grads, after, last=False):
    dim, half = ent.shape
    sds = jax.ShapeDtypeStruct
    outs = [sds((dim, half), F32), sds((1, half), F32), sds((dim, half), BF)]
    if last:
        outs = [sds((dim + 8, half), F32)]
    return pl.pallas_call(
        functools.partial(update_kernel, len(grads), last),
        in_specs=[vmem()] * (2 + len(grads)) + [anywhere()] * len(after),
        out_specs=[vmem()] * len(outs),
        out_shape=outs,
        compiler_params=params(),
        cost_estimate=cost(10 * dim * half, 16 * dim * half),
        name="update",
    )(ent, state, *grads, *after)


def pair_kernel(a_ref, b_ref, out_ref):
    out_ref[...] = (a_ref[...] + b_ref[...].astype(F32)).astype(out_ref.dtype)


def sum_pair(a, b, dtype=BF):
    return pl.pallas_call(
        pair_kernel,
        in_specs=[vmem()] * 2,
        out_specs=vmem(),
        out_shape=jax.ShapeDtypeStruct(a.shape, dtype),
        compiler_params=params(),
        name="sum_pair",
    )(a, b)


def held_kernel(x_ref, *refs):
    pass


def held(x, after):
    return pl.pallas_call(
        held_kernel,
        in_specs=[anywhere()] * (1 + len(after)),
        out_specs=anywhere(),
        out_shape=jax.ShapeDtypeStruct(x.shape, x.dtype),
        input_output_aliases={0: 0},
        compiler_params=params(),
        name="held",
    )(x, *after)


def whole_kernel(mine, theirs, ent_out, state_out, token):
    token[...] = jnp.zeros_like(token)
    dim, rows = ent_out.shape
    half = rows // 2
    edge = place()[2]
    for core, part in ((edge, mine), (1 - edge, theirs)):
        at = pl.ds(pl.multiple_of(core * half, half), half)
        ent_out[:, at] = part[:dim]
        state_out[:, at] = part[dim : dim + 1]


def whole_partition(mine, theirs):
    dim, half = mine.shape[0] - 8, mine.shape[1]
    return pl.pallas_call(
        whole_kernel,
        in_specs=[vmem()] * 2,
        out_specs=[vmem()] * 3,
        out_shape=[
            jax.ShapeDtypeStruct((dim, 2 * half), F32),
            jax.ShapeDtypeStruct((1, 2 * half), F32),
            jax.ShapeDtypeStruct((8, 128), F32),
        ],
        compiler_params=params(),
        name="whole_partition",
    )(mine, theirs)


def first_column(owner, core, w):
    return pl.multiple_of((2 * owner + core) * w, w)


def pieces_kernel(t, nz, same, ids_ref, drel_ref, acc_ref, *refs):
    mine, other = refs[-nz - 1 : -1], refs[-1]
    w = other.shape[2]
    z, x, edge = place()
    drel = drel_ref[...]
    for k in range(nz):
        owner = 2 * lax.bitwise_xor(z, k) + (x if same else 1 - x)
        at = [first_column(owner, core, w) for core in (edge, 1 - edge)]
        hot = jnp.concatenate([one_hot(ids_ref, t, w, lambda i, lo=lo: i - lo) for lo in at], axis=0)
        part = mm(drel, hot, NT)
        mine[k][...] = acc_ref[:, pl.ds(at[0], w)] + part[:, :w]
        other[k] = (acc_ref[:, pl.ds(at[1], w)] + part[:, w:]).astype(BF)


def pieces(t, n, same, rel_ids, drel, acc, after):
    dim, rels = acc.shape
    w = rels // (2 * n)
    sds = jax.ShapeDtypeStruct
    out = pl.pallas_call(
        functools.partial(pieces_kernel, t, n // 2, same),
        in_specs=[vmem()] * 3 + [anywhere()] * len(after),
        out_specs=[vmem()] * (n // 2 + 1),
        out_shape=[sds((dim, w), F32)] * (n // 2) + [sds((n // 2, dim, w), BF)],
        compiler_params=params(),
        cost_estimate=cost(dim * rels * drel.shape[1], 4 * dim * rels),
        name="pieces",
    )(rel_ids, drel, acc, *after)
    return out[:-1], out[-1]


def add_kernel(n, *refs):
    for k in range(n):
        refs[n + 1 + k][...] = (refs[k][...] + refs[n][k].astype(F32)).astype(BF)


def add_each(mine, theirs):
    n = len(mine)
    return pl.pallas_call(
        functools.partial(add_kernel, n),
        in_specs=[vmem()] * (n + 1),
        out_specs=[vmem()] * n,
        out_shape=[jax.ShapeDtypeStruct(x.shape, BF) for x in mine],
        compiler_params=params(),
        name="add_each",
    )(*mine, theirs)


def sum_kernel(k, count, mine, theirs, *refs):
    total = mine[...] + theirs[k].astype(F32)
    for r in refs[:count]:
        total = total + r[...].astype(F32)
    refs[-1][...] = total.astype(BF)


def sum_piece(k, mine, theirs, parts, after):
    return pl.pallas_call(
        functools.partial(sum_kernel, k, len(parts)),
        in_specs=[vmem()] * (2 + len(parts)) + [anywhere()] * len(after),
        out_specs=vmem(),
        out_shape=jax.ShapeDtypeStruct(mine.shape, BF),
        compiler_params=params(),
        name="sum_piece",
    )(mine, theirs, *parts, *after)


def stacked_kernel(*refs):
    for i in range(refs[-1].shape[0]):
        refs[-1][i] = refs[i][...]


def stacked(parts, after):
    return pl.pallas_call(
        stacked_kernel,
        in_specs=[vmem()] * len(parts) + [anywhere()] * len(after),
        out_specs=vmem(),
        out_shape=jax.ShapeDtypeStruct((len(parts), *parts[0].shape), parts[0].dtype),
        compiler_params=params(),
        name="stacked",
    )(*parts, *after)


def relnew_kernel(nz, kinds, count, first, last, rel_ref, state_ref, *refs):
    arrays = refs[:count]
    rel_out, state_to, buf, sems = refs[-5:-1] if last else refs[-4:]
    state_out = refs[-1] if last else state_to
    w = buf.shape[2]
    state_out[...] = refs[count + (0 if first else 1)][...]
    z, x, edge = place()
    copies = []
    for i, (k, same, own, source, index) in enumerate(kinds):
        owner = 2 * lax.bitwise_xor(z, k) + (x if same else 1 - x)
        at = pl.ds(first_column(owner, edge if own else 1 - edge, w), w)
        grad = (arrays[source][...] if index is None else arrays[source][index]).astype(F32)
        state = state_ref[:, at] + jnp.sum(grad * grad, axis=0, keepdims=True) / grad.shape[0]
        state_out[:, at] = state
        buf[i] = rel_ref[:, at] - grad * (learn_rate / jnp.sqrt(state))
        copy = pltpu.make_async_copy(buf.at[i], rel_out.at[:, at], sems.at[i])
        copy.start()
        copies.append(copy)
    if last:
        copy = pltpu.make_async_copy(state_out, state_to, sems.at[len(kinds)])
        copy.start()
        copies.append(copy)
    for copy in copies:
        copy.wait()


def relnew(nz, relations, state, groups, before, last=False):
    dim, rels = relations.shape
    w = rels // (4 * nz)
    kinds, arrays = [], []
    for ks, same, own, parts in groups:
        one = not isinstance(parts, list)
        for i, k in enumerate(ks):
            kinds.append((k, same, own, len(arrays) + (0 if one else i), i if one else None))
        arrays += [parts] if one else parts
    count = len(kinds)
    start = [state] if before is None else list(before)
    return pl.pallas_call(
        functools.partial(relnew_kernel, nz, tuple(kinds), len(arrays), before is None, last),
        in_specs=[vmem()] * (2 + len(arrays))
        + ([anywhere()] if before else [])
        + [vmem()],
        out_specs=[anywhere(), anywhere() if last else vmem()],
        out_shape=[jax.ShapeDtypeStruct((dim, rels), F32), jax.ShapeDtypeStruct((1, rels), F32)],
        input_output_aliases={2 + len(arrays): 0} if before else {},
        scratch_shapes=[pltpu.VMEM((count, dim, w), F32), pltpu.SemaphoreType.DMA((count + 1,))]
        + ([pltpu.VMEM((1, rels), F32)] if last else []),
        compiler_params=params(),
        cost_estimate=cost(dim, dim),
        name="relnew",
    )(relations, state, *arrays, *start)


def relation_update(t, rel_ids, drel, acc, relations, state, send, finish):
    n = lax.axis_size("dom")
    dim, rels = relations.shape
    if n < 4 or n & (n - 1) or rels % (256 * n):
        total = lax.psum(relsum(t, rel_ids, drel, acc, rels), ("dom", "edge"))
        state = state + jnp.mean(total * total, axis=0)
        return relations - learn_rate * total / jnp.sqrt(state)[None, :], state, finish(send(drel), [])
    nz = n // 2
    mine_x, other_x = pieces(t, n, False, rel_ids, drel, acc, [])
    grads = send(other_x)
    mine_s, other_s = pieces(t, n, True, rel_ids, drel, acc, [other_x])
    to_x = add_each(mine_x, across(other_x))
    theirs = across(other_s)
    down = range(nz - 1, -1, -1)
    from_x = {k: swapped(to_x[k], 1) for k in down}
    turned = {
        k: sum_piece(k, mine_s[k], theirs, [from_x[k]], grads[1:2] if k == nz - 1 else [])
        for k in down[:-1]
    }
    from_z = [swapped(turned[k], 2 * k) for k in down[:-1]]
    done = finish(grads, [turned[nz - 1]])
    summed = sum_piece(0, mine_s[0], theirs, [from_x[0]] + from_z, [])
    got = [summed if k == 0 else swapped(summed, 2 * k) for k in range(nz)]
    got_x = [swapped(piece, 1) for piece in got]
    state = state.reshape(1, rels)
    ks = [0, *down[:-1]]
    mine = [got[k] for k in ks]
    mine_x = [got_x[k] for k in ks]
    there = across(stacked(mine, [done[2]]))
    new = relnew(nz, relations, state, [(ks, True, True, mine)], None)
    there_x = across(stacked(mine_x, [new[1]]))
    groups = [(ks, True, False, there), (ks, False, True, mine_x)]
    new = relnew(nz, relations, state, groups, new)
    groups = [(ks, False, False, there_x)]
    rel_new, state_new = relnew(nz, relations, state, groups, new, last=True)
    return rel_new, state_new.reshape(rels), done


def on_device(
    entities,
    entity_state,
    relations,
    relation_state,
    src_rows,
    rel_ids,
    dst_rows,
    counts,
    neg_blocks,
):
    rounds = src_rows.shape[0]
    rels = relations.shape[1]
    shape = src_rows.shape
    cnt, neg = counts.T, neg_blocks.T
    g_mine, g_other, drel, rel16, ent, state = first_round(
        cnt, neg, src_rows, dst_rows, rel_ids, entities, entity_state.reshape(1, -1), relations
    )
    acc = relsum(0, rel_ids, drel, None, rels)
    ent, state, low = update(ent, state, [g_mine, across(g_other)], [])
    rel = relvec(1, rel_ids, rel16)
    for t in range(1, rounds):
        far = shifted(low, -t)
        own = (low, across(low))
        query, query_t, source, s_hot, d_hot, *hots = source_side(
            t, shape, cnt, neg, src_rows, dst_rows, own, rel
        )
        far = held(far, [query, acc])
        far = (far, across(far))
        if t == rounds - 1:
            break
        near = near_products(query_t, far[0])
        gd_mine, gd_other, weight = target_grad(near, far[1], query, query_t, *hots)
        gd = sum_pair(gd_mine, across(gd_other))
        gs_mine, gs_other, drel = source_grad(
            t, shape, cnt, neg, gd, far, d_hot, query, weight, source, rel, s_hot
        )
        acc = relsum(t, rel_ids, drel, acc, rels)
        rel = relvec(t + 1, rel_ids, rel16)
        grads = [sum_pair(gs_mine, shifted(gd, t), F32), across(gs_other)]
        ent, state, low = update(ent, state, grads, [rel])
    drel, dsource, dterm = last_terms(t, shape, cnt, neg, far, query, query_t, d_hot, source, rel)

    def send(after):
        gs_mine, gs_other, gd_mine, gd_other = both_grads(after, dsource, s_hot, dterm, hots[0])
        gd = sum_pair(gd_mine, across(gd_other))
        return [gs_mine, across(gs_other), shifted(gd, t)]

    def finish(grads, after):
        (mine,) = update(ent, state, grads, after, last=True)
        return whole_partition(mine, across(mine))

    rel_new, rel_state, done = relation_update(
        t, rel_ids, drel, acc, relations, relation_state, send, finish
    )
    return (done[0], done[1].reshape(-1), rel_new, rel_state)


def solution(mesh):
    return jax.shard_map(
        on_device,
        mesh=mesh,
        in_specs=(
            P(None, ("groups", "dom")),
            P(("groups", "dom")),
            P(None, "groups"),
            P("groups"),
            P(None, ("groups", "dom", "edge"), None),
            P(None, ("groups", "dom", "edge"), None),
            P(None, ("groups", "dom", "edge"), None),
            P(None, ("groups", "dom", "edge")),
            P(None, ("groups", "dom", "edge")),
        ),
        out_specs=(
            P(None, ("groups", "dom")),
            P(("groups", "dom")),
            P(None, "groups"),
            P("groups"),
        ),
        check_vma=False,
    )
```

```python
import functools

import jax
import jax.numpy as jnp
from jax import lax
from jax.experimental import pallas as pl
from jax.experimental.pallas import tpu as pltpu
from jax.sharding import PartitionSpec as P

learn_rate = 0.1
BF = jnp.bfloat16
F32 = jnp.float32
VMEM_LIMIT = 24 * 1024 * 1024
NN = (((1,), (0,)), ((), ()))
NT = (((1,), (1,)), ((), ()))
TN = (((0,), (0,)), ((), ()))


def mm(a, b, dims=NN):
    return lax.dot_general(a, b, dims, preferred_element_type=F32)


def vmem():
    return pl.BlockSpec(memory_space=pltpu.VMEM)


def smem():
    return pl.BlockSpec(memory_space=pltpu.SMEM)


def anywhere():
    return pl.BlockSpec(memory_space=pl.ANY)


def in_hbm(x):
    return pltpu.with_memory_space_constraint(x, pltpu.HBM)


def cost(flops, size):
    return pl.CostEstimate(flops=flops, bytes_accessed=size, transcendentals=0)


def params():
    return pltpu.CompilerParams(vmem_limit_bytes=VMEM_LIMIT)


def shifted(x, by):
    n = lax.axis_size("dom")
    return lax.ppermute(x, "dom", [(i, (i + by) % n) for i in range(n)])


def swapped(x, bits):
    n = lax.axis_size("dom")
    return lax.ppermute(x, "dom", [(i, i ^ bits) for i in range(n)])


def across(x):
    return lax.ppermute(x, "edge", [(0, 1), (1, 0)])


def one_hot(rows_ref, t, count, base):
    blocks, width = rows_ref.shape[1:]
    at = lax.broadcasted_iota(jnp.int32, (count, width), 0)
    idx = rows_ref[t]
    return jnp.concatenate(
        [
            jnp.where(at == base(idx[b : b + 1, :]), 1.0, 0.0).astype(BF)
            for b in range(blocks)
        ],
        axis=1,
    )


def relvec_kernel(t, ids_ref, rel_ref, out_ref):
    rels = rel_ref.shape[1]
    tile = min(rels, 512)
    out = None
    for lo in range(0, rels, tile):
        hot = one_hot(ids_ref, t, tile, lambda i, lo=lo: i - lo)
        part = mm(rel_ref[:, lo : lo + tile], hot)
        out = part if out is None else out + part
    out_ref[...] = out.astype(BF)


def relvec(t, rel_ids, rel16):
    width, rels = rel16.shape
    slots = rel_ids.shape[1] * rel_ids.shape[2]
    return pl.pallas_call(
        functools.partial(relvec_kernel, t),
        in_specs=[vmem()] * 2,
        out_specs=vmem(),
        out_shape=jax.ShapeDtypeStruct((width, slots), BF),
        compiler_params=params(),
        cost_estimate=cost(width * slots, width * slots),
        name="relvec",
    )(rel_ids, rel16)


def relsum_kernel(t, first, ids_ref, drel_ref, *refs):
    out_ref = refs[-1]
    rels = out_ref.shape[1]
    tile = min(rels, 512)
    drel = drel_ref[...]
    for lo in range(0, rels, tile):
        hot = one_hot(ids_ref, t, tile, lambda i, lo=lo: i - lo)
        part = mm(drel, hot, NT)
        out_ref[:, lo : lo + tile] = part if first else refs[0][:, lo : lo + tile] + part


def relsum(t, rel_ids, drel, acc, rels):
    width, slots = drel.shape
    ins = [rel_ids, drel] + ([] if acc is None else [acc])
    return pl.pallas_call(
        functools.partial(relsum_kernel, t, acc is None),
        in_specs=[vmem()] * len(ins),
        out_specs=vmem(),
        out_shape=jax.ShapeDtypeStruct((width, rels), F32),
        input_output_aliases={} if acc is None else {2: 0},
        compiler_params=params(),
        cost_estimate=cost(width * slots, width * slots),
        name="relsum",
    )(*ins)


class Limits:
    scratch = lambda shape: [
        pltpu.SMEM((shape[1], shape[0]), jnp.int32),
        pltpu.SMEM((shape[1], shape[0]), jnp.int32),
        pltpu.SemaphoreType.DMA((2,)),
    ]

    def __init__(self, t, from_cnt, from_neg, cnt, neg, sems):
        self.t, self.cnt, self.neg = t, cnt, neg
        self.copies = [
            pltpu.make_async_copy(from_cnt, cnt, sems.at[0]),
            pltpu.make_async_copy(from_neg, neg, sems.at[1]),
        ]
        for copy in self.copies:
            copy.start()

    def wait(self):
        for copy in self.copies:
            copy.wait()

    def count(self, b):
        return self.cnt[b, self.t]

    def negative(self, b):
        return self.neg[b, self.t]


def place():
    dom = lax.axis_index("dom")
    return dom // 2, lax.rem(dom, 2), lax.axis_index("edge")


def localize(edge, half):
    def local(idx):
        moved = idx + edge * half
        return jnp.where(moved >= 2 * half, moved - 2 * half, moved)

    return local


def halves(x):
    hd = x.shape[0] // 2
    return x[:hd], x[hd:]


def make_query(source, rel):
    (s_re, s_im), (w_re, w_im) = halves(source), halves(rel)
    return jnp.concatenate(
        [s_re * w_re - s_im * w_im, s_re * w_im + s_im * w_re], axis=0
    ).astype(BF)


def conj_times(dq, v):
    (dq_re, dq_im), (v_re, v_im) = halves(dq), halves(v)
    return jnp.concatenate(
        [dq_re * v_re + dq_im * v_im, dq_im * v_re - dq_re * v_im], axis=0
    ).astype(BF)


def positive_factors(shape, limits, query, target):
    _, blocks, width = shape
    pos = jnp.sum(query.astype(F32) * target, axis=0, keepdims=True)
    lane = lax.broadcasted_iota(jnp.int32, (1, width), 1)
    valid = jnp.concatenate(
        [jnp.where(lane < limits.count(b), 1.0, 0.0) for b in range(blocks)], axis=1
    )
    return -jax.nn.sigmoid(-pos) * valid


def target_side(shape, limits, query, query_t, target, o_ref, w_ref):
    _, blocks, width = shape
    lanes = lambda b: pl.ds(pl.multiple_of(b * width, width), width)
    count = limits.count
    o_ref[...] = target.astype(BF)
    limits.wait()
    gpos = positive_factors(shape, limits, query, target)
    row_i = lax.broadcasted_iota(jnp.int32, (width, width), 0)
    col_j = lax.broadcasted_iota(jnp.int32, (width, width), 1)
    for b in range(blocks):
        nb = limits.negative(b)
        neg = o_ref[:, lanes(nb)]
        at = slice(b * width, (b + 1) * width)
        scores = mm(query[:, at], neg, TN) if query_t is None else mm(query_t[at], neg)
        keep = jnp.logical_and(row_i < count(b), col_j < count(nb))
        w_ref[:, at] = jnp.where(keep, jax.nn.sigmoid(scores) / width, 0.0).astype(BF)
    return gpos


def target_terms(shape, limits, query, gpos, w_ref, d_ref):
    _, blocks, width = shape
    d_ref[...] = gpos * query.astype(F32)
    for b in range(blocks):
        at = slice(b * width, (b + 1) * width)
        to = pl.ds(pl.multiple_of(limits.negative(b) * width, width), width)
        d_ref[:, to] += mm(query[:, at], w_ref[:, at])
    return d_ref[...].astype(BF)


def make_dquery(shape, limits, gpos, o_ref, w_ref):
    _, blocks, width = shape
    lanes = lambda b: pl.ds(pl.multiple_of(b * width, width), width)
    out = []
    for b in range(blocks):
        nb = limits.negative(b)
        at = slice(b * width, (b + 1) * width)
        own = gpos[:, at] * o_ref[:, at].astype(F32)
        out.append(own + mm(o_ref[:, lanes(nb)], w_ref[:, at], NT))
    return jnp.concatenate(out, axis=1)


def first_kernel(
    shape, cnt_ref, neg_ref, src_ref, dst_ref, ids_ref, ent_ref, state_ref, rel_ref,
    g_mine, g_other, drel_ref, rel16_ref, ent_mine, state_mine,
    cnt, neg, lim_sems, src, dst, ids, ent, state, rel_buf, o_scr, d_scr, w_scr, in_sems, sems,
):
    rels = rel_buf.shape[1]
    tile = min(rels, 512)
    spans = range(0, rels, tile)
    inputs = [
        pltpu.make_async_copy(there, here, in_sems.at[i])
        for i, (there, here) in enumerate(
            [(src_ref.at[:1], src), (dst_ref.at[:1], dst), (ids_ref.at[:1], ids), (ent_ref, ent), (state_ref, state)]
        )
    ]
    loads = [
        pltpu.make_async_copy(
            rel_ref.at[:, lo : lo + tile], rel_buf.at[:, lo : lo + tile], sems.at[i]
        )
        for i, lo in enumerate(spans)
    ]
    for load in inputs:
        load.start()
    limits = Limits(0, cnt_ref, neg_ref, cnt, neg, lim_sems)
    for load in loads:
        load.start()
    half = ent.shape[1] // 2
    _, _, edge = place()
    local = localize(edge, half)
    inputs[0].wait()
    s_hot = one_hot(src, 0, 2 * half, local)
    inputs[1].wait()
    d_hot = one_hot(dst, 0, 2 * half, local)
    inputs[2].wait()
    ids_hot = [one_hot(ids, 0, tile, lambda i, lo=lo: i - lo) for lo in spans]
    inputs[3].wait()
    inputs[4].wait()
    mine = pl.ds(pl.multiple_of(edge * half, half), half)
    ent_mine[...] = ent[:, mine]
    state_mine[...] = state[:, mine]
    table = jnp.concatenate(
        [ent[:, pl.ds(pl.multiple_of(h * half, half), half)].astype(BF) for h in (edge, 1 - edge)],
        axis=1,
    )
    source = mm(table, s_hot)
    target = mm(table, d_hot)
    rel = None
    for load, lo, hot in zip(loads, spans, ids_hot):
        load.wait()
        low = rel_buf[:, lo : lo + tile].astype(BF)
        rel16_ref[:, lo : lo + tile] = low
        part = mm(low, hot)
        rel = part if rel is None else rel + part
    query = make_query(source, rel)
    gpos = target_side(shape, limits, query, None, target, o_scr, w_scr)
    dq = make_dquery(shape, limits, gpos, o_scr, w_scr)
    drel_ref[...] = conj_times(dq, source)
    total = mm(conj_times(dq, rel), s_hot, NT) + mm(
        target_terms(shape, limits, query, gpos, w_scr, d_scr), d_hot, NT
    )
    g_mine[...] = total[:, :half]
    g_other[...] = total[:, half:].astype(BF)


def first_round(cnt, neg, src, dst, rel_ids, entities, state, relations):
    dim, rows = entities.shape
    rels = relations.shape[1]
    _, blocks, width = src.shape
    slots = blocks * width
    sds = jax.ShapeDtypeStruct
    return pl.pallas_call(
        functools.partial(first_kernel, src.shape),
        in_specs=[anywhere()] * 8,
        out_specs=[vmem()] * 6,
        out_shape=[
            sds((dim, rows // 2), F32),
            sds((dim, rows // 2), BF),
            sds((dim, slots), BF),
            sds((dim, rels), BF),
            sds((dim, rows // 2), F32),
            sds((1, rows // 2), F32),
        ],
        scratch_shapes=Limits.scratch(src.shape)
        + [
            pltpu.VMEM((1, blocks, width), jnp.int32),
            pltpu.VMEM((1, blocks, width), jnp.int32),
            pltpu.VMEM((1, blocks, width), jnp.int32),
            pltpu.VMEM((dim, rows), F32),
            pltpu.VMEM((1, rows), F32),
            pltpu.VMEM((dim, rels), F32),
            pltpu.VMEM((dim, slots), BF),
            pltpu.VMEM((dim, slots), F32),
            pltpu.VMEM((width, slots), BF),
            pltpu.SemaphoreType.DMA((5,)),
            pltpu.SemaphoreType.DMA((-(-rels // min(rels, 512)),)),
        ],
        compiler_params=params(),
        cost_estimate=cost(2 * dim * slots * (rels + 4 * rows), 8 * dim * rels),
        name="first_round",
    )(*(in_hbm(x) for x in (cnt, neg, src, dst, rel_ids, entities, state, relations)))


def source_kernel(t, shape, last, cnt_ref, neg_ref, src_ref, dst_ref, own0, own1, rel_ref, *refs):
    query_ref, query_t_ref, source_ref, s_hot_ref, d_hot_ref = refs[:5]
    if last:
        (d_hot_t_ref,) = refs[5:]
    else:
        v_hot_t_ref, n_hot_ref, n_hot_t_ref, mask_ref, cnt, neg, sems, d_hot_t_ref = refs[5:]
        limits = Limits(t, cnt_ref, neg_ref, cnt, neg, sems)
    _, blocks, width = shape
    half = own0.shape[1]
    local = localize(place()[2], half)
    s_hot = one_hot(src_ref, t, 2 * half, local)
    d_hot = one_hot(dst_ref, t, 2 * half, local)
    s_hot_ref[...] = s_hot
    d_hot_ref[...] = d_hot
    d_hot_t_ref[...] = d_hot.T
    source = mm(jnp.concatenate([own0[...], own1[...]], axis=1), s_hot)
    source_ref[...] = source.astype(BF)
    query = make_query(source, rel_ref[...].astype(F32))
    query_ref[...] = query
    query_t_ref[...] = query.T
    if last:
        return
    limits.wait()
    row_i = lax.broadcasted_iota(jnp.int32, (width, width), 0)
    col_j = lax.broadcasted_iota(jnp.int32, (width, width), 1)
    slot = lax.broadcasted_iota(jnp.int32, (width, 2 * half), 0)
    for b in range(blocks):
        nb = limits.negative(b)
        at = slice(b * width, (b + 1) * width)
        there = pl.ds(pl.multiple_of(nb * width, width), width)
        n_hot_ref[:, at] = d_hot_ref[:, there]
        n_hot_t_ref[at] = d_hot_t_ref[there, :]
        keep = jnp.logical_and(row_i < limits.count(b), col_j < limits.count(nb))
        mask_ref[:, at] = jnp.where(keep, 1.0 / width, 0.0)
        hot = d_hot_t_ref[at].astype(F32)
        v_hot_t_ref[at] = jnp.where(slot < limits.count(b), hot, 0.0).astype(BF)


def source_side(t, shape, cnt, neg, src, dst, own, rel):
    dim, slots = rel.shape
    width = shape[2]
    rows = 2 * own[0].shape[1]
    last = t == shape[0] - 1
    sds = lambda *shape: jax.ShapeDtypeStruct(shape, BF)
    outs = [sds(dim, slots), sds(slots, dim), sds(dim, slots), sds(rows, slots), sds(rows, slots)]
    if last:
        outs += [sds(slots, rows)]
    else:
        outs += [sds(slots, rows), sds(rows, slots), sds(slots, rows)]
        outs += [jax.ShapeDtypeStruct((width, slots), F32)]
    return pl.pallas_call(
        functools.partial(source_kernel, t, shape, last),
        in_specs=[anywhere()] * 2 + [vmem()] * 5,
        out_specs=[vmem()] * len(outs),
        out_shape=outs,
        scratch_shapes=[] if last else Limits.scratch(shape) + [pltpu.VMEM((slots, rows), BF)],
        compiler_params=params(),
        cost_estimate=cost(dim * slots, dim * slots),
        name="source_side",
    )(cnt, neg, src, dst, *own, rel)


def near_kernel(query_t_ref, far0, out_ref):
    out_ref[...] = mm(query_t_ref[...], far0[...])


def near_products(query_t, far0):
    slots, half = query_t.shape[0], far0.shape[1]
    return pl.pallas_call(
        near_kernel,
        in_specs=[vmem()] * 2,
        out_specs=vmem(),
        out_shape=jax.ShapeDtypeStruct((slots, half), F32),
        compiler_params=params(),
        cost_estimate=cost(slots * half, slots * half),
        name="near_products",
    )(query_t, far0)


def target_kernel(
    near, far1, query_ref, query_t_ref, v_hot_t_ref, n_hot_ref, n_hot_t_ref, mask_ref,
    gd_mine, gd_other, w_ref,
):
    width, slots = mask_ref.shape
    half = far1.shape[1]
    products = jnp.concatenate([near[...], mm(query_t_ref[...], far1[...])], axis=1)
    high = products.astype(BF)
    low = (products - high.astype(F32)).astype(BF)
    factors = []
    for lo in range(0, slots, width):
        at = slice(lo, lo + width)
        n_hot = n_hot_ref[:, at]
        scores = mm(high[at], n_hot) + mm(low[at], n_hot)
        weight = (jax.nn.sigmoid(scores) * mask_ref[:, at]).astype(BF)
        w_ref[:, at] = weight
        positive = jax.nn.sigmoid(-products[at]) * v_hot_t_ref[at].astype(F32)
        factors.append((mm(weight, n_hot_t_ref[at]) - positive).astype(BF))
    gd = mm(query_ref[...], jnp.concatenate(factors, axis=0))
    gd_mine[...] = gd[:, :half]
    gd_other[...] = gd[:, half:].astype(BF)


def target_grad(near, far1, query, query_t, v_hot_t, n_hot, n_hot_t, mask):
    dim, slots = query.shape
    half = far1.shape[1]
    sds = jax.ShapeDtypeStruct
    return pl.pallas_call(
        target_kernel,
        in_specs=[vmem()] * 8,
        out_specs=[vmem()] * 3,
        out_shape=[sds((dim, half), F32), sds((dim, half), BF), sds(mask.shape, BF)],
        compiler_params=params(),
        cost_estimate=cost(4 * dim * slots * half, 12 * dim * slots),
        name="target_grad",
    )(near, far1, query, query_t, v_hot_t, n_hot, n_hot_t, mask)


def source_grad_kernel(
    t, shape, cnt_ref, neg_ref, _, far0, far1, d_hot_ref, query_ref, w_ref, source_ref, rel_ref, s_hot_ref,
    gs_mine, gs_other, drel_ref, cnt, neg, sems, o_scr,
):
    limits = Limits(t, cnt_ref, neg_ref, cnt, neg, sems)
    half = gs_mine.shape[1]
    target = mm(jnp.concatenate([far0[...], far1[...]], axis=1), d_hot_ref[...])
    o_scr[...] = target.astype(BF)
    limits.wait()
    gpos = positive_factors(shape, limits, query_ref[...], target)
    dq = make_dquery(shape, limits, gpos, o_scr, w_ref)
    drel_ref[...] = conj_times(dq, source_ref[...].astype(F32))
    gs = mm(conj_times(dq, rel_ref[...].astype(F32)), s_hot_ref[...], NT)
    gs_mine[...] = gs[:, :half]
    gs_other[...] = gs[:, half:].astype(BF)


def source_grad(t, shape, cnt, neg, after, far, d_hot, query, weight, source, rel, s_hot):
    dim, slots = rel.shape
    half = s_hot.shape[0] // 2
    sds = jax.ShapeDtypeStruct
    return pl.pallas_call(
        functools.partial(source_grad_kernel, t, shape),
        in_specs=[anywhere()] * 3 + [vmem()] * 8,
        out_specs=[vmem()] * 3,
        out_shape=[sds((dim, half), F32), sds((dim, half), BF), sds((dim, slots), BF)],
        scratch_shapes=Limits.scratch(shape) + [pltpu.VMEM((dim, slots), BF)],
        compiler_params=params(),
        cost_estimate=cost(dim * slots, dim * slots),
        name="source_grad",
    )(cnt, neg, after, *far, d_hot, query, weight, source, rel, s_hot)


def last_kernel(
    t, shape, cnt_ref, neg_ref, far0, far1, query_ref, query_t_ref, d_hot_ref, source_ref, rel_ref,
    drel_ref, dsource_ref, dterm_ref, cnt, neg, sems, o_scr, d_scr, w_scr,
):
    limits = Limits(t, cnt_ref, neg_ref, cnt, neg, sems)
    far = jnp.concatenate([far0[...], far1[...]], axis=1)
    target = mm(far, d_hot_ref[...])
    query = query_ref[...]
    gpos = target_side(shape, limits, query, query_t_ref, target, o_scr, w_scr)
    dterm_ref[...] = target_terms(shape, limits, query, gpos, w_scr, d_scr)
    dq = make_dquery(shape, limits, gpos, o_scr, w_scr)
    drel_ref[...] = conj_times(dq, source_ref[...].astype(F32))
    dsource_ref[...] = conj_times(dq, rel_ref[...].astype(F32))


def last_terms(t, shape, cnt, neg, far, query, query_t, d_hot, source, rel):
    dim, slots = query.shape
    sds = jax.ShapeDtypeStruct
    return pl.pallas_call(
        functools.partial(last_kernel, t, shape),
        in_specs=[anywhere()] * 2 + [vmem()] * 7,
        out_specs=[vmem()] * 3,
        out_shape=[sds((dim, slots), BF)] * 3,
        scratch_shapes=Limits.scratch(shape)
        + [
            pltpu.VMEM((dim, slots), BF),
            pltpu.VMEM((dim, slots), F32),
            pltpu.VMEM((shape[2], slots), BF),
        ],
        compiler_params=params(),
        cost_estimate=cost(6 * dim * slots * shape[2], 12 * dim * slots),
        name="last_terms",
    )(cnt, neg, *far, query, query_t, d_hot, source, rel)


def both_kernel(_, dsource_ref, s_hot_ref, dterm_ref, d_hot_t_ref, gs_mine, gs_other, gd_mine, gd_other):
    half = gs_mine.shape[1]
    for terms, hot, dims, mine, other in (
        (dterm_ref, d_hot_t_ref, NN, gd_mine, gd_other),
        (dsource_ref, s_hot_ref, NT, gs_mine, gs_other),
    ):
        grad = mm(terms[...], hot[...], dims)
        mine[...] = grad[:, :half]
        other[...] = grad[:, half:].astype(BF)


def both_grads(after, dsource, s_hot, dterm, d_hot_t):
    dim, slots = dterm.shape
    half = s_hot.shape[0] // 2
    sds = jax.ShapeDtypeStruct
    return pl.pallas_call(
        both_kernel,
        in_specs=[anywhere()] + [vmem()] * 4,
        out_specs=[vmem()] * 4,
        out_shape=[sds((dim, half), F32), sds((dim, half), BF)] * 2,
        compiler_params=params(),
        cost_estimate=cost(8 * dim * slots * half, 12 * dim * slots),
        name="both_grads",
    )(after, dsource, s_hot, dterm, d_hot_t)


def update_kernel(n_grads, last, *refs):
    ent_ref, state_ref, grads = refs[0], refs[1], refs[2 : 2 + n_grads]
    grad = grads[0][...].astype(F32)
    for g in grads[1:]:
        grad = grad + g[...].astype(F32)
    dim = grad.shape[0]
    state = state_ref[...] + jnp.sum(grad * grad, axis=0, keepdims=True) / dim
    new = ent_ref[...] - grad * (learn_rate / jnp.sqrt(state))
    if last:
        refs[-1][:dim] = new
        refs[-1][dim:] = jnp.broadcast_to(state, (refs[-1].shape[0] - dim, state.shape[1]))
    else:
        refs[-3][...] = new
        refs[-2][...] = state
        refs[-1][...] = new.astype(BF)


def update(ent, state, grads, after, last=False):
    dim, half = ent.shape
    sds = jax.ShapeDtypeStruct
    outs = [sds((dim, half), F32), sds((1, half), F32), sds((dim, half), BF)]
    if last:
        outs = [sds((dim + 8, half), F32)]
    return pl.pallas_call(
        functools.partial(update_kernel, len(grads), last),
        in_specs=[vmem()] * (2 + len(grads)) + [anywhere()] * len(after),
        out_specs=[vmem()] * len(outs),
        out_shape=outs,
        compiler_params=params(),
        cost_estimate=cost(10 * dim * half, 16 * dim * half),
        name="update",
    )(ent, state, *grads, *after)


def pair_kernel(a_ref, b_ref, out_ref):
    out_ref[...] = (a_ref[...] + b_ref[...].astype(F32)).astype(out_ref.dtype)


def sum_pair(a, b, dtype=BF):
    return pl.pallas_call(
        pair_kernel,
        in_specs=[vmem()] * 2,
        out_specs=vmem(),
        out_shape=jax.ShapeDtypeStruct(a.shape, dtype),
        compiler_params=params(),
        name="sum_pair",
    )(a, b)


def held_kernel(x_ref, *refs):
    pass


def held(x, after):
    return pl.pallas_call(
        held_kernel,
        in_specs=[anywhere()] * (1 + len(after)),
        out_specs=anywhere(),
        out_shape=jax.ShapeDtypeStruct(x.shape, x.dtype),
        input_output_aliases={0: 0},
        compiler_params=params(),
        name="held",
    )(x, *after)


def whole_kernel(mine, theirs, ent_out, state_out, token):
    token[...] = jnp.zeros_like(token)
    dim, rows = ent_out.shape
    half = rows // 2
    edge = place()[2]
    for core, part in ((edge, mine), (1 - edge, theirs)):
        at = pl.ds(pl.multiple_of(core * half, half), half)
        ent_out[:, at] = part[:dim]
        state_out[:, at] = part[dim : dim + 1]


def whole_partition(mine, theirs):
    dim, half = mine.shape[0] - 8, mine.shape[1]
    return pl.pallas_call(
        whole_kernel,
        in_specs=[vmem()] * 2,
        out_specs=[vmem()] * 3,
        out_shape=[
            jax.ShapeDtypeStruct((dim, 2 * half), F32),
            jax.ShapeDtypeStruct((1, 2 * half), F32),
            jax.ShapeDtypeStruct((8, 128), F32),
        ],
        compiler_params=params(),
        name="whole_partition",
    )(mine, theirs)


def first_column(owner, core, w):
    return pl.multiple_of((2 * owner + core) * w, w)


def pieces_kernel(t, nz, same, ids_ref, drel_ref, acc_ref, *refs):
    mine, other = refs[-nz - 1 : -1], refs[-1]
    w = other.shape[2]
    z, x, edge = place()
    drel = drel_ref[...]
    for k in range(nz):
        owner = 2 * lax.bitwise_xor(z, k) + (x if same else 1 - x)
        at = [first_column(owner, core, w) for core in (edge, 1 - edge)]
        hot = jnp.concatenate([one_hot(ids_ref, t, w, lambda i, lo=lo: i - lo) for lo in at], axis=0)
        part = mm(drel, hot, NT)
        mine[k][...] = acc_ref[:, pl.ds(at[0], w)] + part[:, :w]
        other[k] = (acc_ref[:, pl.ds(at[1], w)] + part[:, w:]).astype(BF)


def pieces(t, n, same, rel_ids, drel, acc, after):
    dim, rels = acc.shape
    w = rels // (2 * n)
    sds = jax.ShapeDtypeStruct
    out = pl.pallas_call(
        functools.partial(pieces_kernel, t, n // 2, same),
        in_specs=[vmem()] * 3 + [anywhere()] * len(after),
        out_specs=[vmem()] * (n // 2 + 1),
        out_shape=[sds((dim, w), F32)] * (n // 2) + [sds((n // 2, dim, w), BF)],
        compiler_params=params(),
        cost_estimate=cost(dim * rels * drel.shape[1], 4 * dim * rels),
        name="pieces",
    )(rel_ids, drel, acc, *after)
    return out[:-1], out[-1]


def add_kernel(n, *refs):
    for k in range(n):
        refs[n + 1 + k][...] = (refs[k][...] + refs[n][k].astype(F32)).astype(BF)


def add_each(mine, theirs):
    n = len(mine)
    return pl.pallas_call(
        functools.partial(add_kernel, n),
        in_specs=[vmem()] * (n + 1),
        out_specs=[vmem()] * n,
        out_shape=[jax.ShapeDtypeStruct(x.shape, BF) for x in mine],
        compiler_params=params(),
        name="add_each",
    )(*mine, theirs)


def sum_kernel(k, count, mine, theirs, *refs):
    total = mine[...] + theirs[k].astype(F32)
    for r in refs[:count]:
        total = total + r[...].astype(F32)
    refs[-1][...] = total.astype(BF)


def sum_piece(k, mine, theirs, parts, after):
    return pl.pallas_call(
        functools.partial(sum_kernel, k, len(parts)),
        in_specs=[vmem()] * (2 + len(parts)) + [anywhere()] * len(after),
        out_specs=vmem(),
        out_shape=jax.ShapeDtypeStruct(mine.shape, BF),
        compiler_params=params(),
        name="sum_piece",
    )(mine, theirs, *parts, *after)


def stacked_kernel(*refs):
    for i in range(refs[-1].shape[0]):
        refs[-1][i] = refs[i][...]


def stacked(parts, after):
    return pl.pallas_call(
        stacked_kernel,
        in_specs=[vmem()] * len(parts) + [anywhere()] * len(after),
        out_specs=vmem(),
        out_shape=jax.ShapeDtypeStruct((len(parts), *parts[0].shape), parts[0].dtype),
        compiler_params=params(),
        name="stacked",
    )(*parts, *after)


def relnew_kernel(nz, kinds, count, first, last, rel_ref, state_ref, *refs):
    arrays = refs[:count]
    rel_out, state_to, buf, sems = refs[-5:-1] if last else refs[-4:]
    state_out = refs[-1] if last else state_to
    w = buf.shape[2]
    state_out[...] = refs[count + (0 if first else 1)][...]
    z, x, edge = place()
    copies = []
    for i, (k, same, own, source, index) in enumerate(kinds):
        owner = 2 * lax.bitwise_xor(z, k) + (x if same else 1 - x)
        at = pl.ds(first_column(owner, edge if own else 1 - edge, w), w)
        grad = (arrays[source][...] if index is None else arrays[source][index]).astype(F32)
        state = state_ref[:, at] + jnp.sum(grad * grad, axis=0, keepdims=True) / grad.shape[0]
        state_out[:, at] = state
        buf[i] = rel_ref[:, at] - grad * (learn_rate / jnp.sqrt(state))
        copy = pltpu.make_async_copy(buf.at[i], rel_out.at[:, at], sems.at[i])
        copy.start()
        copies.append(copy)
    if last:
        copy = pltpu.make_async_copy(state_out, state_to, sems.at[len(kinds)])
        copy.start()
        copies.append(copy)
    for copy in copies:
        copy.wait()


def relnew(nz, relations, state, groups, before, last=False):
    dim, rels = relations.shape
    w = rels // (4 * nz)
    kinds, arrays = [], []
    for ks, same, own, parts in groups:
        one = not isinstance(parts, list)
        for i, k in enumerate(ks):
            kinds.append((k, same, own, len(arrays) + (0 if one else i), i if one else None))
        arrays += [parts] if one else parts
    count = len(kinds)
    start = [state] if before is None else list(before)
    return pl.pallas_call(
        functools.partial(relnew_kernel, nz, tuple(kinds), len(arrays), before is None, last),
        in_specs=[vmem()] * (2 + len(arrays))
        + ([anywhere()] if before else [])
        + [vmem()],
        out_specs=[anywhere(), anywhere() if last else vmem()],
        out_shape=[jax.ShapeDtypeStruct((dim, rels), F32), jax.ShapeDtypeStruct((1, rels), F32)],
        input_output_aliases={2 + len(arrays): 0} if before else {},
        scratch_shapes=[pltpu.VMEM((count, dim, w), F32), pltpu.SemaphoreType.DMA((count + 1,))]
        + ([pltpu.VMEM((1, rels), F32)] if last else []),
        compiler_params=params(),
        cost_estimate=cost(dim, dim),
        name="relnew",
    )(relations, state, *arrays, *start)


def relation_update(t, rel_ids, drel, acc, relations, state, send, finish):
    n = lax.axis_size("dom")
    dim, rels = relations.shape
    if n < 4 or n & (n - 1) or rels % (256 * n):
        total = lax.psum(relsum(t, rel_ids, drel, acc, rels), ("dom", "edge"))
        state = state + jnp.mean(total * total, axis=0)
        return relations - learn_rate * total / jnp.sqrt(state)[None, :], state, finish(send(drel), [])
    nz = n // 2
    mine_x, other_x = pieces(t, n, False, rel_ids, drel, acc, [])
    grads = send(other_x)
    mine_s, other_s = pieces(t, n, True, rel_ids, drel, acc, [other_x])
    to_x = add_each(mine_x, across(other_x))
    theirs = across(other_s)
    down = range(nz - 1, -1, -1)
    from_x = {k: swapped(to_x[k], 1) for k in down}
    turned = {
        k: sum_piece(k, mine_s[k], theirs, [from_x[k]], grads[1:2] if k == nz - 1 else [])
        for k in down[:-1]
    }
    from_z = [swapped(turned[k], 2 * k) for k in down[:-1]]
    done = finish(grads, [turned[nz - 1]])
    summed = sum_piece(0, mine_s[0], theirs, [from_x[0]] + from_z, [])
    got = [summed if k == 0 else swapped(summed, 2 * k) for k in range(nz)]
    got_x = [swapped(piece, 1) for piece in got]
    state = state.reshape(1, rels)
    ks = [0, *down[:-1]]
    mine = [got[k] for k in ks]
    mine_x = [got_x[k] for k in ks]
    there = across(stacked(mine, [done[2]]))
    new = relnew(nz, relations, state, [(ks, True, True, mine)], None)
    there_x = across(stacked(mine_x, [new[1]]))
    groups = [(ks, True, False, there), (ks, False, True, mine_x)]
    new = relnew(nz, relations, state, groups, new)
    groups = [(ks, False, False, there_x)]
    rel_new, state_new = relnew(nz, relations, state, groups, new, last=True)
    return rel_new, state_new.reshape(rels), done


def on_device(
    entities,
    entity_state,
    relations,
    relation_state,
    src_rows,
    rel_ids,
    dst_rows,
    counts,
    neg_blocks,
):
    rounds = src_rows.shape[0]
    rels = relations.shape[1]
    shape = src_rows.shape
    cnt, neg = counts.T, neg_blocks.T
    g_mine, g_other, drel, rel16, ent, state = first_round(
        cnt, neg, src_rows, dst_rows, rel_ids, entities, entity_state.reshape(1, -1), relations
    )
    acc = relsum(0, rel_ids, drel, None, rels)
    ent, state, low = update(ent, state, [g_mine, across(g_other)], [])
    rel = relvec(1, rel_ids, rel16)
    for t in range(1, rounds):
        far = shifted(low, -t)
        own = (low, across(low))
        query, query_t, source, s_hot, d_hot, *hots = source_side(
            t, shape, cnt, neg, src_rows, dst_rows, own, rel
        )
        far = held(far, [query, acc])
        far = (far, across(far))
        if t == rounds - 1:
            break
        near = near_products(query_t, far[0])
        gd_mine, gd_other, weight = target_grad(near, far[1], query, query_t, *hots)
        gd = sum_pair(gd_mine, across(gd_other))
        gs_mine, gs_other, drel = source_grad(
            t, shape, cnt, neg, gd, far, d_hot, query, weight, source, rel, s_hot
        )
        acc = relsum(t, rel_ids, drel, acc, rels)
        rel = relvec(t + 1, rel_ids, rel16)
        grads = [sum_pair(gs_mine, shifted(gd, t), F32), across(gs_other)]
        ent, state, low = update(ent, state, grads, [rel])
    drel, dsource, dterm = last_terms(t, shape, cnt, neg, far, query, query_t, d_hot, source, rel)

    def send(after):
        gs_mine, gs_other, gd_mine, gd_other = both_grads(after, dsource, s_hot, dterm, hots[0])
        gd = sum_pair(gd_mine, across(gd_other))
        return [gs_mine, across(gs_other), shifted(gd, t)]

    def finish(grads, after):
        (mine,) = update(ent, state, grads, after, last=True)
        return whole_partition(mine, across(mine))

    rel_new, rel_state, done = relation_update(
        t, rel_ids, drel, acc, relations, relation_state, send, finish
    )
    return (done[0], done[1].reshape(-1), rel_new, rel_state)


def solution(mesh):
    return jax.shard_map(
        on_device,
        mesh=mesh,
        in_specs=(
            P(None, ("groups", "dom")),
            P(("groups", "dom")),
            P(None, "groups"),
            P("groups"),
            P(None, ("groups", "dom", "edge"), None),
            P(None, ("groups", "dom", "edge"), None),
            P(None, ("groups", "dom", "edge"), None),
            P(None, ("groups", "dom", "edge")),
            P(None, ("groups", "dom", "edge")),
        ),
        out_specs=(
            P(None, ("groups", "dom")),
            P(("groups", "dom")),
            P(None, "groups"),
            P("groups"),
        ),
        check_vma=False,
    )
```

```python
import functools

import jax
import jax.numpy as jnp
from jax import lax
from jax.experimental import pallas as pl
from jax.experimental.pallas import tpu as pltpu
from jax.sharding import PartitionSpec as P

learn_rate = 0.1
BF = jnp.bfloat16
F32 = jnp.float32
VMEM_LIMIT = 24 * 1024 * 1024
NN = (((1,), (0,)), ((), ()))
NT = (((1,), (1,)), ((), ()))
TN = (((0,), (0,)), ((), ()))


def mm(a, b, dims=NN):
    return lax.dot_general(a, b, dims, preferred_element_type=F32)


def vmem():
    return pl.BlockSpec(memory_space=pltpu.VMEM)


def smem():
    return pl.BlockSpec(memory_space=pltpu.SMEM)


def anywhere():
    return pl.BlockSpec(memory_space=pl.ANY)


def in_hbm(x):
    return pltpu.with_memory_space_constraint(x, pltpu.HBM)


def cost(flops, size):
    return pl.CostEstimate(flops=flops, bytes_accessed=size, transcendentals=0)


def params():
    return pltpu.CompilerParams(vmem_limit_bytes=VMEM_LIMIT)


def shifted(x, by):
    n = lax.axis_size("dom")
    return lax.ppermute(x, "dom", [(i, (i + by) % n) for i in range(n)])


def swapped(x, bits):
    n = lax.axis_size("dom")
    return lax.ppermute(x, "dom", [(i, i ^ bits) for i in range(n)])


def across(x):
    return lax.ppermute(x, "edge", [(0, 1), (1, 0)])


def one_hot(rows_ref, t, count, base):
    blocks, width = rows_ref.shape[1:]
    at = lax.broadcasted_iota(jnp.int32, (count, width), 0)
    idx = rows_ref[t]
    return jnp.concatenate(
        [
            jnp.where(at == base(idx[b : b + 1, :]), 1.0, 0.0).astype(BF)
            for b in range(blocks)
        ],
        axis=1,
    )


def relvec_kernel(t, ids_ref, rel_ref, out_ref):
    rels = rel_ref.shape[1]
    tile = min(rels, 512)
    out = None
    for lo in range(0, rels, tile):
        hot = one_hot(ids_ref, t, tile, lambda i, lo=lo: i - lo)
        part = mm(rel_ref[:, lo : lo + tile], hot)
        out = part if out is None else out + part
    out_ref[...] = out.astype(BF)


def relvec(t, rel_ids, rel16):
    width, rels = rel16.shape
    slots = rel_ids.shape[1] * rel_ids.shape[2]
    return pl.pallas_call(
        functools.partial(relvec_kernel, t),
        in_specs=[vmem()] * 2,
        out_specs=vmem(),
        out_shape=jax.ShapeDtypeStruct((width, slots), BF),
        compiler_params=params(),
        cost_estimate=cost(width * slots, width * slots),
        name="relvec",
    )(rel_ids, rel16)


def relsum_kernel(t, first, ids_ref, drel_ref, *refs):
    out_ref = refs[-1]
    rels = out_ref.shape[1]
    tile = min(rels, 512)
    drel = drel_ref[...]
    for lo in range(0, rels, tile):
        hot = one_hot(ids_ref, t, tile, lambda i, lo=lo: i - lo)
        part = mm(drel, hot, NT)
        out_ref[:, lo : lo + tile] = part if first else refs[0][:, lo : lo + tile] + part


def relsum(t, rel_ids, drel, acc, rels):
    width, slots = drel.shape
    ins = [rel_ids, drel] + ([] if acc is None else [acc])
    return pl.pallas_call(
        functools.partial(relsum_kernel, t, acc is None),
        in_specs=[vmem()] * len(ins),
        out_specs=vmem(),
        out_shape=jax.ShapeDtypeStruct((width, rels), F32),
        input_output_aliases={} if acc is None else {2: 0},
        compiler_params=params(),
        cost_estimate=cost(width * slots, width * slots),
        name="relsum",
    )(*ins)


class Limits:
    scratch = lambda shape: [
        pltpu.SMEM((shape[1], shape[0]), jnp.int32),
        pltpu.SMEM((shape[1], shape[0]), jnp.int32),
        pltpu.SemaphoreType.DMA((2,)),
    ]

    def __init__(self, t, from_cnt, from_neg, cnt, neg, sems):
        self.t, self.cnt, self.neg = t, cnt, neg
        self.copies = [
            pltpu.make_async_copy(from_cnt, cnt, sems.at[0]),
            pltpu.make_async_copy(from_neg, neg, sems.at[1]),
        ]
        for copy in self.copies:
            copy.start()

    def wait(self):
        for copy in self.copies:
            copy.wait()

    def count(self, b):
        return self.cnt[b, self.t]

    def negative(self, b):
        return self.neg[b, self.t]


def place():
    dom = lax.axis_index("dom")
    return dom // 2, lax.rem(dom, 2), lax.axis_index("edge")


def localize(edge, half):
    def local(idx):
        moved = idx + edge * half
        return jnp.where(moved >= 2 * half, moved - 2 * half, moved)

    return local


def halves(x):
    hd = x.shape[0] // 2
    return x[:hd], x[hd:]


def make_query(source, rel):
    (s_re, s_im), (w_re, w_im) = halves(source), halves(rel)
    return jnp.concatenate(
        [s_re * w_re - s_im * w_im, s_re * w_im + s_im * w_re], axis=0
    ).astype(BF)


def conj_times(dq, v):
    (dq_re, dq_im), (v_re, v_im) = halves(dq), halves(v)
    return jnp.concatenate(
        [dq_re * v_re + dq_im * v_im, dq_im * v_re - dq_re * v_im], axis=0
    ).astype(BF)


def positive_factors(shape, limits, query, target):
    _, blocks, width = shape
    pos = jnp.sum(query.astype(F32) * target, axis=0, keepdims=True)
    lane = lax.broadcasted_iota(jnp.int32, (1, width), 1)
    valid = jnp.concatenate(
        [jnp.where(lane < limits.count(b), 1.0, 0.0) for b in range(blocks)], axis=1
    )
    return -jax.nn.sigmoid(-pos) * valid


def target_side(shape, limits, query, query_t, target, o_ref, w_ref):
    _, blocks, width = shape
    lanes = lambda b: pl.ds(pl.multiple_of(b * width, width), width)
    count = limits.count
    o_ref[...] = target.astype(BF)
    limits.wait()
    gpos = positive_factors(shape, limits, query, target)
    row_i = lax.broadcasted_iota(jnp.int32, (width, width), 0)
    col_j = lax.broadcasted_iota(jnp.int32, (width, width), 1)
    for b in range(blocks):
        nb = limits.negative(b)
        neg = o_ref[:, lanes(nb)]
        at = slice(b * width, (b + 1) * width)
        scores = mm(query[:, at], neg, TN) if query_t is None else mm(query_t[at], neg)
        keep = jnp.logical_and(row_i < count(b), col_j < count(nb))
        w_ref[:, at] = jnp.where(keep, jax.nn.sigmoid(scores) / width, 0.0).astype(BF)
    return gpos


def target_terms(shape, limits, query, gpos, w_ref, d_ref):
    _, blocks, width = shape
    d_ref[...] = gpos * query.astype(F32)
    for b in range(blocks):
        at = slice(b * width, (b + 1) * width)
        to = pl.ds(pl.multiple_of(limits.negative(b) * width, width), width)
        d_ref[:, to] += mm(query[:, at], w_ref[:, at])
    return d_ref[...].astype(BF)


def make_dquery(shape, limits, gpos, o_ref, w_ref):
    _, blocks, width = shape
    lanes = lambda b: pl.ds(pl.multiple_of(b * width, width), width)
    out = []
    for b in range(blocks):
        nb = limits.negative(b)
        at = slice(b * width, (b + 1) * width)
        own = gpos[:, at] * o_ref[:, at].astype(F32)
        out.append(own + mm(o_ref[:, lanes(nb)], w_ref[:, at], NT))
    return jnp.concatenate(out, axis=1)


def first_kernel(
    shape, cnt_ref, neg_ref, src_ref, dst_ref, ids_ref, ent_ref, state_ref, rel_ref,
    g_mine, g_other, drel_ref, rel16_ref, ent_mine, state_mine,
    cnt, neg, lim_sems, src, dst, ids, ent, state, rel_buf, o_scr, d_scr, w_scr, in_sems, sems,
):
    rels = rel_buf.shape[1]
    tile = min(rels, 512)
    spans = range(0, rels, tile)
    inputs = [
        pltpu.make_async_copy(there, here, in_sems.at[i])
        for i, (there, here) in enumerate(
            [(src_ref.at[:1], src), (dst_ref.at[:1], dst), (ids_ref.at[:1], ids), (ent_ref, ent), (state_ref, state)]
        )
    ]
    loads = [
        pltpu.make_async_copy(
            rel_ref.at[:, lo : lo + tile], rel_buf.at[:, lo : lo + tile], sems.at[i]
        )
        for i, lo in enumerate(spans)
    ]
    for load in inputs:
        load.start()
    limits = Limits(0, cnt_ref, neg_ref, cnt, neg, lim_sems)
    for load in loads:
        load.start()
    half = ent.shape[1] // 2
    _, _, edge = place()
    local = localize(edge, half)
    inputs[0].wait()
    s_hot = one_hot(src, 0, 2 * half, local)
    inputs[1].wait()
    d_hot = one_hot(dst, 0, 2 * half, local)
    inputs[2].wait()
    ids_hot = [one_hot(ids, 0, tile, lambda i, lo=lo: i - lo) for lo in spans]
    inputs[3].wait()
    inputs[4].wait()
    mine = pl.ds(pl.multiple_of(edge * half, half), half)
    ent_mine[...] = ent[:, mine]
    state_mine[...] = state[:, mine]
    table = jnp.concatenate(
        [ent[:, pl.ds(pl.multiple_of(h * half, half), half)].astype(BF) for h in (edge, 1 - edge)],
        axis=1,
    )
    source = mm(table, s_hot)
    target = mm(table, d_hot)
    rel = None
    for load, lo, hot in zip(loads, spans, ids_hot):
        load.wait()
        low = rel_buf[:, lo : lo + tile].astype(BF)
        rel16_ref[:, lo : lo + tile] = low
        part = mm(low, hot)
        rel = part if rel is None else rel + part
    query = make_query(source, rel)
    gpos = target_side(shape, limits, query, None, target, o_scr, w_scr)
    dq = make_dquery(shape, limits, gpos, o_scr, w_scr)
    drel_ref[...] = conj_times(dq, source)
    total = mm(conj_times(dq, rel), s_hot, NT) + mm(
        target_terms(shape, limits, query, gpos, w_scr, d_scr), d_hot, NT
    )
    g_mine[...] = total[:, :half]
    g_other[...] = total[:, half:].astype(BF)


def first_round(cnt, neg, src, dst, rel_ids, entities, state, relations):
    dim, rows = entities.shape
    rels = relations.shape[1]
    _, blocks, width = src.shape
    slots = blocks * width
    sds = jax.ShapeDtypeStruct
    return pl.pallas_call(
        functools.partial(first_kernel, src.shape),
        in_specs=[anywhere()] * 8,
        out_specs=[vmem()] * 6,
        out_shape=[
            sds((dim, rows // 2), F32),
            sds((dim, rows // 2), BF),
            sds((dim, slots), BF),
            sds((dim, rels), BF),
            sds((dim, rows // 2), F32),
            sds((1, rows // 2), F32),
        ],
        scratch_shapes=Limits.scratch(src.shape)
        + [
            pltpu.VMEM((1, blocks, width), jnp.int32),
            pltpu.VMEM((1, blocks, width), jnp.int32),
            pltpu.VMEM((1, blocks, width), jnp.int32),
            pltpu.VMEM((dim, rows), F32),
            pltpu.VMEM((1, rows), F32),
            pltpu.VMEM((dim, rels), F32),
            pltpu.VMEM((dim, slots), BF),
            pltpu.VMEM((dim, slots), F32),
            pltpu.VMEM((width, slots), BF),
            pltpu.SemaphoreType.DMA((5,)),
            pltpu.SemaphoreType.DMA((-(-rels // min(rels, 512)),)),
        ],
        compiler_params=params(),
        cost_estimate=cost(2 * dim * slots * (rels + 4 * rows), 8 * dim * rels),
        name="first_round",
    )(*(in_hbm(x) for x in (cnt, neg, src, dst, rel_ids, entities, state, relations)))


def source_kernel(t, shape, last, cnt_ref, neg_ref, src_ref, dst_ref, own0, own1, rel_ref, *refs):
    query_ref, query_t_ref, source_ref, s_hot_ref, d_hot_ref = refs[:5]
    if last:
        (d_hot_t_ref,) = refs[5:]
    else:
        v_hot_t_ref, n_hot_ref, n_hot_t_ref, mask_ref, cnt, neg, sems, d_hot_t_ref = refs[5:]
        limits = Limits(t, cnt_ref, neg_ref, cnt, neg, sems)
    _, blocks, width = shape
    half = own0.shape[1]
    local = localize(place()[2], half)
    s_hot = one_hot(src_ref, t, 2 * half, local)
    d_hot = one_hot(dst_ref, t, 2 * half, local)
    s_hot_ref[...] = s_hot
    d_hot_ref[...] = d_hot
    d_hot_t_ref[...] = d_hot.T
    source = mm(jnp.concatenate([own0[...], own1[...]], axis=1), s_hot)
    source_ref[...] = source.astype(BF)
    query = make_query(source, rel_ref[...].astype(F32))
    query_ref[...] = query
    query_t_ref[...] = query.T
    if last:
        return
    limits.wait()
    row_i = lax.broadcasted_iota(jnp.int32, (width, width), 0)
    col_j = lax.broadcasted_iota(jnp.int32, (width, width), 1)
    slot = lax.broadcasted_iota(jnp.int32, (width, 2 * half), 0)
    for b in range(blocks):
        nb = limits.negative(b)
        at = slice(b * width, (b + 1) * width)
        there = pl.ds(pl.multiple_of(nb * width, width), width)
        n_hot_ref[:, at] = d_hot_ref[:, there]
        n_hot_t_ref[at] = d_hot_t_ref[there, :]
        keep = jnp.logical_and(row_i < limits.count(b), col_j < limits.count(nb))
        mask_ref[:, at] = jnp.where(keep, 1.0 / width, 0.0)
        hot = d_hot_t_ref[at].astype(F32)
        v_hot_t_ref[at] = jnp.where(slot < limits.count(b), hot, 0.0).astype(BF)


def source_side(t, shape, cnt, neg, src, dst, own, rel):
    dim, slots = rel.shape
    width = shape[2]
    rows = 2 * own[0].shape[1]
    last = t == shape[0] - 1
    sds = lambda *shape: jax.ShapeDtypeStruct(shape, BF)
    outs = [sds(dim, slots), sds(slots, dim), sds(dim, slots), sds(rows, slots), sds(rows, slots)]
    if last:
        outs += [sds(slots, rows)]
    else:
        outs += [sds(slots, rows), sds(rows, slots), sds(slots, rows)]
        outs += [jax.ShapeDtypeStruct((width, slots), F32)]
    return pl.pallas_call(
        functools.partial(source_kernel, t, shape, last),
        in_specs=[anywhere()] * 2 + [vmem()] * 5,
        out_specs=[vmem()] * len(outs),
        out_shape=outs,
        scratch_shapes=[] if last else Limits.scratch(shape) + [pltpu.VMEM((slots, rows), BF)],
        compiler_params=params(),
        cost_estimate=cost(dim * slots, dim * slots),
        name="source_side",
    )(cnt, neg, src, dst, *own, rel)


def near_kernel(query_t_ref, far0, out_ref):
    out_ref[...] = mm(query_t_ref[...], far0[...])


def near_products(query_t, far0):
    slots, half = query_t.shape[0], far0.shape[1]
    return pl.pallas_call(
        near_kernel,
        in_specs=[vmem()] * 2,
        out_specs=vmem(),
        out_shape=jax.ShapeDtypeStruct((slots, half), F32),
        compiler_params=params(),
        cost_estimate=cost(slots * half, slots * half),
        name="near_products",
    )(query_t, far0)


def target_kernel(
    near, far1, query_ref, query_t_ref, v_hot_t_ref, n_hot_ref, n_hot_t_ref, mask_ref,
    gd_mine, gd_other, w_ref,
):
    width, slots = mask_ref.shape
    half = far1.shape[1]
    products = jnp.concatenate([near[...], mm(query_t_ref[...], far1[...])], axis=1)
    high = products.astype(BF)
    low = (products - high.astype(F32)).astype(BF)
    factors = []
    for lo in range(0, slots, width):
        at = slice(lo, lo + width)
        n_hot = n_hot_ref[:, at]
        scores = mm(high[at], n_hot) + mm(low[at], n_hot)
        weight = (jax.nn.sigmoid(scores) * mask_ref[:, at]).astype(BF)
        w_ref[:, at] = weight
        positive = jax.nn.sigmoid(-products[at]) * v_hot_t_ref[at].astype(F32)
        factors.append((mm(weight, n_hot_t_ref[at]) - positive).astype(BF))
    gd = mm(query_ref[...], jnp.concatenate(factors, axis=0))
    gd_mine[...] = gd[:, :half]
    gd_other[...] = gd[:, half:].astype(BF)


def target_grad(near, far1, query, query_t, v_hot_t, n_hot, n_hot_t, mask):
    dim, slots = query.shape
    half = far1.shape[1]
    sds = jax.ShapeDtypeStruct
    return pl.pallas_call(
        target_kernel,
        in_specs=[vmem()] * 8,
        out_specs=[vmem()] * 3,
        out_shape=[sds((dim, half), F32), sds((dim, half), BF), sds(mask.shape, BF)],
        compiler_params=params(),
        cost_estimate=cost(4 * dim * slots * half, 12 * dim * slots),
        name="target_grad",
    )(near, far1, query, query_t, v_hot_t, n_hot, n_hot_t, mask)


def source_grad_kernel(
    t, shape, cnt_ref, neg_ref, _, far0, far1, d_hot_ref, query_ref, w_ref, source_ref, rel_ref, s_hot_ref,
    gs_mine, gs_other, drel_ref, cnt, neg, sems, o_scr,
):
    limits = Limits(t, cnt_ref, neg_ref, cnt, neg, sems)
    half = gs_mine.shape[1]
    target = mm(jnp.concatenate([far0[...], far1[...]], axis=1), d_hot_ref[...])
    o_scr[...] = target.astype(BF)
    limits.wait()
    gpos = positive_factors(shape, limits, query_ref[...], target)
    dq = make_dquery(shape, limits, gpos, o_scr, w_ref)
    drel_ref[...] = conj_times(dq, source_ref[...].astype(F32))
    gs = mm(conj_times(dq, rel_ref[...].astype(F32)), s_hot_ref[...], NT)
    gs_mine[...] = gs[:, :half]
    gs_other[...] = gs[:, half:].astype(BF)


def source_grad(t, shape, cnt, neg, after, far, d_hot, query, weight, source, rel, s_hot):
    dim, slots = rel.shape
    half = s_hot.shape[0] // 2
    sds = jax.ShapeDtypeStruct
    return pl.pallas_call(
        functools.partial(source_grad_kernel, t, shape),
        in_specs=[anywhere()] * 3 + [vmem()] * 8,
        out_specs=[vmem()] * 3,
        out_shape=[sds((dim, half), F32), sds((dim, half), BF), sds((dim, slots), BF)],
        scratch_shapes=Limits.scratch(shape) + [pltpu.VMEM((dim, slots), BF)],
        compiler_params=params(),
        cost_estimate=cost(dim * slots, dim * slots),
        name="source_grad",
    )(cnt, neg, after, *far, d_hot, query, weight, source, rel, s_hot)


def last_kernel(
    t, shape, cnt_ref, neg_ref, far0, far1, query_ref, query_t_ref, d_hot_ref, source_ref, rel_ref,
    drel_ref, dsource_ref, dterm_ref, cnt, neg, sems, o_scr, d_scr, w_scr,
):
    limits = Limits(t, cnt_ref, neg_ref, cnt, neg, sems)
    far = jnp.concatenate([far0[...], far1[...]], axis=1)
    target = mm(far, d_hot_ref[...])
    query = query_ref[...]
    gpos = target_side(shape, limits, query, query_t_ref, target, o_scr, w_scr)
    dterm_ref[...] = target_terms(shape, limits, query, gpos, w_scr, d_scr)
    dq = make_dquery(shape, limits, gpos, o_scr, w_scr)
    drel_ref[...] = conj_times(dq, source_ref[...].astype(F32))
    dsource_ref[...] = conj_times(dq, rel_ref[...].astype(F32))


def last_terms(t, shape, cnt, neg, far, query, query_t, d_hot, source, rel):
    dim, slots = query.shape
    sds = jax.ShapeDtypeStruct
    return pl.pallas_call(
        functools.partial(last_kernel, t, shape),
        in_specs=[anywhere()] * 2 + [vmem()] * 7,
        out_specs=[vmem()] * 3,
        out_shape=[sds((dim, slots), BF)] * 3,
        scratch_shapes=Limits.scratch(shape)
        + [
            pltpu.VMEM((dim, slots), BF),
            pltpu.VMEM((dim, slots), F32),
            pltpu.VMEM((shape[2], slots), BF),
        ],
        compiler_params=params(),
        cost_estimate=cost(6 * dim * slots * shape[2], 12 * dim * slots),
        name="last_terms",
    )(cnt, neg, *far, query, query_t, d_hot, source, rel)


def both_kernel(_, dsource_ref, s_hot_ref, dterm_ref, d_hot_t_ref, gs_mine, gs_other, gd_mine, gd_other):
    half = gs_mine.shape[1]
    for terms, hot, dims, mine, other in (
        (dterm_ref, d_hot_t_ref, NN, gd_mine, gd_other),
        (dsource_ref, s_hot_ref, NT, gs_mine, gs_other),
    ):
        grad = mm(terms[...], hot[...], dims)
        mine[...] = grad[:, :half]
        other[...] = grad[:, half:].astype(BF)


def both_grads(after, dsource, s_hot, dterm, d_hot_t):
    dim, slots = dterm.shape
    half = s_hot.shape[0] // 2
    sds = jax.ShapeDtypeStruct
    return pl.pallas_call(
        both_kernel,
        in_specs=[anywhere()] + [vmem()] * 4,
        out_specs=[vmem()] * 4,
        out_shape=[sds((dim, half), F32), sds((dim, half), BF)] * 2,
        compiler_params=params(),
        cost_estimate=cost(8 * dim * slots * half, 12 * dim * slots),
        name="both_grads",
    )(after, dsource, s_hot, dterm, d_hot_t)


def update_kernel(n_grads, last, *refs):
    ent_ref, state_ref, grads = refs[0], refs[1], refs[2 : 2 + n_grads]
    grad = grads[0][...].astype(F32)
    for g in grads[1:]:
        grad = grad + g[...].astype(F32)
    dim = grad.shape[0]
    state = state_ref[...] + jnp.sum(grad * grad, axis=0, keepdims=True) / dim
    new = ent_ref[...] - grad * (learn_rate / jnp.sqrt(state))
    if last:
        refs[-1][:dim] = new
        refs[-1][dim:] = jnp.broadcast_to(state, (refs[-1].shape[0] - dim, state.shape[1]))
    else:
        refs[-3][...] = new
        refs[-2][...] = state
        refs[-1][...] = new.astype(BF)


def update(ent, state, grads, after, last=False):
    dim, half = ent.shape
    sds = jax.ShapeDtypeStruct
    outs = [sds((dim, half), F32), sds((1, half), F32), sds((dim, half), BF)]
    if last:
        outs = [sds((dim + 8, half), F32)]
    return pl.pallas_call(
        functools.partial(update_kernel, len(grads), last),
        in_specs=[vmem()] * (2 + len(grads)) + [anywhere()] * len(after),
        out_specs=[vmem()] * len(outs),
        out_shape=outs,
        compiler_params=params(),
        cost_estimate=cost(10 * dim * half, 16 * dim * half),
        name="update",
    )(ent, state, *grads, *after)


def pair_kernel(a_ref, b_ref, out_ref):
    out_ref[...] = (a_ref[...] + b_ref[...].astype(F32)).astype(out_ref.dtype)


def sum_pair(a, b, dtype=BF):
    return pl.pallas_call(
        pair_kernel,
        in_specs=[vmem()] * 2,
        out_specs=vmem(),
        out_shape=jax.ShapeDtypeStruct(a.shape, dtype),
        compiler_params=params(),
        name="sum_pair",
    )(a, b)


def held_kernel(x_ref, *refs):
    pass


def held(x, after):
    return pl.pallas_call(
        held_kernel,
        in_specs=[anywhere()] * (1 + len(after)),
        out_specs=anywhere(),
        out_shape=jax.ShapeDtypeStruct(x.shape, x.dtype),
        input_output_aliases={0: 0},
        compiler_params=params(),
        name="held",
    )(x, *after)


def whole_kernel(mine, theirs, ent_out, state_out, token):
    token[...] = jnp.zeros_like(token)
    dim, rows = ent_out.shape
    half = rows // 2
    edge = place()[2]
    for core, part in ((edge, mine), (1 - edge, theirs)):
        at = pl.ds(pl.multiple_of(core * half, half), half)
        ent_out[:, at] = part[:dim]
        state_out[:, at] = part[dim : dim + 1]


def whole_partition(mine, theirs):
    dim, half = mine.shape[0] - 8, mine.shape[1]
    return pl.pallas_call(
        whole_kernel,
        in_specs=[vmem()] * 2,
        out_specs=[vmem()] * 3,
        out_shape=[
            jax.ShapeDtypeStruct((dim, 2 * half), F32),
            jax.ShapeDtypeStruct((1, 2 * half), F32),
            jax.ShapeDtypeStruct((8, 128), F32),
        ],
        compiler_params=params(),
        name="whole_partition",
    )(mine, theirs)


def first_column(owner, core, w):
    return pl.multiple_of((2 * owner + core) * w, w)


def pieces_kernel(t, nz, same, ids_ref, drel_ref, acc_ref, *refs):
    mine, other = refs[-nz - 1 : -1], refs[-1]
    w = other.shape[2]
    z, x, edge = place()
    drel = drel_ref[...]
    for k in range(nz):
        owner = 2 * lax.bitwise_xor(z, k) + (x if same else 1 - x)
        at = [first_column(owner, core, w) for core in (edge, 1 - edge)]
        hot = jnp.concatenate([one_hot(ids_ref, t, w, lambda i, lo=lo: i - lo) for lo in at], axis=0)
        part = mm(drel, hot, NT)
        mine[k][...] = acc_ref[:, pl.ds(at[0], w)] + part[:, :w]
        other[k] = (acc_ref[:, pl.ds(at[1], w)] + part[:, w:]).astype(BF)


def pieces(t, n, same, rel_ids, drel, acc, after):
    dim, rels = acc.shape
    w = rels // (2 * n)
    sds = jax.ShapeDtypeStruct
    out = pl.pallas_call(
        functools.partial(pieces_kernel, t, n // 2, same),
        in_specs=[vmem()] * 3 + [anywhere()] * len(after),
        out_specs=[vmem()] * (n // 2 + 1),
        out_shape=[sds((dim, w), F32)] * (n // 2) + [sds((n // 2, dim, w), BF)],
        compiler_params=params(),
        cost_estimate=cost(dim * rels * drel.shape[1], 4 * dim * rels),
        name="pieces",
    )(rel_ids, drel, acc, *after)
    return out[:-1], out[-1]


def add_kernel(n, *refs):
    for k in range(n):
        refs[n + 1 + k][...] = (refs[k][...] + refs[n][k].astype(F32)).astype(BF)


def add_each(mine, theirs):
    n = len(mine)
    return pl.pallas_call(
        functools.partial(add_kernel, n),
        in_specs=[vmem()] * (n + 1),
        out_specs=[vmem()] * n,
        out_shape=[jax.ShapeDtypeStruct(x.shape, BF) for x in mine],
        compiler_params=params(),
        name="add_each",
    )(*mine, theirs)


def sum_kernel(k, count, mine, theirs, *refs):
    total = mine[...] + theirs[k].astype(F32)
    for r in refs[:count]:
        total = total + r[...].astype(F32)
    refs[-1][...] = total.astype(BF)


def sum_piece(k, mine, theirs, parts, after):
    return pl.pallas_call(
        functools.partial(sum_kernel, k, len(parts)),
        in_specs=[vmem()] * (2 + len(parts)) + [anywhere()] * len(after),
        out_specs=vmem(),
        out_shape=jax.ShapeDtypeStruct(mine.shape, BF),
        compiler_params=params(),
        name="sum_piece",
    )(mine, theirs, *parts, *after)


def stacked_kernel(*refs):
    for i in range(refs[-1].shape[0]):
        refs[-1][i] = refs[i][...]


def stacked(parts, after):
    return pl.pallas_call(
        stacked_kernel,
        in_specs=[vmem()] * len(parts) + [anywhere()] * len(after),
        out_specs=vmem(),
        out_shape=jax.ShapeDtypeStruct((len(parts), *parts[0].shape), parts[0].dtype),
        compiler_params=params(),
        name="stacked",
    )(*parts, *after)


def relnew_kernel(nz, kinds, count, first, last, rel_ref, state_ref, *refs):
    arrays = refs[:count]
    rel_out, state_to, buf, sems = refs[-5:-1] if last else refs[-4:]
    state_out = refs[-1] if last else state_to
    w = buf.shape[2]
    state_out[...] = refs[count + (0 if first else 1)][...]
    z, x, edge = place()
    copies = []
    for i, (k, same, own, source, index) in enumerate(kinds):
        owner = 2 * lax.bitwise_xor(z, k) + (x if same else 1 - x)
        at = pl.ds(first_column(owner, edge if own else 1 - edge, w), w)
        grad = (arrays[source][...] if index is None else arrays[source][index]).astype(F32)
        state = state_ref[:, at] + jnp.sum(grad * grad, axis=0, keepdims=True) / grad.shape[0]
        state_out[:, at] = state
        buf[i] = rel_ref[:, at] - grad * (learn_rate / jnp.sqrt(state))
        copy = pltpu.make_async_copy(buf.at[i], rel_out.at[:, at], sems.at[i])
        copy.start()
        copies.append(copy)
    if last:
        copy = pltpu.make_async_copy(state_out, state_to, sems.at[len(kinds)])
        copy.start()
        copies.append(copy)
    for copy in copies:
        copy.wait()


def relnew(nz, relations, state, groups, before, last=False):
    dim, rels = relations.shape
    w = rels // (4 * nz)
    kinds, arrays = [], []
    for ks, same, own, parts in groups:
        one = not isinstance(parts, list)
        for i, k in enumerate(ks):
            kinds.append((k, same, own, len(arrays) + (0 if one else i), i if one else None))
        arrays += [parts] if one else parts
    count = len(kinds)
    start = [state] if before is None else list(before)
    return pl.pallas_call(
        functools.partial(relnew_kernel, nz, tuple(kinds), len(arrays), before is None, last),
        in_specs=[vmem()] * (2 + len(arrays))
        + ([anywhere()] if before else [])
        + [vmem()],
        out_specs=[anywhere(), anywhere() if last else vmem()],
        out_shape=[jax.ShapeDtypeStruct((dim, rels), F32), jax.ShapeDtypeStruct((1, rels), F32)],
        input_output_aliases={2 + len(arrays): 0} if before else {},
        scratch_shapes=[pltpu.VMEM((count, dim, w), F32), pltpu.SemaphoreType.DMA((count + 1,))]
        + ([pltpu.VMEM((1, rels), F32)] if last else []),
        compiler_params=params(),
        cost_estimate=cost(dim, dim),
        name="relnew",
    )(relations, state, *arrays, *start)


def relation_update(t, rel_ids, drel, acc, relations, state, send, finish):
    n = lax.axis_size("dom")
    dim, rels = relations.shape
    if n < 4 or n & (n - 1) or rels % (256 * n):
        total = lax.psum(relsum(t, rel_ids, drel, acc, rels), ("dom", "edge"))
        state = state + jnp.mean(total * total, axis=0)
        return relations - learn_rate * total / jnp.sqrt(state)[None, :], state, finish(send(drel), [])
    nz = n // 2
    mine_x, other_x = pieces(t, n, False, rel_ids, drel, acc, [])
    grads = send(other_x)
    mine_s, other_s = pieces(t, n, True, rel_ids, drel, acc, [other_x])
    to_x = add_each(mine_x, across(other_x))
    theirs = across(other_s)
    down = range(nz - 1, -1, -1)
    from_x = {k: swapped(to_x[k], 1) for k in down}
    addends = {k: [from_x[k]] for k in range(nz)}
    turned = []
    bit = 1
    while bit < nz:
        for k in reversed(range(bit, nz, 2 * bit)):
            after = [] if turned else grads[1:2]
            turned.append(sum_piece(k, mine_s[k], theirs, addends[k], after))
            addends[k ^ bit].append(swapped(turned[-1], 2 * bit))
        bit *= 2
    done = finish(grads, [turned[-1]])
    summed = sum_piece(0, mine_s[0], theirs, addends[0], [])
    got = [summed if k == 0 else swapped(summed, 2 * k) for k in range(nz)]
    got_x = [swapped(piece, 1) for piece in got]
    state = state.reshape(1, rels)
    ks = [0, *down[:-1]]
    mine = [got[k] for k in ks]
    mine_x = [got_x[k] for k in ks]
    there = across(stacked(mine, [done[2]]))
    new = relnew(nz, relations, state, [(ks, True, True, mine)], None)
    there_x = across(stacked(mine_x, [new[1]]))
    groups = [(ks, True, False, there), (ks, False, True, mine_x)]
    new = relnew(nz, relations, state, groups, new)
    groups = [(ks, False, False, there_x)]
    rel_new, state_new = relnew(nz, relations, state, groups, new, last=True)
    return rel_new, state_new.reshape(rels), done


def on_device(
    entities,
    entity_state,
    relations,
    relation_state,
    src_rows,
    rel_ids,
    dst_rows,
    counts,
    neg_blocks,
):
    rounds = src_rows.shape[0]
    rels = relations.shape[1]
    shape = src_rows.shape
    cnt, neg = counts.T, neg_blocks.T
    g_mine, g_other, drel, rel16, ent, state = first_round(
        cnt, neg, src_rows, dst_rows, rel_ids, entities, entity_state.reshape(1, -1), relations
    )
    acc = relsum(0, rel_ids, drel, None, rels)
    ent, state, low = update(ent, state, [g_mine, across(g_other)], [])
    rel = relvec(1, rel_ids, rel16)
    for t in range(1, rounds):
        far = shifted(low, -t)
        own = (low, across(low))
        query, query_t, source, s_hot, d_hot, *hots = source_side(
            t, shape, cnt, neg, src_rows, dst_rows, own, rel
        )
        far = held(far, [query, acc])
        far = (far, across(far))
        if t == rounds - 1:
            break
        near = near_products(query_t, far[0])
        gd_mine, gd_other, weight = target_grad(near, far[1], query, query_t, *hots)
        gd = sum_pair(gd_mine, across(gd_other))
        gs_mine, gs_other, drel = source_grad(
            t, shape, cnt, neg, gd, far, d_hot, query, weight, source, rel, s_hot
        )
        acc = relsum(t, rel_ids, drel, acc, rels)
        rel = relvec(t + 1, rel_ids, rel16)
        grads = [sum_pair(gs_mine, shifted(gd, t), F32), across(gs_other)]
        ent, state, low = update(ent, state, grads, [rel])
    drel, dsource, dterm = last_terms(t, shape, cnt, neg, far, query, query_t, d_hot, source, rel)

    def send(after):
        gs_mine, gs_other, gd_mine, gd_other = both_grads(after, dsource, s_hot, dterm, hots[0])
        gd = sum_pair(gd_mine, across(gd_other))
        return [gs_mine, across(gs_other), shifted(gd, t)]

    def finish(grads, after):
        (mine,) = update(ent, state, grads, after, last=True)
        return whole_partition(mine, across(mine))

    rel_new, rel_state, done = relation_update(
        t, rel_ids, drel, acc, relations, relation_state, send, finish
    )
    return (done[0], done[1].reshape(-1), rel_new, rel_state)


def solution(mesh):
    return jax.shard_map(
        on_device,
        mesh=mesh,
        in_specs=(
            P(None, ("groups", "dom")),
            P(("groups", "dom")),
            P(None, "groups"),
            P("groups"),
            P(None, ("groups", "dom", "edge"), None),
            P(None, ("groups", "dom", "edge"), None),
            P(None, ("groups", "dom", "edge"), None),
            P(None, ("groups", "dom", "edge")),
            P(None, ("groups", "dom", "edge")),
        ),
        out_specs=(
            P(None, ("groups", "dom")),
            P(("groups", "dom")),
            P(None, "groups"),
            P("groups"),
        ),
        check_vma=False,
    )
```

```python
import functools

import jax
import jax.numpy as jnp
from jax import lax
from jax.experimental import pallas as pl
from jax.experimental.pallas import tpu as pltpu
from jax.sharding import PartitionSpec as P

learn_rate = 0.1
BF = jnp.bfloat16
F32 = jnp.float32
VMEM_LIMIT = 24 * 1024 * 1024
NN = (((1,), (0,)), ((), ()))
NT = (((1,), (1,)), ((), ()))
TN = (((0,), (0,)), ((), ()))


def mm(a, b, dims=NN):
    return lax.dot_general(a, b, dims, preferred_element_type=F32)


def vmem():
    return pl.BlockSpec(memory_space=pltpu.VMEM)


def smem():
    return pl.BlockSpec(memory_space=pltpu.SMEM)


def anywhere():
    return pl.BlockSpec(memory_space=pl.ANY)


def in_hbm(x):
    return pltpu.with_memory_space_constraint(x, pltpu.HBM)


def cost(flops, size):
    return pl.CostEstimate(flops=flops, bytes_accessed=size, transcendentals=0)


def params():
    return pltpu.CompilerParams(vmem_limit_bytes=VMEM_LIMIT)


def shifted(x, by):
    n = lax.axis_size("dom")
    return lax.ppermute(x, "dom", [(i, (i + by) % n) for i in range(n)])


def swapped(x, bits):
    n = lax.axis_size("dom")
    return lax.ppermute(x, "dom", [(i, i ^ bits) for i in range(n)])


def across(x):
    return lax.ppermute(x, "edge", [(0, 1), (1, 0)])


def one_hot(rows_ref, t, count, base):
    blocks, width = rows_ref.shape[1:]
    at = lax.broadcasted_iota(jnp.int32, (count, width), 0)
    idx = rows_ref[t]
    return jnp.concatenate(
        [
            jnp.where(at == base(idx[b : b + 1, :]), 1.0, 0.0).astype(BF)
            for b in range(blocks)
        ],
        axis=1,
    )


def relvec_kernel(t, ids_ref, rel_ref, out_ref):
    rels = rel_ref.shape[1]
    tile = min(rels, 512)
    out = None
    for lo in range(0, rels, tile):
        hot = one_hot(ids_ref, t, tile, lambda i, lo=lo: i - lo)
        part = mm(rel_ref[:, lo : lo + tile], hot)
        out = part if out is None else out + part
    out_ref[...] = out.astype(BF)


def relvec(t, rel_ids, rel16):
    width, rels = rel16.shape
    slots = rel_ids.shape[1] * rel_ids.shape[2]
    return pl.pallas_call(
        functools.partial(relvec_kernel, t),
        in_specs=[vmem()] * 2,
        out_specs=vmem(),
        out_shape=jax.ShapeDtypeStruct((width, slots), BF),
        compiler_params=params(),
        cost_estimate=cost(width * slots, width * slots),
        name="relvec",
    )(rel_ids, rel16)


def relsum_kernel(t, first, ids_ref, drel_ref, *refs):
    out_ref = refs[-1]
    rels = out_ref.shape[1]
    tile = min(rels, 512)
    drel = drel_ref[...]
    for lo in range(0, rels, tile):
        hot = one_hot(ids_ref, t, tile, lambda i, lo=lo: i - lo)
        part = mm(drel, hot, NT)
        out_ref[:, lo : lo + tile] = part if first else refs[0][:, lo : lo + tile] + part


def relsum(t, rel_ids, drel, acc, rels):
    width, slots = drel.shape
    ins = [rel_ids, drel] + ([] if acc is None else [acc])
    return pl.pallas_call(
        functools.partial(relsum_kernel, t, acc is None),
        in_specs=[vmem()] * len(ins),
        out_specs=vmem(),
        out_shape=jax.ShapeDtypeStruct((width, rels), F32),
        input_output_aliases={} if acc is None else {2: 0},
        compiler_params=params(),
        cost_estimate=cost(width * slots, width * slots),
        name="relsum",
    )(*ins)


class Limits:
    scratch = lambda shape: [
        pltpu.SMEM((shape[1], shape[0]), jnp.int32),
        pltpu.SMEM((shape[1], shape[0]), jnp.int32),
        pltpu.SemaphoreType.DMA((2,)),
    ]

    def __init__(self, t, from_cnt, from_neg, cnt, neg, sems):
        self.t, self.cnt, self.neg = t, cnt, neg
        self.copies = [
            pltpu.make_async_copy(from_cnt, cnt, sems.at[0]),
            pltpu.make_async_copy(from_neg, neg, sems.at[1]),
        ]
        for copy in self.copies:
            copy.start()

    def wait(self):
        for copy in self.copies:
            copy.wait()

    def count(self, b):
        return self.cnt[b, self.t]

    def negative(self, b):
        return self.neg[b, self.t]


def place():
    dom = lax.axis_index("dom")
    return dom // 2, lax.rem(dom, 2), lax.axis_index("edge")


def localize(edge, half):
    def local(idx):
        moved = idx + edge * half
        return jnp.where(moved >= 2 * half, moved - 2 * half, moved)

    return local


def halves(x):
    hd = x.shape[0] // 2
    return x[:hd], x[hd:]


def make_query(source, rel):
    (s_re, s_im), (w_re, w_im) = halves(source), halves(rel)
    return jnp.concatenate(
        [s_re * w_re - s_im * w_im, s_re * w_im + s_im * w_re], axis=0
    ).astype(BF)


def conj_times(dq, v):
    (dq_re, dq_im), (v_re, v_im) = halves(dq), halves(v)
    return jnp.concatenate(
        [dq_re * v_re + dq_im * v_im, dq_im * v_re - dq_re * v_im], axis=0
    ).astype(BF)


def positive_factors(shape, limits, query, target):
    _, blocks, width = shape
    pos = jnp.sum(query.astype(F32) * target, axis=0, keepdims=True)
    lane = lax.broadcasted_iota(jnp.int32, (1, width), 1)
    valid = jnp.concatenate(
        [jnp.where(lane < limits.count(b), 1.0, 0.0) for b in range(blocks)], axis=1
    )
    return -jax.nn.sigmoid(-pos) * valid


def target_side(shape, limits, query, query_t, target, o_ref, w_ref):
    _, blocks, width = shape
    lanes = lambda b: pl.ds(pl.multiple_of(b * width, width), width)
    count = limits.count
    o_ref[...] = target.astype(BF)
    limits.wait()
    gpos = positive_factors(shape, limits, query, target)
    row_i = lax.broadcasted_iota(jnp.int32, (width, width), 0)
    col_j = lax.broadcasted_iota(jnp.int32, (width, width), 1)
    for b in range(blocks):
        nb = limits.negative(b)
        neg = o_ref[:, lanes(nb)]
        at = slice(b * width, (b + 1) * width)
        scores = mm(query[:, at], neg, TN) if query_t is None else mm(query_t[at], neg)
        keep = jnp.logical_and(row_i < count(b), col_j < count(nb))
        w_ref[:, at] = jnp.where(keep, jax.nn.sigmoid(scores) / width, 0.0).astype(BF)
    return gpos


def target_terms(shape, limits, query, gpos, w_ref, d_ref):
    _, blocks, width = shape
    d_ref[...] = gpos * query.astype(F32)
    for b in range(blocks):
        at = slice(b * width, (b + 1) * width)
        to = pl.ds(pl.multiple_of(limits.negative(b) * width, width), width)
        d_ref[:, to] += mm(query[:, at], w_ref[:, at])
    return d_ref[...].astype(BF)


def make_dquery(shape, limits, gpos, o_ref, w_ref):
    _, blocks, width = shape
    lanes = lambda b: pl.ds(pl.multiple_of(b * width, width), width)
    out = []
    for b in range(blocks):
        nb = limits.negative(b)
        at = slice(b * width, (b + 1) * width)
        own = gpos[:, at] * o_ref[:, at].astype(F32)
        out.append(own + mm(o_ref[:, lanes(nb)], w_ref[:, at], NT))
    return jnp.concatenate(out, axis=1)


def first_kernel(
    shape, cnt_ref, neg_ref, src_ref, dst_ref, ids_ref, ent_ref, state_ref, rel_ref,
    g_mine, g_other, drel_ref, rel16_ref, ent_mine, state_mine,
    cnt, neg, lim_sems, src, dst, ids, ent, state, rel_buf, o_scr, d_scr, w_scr, in_sems, sems,
):
    rels = rel_buf.shape[1]
    tile = min(rels, 512)
    spans = range(0, rels, tile)
    inputs = [
        pltpu.make_async_copy(there, here, in_sems.at[i])
        for i, (there, here) in enumerate(
            [(src_ref.at[:1], src), (dst_ref.at[:1], dst), (ids_ref.at[:1], ids), (ent_ref, ent), (state_ref, state)]
        )
    ]
    loads = [
        pltpu.make_async_copy(
            rel_ref.at[:, lo : lo + tile], rel_buf.at[:, lo : lo + tile], sems.at[i]
        )
        for i, lo in enumerate(spans)
    ]
    for load in inputs:
        load.start()
    limits = Limits(0, cnt_ref, neg_ref, cnt, neg, lim_sems)
    for load in loads:
        load.start()
    half = ent.shape[1] // 2
    _, _, edge = place()
    local = localize(edge, half)
    inputs[0].wait()
    s_hot = one_hot(src, 0, 2 * half, local)
    inputs[1].wait()
    d_hot = one_hot(dst, 0, 2 * half, local)
    inputs[2].wait()
    ids_hot = [one_hot(ids, 0, tile, lambda i, lo=lo: i - lo) for lo in spans]
    inputs[3].wait()
    inputs[4].wait()
    mine = pl.ds(pl.multiple_of(edge * half, half), half)
    ent_mine[...] = ent[:, mine]
    state_mine[...] = state[:, mine]
    table = jnp.concatenate(
        [ent[:, pl.ds(pl.multiple_of(h * half, half), half)].astype(BF) for h in (edge, 1 - edge)],
        axis=1,
    )
    source = mm(table, s_hot)
    target = mm(table, d_hot)
    rel = None
    for load, lo, hot in zip(loads, spans, ids_hot):
        load.wait()
        low = rel_buf[:, lo : lo + tile].astype(BF)
        rel16_ref[:, lo : lo + tile] = low
        part = mm(low, hot)
        rel = part if rel is None else rel + part
    query = make_query(source, rel)
    gpos = target_side(shape, limits, query, None, target, o_scr, w_scr)
    dq = make_dquery(shape, limits, gpos, o_scr, w_scr)
    drel_ref[...] = conj_times(dq, source)
    total = mm(conj_times(dq, rel), s_hot, NT) + mm(
        target_terms(shape, limits, query, gpos, w_scr, d_scr), d_hot, NT
    )
    g_mine[...] = total[:, :half]
    g_other[...] = total[:, half:].astype(BF)


def first_round(cnt, neg, src, dst, rel_ids, entities, state, relations):
    dim, rows = entities.shape
    rels = relations.shape[1]
    _, blocks, width = src.shape
    slots = blocks * width
    sds = jax.ShapeDtypeStruct
    return pl.pallas_call(
        functools.partial(first_kernel, src.shape),
        in_specs=[anywhere()] * 8,
        out_specs=[vmem()] * 6,
        out_shape=[
            sds((dim, rows // 2), F32),
            sds((dim, rows // 2), BF),
            sds((dim, slots), BF),
            sds((dim, rels), BF),
            sds((dim, rows // 2), F32),
            sds((1, rows // 2), F32),
        ],
        scratch_shapes=Limits.scratch(src.shape)
        + [
            pltpu.VMEM((1, blocks, width), jnp.int32),
            pltpu.VMEM((1, blocks, width), jnp.int32),
            pltpu.VMEM((1, blocks, width), jnp.int32),
            pltpu.VMEM((dim, rows), F32),
            pltpu.VMEM((1, rows), F32),
            pltpu.VMEM((dim, rels), F32),
            pltpu.VMEM((dim, slots), BF),
            pltpu.VMEM((dim, slots), F32),
            pltpu.VMEM((width, slots), BF),
            pltpu.SemaphoreType.DMA((5,)),
            pltpu.SemaphoreType.DMA((-(-rels // min(rels, 512)),)),
        ],
        compiler_params=params(),
        cost_estimate=cost(2 * dim * slots * (rels + 4 * rows), 8 * dim * rels),
        name="first_round",
    )(*(in_hbm(x) for x in (cnt, neg, src, dst, rel_ids, entities, state, relations)))


def source_kernel(t, shape, last, cnt_ref, neg_ref, src_ref, dst_ref, own0, own1, rel_ref, *refs):
    query_ref, query_t_ref, source_ref, s_hot_ref, d_hot_ref = refs[:5]
    if last:
        (d_hot_t_ref,) = refs[5:]
    else:
        v_hot_t_ref, n_hot_ref, n_hot_t_ref, mask_ref, cnt, neg, sems, d_hot_t_ref = refs[5:]
        limits = Limits(t, cnt_ref, neg_ref, cnt, neg, sems)
    _, blocks, width = shape
    half = own0.shape[1]
    local = localize(place()[2], half)
    s_hot = one_hot(src_ref, t, 2 * half, local)
    d_hot = one_hot(dst_ref, t, 2 * half, local)
    s_hot_ref[...] = s_hot
    d_hot_ref[...] = d_hot
    d_hot_t_ref[...] = d_hot.T
    source = mm(jnp.concatenate([own0[...], own1[...]], axis=1), s_hot)
    source_ref[...] = source.astype(BF)
    query = make_query(source, rel_ref[...].astype(F32))
    query_ref[...] = query
    query_t_ref[...] = query.T
    if last:
        return
    limits.wait()
    row_i = lax.broadcasted_iota(jnp.int32, (width, width), 0)
    col_j = lax.broadcasted_iota(jnp.int32, (width, width), 1)
    slot = lax.broadcasted_iota(jnp.int32, (width, 2 * half), 0)
    for b in range(blocks):
        nb = limits.negative(b)
        at = slice(b * width, (b + 1) * width)
        there = pl.ds(pl.multiple_of(nb * width, width), width)
        n_hot_ref[:, at] = d_hot_ref[:, there]
        n_hot_t_ref[at] = d_hot_t_ref[there, :]
        keep = jnp.logical_and(row_i < limits.count(b), col_j < limits.count(nb))
        mask_ref[:, at] = jnp.where(keep, 1.0 / width, 0.0)
        hot = d_hot_t_ref[at].astype(F32)
        v_hot_t_ref[at] = jnp.where(slot < limits.count(b), hot, 0.0).astype(BF)


def source_side(t, shape, cnt, neg, src, dst, own, rel):
    dim, slots = rel.shape
    width = shape[2]
    rows = 2 * own[0].shape[1]
    last = t == shape[0] - 1
    sds = lambda *shape: jax.ShapeDtypeStruct(shape, BF)
    outs = [sds(dim, slots), sds(slots, dim), sds(dim, slots), sds(rows, slots), sds(rows, slots)]
    if last:
        outs += [sds(slots, rows)]
    else:
        outs += [sds(slots, rows), sds(rows, slots), sds(slots, rows)]
        outs += [jax.ShapeDtypeStruct((width, slots), F32)]
    return pl.pallas_call(
        functools.partial(source_kernel, t, shape, last),
        in_specs=[anywhere()] * 2 + [vmem()] * 5,
        out_specs=[vmem()] * len(outs),
        out_shape=outs,
        scratch_shapes=[] if last else Limits.scratch(shape) + [pltpu.VMEM((slots, rows), BF)],
        compiler_params=params(),
        cost_estimate=cost(dim * slots, dim * slots),
        name="source_side",
    )(cnt, neg, src, dst, *own, rel)


def near_kernel(query_t_ref, far0, out_ref):
    out_ref[...] = mm(query_t_ref[...], far0[...])


def near_products(query_t, far0):
    slots, half = query_t.shape[0], far0.shape[1]
    return pl.pallas_call(
        near_kernel,
        in_specs=[vmem()] * 2,
        out_specs=vmem(),
        out_shape=jax.ShapeDtypeStruct((slots, half), F32),
        compiler_params=params(),
        cost_estimate=cost(slots * half, slots * half),
        name="near_products",
    )(query_t, far0)


def target_kernel(
    near, far1, query_ref, query_t_ref, v_hot_t_ref, n_hot_ref, n_hot_t_ref, mask_ref,
    gd_mine, gd_other, w_ref,
):
    width, slots = mask_ref.shape
    half = far1.shape[1]
    products = jnp.concatenate([near[...], mm(query_t_ref[...], far1[...])], axis=1)
    high = products.astype(BF)
    low = (products - high.astype(F32)).astype(BF)
    factors = []
    for lo in range(0, slots, width):
        at = slice(lo, lo + width)
        n_hot = n_hot_ref[:, at]
        scores = mm(high[at], n_hot) + mm(low[at], n_hot)
        weight = (jax.nn.sigmoid(scores) * mask_ref[:, at]).astype(BF)
        w_ref[:, at] = weight
        positive = jax.nn.sigmoid(-products[at]) * v_hot_t_ref[at].astype(F32)
        factors.append((mm(weight, n_hot_t_ref[at]) - positive).astype(BF))
    gd = mm(query_ref[...], jnp.concatenate(factors, axis=0))
    gd_mine[...] = gd[:, :half]
    gd_other[...] = gd[:, half:].astype(BF)


def target_grad(near, far1, query, query_t, v_hot_t, n_hot, n_hot_t, mask):
    dim, slots = query.shape
    half = far1.shape[1]
    sds = jax.ShapeDtypeStruct
    return pl.pallas_call(
        target_kernel,
        in_specs=[vmem()] * 8,
        out_specs=[vmem()] * 3,
        out_shape=[sds((dim, half), F32), sds((dim, half), BF), sds(mask.shape, BF)],
        compiler_params=params(),
        cost_estimate=cost(4 * dim * slots * half, 12 * dim * slots),
        name="target_grad",
    )(near, far1, query, query_t, v_hot_t, n_hot, n_hot_t, mask)


def source_grad_kernel(
    t, shape, cnt_ref, neg_ref, _, far0, far1, d_hot_ref, query_ref, w_ref, source_ref, rel_ref, s_hot_ref,
    gs_mine, gs_other, drel_ref, cnt, neg, sems, o_scr,
):
    limits = Limits(t, cnt_ref, neg_ref, cnt, neg, sems)
    half = gs_mine.shape[1]
    target = mm(jnp.concatenate([far0[...], far1[...]], axis=1), d_hot_ref[...])
    o_scr[...] = target.astype(BF)
    limits.wait()
    gpos = positive_factors(shape, limits, query_ref[...], target)
    dq = make_dquery(shape, limits, gpos, o_scr, w_ref)
    drel_ref[...] = conj_times(dq, source_ref[...].astype(F32))
    gs = mm(conj_times(dq, rel_ref[...].astype(F32)), s_hot_ref[...], NT)
    gs_mine[...] = gs[:, :half]
    gs_other[...] = gs[:, half:].astype(BF)


def source_grad(t, shape, cnt, neg, after, far, d_hot, query, weight, source, rel, s_hot):
    dim, slots = rel.shape
    half = s_hot.shape[0] // 2
    sds = jax.ShapeDtypeStruct
    return pl.pallas_call(
        functools.partial(source_grad_kernel, t, shape),
        in_specs=[anywhere()] * 3 + [vmem()] * 8,
        out_specs=[vmem()] * 3,
        out_shape=[sds((dim, half), F32), sds((dim, half), BF), sds((dim, slots), BF)],
        scratch_shapes=Limits.scratch(shape) + [pltpu.VMEM((dim, slots), BF)],
        compiler_params=params(),
        cost_estimate=cost(dim * slots, dim * slots),
        name="source_grad",
    )(cnt, neg, after, *far, d_hot, query, weight, source, rel, s_hot)


def last_kernel(
    t, shape, cnt_ref, neg_ref, far0, far1, query_ref, query_t_ref, d_hot_ref, source_ref, rel_ref,
    drel_ref, dsource_ref, dterm_ref, cnt, neg, sems, o_scr, d_scr, w_scr,
):
    limits = Limits(t, cnt_ref, neg_ref, cnt, neg, sems)
    far = jnp.concatenate([far0[...], far1[...]], axis=1)
    target = mm(far, d_hot_ref[...])
    query = query_ref[...]
    gpos = target_side(shape, limits, query, query_t_ref, target, o_scr, w_scr)
    dterm_ref[...] = target_terms(shape, limits, query, gpos, w_scr, d_scr)
    dq = make_dquery(shape, limits, gpos, o_scr, w_scr)
    drel_ref[...] = conj_times(dq, source_ref[...].astype(F32))
    dsource_ref[...] = conj_times(dq, rel_ref[...].astype(F32))


def last_terms(t, shape, cnt, neg, far, query, query_t, d_hot, source, rel):
    dim, slots = query.shape
    sds = jax.ShapeDtypeStruct
    return pl.pallas_call(
        functools.partial(last_kernel, t, shape),
        in_specs=[anywhere()] * 2 + [vmem()] * 7,
        out_specs=[vmem()] * 3,
        out_shape=[sds((dim, slots), BF)] * 3,
        scratch_shapes=Limits.scratch(shape)
        + [
            pltpu.VMEM((dim, slots), BF),
            pltpu.VMEM((dim, slots), F32),
            pltpu.VMEM((shape[2], slots), BF),
        ],
        compiler_params=params(),
        cost_estimate=cost(6 * dim * slots * shape[2], 12 * dim * slots),
        name="last_terms",
    )(cnt, neg, *far, query, query_t, d_hot, source, rel)


def both_kernel(_, dsource_ref, s_hot_ref, dterm_ref, d_hot_t_ref, gs_mine, gs_other, gd_mine, gd_other):
    half = gs_mine.shape[1]
    for terms, hot, dims, mine, other in (
        (dterm_ref, d_hot_t_ref, NN, gd_mine, gd_other),
        (dsource_ref, s_hot_ref, NT, gs_mine, gs_other),
    ):
        grad = mm(terms[...], hot[...], dims)
        mine[...] = grad[:, :half]
        other[...] = grad[:, half:].astype(BF)


def both_grads(after, dsource, s_hot, dterm, d_hot_t):
    dim, slots = dterm.shape
    half = s_hot.shape[0] // 2
    sds = jax.ShapeDtypeStruct
    return pl.pallas_call(
        both_kernel,
        in_specs=[anywhere()] + [vmem()] * 4,
        out_specs=[vmem()] * 4,
        out_shape=[sds((dim, half), F32), sds((dim, half), BF)] * 2,
        compiler_params=params(),
        cost_estimate=cost(8 * dim * slots * half, 12 * dim * slots),
        name="both_grads",
    )(after, dsource, s_hot, dterm, d_hot_t)


def update_kernel(n_grads, last, *refs):
    ent_ref, state_ref, grads = refs[0], refs[1], refs[2 : 2 + n_grads]
    grad = grads[0][...].astype(F32)
    for g in grads[1:]:
        grad = grad + g[...].astype(F32)
    dim = grad.shape[0]
    state = state_ref[...] + jnp.sum(grad * grad, axis=0, keepdims=True) / dim
    new = ent_ref[...] - grad * (learn_rate / jnp.sqrt(state))
    if last:
        refs[-1][:dim] = new
        refs[-1][dim:] = jnp.broadcast_to(state, (refs[-1].shape[0] - dim, state.shape[1]))
    else:
        refs[-3][...] = new
        refs[-2][...] = state
        refs[-1][...] = new.astype(BF)


def update(ent, state, grads, after, last=False):
    dim, half = ent.shape
    sds = jax.ShapeDtypeStruct
    outs = [sds((dim, half), F32), sds((1, half), F32), sds((dim, half), BF)]
    if last:
        outs = [sds((dim + 8, half), F32)]
    return pl.pallas_call(
        functools.partial(update_kernel, len(grads), last),
        in_specs=[vmem()] * (2 + len(grads)) + [anywhere()] * len(after),
        out_specs=[vmem()] * len(outs),
        out_shape=outs,
        compiler_params=params(),
        cost_estimate=cost(10 * dim * half, 16 * dim * half),
        name="update",
    )(ent, state, *grads, *after)


def pair_kernel(a_ref, b_ref, out_ref):
    out_ref[...] = (a_ref[...] + b_ref[...].astype(F32)).astype(out_ref.dtype)


def sum_pair(a, b, dtype=BF):
    return pl.pallas_call(
        pair_kernel,
        in_specs=[vmem()] * 2,
        out_specs=vmem(),
        out_shape=jax.ShapeDtypeStruct(a.shape, dtype),
        compiler_params=params(),
        name="sum_pair",
    )(a, b)


def held_kernel(x_ref, *refs):
    pass


def held(x, after):
    return pl.pallas_call(
        held_kernel,
        in_specs=[anywhere()] * (1 + len(after)),
        out_specs=anywhere(),
        out_shape=jax.ShapeDtypeStruct(x.shape, x.dtype),
        input_output_aliases={0: 0},
        compiler_params=params(),
        name="held",
    )(x, *after)


def whole_kernel(mine, theirs, ent_out, state_out, token):
    token[...] = jnp.zeros_like(token)
    dim, rows = ent_out.shape
    half = rows // 2
    edge = place()[2]
    for core, part in ((edge, mine), (1 - edge, theirs)):
        at = pl.ds(pl.multiple_of(core * half, half), half)
        ent_out[:, at] = part[:dim]
        state_out[:, at] = part[dim : dim + 1]


def whole_partition(mine, theirs):
    dim, half = mine.shape[0] - 8, mine.shape[1]
    return pl.pallas_call(
        whole_kernel,
        in_specs=[vmem()] * 2,
        out_specs=[vmem()] * 3,
        out_shape=[
            jax.ShapeDtypeStruct((dim, 2 * half), F32),
            jax.ShapeDtypeStruct((1, 2 * half), F32),
            jax.ShapeDtypeStruct((8, 128), F32),
        ],
        compiler_params=params(),
        name="whole_partition",
    )(mine, theirs)


def first_column(owner, core, w):
    return pl.multiple_of((2 * owner + core) * w, w)


def pieces_kernel(t, nz, same, ids_ref, drel_ref, acc_ref, *refs):
    mine, other = refs[-nz - 1 : -1], refs[-1]
    w = other.shape[2]
    z, x, edge = place()
    drel = drel_ref[...]
    for k in range(nz):
        owner = 2 * lax.bitwise_xor(z, k) + (x if same else 1 - x)
        at = [first_column(owner, core, w) for core in (edge, 1 - edge)]
        hot = jnp.concatenate([one_hot(ids_ref, t, w, lambda i, lo=lo: i - lo) for lo in at], axis=0)
        part = mm(drel, hot, NT)
        mine[k][...] = acc_ref[:, pl.ds(at[0], w)] + part[:, :w]
        other[k] = (acc_ref[:, pl.ds(at[1], w)] + part[:, w:]).astype(BF)


def pieces(t, n, same, rel_ids, drel, acc, after):
    dim, rels = acc.shape
    w = rels // (2 * n)
    sds = jax.ShapeDtypeStruct
    out = pl.pallas_call(
        functools.partial(pieces_kernel, t, n // 2, same),
        in_specs=[vmem()] * 3 + [anywhere()] * len(after),
        out_specs=[vmem()] * (n // 2 + 1),
        out_shape=[sds((dim, w), F32)] * (n // 2) + [sds((n // 2, dim, w), BF)],
        compiler_params=params(),
        cost_estimate=cost(dim * rels * drel.shape[1], 4 * dim * rels),
        name="pieces",
    )(rel_ids, drel, acc, *after)
    return out[:-1], out[-1]


def add_kernel(n, *refs):
    for k in range(n):
        refs[n + 1 + k][...] = (refs[k][...] + refs[n][k].astype(F32)).astype(BF)


def add_each(mine, theirs):
    n = len(mine)
    return pl.pallas_call(
        functools.partial(add_kernel, n),
        in_specs=[vmem()] * (n + 1),
        out_specs=[vmem()] * n,
        out_shape=[jax.ShapeDtypeStruct(x.shape, BF) for x in mine],
        compiler_params=params(),
        name="add_each",
    )(*mine, theirs)


def sum_kernel(k, count, mine, theirs, *refs):
    total = mine[...] + theirs[k].astype(F32)
    for r in refs[:count]:
        total = total + r[...].astype(F32)
    refs[-1][...] = total.astype(BF)


def sum_piece(k, mine, theirs, parts, after):
    return pl.pallas_call(
        functools.partial(sum_kernel, k, len(parts)),
        in_specs=[vmem()] * (2 + len(parts)) + [anywhere()] * len(after),
        out_specs=vmem(),
        out_shape=jax.ShapeDtypeStruct(mine.shape, BF),
        compiler_params=params(),
        name="sum_piece",
    )(mine, theirs, *parts, *after)


def stacked_kernel(*refs):
    for i in range(refs[-1].shape[0]):
        refs[-1][i] = refs[i][...]


def stacked(parts, after):
    return pl.pallas_call(
        stacked_kernel,
        in_specs=[vmem()] * len(parts) + [anywhere()] * len(after),
        out_specs=vmem(),
        out_shape=jax.ShapeDtypeStruct((len(parts), *parts[0].shape), parts[0].dtype),
        compiler_params=params(),
        name="stacked",
    )(*parts, *after)


def relnew_kernel(nz, kinds, count, first, last, rel_ref, state_ref, *refs):
    arrays = refs[:count]
    rel_out, state_to, buf, sems = refs[-5:-1] if last else refs[-4:]
    state_out = refs[-1] if last else state_to
    w = buf.shape[2]
    state_out[...] = refs[count + (0 if first else 1)][...]
    z, x, edge = place()
    copies = []
    for i, (k, same, own, source, index) in enumerate(kinds):
        owner = 2 * lax.bitwise_xor(z, k) + (x if same else 1 - x)
        at = pl.ds(first_column(owner, edge if own else 1 - edge, w), w)
        grad = (arrays[source][...] if index is None else arrays[source][index]).astype(F32)
        state = state_ref[:, at] + jnp.sum(grad * grad, axis=0, keepdims=True) / grad.shape[0]
        state_out[:, at] = state
        buf[i] = rel_ref[:, at] - grad * (learn_rate / jnp.sqrt(state))
        copy = pltpu.make_async_copy(buf.at[i], rel_out.at[:, at], sems.at[i])
        copy.start()
        copies.append(copy)
    if last:
        copy = pltpu.make_async_copy(state_out, state_to, sems.at[len(kinds)])
        copy.start()
        copies.append(copy)
    for copy in copies:
        copy.wait()


def relnew(nz, relations, state, groups, before, last=False):
    dim, rels = relations.shape
    w = rels // (4 * nz)
    kinds, arrays = [], []
    for ks, same, own, parts in groups:
        one = not isinstance(parts, list)
        for i, k in enumerate(ks):
            kinds.append((k, same, own, len(arrays) + (0 if one else i), i if one else None))
        arrays += [parts] if one else parts
    count = len(kinds)
    start = [state] if before is None else list(before)
    return pl.pallas_call(
        functools.partial(relnew_kernel, nz, tuple(kinds), len(arrays), before is None, last),
        in_specs=[vmem()] * (2 + len(arrays))
        + ([anywhere()] if before else [])
        + [vmem()],
        out_specs=[anywhere(), anywhere() if last else vmem()],
        out_shape=[jax.ShapeDtypeStruct((dim, rels), F32), jax.ShapeDtypeStruct((1, rels), F32)],
        input_output_aliases={2 + len(arrays): 0} if before else {},
        scratch_shapes=[pltpu.VMEM((count, dim, w), F32), pltpu.SemaphoreType.DMA((count + 1,))]
        + ([pltpu.VMEM((1, rels), F32)] if last else []),
        compiler_params=params(),
        cost_estimate=cost(dim, dim),
        name="relnew",
    )(relations, state, *arrays, *start)


def relation_update(t, rel_ids, drel, acc, relations, state, send, finish):
    n = lax.axis_size("dom")
    dim, rels = relations.shape
    if n < 4 or n & (n - 1) or rels % (256 * n):
        total = lax.psum(relsum(t, rel_ids, drel, acc, rels), ("dom", "edge"))
        state = state + jnp.mean(total * total, axis=0)
        return relations - learn_rate * total / jnp.sqrt(state)[None, :], state, finish(send(drel), [])
    nz = n // 2
    mine_x, other_x = pieces(t, n, False, rel_ids, drel, acc, [])
    mine_s, other_s = pieces(t, n, True, rel_ids, drel, acc, [other_x])
    to_x = add_each(mine_x, across(other_x))
    theirs = across(other_s)
    down = range(nz - 1, -1, -1)
    from_x = {k: swapped(to_x[k], 1) for k in down}
    grads = send(to_x[0])
    addends = {k: [from_x[k]] for k in range(nz)}
    turned = []
    bit = 1
    while bit < nz:
        for k in reversed(range(bit, nz, 2 * bit)):
            after = [] if turned else grads[1:2]
            turned.append(sum_piece(k, mine_s[k], theirs, addends[k], after))
            addends[k ^ bit].append(swapped(turned[-1], 2 * bit))
        bit *= 2
    done = finish(grads, [turned[-1]])
    summed = sum_piece(0, mine_s[0], theirs, addends[0], [])
    got = [summed if k == 0 else swapped(summed, 2 * k) for k in range(nz)]
    got_x = [swapped(piece, 1) for piece in got]
    state = state.reshape(1, rels)
    ks = [0, *down[:-1]]
    mine = [got[k] for k in ks]
    mine_x = [got_x[k] for k in ks]
    there = across(stacked(mine, [done[2]]))
    new = relnew(nz, relations, state, [(ks, True, True, mine)], None)
    there_x = across(stacked(mine_x, [new[1]]))
    groups = [(ks, True, False, there), (ks, False, True, mine_x)]
    new = relnew(nz, relations, state, groups, new)
    groups = [(ks, False, False, there_x)]
    rel_new, state_new = relnew(nz, relations, state, groups, new, last=True)
    return rel_new, state_new.reshape(rels), done


def on_device(
    entities,
    entity_state,
    relations,
    relation_state,
    src_rows,
    rel_ids,
    dst_rows,
    counts,
    neg_blocks,
):
    rounds = src_rows.shape[0]
    rels = relations.shape[1]
    shape = src_rows.shape
    cnt, neg = counts.T, neg_blocks.T
    g_mine, g_other, drel, rel16, ent, state = first_round(
        cnt, neg, src_rows, dst_rows, rel_ids, entities, entity_state.reshape(1, -1), relations
    )
    acc = relsum(0, rel_ids, drel, None, rels)
    ent, state, low = update(ent, state, [g_mine, across(g_other)], [])
    rel = relvec(1, rel_ids, rel16)
    for t in range(1, rounds):
        far = shifted(low, -t)
        own = (low, across(low))
        query, query_t, source, s_hot, d_hot, *hots = source_side(
            t, shape, cnt, neg, src_rows, dst_rows, own, rel
        )
        far = held(far, [query, acc])
        far = (far, across(far))
        if t == rounds - 1:
            break
        near = near_products(query_t, far[0])
        gd_mine, gd_other, weight = target_grad(near, far[1], query, query_t, *hots)
        gd = sum_pair(gd_mine, across(gd_other))
        gs_mine, gs_other, drel = source_grad(
            t, shape, cnt, neg, gd, far, d_hot, query, weight, source, rel, s_hot
        )
        acc = relsum(t, rel_ids, drel, acc, rels)
        rel = relvec(t + 1, rel_ids, rel16)
        grads = [sum_pair(gs_mine, shifted(gd, t), F32), across(gs_other)]
        ent, state, low = update(ent, state, grads, [rel])
    drel, dsource, dterm = last_terms(t, shape, cnt, neg, far, query, query_t, d_hot, source, rel)

    def send(after):
        gs_mine, gs_other, gd_mine, gd_other = both_grads(after, dsource, s_hot, dterm, hots[0])
        gd = sum_pair(gd_mine, across(gd_other))
        return [gs_mine, across(gs_other), shifted(gd, t)]

    def finish(grads, after):
        (mine,) = update(ent, state, grads, after, last=True)
        return whole_partition(mine, across(mine))

    rel_new, rel_state, done = relation_update(
        t, rel_ids, drel, acc, relations, relation_state, send, finish
    )
    return (done[0], done[1].reshape(-1), rel_new, rel_state)


def solution(mesh):
    return jax.shard_map(
        on_device,
        mesh=mesh,
        in_specs=(
            P(None, ("groups", "dom")),
            P(("groups", "dom")),
            P(None, "groups"),
            P("groups"),
            P(None, ("groups", "dom", "edge"), None),
            P(None, ("groups", "dom", "edge"), None),
            P(None, ("groups", "dom", "edge"), None),
            P(None, ("groups", "dom", "edge")),
            P(None, ("groups", "dom", "edge")),
        ),
        out_specs=(
            P(None, ("groups", "dom")),
            P(("groups", "dom")),
            P(None, "groups"),
            P("groups"),
        ),
        check_vma=False,
    )
```

```python
import functools

import jax
import jax.numpy as jnp
from jax import lax
from jax.experimental import pallas as pl
from jax.experimental.pallas import tpu as pltpu
from jax.sharding import PartitionSpec as P

learn_rate = 0.1
BF = jnp.bfloat16
F32 = jnp.float32
VMEM_LIMIT = 24 * 1024 * 1024
NN = (((1,), (0,)), ((), ()))
NT = (((1,), (1,)), ((), ()))
TN = (((0,), (0,)), ((), ()))


def mm(a, b, dims=NN):
    return lax.dot_general(a, b, dims, preferred_element_type=F32)


def vmem():
    return pl.BlockSpec(memory_space=pltpu.VMEM)


def smem():
    return pl.BlockSpec(memory_space=pltpu.SMEM)


def anywhere():
    return pl.BlockSpec(memory_space=pl.ANY)


def in_hbm(x):
    return pltpu.with_memory_space_constraint(x, pltpu.HBM)


def cost(flops, size):
    return pl.CostEstimate(flops=flops, bytes_accessed=size, transcendentals=0)


def params():
    return pltpu.CompilerParams(vmem_limit_bytes=VMEM_LIMIT)


def shifted(x, by):
    n = lax.axis_size("dom")
    return lax.ppermute(x, "dom", [(i, (i + by) % n) for i in range(n)])


def swapped(x, bits):
    n = lax.axis_size("dom")
    return lax.ppermute(x, "dom", [(i, i ^ bits) for i in range(n)])


def across(x):
    return lax.ppermute(x, "edge", [(0, 1), (1, 0)])


def one_hot(rows_ref, t, count, base):
    blocks, width = rows_ref.shape[1:]
    at = lax.broadcasted_iota(jnp.int32, (count, width), 0)
    idx = rows_ref[t]
    return jnp.concatenate(
        [
            jnp.where(at == base(idx[b : b + 1, :]), 1.0, 0.0).astype(BF)
            for b in range(blocks)
        ],
        axis=1,
    )


def relvec_kernel(t, ids_ref, rel_ref, out_ref):
    rels = rel_ref.shape[1]
    tile = min(rels, 512)
    out = None
    for lo in range(0, rels, tile):
        hot = one_hot(ids_ref, t, tile, lambda i, lo=lo: i - lo)
        part = mm(rel_ref[:, lo : lo + tile], hot)
        out = part if out is None else out + part
    out_ref[...] = out.astype(BF)


def relvec(t, rel_ids, rel16):
    width, rels = rel16.shape
    slots = rel_ids.shape[1] * rel_ids.shape[2]
    return pl.pallas_call(
        functools.partial(relvec_kernel, t),
        in_specs=[vmem()] * 2,
        out_specs=vmem(),
        out_shape=jax.ShapeDtypeStruct((width, slots), BF),
        compiler_params=params(),
        cost_estimate=cost(width * slots, width * slots),
        name="relvec",
    )(rel_ids, rel16)


def relsum_kernel(t, first, ids_ref, drel_ref, *refs):
    out_ref = refs[-1]
    rels = out_ref.shape[1]
    tile = min(rels, 512)
    drel = drel_ref[...]
    for lo in range(0, rels, tile):
        hot = one_hot(ids_ref, t, tile, lambda i, lo=lo: i - lo)
        part = mm(drel, hot, NT)
        out_ref[:, lo : lo + tile] = part if first else refs[0][:, lo : lo + tile] + part


def relsum(t, rel_ids, drel, acc, rels):
    width, slots = drel.shape
    ins = [rel_ids, drel] + ([] if acc is None else [acc])
    return pl.pallas_call(
        functools.partial(relsum_kernel, t, acc is None),
        in_specs=[vmem()] * len(ins),
        out_specs=vmem(),
        out_shape=jax.ShapeDtypeStruct((width, rels), F32),
        input_output_aliases={} if acc is None else {2: 0},
        compiler_params=params(),
        cost_estimate=cost(width * slots, width * slots),
        name="relsum",
    )(*ins)


class Limits:
    scratch = lambda shape: [
        pltpu.SMEM((shape[1], shape[0]), jnp.int32),
        pltpu.SMEM((shape[1], shape[0]), jnp.int32),
        pltpu.SemaphoreType.DMA((2,)),
    ]

    def __init__(self, t, from_cnt, from_neg, cnt, neg, sems):
        self.t, self.cnt, self.neg = t, cnt, neg
        self.copies = [
            pltpu.make_async_copy(from_cnt, cnt, sems.at[0]),
            pltpu.make_async_copy(from_neg, neg, sems.at[1]),
        ]
        for copy in self.copies:
            copy.start()

    def wait(self):
        for copy in self.copies:
            copy.wait()

    def count(self, b):
        return self.cnt[b, self.t]

    def negative(self, b):
        return self.neg[b, self.t]


def place():
    dom = lax.axis_index("dom")
    return dom // 2, lax.rem(dom, 2), lax.axis_index("edge")


def localize(edge, half):
    def local(idx):
        moved = idx + edge * half
        return jnp.where(moved >= 2 * half, moved - 2 * half, moved)

    return local


def halves(x):
    hd = x.shape[0] // 2
    return x[:hd], x[hd:]


def make_query(source, rel):
    (s_re, s_im), (w_re, w_im) = halves(source), halves(rel)
    return jnp.concatenate(
        [s_re * w_re - s_im * w_im, s_re * w_im + s_im * w_re], axis=0
    ).astype(BF)


def conj_times(dq, v):
    (dq_re, dq_im), (v_re, v_im) = halves(dq), halves(v)
    return jnp.concatenate(
        [dq_re * v_re + dq_im * v_im, dq_im * v_re - dq_re * v_im], axis=0
    ).astype(BF)


def positive_factors(shape, limits, query, target):
    _, blocks, width = shape
    pos = jnp.sum(query.astype(F32) * target, axis=0, keepdims=True)
    lane = lax.broadcasted_iota(jnp.int32, (1, width), 1)
    valid = jnp.concatenate(
        [jnp.where(lane < limits.count(b), 1.0, 0.0) for b in range(blocks)], axis=1
    )
    return -jax.nn.sigmoid(-pos) * valid


def target_side(shape, limits, query, query_t, target, o_ref, w_ref):
    _, blocks, width = shape
    lanes = lambda b: pl.ds(pl.multiple_of(b * width, width), width)
    count = limits.count
    o_ref[...] = target.astype(BF)
    limits.wait()
    gpos = positive_factors(shape, limits, query, target)
    row_i = lax.broadcasted_iota(jnp.int32, (width, width), 0)
    col_j = lax.broadcasted_iota(jnp.int32, (width, width), 1)
    for b in range(blocks):
        nb = limits.negative(b)
        neg = o_ref[:, lanes(nb)]
        at = slice(b * width, (b + 1) * width)
        scores = mm(query[:, at], neg, TN) if query_t is None else mm(query_t[at], neg)
        keep = jnp.logical_and(row_i < count(b), col_j < count(nb))
        w_ref[:, at] = jnp.where(keep, jax.nn.sigmoid(scores) / width, 0.0).astype(BF)
    return gpos


def target_terms(shape, limits, query, gpos, w_ref, d_ref):
    _, blocks, width = shape
    d_ref[...] = gpos * query.astype(F32)
    for b in range(blocks):
        at = slice(b * width, (b + 1) * width)
        to = pl.ds(pl.multiple_of(limits.negative(b) * width, width), width)
        d_ref[:, to] += mm(query[:, at], w_ref[:, at])
    return d_ref[...].astype(BF)


def make_dquery(shape, limits, gpos, o_ref, w_ref):
    _, blocks, width = shape
    lanes = lambda b: pl.ds(pl.multiple_of(b * width, width), width)
    out = []
    for b in range(blocks):
        nb = limits.negative(b)
        at = slice(b * width, (b + 1) * width)
        own = gpos[:, at] * o_ref[:, at].astype(F32)
        out.append(own + mm(o_ref[:, lanes(nb)], w_ref[:, at], NT))
    return jnp.concatenate(out, axis=1)


def first_kernel(
    shape, cnt_ref, neg_ref, src_ref, dst_ref, ids_ref, ent_ref, state_ref, rel_ref,
    g_mine, g_other, drel_ref, rel16_ref, ent_mine, state_mine,
    cnt, neg, lim_sems, src, dst, ids, ent, state, rel_buf, o_scr, d_scr, w_scr, in_sems, sems,
):
    rels = rel_buf.shape[1]
    tile = min(rels, 512)
    spans = range(0, rels, tile)
    inputs = [
        pltpu.make_async_copy(there, here, in_sems.at[i])
        for i, (there, here) in enumerate(
            [(src_ref.at[:1], src), (dst_ref.at[:1], dst), (ids_ref.at[:1], ids), (ent_ref, ent), (state_ref, state)]
        )
    ]
    loads = [
        pltpu.make_async_copy(
            rel_ref.at[:, lo : lo + tile], rel_buf.at[:, lo : lo + tile], sems.at[i]
        )
        for i, lo in enumerate(spans)
    ]
    for load in inputs:
        load.start()
    limits = Limits(0, cnt_ref, neg_ref, cnt, neg, lim_sems)
    for load in loads:
        load.start()
    half = ent.shape[1] // 2
    _, _, edge = place()
    local = localize(edge, half)
    inputs[0].wait()
    s_hot = one_hot(src, 0, 2 * half, local)
    inputs[1].wait()
    d_hot = one_hot(dst, 0, 2 * half, local)
    inputs[2].wait()
    ids_hot = [one_hot(ids, 0, tile, lambda i, lo=lo: i - lo) for lo in spans]
    inputs[3].wait()
    inputs[4].wait()
    mine = pl.ds(pl.multiple_of(edge * half, half), half)
    ent_mine[...] = ent[:, mine]
    state_mine[...] = state[:, mine]
    table = jnp.concatenate(
        [ent[:, pl.ds(pl.multiple_of(h * half, half), half)].astype(BF) for h in (edge, 1 - edge)],
        axis=1,
    )
    source = mm(table, s_hot)
    target = mm(table, d_hot)
    rel = None
    for load, lo, hot in zip(loads, spans, ids_hot):
        load.wait()
        low = rel_buf[:, lo : lo + tile].astype(BF)
        rel16_ref[:, lo : lo + tile] = low
        part = mm(low, hot)
        rel = part if rel is None else rel + part
    query = make_query(source, rel)
    gpos = target_side(shape, limits, query, None, target, o_scr, w_scr)
    dq = make_dquery(shape, limits, gpos, o_scr, w_scr)
    drel_ref[...] = conj_times(dq, source)
    total = mm(conj_times(dq, rel), s_hot, NT) + mm(
        target_terms(shape, limits, query, gpos, w_scr, d_scr), d_hot, NT
    )
    g_mine[...] = total[:, :half]
    g_other[...] = total[:, half:].astype(BF)


def first_round(cnt, neg, src, dst, rel_ids, entities, state, relations):
    dim, rows = entities.shape
    rels = relations.shape[1]
    _, blocks, width = src.shape
    slots = blocks * width
    sds = jax.ShapeDtypeStruct
    return pl.pallas_call(
        functools.partial(first_kernel, src.shape),
        in_specs=[anywhere()] * 8,
        out_specs=[vmem()] * 6,
        out_shape=[
            sds((dim, rows // 2), F32),
            sds((dim, rows // 2), BF),
            sds((dim, slots), BF),
            sds((dim, rels), BF),
            sds((dim, rows // 2), F32),
            sds((1, rows // 2), F32),
        ],
        scratch_shapes=Limits.scratch(src.shape)
        + [
            pltpu.VMEM((1, blocks, width), jnp.int32),
            pltpu.VMEM((1, blocks, width), jnp.int32),
            pltpu.VMEM((1, blocks, width), jnp.int32),
            pltpu.VMEM((dim, rows), F32),
            pltpu.VMEM((1, rows), F32),
            pltpu.VMEM((dim, rels), F32),
            pltpu.VMEM((dim, slots), BF),
            pltpu.VMEM((dim, slots), F32),
            pltpu.VMEM((width, slots), BF),
            pltpu.SemaphoreType.DMA((5,)),
            pltpu.SemaphoreType.DMA((-(-rels // min(rels, 512)),)),
        ],
        compiler_params=params(),
        cost_estimate=cost(2 * dim * slots * (rels + 4 * rows), 8 * dim * rels),
        name="first_round",
    )(*(in_hbm(x) for x in (cnt, neg, src, dst, rel_ids, entities, state, relations)))


def source_kernel(t, shape, last, cnt_ref, neg_ref, src_ref, dst_ref, own0, own1, rel_ref, *refs):
    query_ref, query_t_ref, source_ref, s_hot_ref, d_hot_ref = refs[:5]
    if last:
        (d_hot_t_ref,) = refs[5:]
    else:
        v_hot_t_ref, n_hot_ref, n_hot_t_ref, mask_ref, cnt, neg, sems, d_hot_t_ref = refs[5:]
        limits = Limits(t, cnt_ref, neg_ref, cnt, neg, sems)
    _, blocks, width = shape
    half = own0.shape[1]
    local = localize(place()[2], half)
    s_hot = one_hot(src_ref, t, 2 * half, local)
    d_hot = one_hot(dst_ref, t, 2 * half, local)
    s_hot_ref[...] = s_hot
    d_hot_ref[...] = d_hot
    d_hot_t_ref[...] = d_hot.T
    source = mm(jnp.concatenate([own0[...], own1[...]], axis=1), s_hot)
    source_ref[...] = source.astype(BF)
    query = make_query(source, rel_ref[...].astype(F32))
    query_ref[...] = query
    query_t_ref[...] = query.T
    if last:
        return
    limits.wait()
    row_i = lax.broadcasted_iota(jnp.int32, (width, width), 0)
    col_j = lax.broadcasted_iota(jnp.int32, (width, width), 1)
    slot = lax.broadcasted_iota(jnp.int32, (width, 2 * half), 0)
    for b in range(blocks):
        nb = limits.negative(b)
        at = slice(b * width, (b + 1) * width)
        there = pl.ds(pl.multiple_of(nb * width, width), width)
        n_hot_ref[:, at] = d_hot_ref[:, there]
        n_hot_t_ref[at] = d_hot_t_ref[there, :]
        keep = jnp.logical_and(row_i < limits.count(b), col_j < limits.count(nb))
        mask_ref[:, at] = jnp.where(keep, 1.0 / width, 0.0)
        hot = d_hot_t_ref[at].astype(F32)
        v_hot_t_ref[at] = jnp.where(slot < limits.count(b), hot, 0.0).astype(BF)


def source_side(t, shape, cnt, neg, src, dst, own, rel):
    dim, slots = rel.shape
    width = shape[2]
    rows = 2 * own[0].shape[1]
    last = t == shape[0] - 1
    sds = lambda *shape: jax.ShapeDtypeStruct(shape, BF)
    outs = [sds(dim, slots), sds(slots, dim), sds(dim, slots), sds(rows, slots), sds(rows, slots)]
    if last:
        outs += [sds(slots, rows)]
    else:
        outs += [sds(slots, rows), sds(rows, slots), sds(slots, rows)]
        outs += [jax.ShapeDtypeStruct((width, slots), F32)]
    return pl.pallas_call(
        functools.partial(source_kernel, t, shape, last),
        in_specs=[anywhere()] * 2 + [vmem()] * 5,
        out_specs=[vmem()] * len(outs),
        out_shape=outs,
        scratch_shapes=[] if last else Limits.scratch(shape) + [pltpu.VMEM((slots, rows), BF)],
        compiler_params=params(),
        cost_estimate=cost(dim * slots, dim * slots),
        name="source_side",
    )(cnt, neg, src, dst, *own, rel)


def near_kernel(query_t_ref, far0, out_ref):
    out_ref[...] = mm(query_t_ref[...], far0[...])


def near_products(query_t, far0):
    slots, half = query_t.shape[0], far0.shape[1]
    return pl.pallas_call(
        near_kernel,
        in_specs=[vmem()] * 2,
        out_specs=vmem(),
        out_shape=jax.ShapeDtypeStruct((slots, half), F32),
        compiler_params=params(),
        cost_estimate=cost(slots * half, slots * half),
        name="near_products",
    )(query_t, far0)


def target_kernel(
    near, far1, query_ref, query_t_ref, v_hot_t_ref, n_hot_ref, n_hot_t_ref, mask_ref,
    gd_mine, gd_other, w_ref,
):
    width, slots = mask_ref.shape
    half = far1.shape[1]
    products = jnp.concatenate([near[...], mm(query_t_ref[...], far1[...])], axis=1)
    high = products.astype(BF)
    low = (products - high.astype(F32)).astype(BF)
    factors = []
    for lo in range(0, slots, width):
        at = slice(lo, lo + width)
        n_hot = n_hot_ref[:, at]
        scores = mm(high[at], n_hot) + mm(low[at], n_hot)
        weight = (jax.nn.sigmoid(scores) * mask_ref[:, at]).astype(BF)
        w_ref[:, at] = weight
        positive = jax.nn.sigmoid(-products[at]) * v_hot_t_ref[at].astype(F32)
        factors.append((mm(weight, n_hot_t_ref[at]) - positive).astype(BF))
    gd = mm(query_ref[...], jnp.concatenate(factors, axis=0))
    gd_mine[...] = gd[:, :half]
    gd_other[...] = gd[:, half:].astype(BF)


def target_grad(near, far1, query, query_t, v_hot_t, n_hot, n_hot_t, mask):
    dim, slots = query.shape
    half = far1.shape[1]
    sds = jax.ShapeDtypeStruct
    return pl.pallas_call(
        target_kernel,
        in_specs=[vmem()] * 8,
        out_specs=[vmem()] * 3,
        out_shape=[sds((dim, half), F32), sds((dim, half), BF), sds(mask.shape, BF)],
        compiler_params=params(),
        cost_estimate=cost(4 * dim * slots * half, 12 * dim * slots),
        name="target_grad",
    )(near, far1, query, query_t, v_hot_t, n_hot, n_hot_t, mask)


def source_grad_kernel(
    t, shape, cnt_ref, neg_ref, _, far0, far1, d_hot_ref, query_ref, w_ref, source_ref, rel_ref, s_hot_ref,
    gs_mine, gs_other, drel_ref, cnt, neg, sems, o_scr,
):
    limits = Limits(t, cnt_ref, neg_ref, cnt, neg, sems)
    half = gs_mine.shape[1]
    target = mm(jnp.concatenate([far0[...], far1[...]], axis=1), d_hot_ref[...])
    o_scr[...] = target.astype(BF)
    limits.wait()
    gpos = positive_factors(shape, limits, query_ref[...], target)
    dq = make_dquery(shape, limits, gpos, o_scr, w_ref)
    drel_ref[...] = conj_times(dq, source_ref[...].astype(F32))
    gs = mm(conj_times(dq, rel_ref[...].astype(F32)), s_hot_ref[...], NT)
    gs_mine[...] = gs[:, :half]
    gs_other[...] = gs[:, half:].astype(BF)


def source_grad(t, shape, cnt, neg, after, far, d_hot, query, weight, source, rel, s_hot):
    dim, slots = rel.shape
    half = s_hot.shape[0] // 2
    sds = jax.ShapeDtypeStruct
    return pl.pallas_call(
        functools.partial(source_grad_kernel, t, shape),
        in_specs=[anywhere()] * 3 + [vmem()] * 8,
        out_specs=[vmem()] * 3,
        out_shape=[sds((dim, half), F32), sds((dim, half), BF), sds((dim, slots), BF)],
        scratch_shapes=Limits.scratch(shape) + [pltpu.VMEM((dim, slots), BF)],
        compiler_params=params(),
        cost_estimate=cost(dim * slots, dim * slots),
        name="source_grad",
    )(cnt, neg, after, *far, d_hot, query, weight, source, rel, s_hot)


def last_kernel(
    t, shape, cnt_ref, neg_ref, far0, far1, query_ref, query_t_ref, d_hot_ref, source_ref, rel_ref,
    drel_ref, dsource_ref, dterm_ref, cnt, neg, sems, o_scr, d_scr, w_scr,
):
    limits = Limits(t, cnt_ref, neg_ref, cnt, neg, sems)
    far = jnp.concatenate([far0[...], far1[...]], axis=1)
    target = mm(far, d_hot_ref[...])
    query = query_ref[...]
    gpos = target_side(shape, limits, query, query_t_ref, target, o_scr, w_scr)
    dterm_ref[...] = target_terms(shape, limits, query, gpos, w_scr, d_scr)
    dq = make_dquery(shape, limits, gpos, o_scr, w_scr)
    drel_ref[...] = conj_times(dq, source_ref[...].astype(F32))
    dsource_ref[...] = conj_times(dq, rel_ref[...].astype(F32))


def last_terms(t, shape, cnt, neg, far, query, query_t, d_hot, source, rel):
    dim, slots = query.shape
    sds = jax.ShapeDtypeStruct
    return pl.pallas_call(
        functools.partial(last_kernel, t, shape),
        in_specs=[anywhere()] * 2 + [vmem()] * 7,
        out_specs=[vmem()] * 3,
        out_shape=[sds((dim, slots), BF)] * 3,
        scratch_shapes=Limits.scratch(shape)
        + [
            pltpu.VMEM((dim, slots), BF),
            pltpu.VMEM((dim, slots), F32),
            pltpu.VMEM((shape[2], slots), BF),
        ],
        compiler_params=params(),
        cost_estimate=cost(6 * dim * slots * shape[2], 12 * dim * slots),
        name="last_terms",
    )(cnt, neg, *far, query, query_t, d_hot, source, rel)


def both_kernel(_, dsource_ref, s_hot_ref, dterm_ref, d_hot_t_ref, gs_mine, gs_other, gd_mine, gd_other):
    half = gs_mine.shape[1]
    for terms, hot, dims, mine, other in (
        (dterm_ref, d_hot_t_ref, NN, gd_mine, gd_other),
        (dsource_ref, s_hot_ref, NT, gs_mine, gs_other),
    ):
        grad = mm(terms[...], hot[...], dims)
        mine[...] = grad[:, :half]
        other[...] = grad[:, half:].astype(BF)


def both_grads(after, dsource, s_hot, dterm, d_hot_t):
    dim, slots = dterm.shape
    half = s_hot.shape[0] // 2
    sds = jax.ShapeDtypeStruct
    return pl.pallas_call(
        both_kernel,
        in_specs=[anywhere()] + [vmem()] * 4,
        out_specs=[vmem()] * 4,
        out_shape=[sds((dim, half), F32), sds((dim, half), BF)] * 2,
        compiler_params=params(),
        cost_estimate=cost(8 * dim * slots * half, 12 * dim * slots),
        name="both_grads",
    )(after, dsource, s_hot, dterm, d_hot_t)


def update_kernel(n_grads, last, *refs):
    ent_ref, state_ref, grads = refs[0], refs[1], refs[2 : 2 + n_grads]
    grad = grads[0][...].astype(F32)
    for g in grads[1:]:
        grad = grad + g[...].astype(F32)
    dim = grad.shape[0]
    state = state_ref[...] + jnp.sum(grad * grad, axis=0, keepdims=True) / dim
    new = ent_ref[...] - grad * (learn_rate / jnp.sqrt(state))
    if last:
        refs[-1][:dim] = new
        refs[-1][dim:] = jnp.broadcast_to(state, (refs[-1].shape[0] - dim, state.shape[1]))
    else:
        refs[-3][...] = new
        refs[-2][...] = state
        refs[-1][...] = new.astype(BF)


def update(ent, state, grads, after, last=False):
    dim, half = ent.shape
    sds = jax.ShapeDtypeStruct
    outs = [sds((dim, half), F32), sds((1, half), F32), sds((dim, half), BF)]
    if last:
        outs = [sds((dim + 8, half), F32)]
    return pl.pallas_call(
        functools.partial(update_kernel, len(grads), last),
        in_specs=[vmem()] * (2 + len(grads)) + [anywhere()] * len(after),
        out_specs=[vmem()] * len(outs),
        out_shape=outs,
        compiler_params=params(),
        cost_estimate=cost(10 * dim * half, 16 * dim * half),
        name="update",
    )(ent, state, *grads, *after)


def pair_kernel(a_ref, b_ref, out_ref):
    out_ref[...] = (a_ref[...] + b_ref[...].astype(F32)).astype(out_ref.dtype)


def sum_pair(a, b, dtype=BF):
    return pl.pallas_call(
        pair_kernel,
        in_specs=[vmem()] * 2,
        out_specs=vmem(),
        out_shape=jax.ShapeDtypeStruct(a.shape, dtype),
        compiler_params=params(),
        name="sum_pair",
    )(a, b)


def held_kernel(x_ref, *refs):
    pass


def held(x, after):
    return pl.pallas_call(
        held_kernel,
        in_specs=[anywhere()] * (1 + len(after)),
        out_specs=anywhere(),
        out_shape=jax.ShapeDtypeStruct(x.shape, x.dtype),
        input_output_aliases={0: 0},
        compiler_params=params(),
        name="held",
    )(x, *after)


def whole_kernel(mine, theirs, ent_out, state_out, token):
    token[...] = jnp.zeros_like(token)
    dim, rows = ent_out.shape
    half = rows // 2
    edge = place()[2]
    for core, part in ((edge, mine), (1 - edge, theirs)):
        at = pl.ds(pl.multiple_of(core * half, half), half)
        ent_out[:, at] = part[:dim]
        state_out[:, at] = part[dim : dim + 1]


def whole_partition(mine, theirs):
    dim, half = mine.shape[0] - 8, mine.shape[1]
    return pl.pallas_call(
        whole_kernel,
        in_specs=[vmem()] * 2,
        out_specs=[vmem()] * 3,
        out_shape=[
            jax.ShapeDtypeStruct((dim, 2 * half), F32),
            jax.ShapeDtypeStruct((1, 2 * half), F32),
            jax.ShapeDtypeStruct((8, 128), F32),
        ],
        compiler_params=params(),
        name="whole_partition",
    )(mine, theirs)


def first_column(owner, core, w):
    return pl.multiple_of((2 * owner + core) * w, w)


def pieces_kernel(t, nz, same, ids_ref, drel_ref, acc_ref, *refs):
    mine, other = refs[-nz - 1 : -1], refs[-1]
    w = other.shape[2]
    z, x, edge = place()
    drel = drel_ref[...]
    for k in range(nz):
        owner = 2 * lax.bitwise_xor(z, k) + (x if same else 1 - x)
        at = [first_column(owner, core, w) for core in (edge, 1 - edge)]
        hot = jnp.concatenate([one_hot(ids_ref, t, w, lambda i, lo=lo: i - lo) for lo in at], axis=0)
        part = mm(drel, hot, NT)
        mine[k][...] = acc_ref[:, pl.ds(at[0], w)] + part[:, :w]
        other[k] = (acc_ref[:, pl.ds(at[1], w)] + part[:, w:]).astype(BF)


def pieces(t, n, same, rel_ids, drel, acc, after):
    dim, rels = acc.shape
    w = rels // (2 * n)
    sds = jax.ShapeDtypeStruct
    out = pl.pallas_call(
        functools.partial(pieces_kernel, t, n // 2, same),
        in_specs=[vmem()] * 3 + [anywhere()] * len(after),
        out_specs=[vmem()] * (n // 2 + 1),
        out_shape=[sds((dim, w), F32)] * (n // 2) + [sds((n // 2, dim, w), BF)],
        compiler_params=params(),
        cost_estimate=cost(dim * rels * drel.shape[1], 4 * dim * rels),
        name="pieces",
    )(rel_ids, drel, acc, *after)
    return out[:-1], out[-1]


def add_kernel(n, *refs):
    for k in range(n):
        refs[n + 1 + k][...] = (refs[k][...] + refs[n][k].astype(F32)).astype(BF)


def add_each(mine, theirs):
    n = len(mine)
    return pl.pallas_call(
        functools.partial(add_kernel, n),
        in_specs=[vmem()] * (n + 1),
        out_specs=[vmem()] * n,
        out_shape=[jax.ShapeDtypeStruct(x.shape, BF) for x in mine],
        compiler_params=params(),
        name="add_each",
    )(*mine, theirs)


def sum_kernel(k, count, mine, theirs, *refs):
    total = mine[...] + theirs[k].astype(F32)
    for r in refs[:count]:
        total = total + r[...].astype(F32)
    refs[-1][...] = total.astype(BF)


def sum_piece(k, mine, theirs, parts, after):
    return pl.pallas_call(
        functools.partial(sum_kernel, k, len(parts)),
        in_specs=[vmem()] * (2 + len(parts)) + [anywhere()] * len(after),
        out_specs=vmem(),
        out_shape=jax.ShapeDtypeStruct(mine.shape, BF),
        compiler_params=params(),
        name="sum_piece",
    )(mine, theirs, *parts, *after)


def stacked_kernel(*refs):
    for i in range(refs[-1].shape[0]):
        refs[-1][i] = refs[i][...]


def stacked(parts, after):
    return pl.pallas_call(
        stacked_kernel,
        in_specs=[vmem()] * len(parts) + [anywhere()] * len(after),
        out_specs=vmem(),
        out_shape=jax.ShapeDtypeStruct((len(parts), *parts[0].shape), parts[0].dtype),
        compiler_params=params(),
        name="stacked",
    )(*parts, *after)


def relnew_kernel(nz, kinds, count, first, last, rel_ref, state_ref, *refs):
    arrays = refs[:count]
    rel_out, state_to, buf, sems = refs[-5:-1] if last else refs[-4:]
    state_out = refs[-1] if last else state_to
    w = buf.shape[2]
    state_out[...] = refs[count + (0 if first else 1)][...]
    z, x, edge = place()
    copies = []
    for i, (k, same, own, source, index) in enumerate(kinds):
        owner = 2 * lax.bitwise_xor(z, k) + (x if same else 1 - x)
        at = pl.ds(first_column(owner, edge if own else 1 - edge, w), w)
        grad = (arrays[source][...] if index is None else arrays[source][index]).astype(F32)
        state = state_ref[:, at] + jnp.sum(grad * grad, axis=0, keepdims=True) / grad.shape[0]
        state_out[:, at] = state
        buf[i] = rel_ref[:, at] - grad * (learn_rate / jnp.sqrt(state))
        copy = pltpu.make_async_copy(buf.at[i], rel_out.at[:, at], sems.at[i])
        copy.start()
        copies.append(copy)
    if last:
        copy = pltpu.make_async_copy(state_out, state_to, sems.at[len(kinds)])
        copy.start()
        copies.append(copy)
    for copy in copies:
        copy.wait()


def relnew(nz, relations, state, groups, before, last=False):
    dim, rels = relations.shape
    w = rels // (4 * nz)
    kinds, arrays = [], []
    for ks, same, own, parts in groups:
        one = not isinstance(parts, list)
        for i, k in enumerate(ks):
            kinds.append((k, same, own, len(arrays) + (0 if one else i), i if one else None))
        arrays += [parts] if one else parts
    count = len(kinds)
    start = [state] if before is None else list(before)
    return pl.pallas_call(
        functools.partial(relnew_kernel, nz, tuple(kinds), len(arrays), before is None, last),
        in_specs=[vmem()] * (2 + len(arrays))
        + ([anywhere()] if before else [])
        + [vmem()],
        out_specs=[anywhere(), anywhere() if last else vmem()],
        out_shape=[jax.ShapeDtypeStruct((dim, rels), F32), jax.ShapeDtypeStruct((1, rels), F32)],
        input_output_aliases={2 + len(arrays): 0} if before else {},
        scratch_shapes=[pltpu.VMEM((count, dim, w), F32), pltpu.SemaphoreType.DMA((count + 1,))]
        + ([pltpu.VMEM((1, rels), F32)] if last else []),
        compiler_params=params(),
        cost_estimate=cost(dim, dim),
        name="relnew",
    )(relations, state, *arrays, *start)


def relation_update(t, rel_ids, drel, acc, relations, state, send, finish):
    n = lax.axis_size("dom")
    dim, rels = relations.shape
    if n < 4 or n & (n - 1) or rels % (256 * n):
        total = lax.psum(relsum(t, rel_ids, drel, acc, rels), ("dom", "edge"))
        state = state + jnp.mean(total * total, axis=0)
        return relations - learn_rate * total / jnp.sqrt(state)[None, :], state, finish(send(drel), [])
    nz = n // 2
    mine_x, other_x = pieces(t, n, False, rel_ids, drel, acc, [])
    mine_s, other_s = pieces(t, n, True, rel_ids, drel, acc, [other_x])
    to_x = add_each(mine_x, across(other_x))
    theirs = across(other_s)
    down = range(nz - 1, -1, -1)
    from_x = {k: swapped(to_x[k], 1) for k in down}
    grads = send(to_x[0])
    addends = {k: [from_x[k]] for k in range(nz)}
    bits = [1 << i for i in range(nz.bit_length() - 1)]
    steps = [(bit, k) for bit in bits for k in reversed(range(bit + 2 * bit, nz, 2 * bit))]
    steps += [(bit, bit) for bit in reversed(bits)]
    turned = []
    for bit, k in steps:
        after = turned[-1:] if turned else grads[1:2]
        turned.append(sum_piece(k, mine_s[k], theirs, addends[k], after))
        there = swapped(turned[-1], 2 * bit)
        addends[k ^ bit].append(held(there, []) if k == bit == nz // 2 else there)
    done = finish(grads, [turned[-1]])
    summed = sum_piece(0, mine_s[0], theirs, addends[0], [])
    got = [summed if k == 0 else swapped(summed, 2 * k) for k in range(nz)]
    got_x = [swapped(piece, 1) for piece in got]
    state = state.reshape(1, rels)
    ks = [0, *down[:-1]]
    mine = [got[k] for k in ks]
    mine_x = [got_x[k] for k in ks]
    there = across(stacked(mine, [done[2]]))
    new = relnew(nz, relations, state, [(ks, True, True, mine)], None)
    there_x = across(stacked(mine_x, [new[1]]))
    groups = [(ks, True, False, there), (ks, False, True, mine_x)]
    new = relnew(nz, relations, state, groups, new)
    groups = [(ks, False, False, there_x)]
    rel_new, state_new = relnew(nz, relations, state, groups, new, last=True)
    return rel_new, state_new.reshape(rels), done


def on_device(
    entities,
    entity_state,
    relations,
    relation_state,
    src_rows,
    rel_ids,
    dst_rows,
    counts,
    neg_blocks,
):
    rounds = src_rows.shape[0]
    rels = relations.shape[1]
    shape = src_rows.shape
    cnt, neg = counts.T, neg_blocks.T
    g_mine, g_other, drel, rel16, ent, state = first_round(
        cnt, neg, src_rows, dst_rows, rel_ids, entities, entity_state.reshape(1, -1), relations
    )
    acc = relsum(0, rel_ids, drel, None, rels)
    ent, state, low = update(ent, state, [g_mine, across(g_other)], [])
    rel = relvec(1, rel_ids, rel16)
    for t in range(1, rounds):
        far = shifted(low, -t)
        own = (low, across(low))
        query, query_t, source, s_hot, d_hot, *hots = source_side(
            t, shape, cnt, neg, src_rows, dst_rows, own, rel
        )
        far = held(far, [query, acc])
        far = (far, across(far))
        if t == rounds - 1:
            break
        near = near_products(query_t, far[0])
        gd_mine, gd_other, weight = target_grad(near, far[1], query, query_t, *hots)
        gd = sum_pair(gd_mine, across(gd_other))
        gs_mine, gs_other, drel = source_grad(
            t, shape, cnt, neg, gd, far, d_hot, query, weight, source, rel, s_hot
        )
        acc = relsum(t, rel_ids, drel, acc, rels)
        rel = relvec(t + 1, rel_ids, rel16)
        grads = [sum_pair(gs_mine, shifted(gd, t), F32), across(gs_other)]
        ent, state, low = update(ent, state, grads, [rel])
    drel, dsource, dterm = last_terms(t, shape, cnt, neg, far, query, query_t, d_hot, source, rel)

    def send(after):
        gs_mine, gs_other, gd_mine, gd_other = both_grads(after, dsource, s_hot, dterm, hots[0])
        gd = sum_pair(gd_mine, across(gd_other))
        return [gs_mine, across(gs_other), shifted(gd, t)]

    def finish(grads, after):
        (mine,) = update(ent, state, grads, after, last=True)
        return whole_partition(mine, across(mine))

    rel_new, rel_state, done = relation_update(
        t, rel_ids, drel, acc, relations, relation_state, send, finish
    )
    return (done[0], done[1].reshape(-1), rel_new, rel_state)


def solution(mesh):
    return jax.shard_map(
        on_device,
        mesh=mesh,
        in_specs=(
            P(None, ("groups", "dom")),
            P(("groups", "dom")),
            P(None, "groups"),
            P("groups"),
            P(None, ("groups", "dom", "edge"), None),
            P(None, ("groups", "dom", "edge"), None),
            P(None, ("groups", "dom", "edge"), None),
            P(None, ("groups", "dom", "edge")),
            P(None, ("groups", "dom", "edge")),
        ),
        out_specs=(
            P(None, ("groups", "dom")),
            P(("groups", "dom")),
            P(None, "groups"),
            P("groups"),
        ),
        check_vma=False,
    )
```

```python
import functools

import jax
import jax.numpy as jnp
from jax import lax
from jax.experimental import pallas as pl
from jax.experimental.pallas import tpu as pltpu
from jax.sharding import PartitionSpec as P

learn_rate = 0.1
BF = jnp.bfloat16
F32 = jnp.float32
VMEM_LIMIT = 24 * 1024 * 1024
NN = (((1,), (0,)), ((), ()))
NT = (((1,), (1,)), ((), ()))
TN = (((0,), (0,)), ((), ()))


def mm(a, b, dims=NN):
    return lax.dot_general(a, b, dims, preferred_element_type=F32)


def vmem():
    return pl.BlockSpec(memory_space=pltpu.VMEM)


def smem():
    return pl.BlockSpec(memory_space=pltpu.SMEM)


def anywhere():
    return pl.BlockSpec(memory_space=pl.ANY)


def in_hbm(x):
    return pltpu.with_memory_space_constraint(x, pltpu.HBM)


def cost(flops, size):
    return pl.CostEstimate(flops=flops, bytes_accessed=size, transcendentals=0)


def params():
    return pltpu.CompilerParams(vmem_limit_bytes=VMEM_LIMIT)


def shifted(x, by):
    n = lax.axis_size("dom")
    return lax.ppermute(x, "dom", [(i, (i + by) % n) for i in range(n)])


def swapped(x, bits):
    n = lax.axis_size("dom")
    return lax.ppermute(x, "dom", [(i, i ^ bits) for i in range(n)])


def across(x):
    return lax.ppermute(x, "edge", [(0, 1), (1, 0)])


def one_hot(rows_ref, t, count, base):
    blocks, width = rows_ref.shape[1:]
    at = lax.broadcasted_iota(jnp.int32, (count, width), 0)
    idx = rows_ref[t]
    return jnp.concatenate(
        [
            jnp.where(at == base(idx[b : b + 1, :]), 1.0, 0.0).astype(BF)
            for b in range(blocks)
        ],
        axis=1,
    )


def relvec_kernel(t, ids_ref, rel_ref, out_ref):
    rels = rel_ref.shape[1]
    tile = min(rels, 512)
    out = None
    for lo in range(0, rels, tile):
        hot = one_hot(ids_ref, t, tile, lambda i, lo=lo: i - lo)
        part = mm(rel_ref[:, lo : lo + tile], hot)
        out = part if out is None else out + part
    out_ref[...] = out.astype(BF)


def relvec(t, rel_ids, rel16):
    width, rels = rel16.shape
    slots = rel_ids.shape[1] * rel_ids.shape[2]
    return pl.pallas_call(
        functools.partial(relvec_kernel, t),
        in_specs=[vmem()] * 2,
        out_specs=vmem(),
        out_shape=jax.ShapeDtypeStruct((width, slots), BF),
        compiler_params=params(),
        cost_estimate=cost(width * slots, width * slots),
        name="relvec",
    )(rel_ids, rel16)


def relsum_kernel(t, first, ids_ref, drel_ref, *refs):
    out_ref = refs[-1]
    rels = out_ref.shape[1]
    tile = min(rels, 512)
    drel = drel_ref[...]
    for lo in range(0, rels, tile):
        hot = one_hot(ids_ref, t, tile, lambda i, lo=lo: i - lo)
        part = mm(drel, hot, NT)
        out_ref[:, lo : lo + tile] = part if first else refs[0][:, lo : lo + tile] + part


def relsum(t, rel_ids, drel, acc, rels):
    width, slots = drel.shape
    ins = [rel_ids, drel] + ([] if acc is None else [acc])
    return pl.pallas_call(
        functools.partial(relsum_kernel, t, acc is None),
        in_specs=[vmem()] * len(ins),
        out_specs=vmem(),
        out_shape=jax.ShapeDtypeStruct((width, rels), F32),
        input_output_aliases={} if acc is None else {2: 0},
        compiler_params=params(),
        cost_estimate=cost(width * slots, width * slots),
        name="relsum",
    )(*ins)


class Limits:
    scratch = lambda shape: [
        pltpu.SMEM((shape[1], shape[0]), jnp.int32),
        pltpu.SMEM((shape[1], shape[0]), jnp.int32),
        pltpu.SemaphoreType.DMA((2,)),
    ]

    def __init__(self, t, from_cnt, from_neg, cnt, neg, sems):
        self.t, self.cnt, self.neg = t, cnt, neg
        self.copies = [
            pltpu.make_async_copy(from_cnt, cnt, sems.at[0]),
            pltpu.make_async_copy(from_neg, neg, sems.at[1]),
        ]
        for copy in self.copies:
            copy.start()

    def wait(self):
        for copy in self.copies:
            copy.wait()

    def count(self, b):
        return self.cnt[b, self.t]

    def negative(self, b):
        return self.neg[b, self.t]


def place():
    dom = lax.axis_index("dom")
    return dom // 2, lax.rem(dom, 2), lax.axis_index("edge")


def localize(edge, half):
    def local(idx):
        moved = idx + edge * half
        return jnp.where(moved >= 2 * half, moved - 2 * half, moved)

    return local


def halves(x):
    hd = x.shape[0] // 2
    return x[:hd], x[hd:]


def make_query(source, rel):
    (s_re, s_im), (w_re, w_im) = halves(source), halves(rel)
    return jnp.concatenate(
        [s_re * w_re - s_im * w_im, s_re * w_im + s_im * w_re], axis=0
    ).astype(BF)


def conj_times(dq, v):
    (dq_re, dq_im), (v_re, v_im) = halves(dq), halves(v)
    return jnp.concatenate(
        [dq_re * v_re + dq_im * v_im, dq_im * v_re - dq_re * v_im], axis=0
    ).astype(BF)


def positive_factors(shape, limits, query, target):
    _, blocks, width = shape
    pos = jnp.sum(query.astype(F32) * target, axis=0, keepdims=True)
    lane = lax.broadcasted_iota(jnp.int32, (1, width), 1)
    valid = jnp.concatenate(
        [jnp.where(lane < limits.count(b), 1.0, 0.0) for b in range(blocks)], axis=1
    )
    return -jax.nn.sigmoid(-pos) * valid


def target_side(shape, limits, query, query_t, target, o_ref, w_ref):
    _, blocks, width = shape
    lanes = lambda b: pl.ds(pl.multiple_of(b * width, width), width)
    count = limits.count
    o_ref[...] = target.astype(BF)
    limits.wait()
    gpos = positive_factors(shape, limits, query, target)
    row_i = lax.broadcasted_iota(jnp.int32, (width, width), 0)
    col_j = lax.broadcasted_iota(jnp.int32, (width, width), 1)
    for b in range(blocks):
        nb = limits.negative(b)
        neg = o_ref[:, lanes(nb)]
        at = slice(b * width, (b + 1) * width)
        scores = mm(query[:, at], neg, TN) if query_t is None else mm(query_t[at], neg)
        keep = jnp.logical_and(row_i < count(b), col_j < count(nb))
        w_ref[:, at] = jnp.where(keep, jax.nn.sigmoid(scores) / width, 0.0).astype(BF)
    return gpos


def target_terms(shape, limits, query, gpos, w_ref, d_ref):
    _, blocks, width = shape
    d_ref[...] = gpos * query.astype(F32)
    for b in range(blocks):
        at = slice(b * width, (b + 1) * width)
        to = pl.ds(pl.multiple_of(limits.negative(b) * width, width), width)
        d_ref[:, to] += mm(query[:, at], w_ref[:, at])
    return d_ref[...].astype(BF)


def make_dquery(shape, limits, gpos, o_ref, w_ref):
    _, blocks, width = shape
    lanes = lambda b: pl.ds(pl.multiple_of(b * width, width), width)
    out = []
    for b in range(blocks):
        nb = limits.negative(b)
        at = slice(b * width, (b + 1) * width)
        own = gpos[:, at] * o_ref[:, at].astype(F32)
        out.append(own + mm(o_ref[:, lanes(nb)], w_ref[:, at], NT))
    return jnp.concatenate(out, axis=1)


def first_kernel(
    shape, cnt_ref, neg_ref, src_ref, dst_ref, ids_ref, ent_ref, state_ref, rel_ref,
    g_mine, g_other, drel_ref, rel16_ref, ent_mine, state_mine,
    cnt, neg, lim_sems, src, dst, ids, ent, state, rel_buf, o_scr, d_scr, w_scr, in_sems, sems,
):
    rels = rel_buf.shape[1]
    tile = min(rels, 512)
    spans = range(0, rels, tile)
    inputs = [
        pltpu.make_async_copy(there, here, in_sems.at[i])
        for i, (there, here) in enumerate(
            [(src_ref.at[:1], src), (dst_ref.at[:1], dst), (ids_ref.at[:1], ids), (ent_ref, ent), (state_ref, state)]
        )
    ]
    loads = [
        pltpu.make_async_copy(
            rel_ref.at[:, lo : lo + tile], rel_buf.at[:, lo : lo + tile], sems.at[i]
        )
        for i, lo in enumerate(spans)
    ]
    for load in inputs:
        load.start()
    limits = Limits(0, cnt_ref, neg_ref, cnt, neg, lim_sems)
    for load in loads:
        load.start()
    half = ent.shape[1] // 2
    _, _, edge = place()
    local = localize(edge, half)
    inputs[0].wait()
    s_hot = one_hot(src, 0, 2 * half, local)
    inputs[1].wait()
    d_hot = one_hot(dst, 0, 2 * half, local)
    inputs[2].wait()
    ids_hot = [one_hot(ids, 0, tile, lambda i, lo=lo: i - lo) for lo in spans]
    inputs[3].wait()
    inputs[4].wait()
    mine = pl.ds(pl.multiple_of(edge * half, half), half)
    ent_mine[...] = ent[:, mine]
    state_mine[...] = state[:, mine]
    table = jnp.concatenate(
        [ent[:, pl.ds(pl.multiple_of(h * half, half), half)].astype(BF) for h in (edge, 1 - edge)],
        axis=1,
    )
    source = mm(table, s_hot)
    target = mm(table, d_hot)
    rel = None
    for load, lo, hot in zip(loads, spans, ids_hot):
        load.wait()
        low = rel_buf[:, lo : lo + tile].astype(BF)
        rel16_ref[:, lo : lo + tile] = low
        part = mm(low, hot)
        rel = part if rel is None else rel + part
    query = make_query(source, rel)
    gpos = target_side(shape, limits, query, None, target, o_scr, w_scr)
    dq = make_dquery(shape, limits, gpos, o_scr, w_scr)
    drel_ref[...] = conj_times(dq, source)
    total = mm(conj_times(dq, rel), s_hot, NT) + mm(
        target_terms(shape, limits, query, gpos, w_scr, d_scr), d_hot, NT
    )
    g_mine[...] = total[:, :half]
    g_other[...] = total[:, half:].astype(BF)


def first_round(cnt, neg, src, dst, rel_ids, entities, state, relations):
    dim, rows = entities.shape
    rels = relations.shape[1]
    _, blocks, width = src.shape
    slots = blocks * width
    sds = jax.ShapeDtypeStruct
    return pl.pallas_call(
        functools.partial(first_kernel, src.shape),
        in_specs=[anywhere()] * 8,
        out_specs=[vmem()] * 6,
        out_shape=[
            sds((dim, rows // 2), F32),
            sds((dim, rows // 2), BF),
            sds((dim, slots), BF),
            sds((dim, rels), BF),
            sds((dim, rows // 2), F32),
            sds((1, rows // 2), F32),
        ],
        scratch_shapes=Limits.scratch(src.shape)
        + [
            pltpu.VMEM((1, blocks, width), jnp.int32),
            pltpu.VMEM((1, blocks, width), jnp.int32),
            pltpu.VMEM((1, blocks, width), jnp.int32),
            pltpu.VMEM((dim, rows), F32),
            pltpu.VMEM((1, rows), F32),
            pltpu.VMEM((dim, rels), F32),
            pltpu.VMEM((dim, slots), BF),
            pltpu.VMEM((dim, slots), F32),
            pltpu.VMEM((width, slots), BF),
            pltpu.SemaphoreType.DMA((5,)),
            pltpu.SemaphoreType.DMA((-(-rels // min(rels, 512)),)),
        ],
        compiler_params=params(),
        cost_estimate=cost(2 * dim * slots * (rels + 4 * rows), 8 * dim * rels),
        name="first_round",
    )(*(in_hbm(x) for x in (cnt, neg, src, dst, rel_ids, entities, state, relations)))


def source_kernel(t, shape, last, cnt_ref, neg_ref, src_ref, dst_ref, own0, own1, rel_ref, *refs):
    query_ref, query_t_ref, source_ref, s_hot_ref, d_hot_ref = refs[:5]
    if last:
        (d_hot_t_ref,) = refs[5:]
    else:
        v_hot_t_ref, n_hot_ref, n_hot_t_ref, mask_ref, cnt, neg, sems, d_hot_t_ref = refs[5:]
        limits = Limits(t, cnt_ref, neg_ref, cnt, neg, sems)
    _, blocks, width = shape
    half = own0.shape[1]
    local = localize(place()[2], half)
    s_hot = one_hot(src_ref, t, 2 * half, local)
    d_hot = one_hot(dst_ref, t, 2 * half, local)
    s_hot_ref[...] = s_hot
    d_hot_ref[...] = d_hot
    d_hot_t_ref[...] = d_hot.T
    source = mm(jnp.concatenate([own0[...], own1[...]], axis=1), s_hot)
    source_ref[...] = source.astype(BF)
    query = make_query(source, rel_ref[...].astype(F32))
    query_ref[...] = query
    query_t_ref[...] = query.T
    if last:
        return
    limits.wait()
    row_i = lax.broadcasted_iota(jnp.int32, (width, width), 0)
    col_j = lax.broadcasted_iota(jnp.int32, (width, width), 1)
    slot = lax.broadcasted_iota(jnp.int32, (width, 2 * half), 0)
    for b in range(blocks):
        nb = limits.negative(b)
        at = slice(b * width, (b + 1) * width)
        there = pl.ds(pl.multiple_of(nb * width, width), width)
        n_hot_ref[:, at] = d_hot_ref[:, there]
        n_hot_t_ref[at] = d_hot_t_ref[there, :]
        keep = jnp.logical_and(row_i < limits.count(b), col_j < limits.count(nb))
        mask_ref[:, at] = jnp.where(keep, 1.0 / width, 0.0)
        hot = d_hot_t_ref[at].astype(F32)
        v_hot_t_ref[at] = jnp.where(slot < limits.count(b), hot, 0.0).astype(BF)


def source_side(t, shape, cnt, neg, src, dst, own, rel):
    dim, slots = rel.shape
    width = shape[2]
    rows = 2 * own[0].shape[1]
    last = t == shape[0] - 1
    sds = lambda *shape: jax.ShapeDtypeStruct(shape, BF)
    outs = [sds(dim, slots), sds(slots, dim), sds(dim, slots), sds(rows, slots), sds(rows, slots)]
    if last:
        outs += [sds(slots, rows)]
    else:
        outs += [sds(slots, rows), sds(rows, slots), sds(slots, rows)]
        outs += [jax.ShapeDtypeStruct((width, slots), F32)]
    return pl.pallas_call(
        functools.partial(source_kernel, t, shape, last),
        in_specs=[anywhere()] * 2 + [vmem()] * 5,
        out_specs=[vmem()] * len(outs),
        out_shape=outs,
        scratch_shapes=[] if last else Limits.scratch(shape) + [pltpu.VMEM((slots, rows), BF)],
        compiler_params=params(),
        cost_estimate=cost(dim * slots, dim * slots),
        name="source_side",
    )(cnt, neg, src, dst, *own, rel)


def near_kernel(query_t_ref, far0, out_ref):
    out_ref[...] = mm(query_t_ref[...], far0[...])


def near_products(query_t, far0):
    slots, half = query_t.shape[0], far0.shape[1]
    return pl.pallas_call(
        near_kernel,
        in_specs=[vmem()] * 2,
        out_specs=vmem(),
        out_shape=jax.ShapeDtypeStruct((slots, half), F32),
        compiler_params=params(),
        cost_estimate=cost(slots * half, slots * half),
        name="near_products",
    )(query_t, far0)


def target_kernel(
    near, far1, query_ref, query_t_ref, v_hot_t_ref, n_hot_ref, n_hot_t_ref, mask_ref,
    gd_mine, gd_other, w_ref,
):
    width, slots = mask_ref.shape
    half = far1.shape[1]
    products = jnp.concatenate([near[...], mm(query_t_ref[...], far1[...])], axis=1)
    high = products.astype(BF)
    low = (products - high.astype(F32)).astype(BF)
    factors = []
    for lo in range(0, slots, width):
        at = slice(lo, lo + width)
        n_hot = n_hot_ref[:, at]
        both = jnp.concatenate([high[at], low[at]], axis=1)
        scores = mm(both, jnp.concatenate([n_hot, n_hot], axis=0))
        weight = (jax.nn.sigmoid(scores) * mask_ref[:, at]).astype(BF)
        w_ref[:, at] = weight
        positive = jax.nn.sigmoid(-products[at]) * v_hot_t_ref[at].astype(F32)
        factors.append((mm(weight, n_hot_t_ref[at]) - positive).astype(BF))
    gd = mm(query_ref[...], jnp.concatenate(factors, axis=0))
    gd_mine[...] = gd[:, :half]
    gd_other[...] = gd[:, half:].astype(BF)


def target_grad(near, far1, query, query_t, v_hot_t, n_hot, n_hot_t, mask):
    dim, slots = query.shape
    half = far1.shape[1]
    sds = jax.ShapeDtypeStruct
    return pl.pallas_call(
        target_kernel,
        in_specs=[vmem()] * 8,
        out_specs=[vmem()] * 3,
        out_shape=[sds((dim, half), F32), sds((dim, half), BF), sds(mask.shape, BF)],
        compiler_params=params(),
        cost_estimate=cost(4 * dim * slots * half, 12 * dim * slots),
        name="target_grad",
    )(near, far1, query, query_t, v_hot_t, n_hot, n_hot_t, mask)


def source_grad_kernel(
    t, shape, cnt_ref, neg_ref, _, far0, far1, d_hot_ref, query_ref, w_ref, source_ref, rel_ref, s_hot_ref,
    gs_mine, gs_other, drel_ref, cnt, neg, sems, o_scr,
):
    limits = Limits(t, cnt_ref, neg_ref, cnt, neg, sems)
    half = gs_mine.shape[1]
    target = mm(jnp.concatenate([far0[...], far1[...]], axis=1), d_hot_ref[...])
    o_scr[...] = target.astype(BF)
    limits.wait()
    gpos = positive_factors(shape, limits, query_ref[...], target)
    dq = make_dquery(shape, limits, gpos, o_scr, w_ref)
    drel_ref[...] = conj_times(dq, source_ref[...].astype(F32))
    gs = mm(conj_times(dq, rel_ref[...].astype(F32)), s_hot_ref[...], NT)
    gs_mine[...] = gs[:, :half]
    gs_other[...] = gs[:, half:].astype(BF)


def source_grad(t, shape, cnt, neg, after, far, d_hot, query, weight, source, rel, s_hot):
    dim, slots = rel.shape
    half = s_hot.shape[0] // 2
    sds = jax.ShapeDtypeStruct
    return pl.pallas_call(
        functools.partial(source_grad_kernel, t, shape),
        in_specs=[anywhere()] * 3 + [vmem()] * 8,
        out_specs=[vmem()] * 3,
        out_shape=[sds((dim, half), F32), sds((dim, half), BF), sds((dim, slots), BF)],
        scratch_shapes=Limits.scratch(shape) + [pltpu.VMEM((dim, slots), BF)],
        compiler_params=params(),
        cost_estimate=cost(dim * slots, dim * slots),
        name="source_grad",
    )(cnt, neg, after, *far, d_hot, query, weight, source, rel, s_hot)


def last_kernel(
    t, shape, cnt_ref, neg_ref, far0, far1, query_ref, query_t_ref, d_hot_ref, source_ref, rel_ref,
    drel_ref, dsource_ref, dterm_ref, cnt, neg, sems, o_scr, d_scr, w_scr,
):
    limits = Limits(t, cnt_ref, neg_ref, cnt, neg, sems)
    far = jnp.concatenate([far0[...], far1[...]], axis=1)
    target = mm(far, d_hot_ref[...])
    query = query_ref[...]
    gpos = target_side(shape, limits, query, query_t_ref, target, o_scr, w_scr)
    dterm_ref[...] = target_terms(shape, limits, query, gpos, w_scr, d_scr)
    dq = make_dquery(shape, limits, gpos, o_scr, w_scr)
    drel_ref[...] = conj_times(dq, source_ref[...].astype(F32))
    dsource_ref[...] = conj_times(dq, rel_ref[...].astype(F32))


def last_terms(t, shape, cnt, neg, far, query, query_t, d_hot, source, rel):
    dim, slots = query.shape
    sds = jax.ShapeDtypeStruct
    return pl.pallas_call(
        functools.partial(last_kernel, t, shape),
        in_specs=[anywhere()] * 2 + [vmem()] * 7,
        out_specs=[vmem()] * 3,
        out_shape=[sds((dim, slots), BF)] * 3,
        scratch_shapes=Limits.scratch(shape)
        + [
            pltpu.VMEM((dim, slots), BF),
            pltpu.VMEM((dim, slots), F32),
            pltpu.VMEM((shape[2], slots), BF),
        ],
        compiler_params=params(),
        cost_estimate=cost(6 * dim * slots * shape[2], 12 * dim * slots),
        name="last_terms",
    )(cnt, neg, *far, query, query_t, d_hot, source, rel)


def both_kernel(_, dsource_ref, s_hot_ref, dterm_ref, d_hot_t_ref, gs_mine, gs_other, gd_mine, gd_other):
    half = gs_mine.shape[1]
    for terms, hot, dims, mine, other in (
        (dterm_ref, d_hot_t_ref, NN, gd_mine, gd_other),
        (dsource_ref, s_hot_ref, NT, gs_mine, gs_other),
    ):
        grad = mm(terms[...], hot[...], dims)
        mine[...] = grad[:, :half]
        other[...] = grad[:, half:].astype(BF)


def both_grads(after, dsource, s_hot, dterm, d_hot_t):
    dim, slots = dterm.shape
    half = s_hot.shape[0] // 2
    sds = jax.ShapeDtypeStruct
    return pl.pallas_call(
        both_kernel,
        in_specs=[anywhere()] + [vmem()] * 4,
        out_specs=[vmem()] * 4,
        out_shape=[sds((dim, half), F32), sds((dim, half), BF)] * 2,
        compiler_params=params(),
        cost_estimate=cost(8 * dim * slots * half, 12 * dim * slots),
        name="both_grads",
    )(after, dsource, s_hot, dterm, d_hot_t)


def update_kernel(n_grads, last, *refs):
    ent_ref, state_ref, grads = refs[0], refs[1], refs[2 : 2 + n_grads]
    grad = grads[0][...].astype(F32)
    for g in grads[1:]:
        grad = grad + g[...].astype(F32)
    dim = grad.shape[0]
    state = state_ref[...] + jnp.sum(grad * grad, axis=0, keepdims=True) / dim
    new = ent_ref[...] - grad * (learn_rate / jnp.sqrt(state))
    if last:
        refs[-1][:dim] = new
        refs[-1][dim:] = jnp.broadcast_to(state, (refs[-1].shape[0] - dim, state.shape[1]))
    else:
        refs[-3][...] = new
        refs[-2][...] = state
        refs[-1][...] = new.astype(BF)


def update(ent, state, grads, after, last=False):
    dim, half = ent.shape
    sds = jax.ShapeDtypeStruct
    outs = [sds((dim, half), F32), sds((1, half), F32), sds((dim, half), BF)]
    if last:
        outs = [sds((dim + 8, half), F32)]
    return pl.pallas_call(
        functools.partial(update_kernel, len(grads), last),
        in_specs=[vmem()] * (2 + len(grads)) + [anywhere()] * len(after),
        out_specs=[vmem()] * len(outs),
        out_shape=outs,
        compiler_params=params(),
        cost_estimate=cost(10 * dim * half, 16 * dim * half),
        name="update",
    )(ent, state, *grads, *after)


def pair_kernel(a_ref, b_ref, out_ref):
    out_ref[...] = (a_ref[...] + b_ref[...].astype(F32)).astype(out_ref.dtype)


def sum_pair(a, b, dtype=BF):
    return pl.pallas_call(
        pair_kernel,
        in_specs=[vmem()] * 2,
        out_specs=vmem(),
        out_shape=jax.ShapeDtypeStruct(a.shape, dtype),
        compiler_params=params(),
        name="sum_pair",
    )(a, b)


def held_kernel(x_ref, *refs):
    pass


def held(x, after):
    return pl.pallas_call(
        held_kernel,
        in_specs=[anywhere()] * (1 + len(after)),
        out_specs=anywhere(),
        out_shape=jax.ShapeDtypeStruct(x.shape, x.dtype),
        input_output_aliases={0: 0},
        compiler_params=params(),
        name="held",
    )(x, *after)


def whole_kernel(mine, theirs, ent_out, state_out, token):
    token[...] = jnp.zeros_like(token)
    dim, rows = ent_out.shape
    half = rows // 2
    edge = place()[2]
    for core, part in ((edge, mine), (1 - edge, theirs)):
        at = pl.ds(pl.multiple_of(core * half, half), half)
        ent_out[:, at] = part[:dim]
        state_out[:, at] = part[dim : dim + 1]


def whole_partition(mine, theirs):
    dim, half = mine.shape[0] - 8, mine.shape[1]
    return pl.pallas_call(
        whole_kernel,
        in_specs=[vmem()] * 2,
        out_specs=[vmem()] * 3,
        out_shape=[
            jax.ShapeDtypeStruct((dim, 2 * half), F32),
            jax.ShapeDtypeStruct((1, 2 * half), F32),
            jax.ShapeDtypeStruct((8, 128), F32),
        ],
        compiler_params=params(),
        name="whole_partition",
    )(mine, theirs)


def first_column(owner, core, w):
    return pl.multiple_of((2 * owner + core) * w, w)


def pieces_kernel(t, nz, same, ids_ref, drel_ref, acc_ref, *refs):
    mine, other = refs[-nz - 1 : -1], refs[-1]
    w = other.shape[2]
    z, x, edge = place()
    drel = drel_ref[...]
    for k in range(nz):
        owner = 2 * lax.bitwise_xor(z, k) + (x if same else 1 - x)
        at = [first_column(owner, core, w) for core in (edge, 1 - edge)]
        hot = jnp.concatenate([one_hot(ids_ref, t, w, lambda i, lo=lo: i - lo) for lo in at], axis=0)
        part = mm(drel, hot, NT)
        mine[k][...] = acc_ref[:, pl.ds(at[0], w)] + part[:, :w]
        other[k] = (acc_ref[:, pl.ds(at[1], w)] + part[:, w:]).astype(BF)


def pieces(t, n, same, rel_ids, drel, acc, after):
    dim, rels = acc.shape
    w = rels // (2 * n)
    sds = jax.ShapeDtypeStruct
    out = pl.pallas_call(
        functools.partial(pieces_kernel, t, n // 2, same),
        in_specs=[vmem()] * 3 + [anywhere()] * len(after),
        out_specs=[vmem()] * (n // 2 + 1),
        out_shape=[sds((dim, w), F32)] * (n // 2) + [sds((n // 2, dim, w), BF)],
        compiler_params=params(),
        cost_estimate=cost(dim * rels * drel.shape[1], 4 * dim * rels),
        name="pieces",
    )(rel_ids, drel, acc, *after)
    return out[:-1], out[-1]


def add_kernel(n, *refs):
    for k in range(n):
        refs[n + 1 + k][...] = (refs[k][...] + refs[n][k].astype(F32)).astype(BF)


def add_each(mine, theirs):
    n = len(mine)
    return pl.pallas_call(
        functools.partial(add_kernel, n),
        in_specs=[vmem()] * (n + 1),
        out_specs=[vmem()] * n,
        out_shape=[jax.ShapeDtypeStruct(x.shape, BF) for x in mine],
        compiler_params=params(),
        name="add_each",
    )(*mine, theirs)


def sum_kernel(k, count, mine, theirs, *refs):
    total = mine[...] + theirs[k].astype(F32)
    for r in refs[:count]:
        total = total + r[...].astype(F32)
    refs[-1][...] = total.astype(BF)


def sum_piece(k, mine, theirs, parts, after):
    return pl.pallas_call(
        functools.partial(sum_kernel, k, len(parts)),
        in_specs=[vmem()] * (2 + len(parts)) + [anywhere()] * len(after),
        out_specs=vmem(),
        out_shape=jax.ShapeDtypeStruct(mine.shape, BF),
        compiler_params=params(),
        name="sum_piece",
    )(mine, theirs, *parts, *after)


def stacked_kernel(*refs):
    for i in range(refs[-1].shape[0]):
        refs[-1][i] = refs[i][...]


def stacked(parts, after):
    return pl.pallas_call(
        stacked_kernel,
        in_specs=[vmem()] * len(parts) + [anywhere()] * len(after),
        out_specs=vmem(),
        out_shape=jax.ShapeDtypeStruct((len(parts), *parts[0].shape), parts[0].dtype),
        compiler_params=params(),
        name="stacked",
    )(*parts, *after)


def relnew_kernel(nz, kinds, count, first, last, rel_ref, state_ref, *refs):
    arrays = refs[:count]
    rel_out, state_to, buf, sems = refs[-5:-1] if last else refs[-4:]
    state_out = refs[-1] if last else state_to
    w = buf.shape[2]
    state_out[...] = refs[count + (0 if first else 1)][...]
    z, x, edge = place()
    copies = []
    for i, (k, same, own, source, index) in enumerate(kinds):
        owner = 2 * lax.bitwise_xor(z, k) + (x if same else 1 - x)
        at = pl.ds(first_column(owner, edge if own else 1 - edge, w), w)
        grad = (arrays[source][...] if index is None else arrays[source][index]).astype(F32)
        state = state_ref[:, at] + jnp.sum(grad * grad, axis=0, keepdims=True) / grad.shape[0]
        state_out[:, at] = state
        buf[i] = rel_ref[:, at] - grad * (learn_rate / jnp.sqrt(state))
        copy = pltpu.make_async_copy(buf.at[i], rel_out.at[:, at], sems.at[i])
        copy.start()
        copies.append(copy)
    if last:
        copy = pltpu.make_async_copy(state_out, state_to, sems.at[len(kinds)])
        copy.start()
        copies.append(copy)
    for copy in copies:
        copy.wait()


def relnew(nz, relations, state, groups, before, last=False):
    dim, rels = relations.shape
    w = rels // (4 * nz)
    kinds, arrays = [], []
    for ks, same, own, parts in groups:
        one = not isinstance(parts, list)
        for i, k in enumerate(ks):
            kinds.append((k, same, own, len(arrays) + (0 if one else i), i if one else None))
        arrays += [parts] if one else parts
    count = len(kinds)
    start = [state] if before is None else list(before)
    return pl.pallas_call(
        functools.partial(relnew_kernel, nz, tuple(kinds), len(arrays), before is None, last),
        in_specs=[vmem()] * (2 + len(arrays))
        + ([anywhere()] if before else [])
        + [vmem()],
        out_specs=[anywhere(), anywhere() if last else vmem()],
        out_shape=[jax.ShapeDtypeStruct((dim, rels), F32), jax.ShapeDtypeStruct((1, rels), F32)],
        input_output_aliases={2 + len(arrays): 0} if before else {},
        scratch_shapes=[pltpu.VMEM((count, dim, w), F32), pltpu.SemaphoreType.DMA((count + 1,))]
        + ([pltpu.VMEM((1, rels), F32)] if last else []),
        compiler_params=params(),
        cost_estimate=cost(dim, dim),
        name="relnew",
    )(relations, state, *arrays, *start)


def relation_update(t, rel_ids, drel, acc, relations, state, send, finish):
    n = lax.axis_size("dom")
    dim, rels = relations.shape
    if n < 4 or n & (n - 1) or rels % (256 * n):
        total = lax.psum(relsum(t, rel_ids, drel, acc, rels), ("dom", "edge"))
        state = state + jnp.mean(total * total, axis=0)
        return relations - learn_rate * total / jnp.sqrt(state)[None, :], state, finish(send(drel), [])
    nz = n // 2
    mine_x, other_x = pieces(t, n, False, rel_ids, drel, acc, [])
    mine_s, other_s = pieces(t, n, True, rel_ids, drel, acc, [other_x])
    to_x = add_each(mine_x, across(other_x))
    theirs = across(other_s)
    down = range(nz - 1, -1, -1)
    from_x = {k: swapped(to_x[k], 1) for k in down}
    grads = send(to_x[0])
    addends = {k: [from_x[k]] for k in range(nz)}
    turned = []
    bit = 1
    while bit < nz:
        for k in reversed(range(bit, nz, 2 * bit)):
            after = [] if turned else grads[1:2]
            turned.append(sum_piece(k, mine_s[k], theirs, addends[k], after))
            addends[k ^ bit].append(swapped(turned[-1], 2 * bit))
        bit *= 2
    done = finish(grads, [turned[-1]])
    summed = sum_piece(0, mine_s[0], theirs, addends[0], [])
    got = [summed if k == 0 else swapped(summed, 2 * k) for k in range(nz)]
    got_x = [swapped(piece, 1) for piece in got]
    state = state.reshape(1, rels)
    ks = [0, *down[:-1]]
    mine = [got[k] for k in ks]
    mine_x = [got_x[k] for k in ks]
    there = across(stacked(mine, [done[2]]))
    new = relnew(nz, relations, state, [(ks, True, True, mine)], None)
    there_x = across(stacked(mine_x, [new[1]]))
    groups = [(ks, True, False, there), (ks, False, True, mine_x)]
    new = relnew(nz, relations, state, groups, new)
    groups = [(ks, False, False, there_x)]
    rel_new, state_new = relnew(nz, relations, state, groups, new, last=True)
    return rel_new, state_new.reshape(rels), done


def on_device(
    entities,
    entity_state,
    relations,
    relation_state,
    src_rows,
    rel_ids,
    dst_rows,
    counts,
    neg_blocks,
):
    rounds = src_rows.shape[0]
    rels = relations.shape[1]
    shape = src_rows.shape
    cnt, neg = counts.T, neg_blocks.T
    g_mine, g_other, drel, rel16, ent, state = first_round(
        cnt, neg, src_rows, dst_rows, rel_ids, entities, entity_state.reshape(1, -1), relations
    )
    acc = relsum(0, rel_ids, drel, None, rels)
    ent, state, low = update(ent, state, [g_mine, across(g_other)], [])
    rel = relvec(1, rel_ids, rel16)
    for t in range(1, rounds):
        far = shifted(low, -t)
        own = (low, across(low))
        query, query_t, source, s_hot, d_hot, *hots = source_side(
            t, shape, cnt, neg, src_rows, dst_rows, own, rel
        )
        far = held(far, [query, acc])
        far = (far, across(far))
        if t == rounds - 1:
            break
        near = near_products(query_t, far[0])
        gd_mine, gd_other, weight = target_grad(near, far[1], query, query_t, *hots)
        gd = sum_pair(gd_mine, across(gd_other))
        gs_mine, gs_other, drel = source_grad(
            t, shape, cnt, neg, gd, far, d_hot, query, weight, source, rel, s_hot
        )
        acc = relsum(t, rel_ids, drel, acc, rels)
        rel = relvec(t + 1, rel_ids, rel16)
        grads = [sum_pair(gs_mine, shifted(gd, t), F32), across(gs_other)]
        ent, state, low = update(ent, state, grads, [rel])
    drel, dsource, dterm = last_terms(t, shape, cnt, neg, far, query, query_t, d_hot, source, rel)

    def send(after):
        gs_mine, gs_other, gd_mine, gd_other = both_grads(after, dsource, s_hot, dterm, hots[0])
        gd = sum_pair(gd_mine, across(gd_other))
        return [gs_mine, across(gs_other), shifted(gd, t)]

    def finish(grads, after):
        (mine,) = update(ent, state, grads, after, last=True)
        return whole_partition(mine, across(mine))

    rel_new, rel_state, done = relation_update(
        t, rel_ids, drel, acc, relations, relation_state, send, finish
    )
    return (done[0], done[1].reshape(-1), rel_new, rel_state)


def solution(mesh):
    return jax.shard_map(
        on_device,
        mesh=mesh,
        in_specs=(
            P(None, ("groups", "dom")),
            P(("groups", "dom")),
            P(None, "groups"),
            P("groups"),
            P(None, ("groups", "dom", "edge"), None),
            P(None, ("groups", "dom", "edge"), None),
            P(None, ("groups", "dom", "edge"), None),
            P(None, ("groups", "dom", "edge")),
            P(None, ("groups", "dom", "edge")),
        ),
        out_specs=(
            P(None, ("groups", "dom")),
            P(("groups", "dom")),
            P(None, "groups"),
            P("groups"),
        ),
        check_vma=False,
    )
```
